128 devices in a mesh: pipe: 2 (over core), expert: 16 (over y, z), tensor: 4 (over x).
Axes of the slice: x: 4, y: 4, z: 4, core: 2. Of those that a mesh axis runs over, the one named last changes fastest.
Arguments:
- tokens: bfloat16 [2, 2048, 768], P(None, 'expert'), may hold values from -6 to 6
- cotangent: bfloat16 [2, 2048, 768], P(None, 'expert'), may hold values from -6 to 6
- routes: int32 [2, 2, 2048, 2], P('pipe', None, 'expert'), may hold values from 0 to 31, all different within a row; in each aligned block of 128 rows (0 to 127, 128 to 255, ..., all dimensions but the last counted through in order) at most 10 rows name the same one
- buckets: int32 [128, 128], replicated, may hold values from 0 to 31
- gain_attn: float32 [2, 768], P('pipe'), may hold values from 0.5 to 1.5
- w_qkv: bfloat16 [2, 768, 2304], P('pipe', None, 'tensor'), may hold values from -0.21875 to 0.21875
- w_attn_out: bfloat16 [2, 768, 768], P('pipe', 'tensor'), may hold values from -0.875 to 0.875
- rel_table: bfloat16 [2, 12, 32], P('pipe', 'tensor'), may hold values from -4 to 4
- gain_moe: float32 [2, 768], P('pipe'), may hold values from 0.5 to 1.5
- w_router: bfloat16 [2, 768, 32], P('pipe'), may hold values from -0.15625 to 0.15625
- w_expert_in: bfloat16 [2, 32, 768, 3072], P('pipe', 'expert', None, 'tensor'), may hold values from -0.21875 to 0.21875
- w_expert_out: bfloat16 [2, 32, 3072, 768], P('pipe', 'expert', 'tensor'), may hold values from -0.15625 to 0.15625
Outputs:
- activations: bfloat16 [2, 2, 2048, 768], P('pipe', None, 'expert')
- input_grad: float32 [2, 2, 2048, 768], P('pipe', None, 'expert')
- grad_gain_attn: float32 [2, 768], P('pipe')
- grad_w_qkv: float32 [2, 768, 2304], P('pipe', None, 'tensor')
- grad_w_attn_out: float32 [2, 768, 768], P('pipe', 'tensor')
- grad_rel_table: float32 [2, 12, 32], P('pipe', 'tensor')
- grad_gain_moe: float32 [2, 768], P('pipe')
- grad_w_router: float32 [2, 768, 32], P('pipe')
- grad_w_expert_in: float32 [2, 32, 768, 3072], P('pipe', 'expert', None, 'tensor')
- grad_w_expert_out: float32 [2, 32, 3072, 768], P('pipe', 'expert', 'tensor')
The draws below stay inside these ranges and needn't reach their ends.
Inputs may be any that keep to these rules, and one draw needn't show every extreme that they name: `routes`: for each section and micro-batch, the 128 rows of one device name every expert at most 10 times, a bound that some block reaches.
All inputs are finite; a program needn't handle non-finite values.
Results may differ from the reference program's by a relative error of at most 0.035.
Values may be sent and summed in bfloat16 or wider, within the bound.
No kernel may reach another device: no remote copies, remote signals or barrier semaphores. Data moves between devices by JAX's collectives and lax.ppermute only.
A program may use at most 128 MiB of HBM per device.

```python
import math
import jax
import jax.numpy as jnp
import numpy as np
from jax import lax

D = 768
HEADS = 12
HEAD_DIM = 64
FF = 3072
BUCKETS = 32
MB = 2
SEQ = 128
EXPERTS = 32
TOKENS = 2048
CAP = 10
N_EXPERT = 16


def touch_ends(drawn, key, least, high):
    dims = drawn.shape
    spot = [jax.random.randint(jax.random.fold_in(key, axis), (), 0, dims[axis]) for axis in range(len(dims))]
    drawn = drawn.at[tuple(spot)].set(least)
    longest = dims.index(max(dims))
    spot[longest] = (spot[longest] + 1) % dims[longest]
    return drawn.at[tuple(spot)].set(high)


def level_of(rng, dims, pieces, smallest, top_value):
    def one(axis_at, shards_of):
        steps = jax.random.uniform(jax.random.fold_in(jax.random.fold_in(rng, 6), axis_at), (shards_of,), jnp.float32, smallest / len(pieces), top_value / len(pieces))
        return jnp.repeat(jnp.exp(steps), dims[axis_at] // shards_of).reshape((-1,) + (1,) * (len(dims) - axis_at - 1))

    loudness = one(*pieces[0])
    for cut in pieces[1:]:
        loudness = loudness * one(*cut)
    return loudness


def shared_out(rng, own, number, rows, number_of, top, bound, skew):
    order = jax.random.permutation(rng, number_of)
    crowded, ordinary = load_shares(number_of, rows * top, bound, skew, True), load_shares(number_of, rows * top, bound, skew, False)
    places = jnp.arange(number_of)

    def named(sizes, turn):
        used = int((sizes > 0).sum())
        fixed = max(1, used // 4)
        passed = fixed + (places - fixed + turn * (used - fixed)) % max(1, number_of - fixed)
        return jnp.zeros((number_of,), jnp.int32).at[order[jnp.where(places < fixed, places, passed)]].set(jnp.asarray(sizes, jnp.int32))

    sizes = jnp.where(number % 4 == 0, named(crowded, number // 4), named(ordinary, number - number // 4 - 1))
    mixed = jax.random.permutation(jax.random.fold_in(own, 3), number_of)
    giver, sink = mixed[0:number_of // 2 * 2:2], mixed[1:number_of // 2 * 2:2]
    slack = jnp.minimum(sizes[giver] - 1, bound - sizes[sink]) // 2
    slack = jnp.where((giver == order[0]) | (sink == order[0]) | (sizes[sink] == 0), 0, jnp.maximum(slack, 0))
    passed = jax.random.randint(jax.random.fold_in(own, 4), (number_of // 2,), 0, 1 << 20) % (slack + 1)
    sizes = sizes.at[giver].add(-passed).at[sink].add(passed)
    members = jnp.searchsorted(jnp.cumsum(sizes), jnp.arange(rows * top), side="right").astype(jnp.int32)
    grid = members.reshape(top, rows).T
    grid = grid[jax.random.permutation(jax.random.fold_in(own, 1), rows)]
    turn = jax.random.randint(jax.random.fold_in(own, 2), (rows, 1), 0, top)
    return jnp.take_along_axis(grid, (jnp.arange(top)[None, :] + turn) % top, axis=1)


def load_shares(amount, total, limit, lean, full):
    loads = [(1 << 20) // math.isqrt(rank ** lean) + 1 for rank in range(1, amount + 1)]
    largest = limit if full else min(limit, max(-(-total // amount), total * loads[0] // sum(loads)))
    least = 1 if total - largest >= amount - 1 else 0
    given, spare = [largest] + [least] * (amount - 1), total - largest - least * (amount - 1)
    while spare > 0:
        movable = [i for i in range(1, amount) if given[i] < largest] or [i for i in range(1, amount) if given[i] < limit]
        whole, left = sum([loads[i] for i in movable]), spare
        for i in movable:
            extra = min(limit - given[i], max(1, left * loads[i] // whole), spare)
            given[i] = given[i] + extra
            spare = spare - extra
    return np.array(given)


def centred(key, shape, spread, reach, pieces=(), kind=jnp.bfloat16):
    values = jax.random.normal(key, shape, jnp.float32) * spread
    if len(pieces) > 0:
        values = level_of(key, shape, pieces, -0.22, 0.18) * values
    return jnp.clip(values, min=-reach, max=reach).astype(kind)


def setup_inputs(seed: int = 0) -> dict:
    seeds = jax.random.split(jax.random.key(seed), 13)
    tokens = centred(seeds[0], (MB, TOKENS, D), 1.0, 6.0, ((1, 16),))
    cotangent = centred(seeds[1], (MB, TOKENS, D), 1.0, 6.0, ((1, 16),))
    routes_keys = jax.random.split(jax.random.fold_in(seeds[2], 1), 2 * MB * TOKENS // SEQ)
    routes_turns = jax.random.permutation(jax.random.fold_in(seeds[2], 3), 2 * MB * TOKENS // SEQ)
    routes = jax.vmap(lambda own, number: shared_out(jax.random.fold_in(seeds[2], 2), own, number, SEQ, EXPERTS, 2, CAP, 1))(routes_keys, routes_turns).reshape((2, MB, TOKENS, 2))
    buckets = touch_ends(jax.random.randint(seeds[3], (SEQ, SEQ), 0, BUCKETS), jax.random.fold_in(seeds[3], 1), 0, BUCKETS - 1).astype(jnp.int32)
    gain_attn = jnp.clip(1.0 + 0.1 * jax.random.normal(seeds[4], (2, D), jnp.float32), 0.5, 1.5)
    w_qkv = centred(seeds[5], (2, D, 3 * HEADS * HEAD_DIM), D ** -0.5, 0.21875, ((0, 2), (2, 4)))
    w_attn_out = centred(seeds[6], (2, HEADS * HEAD_DIM, D), (HEADS * HEAD_DIM // 16) ** -0.5, 0.875, ((0, 2), (1, 4)))
    rel_table = centred(seeds[7], (2, HEADS, BUCKETS), 1.0, 4.0, ((0, 2), (1, 4)))
    gain_moe = jnp.clip(1.0 + 0.1 * jax.random.normal(seeds[8], (2, D), jnp.float32), 0.5, 1.5)
    w_router = centred(seeds[9], (2, D, EXPERTS), (2 * D) ** -0.5, 0.15625, ((0, 2),))
    w_expert_in = centred(seeds[10], (2, EXPERTS, D, FF), D ** -0.5, 0.21875, ((0, 2), (1, 16), (3, 4)))
    w_expert_out = centred(seeds[11], (2, EXPERTS, FF, D), (FF // 2) ** -0.5, 0.15625, ((0, 2), (1, 16), (2, 4)))
    return {"tokens": tokens, "cotangent": cotangent, "routes": routes, "buckets": buckets, "gain_attn": gain_attn, "w_qkv": w_qkv, "w_attn_out": w_attn_out, "rel_table": rel_table, "gain_moe": gain_moe, "w_router": w_router, "w_expert_in": w_expert_in, "w_expert_out": w_expert_out}


EPSILON = 1e-06
HIGHEST = lax.Precision.HIGHEST

@jax.custom_vjp
def low(v):
    return lax.optimization_barrier(v.astype(jnp.bfloat16)).astype(jnp.float32)

@jax.custom_vjp
def low_back(v):
    return v

def low_keep(v):
    return (low(v), None)

def low_pass(kept, grad):
    return (grad,)

def back_keep(v):
    return (v, None)

def back_low(kept, grad):
    return (low(grad),)
low.defvjp(low_keep, low_pass)
low_back.defvjp(back_keep, back_low)

def norm_rows(values, gain_vec):
    inverse = lax.rsqrt(lax.optimization_barrier(jnp.mean(values * values, axis=-1, keepdims=True)) + EPSILON)
    return values * inverse * gain_vec

def slot_targets(route_ids):
    flat_ids = route_ids.reshape(N_EXPERT, 2 * SEQ)
    one_hot = (flat_ids[:, :, None] == jnp.arange(EXPERTS, dtype=jnp.int32)[None, None, :]).astype(jnp.int32)
    before = jnp.cumsum(one_hot, axis=1) - 1
    slot_ids = lax.optimization_barrier(jnp.sum(one_hot * before, axis=2)).astype(jnp.int32)
    block_ids = jnp.arange(N_EXPERT, dtype=jnp.int32)[:, None]
    return ((flat_ids * N_EXPERT + block_ids) * CAP + slot_ids).reshape(-1).astype(jnp.int32)

def moe_layer(inputs, route_ids, buckets, gain_attn, w_qkv, w_attn_out, rel_table, gain_moe, w_router, w_expert_in, w_expert_out):
    normed = low(norm_rows(inputs, gain_attn))
    projected = low(low_back(jnp.dot(normed, w_qkv, precision=HIGHEST)))
    split_qkv = projected.reshape(N_EXPERT, SEQ, HEADS, 3, HEAD_DIM)
    scores = jnp.einsum('bqhd,bkhd->bhqk', split_qkv[:, :, :, 0], split_qkv[:, :, :, 1], precision=HIGHEST)
    scores = scores * HEAD_DIM ** (-0.5) + jnp.take(rel_table, buckets, axis=1)[None]
    positions = jnp.arange(SEQ)
    causal = positions[:, None] >= positions[None, :]
    scores = low_back(jnp.where(causal, scores, -1e+30))
    probs_low = low(jax.nn.softmax(scores, axis=-1))
    attended = jnp.einsum('bhqk,bkhd->bqhd', probs_low, split_qkv[:, :, :, 2], precision=HIGHEST)
    attended = low(low_back(attended.reshape(TOKENS, HEADS * HEAD_DIM)))
    hidden = inputs + low_back(jnp.dot(attended, w_attn_out, precision=HIGHEST))
    moe_normed = low(norm_rows(hidden, gain_moe))
    logits = low_back(jnp.dot(moe_normed, w_router, precision=HIGHEST))
    gate_vals = jax.nn.softmax(jnp.take_along_axis(logits, route_ids, axis=1), axis=1)
    targets = slot_targets(route_ids)
    slot_rows = jnp.zeros((EXPERTS * N_EXPERT * CAP, D), inputs.dtype).at[targets].set(jnp.repeat(moe_normed, 2, axis=0))
    slot_rows = slot_rows.reshape(EXPERTS, N_EXPERT * CAP, D)
    pre_act = low_back(jnp.einsum('erd,edf->erf', slot_rows, w_expert_in, precision=HIGHEST))
    act_low = low(jax.nn.gelu(pre_act))
    expert_out = low_back(jnp.einsum('erf,efd->erd', act_low, w_expert_out, precision=HIGHEST))
    picked = expert_out.reshape(-1, D)[targets].reshape(TOKENS, 2, D)
    return hidden + lax.optimization_barrier(jnp.sum(gate_vals[:, :, None] * picked, axis=1))

def reference(tokens, cotangent, routes, buckets, gain_attn, w_qkv, w_attn_out, rel_table, gain_moe, w_router, w_expert_in, w_expert_out):
    arrays = (gain_attn, w_qkv, w_attn_out, rel_table, gain_moe, w_router, w_expert_in, w_expert_out)

    def run_section(section_index):

        def run_all(inputs, params):
            return jnp.stack([moe_layer(inputs[micro_index], routes[section_index, micro_index], buckets, *params) for micro_index in range(MB)])
        return run_all
    params_first = tuple((array_item[0].astype(jnp.float32) for array_item in arrays))
    params_second = tuple((array_item[1].astype(jnp.float32) for array_item in arrays))
    out_first, pull_first = jax.vjp(run_section(0), tokens.astype(jnp.float32), params_first)
    middle = low(out_first)
    out_second, pull_second = jax.vjp(run_section(1), middle, params_second)
    grad_middle, grads_second = pull_second(cotangent.astype(jnp.float32))
    grad_first, grads_first = pull_first(low(grad_middle))
    activations = jnp.stack([middle, out_second]).astype(jnp.bfloat16)
    input_grad = jnp.stack([grad_first, grad_middle])
    stacked = [jnp.stack([first_grad, second_grad]) for first_grad, second_grad in zip(grads_first, grads_second)]
    return (activations, input_grad, stacked[0], stacked[1], stacked[2], stacked[3], stacked[4], stacked[5], stacked[6], stacked[7])
```

```python
import jax
import jax.numpy as jnp
from jax import lax
from jax.sharding import PartitionSpec as P

EPSILON = 1e-06
F32 = jnp.float32
BF16 = jnp.bfloat16


def norm_rows(values, gain_vec):
    inverse = lax.rsqrt(jnp.mean(values * values, axis=-1, keepdims=True) + EPSILON)
    return (values * inverse * gain_vec, inverse)


def norm_back(values, inverse, gain_vec, upstream):
    weighted = upstream * gain_vec
    inner_mean = jnp.mean(weighted * values, axis=-1, keepdims=True)
    return inverse * weighted - values * inverse**3 * inner_mean


def dot(a, b):
    return jnp.dot(a, b, preferred_element_type=F32)


def swap(value):
    return lax.ppermute(value, "pipe", [(0, 1), (1, 0)])


def tensor_sum(value):
    count = lax.axis_size("tensor")
    parts = [
        lax.ppermute(value, "tensor", [(i, (i + by) % count) for i in range(count)])
        for by in range(1, count)
    ]
    return sum([part.astype(F32) for part in parts], value.astype(F32))


def exchange(rows, slots):
    blocks = rows.reshape(-1, slots, rows.shape[1])
    moved = lax.all_to_all(blocks, ("pipe", "expert"), split_axis=0, concat_axis=0, tiled=True)
    return moved.reshape(rows.shape)


def attention(inputs, weights):
    gain, qkv_weight, out_weight, rel_bias, causal = weights
    seq_len = inputs.shape[0]
    heads = rel_bias.shape[0]
    head_dim = qkv_weight.shape[1] // (3 * heads)
    normed, inverse = norm_rows(inputs, gain)
    normed_low = normed.astype(BF16)
    projected = dot(normed_low, qkv_weight).astype(BF16)
    split = projected.reshape(seq_len, heads, 3, head_dim)
    scores = jnp.einsum("qhd,khd->hqk", split[:, :, 0], split[:, :, 1], preferred_element_type=F32)
    scores = jnp.where(causal, scores * head_dim**-0.5 + rel_bias, -1e30)
    probs = jax.nn.softmax(scores, axis=-1)
    probs_low = probs.astype(BF16)
    attended = jnp.einsum("hqk,khd->qhd", probs_low, split[:, :, 2], preferred_element_type=F32)
    attended = attended.reshape(seq_len, -1).astype(BF16)
    partial_out = dot(attended, out_weight).astype(BF16)
    return partial_out, (inputs, inverse, normed_low, split, probs, probs_low, attended)


def attention_back(grad_hidden, saved, weights, bucket_hot):
    gain, qkv_weight, out_weight, rel_bias, causal = weights
    inputs, inverse, normed_low, split, probs, probs_low, attended = saved
    seq_len = inputs.shape[0]
    heads = rel_bias.shape[0]
    head_dim = split.shape[-1]
    scale = head_dim**-0.5
    grad_low = grad_hidden.astype(BF16)
    grad_out_weight = dot(grad_low.T, attended)
    grad_heads = dot(grad_low, out_weight.T).astype(BF16).reshape(seq_len, heads, head_dim)
    grad_probs = jnp.einsum("qhd,khd->hqk", grad_heads, split[:, :, 2], preferred_element_type=F32)
    grad_values = jnp.einsum("hqk,qhd->khd", probs_low, grad_heads, preferred_element_type=F32)
    inner = jnp.sum(probs * grad_probs, axis=-1, keepdims=True)
    grad_scores = (probs * (grad_probs - inner)).astype(BF16)
    grad_table = jnp.einsum(
        "hq,qb->hb", grad_scores.reshape(heads, -1), bucket_hot, preferred_element_type=F32
    )
    grad_queries = scale * jnp.einsum(
        "hqk,khd->qhd", grad_scores, split[:, :, 1], preferred_element_type=F32
    )
    grad_keys = scale * jnp.einsum(
        "hqk,qhd->khd", grad_scores, split[:, :, 0], preferred_element_type=F32
    )
    grad_qkv = jnp.stack([grad_queries, grad_keys, grad_values], axis=2)
    grad_qkv = grad_qkv.reshape(seq_len, -1).astype(BF16)
    grad_normed = tensor_sum(dot(grad_qkv, qkv_weight.T).astype(BF16))
    grad_qkv_weight = dot(normed_low.T, grad_qkv)
    grad_gain = jnp.sum(grad_normed * inputs * inverse, axis=0)
    grad_inputs = grad_hidden + norm_back(inputs, inverse, gain, grad_normed)
    return grad_inputs, grad_qkv_weight, grad_out_weight, grad_table, grad_gain


def route(hidden, gain, router_weight, route_ids, capacity, owners):
    seq_len = hidden.shape[0]
    experts = router_weight.shape[1]
    per_owner = experts // owners
    moe_normed, inverse = norm_rows(hidden, gain)
    moe_low = moe_normed.astype(BF16)
    logits = dot(moe_low, router_weight)
    hot = route_ids[:, :, None] == jnp.arange(experts, dtype=jnp.int32)
    chosen = jnp.sum(jnp.where(hot, logits[:, None, :], 0.0), axis=-1)
    gates = jax.nn.softmax(chosen, axis=1)
    per_row = jnp.sum(hot.astype(BF16), axis=1)
    positions = jnp.arange(seq_len)
    earlier = (positions[:, None] > positions[None, :]).astype(BF16)
    before = dot(earlier, per_row)
    slot = jnp.sum(jnp.where(hot, before[:, None, :], 0.0), axis=-1).astype(jnp.int32)
    place = (route_ids % per_owner) * owners + route_ids // per_owner
    targets = place * capacity + slot
    rows = jnp.arange(experts * capacity, dtype=jnp.int32)
    slot_hot = (targets.T[:, :, None] == rows).astype(BF16)
    return moe_low, inverse, gates, hot, slot_hot


def send_rows(moe_low, slot_hot):
    return dot((slot_hot[0] + slot_hot[1]).T, moe_low).astype(BF16)


def send_grads(upstream_low, slot_hot, gates):
    gate_rows = jnp.sum(slot_hot.astype(F32) * gates.T[:, :, None], axis=(0, 1))
    return (dot((slot_hot[0] + slot_hot[1]).T, upstream_low) * gate_rows[:, None]).astype(BF16)


def expert_forward(rows, weight_in, weight_out):
    pre_act = dot(rows, weight_in)
    act_low = jax.nn.gelu(pre_act).astype(BF16)
    return dot(act_low, weight_out).astype(BF16), (rows, pre_act, act_low)


def expert_back(grads, saved, weight_in, weight_out):
    rows, pre_act, act_low = saved
    grad_act = dot(grads, weight_out.T)
    inner = jnp.sum(grad_act * act_low.astype(F32), axis=1)
    grad_pre = jax.vjp(jax.nn.gelu, pre_act)[1](grad_act)[0].astype(BF16)
    grad_rows = dot(grad_pre, weight_in.T).astype(BF16)
    grad_weight_out = dot(act_low.T, grads)
    grad_weight_in = dot(rows.T, grad_pre)
    tail = jnp.broadcast_to(inner.astype(BF16)[:, None], (rows.shape[0], 128))
    return jnp.concatenate([grad_rows, tail], axis=1), grad_weight_in, grad_weight_out


def moe_back(upstream, back, hidden, routed, gain, router_weight):
    moe_low, inverse, gates, hot, slot_hot = routed
    width = hidden.shape[1]
    picked = [dot(slot_hot[k], back) for k in range(2)]
    grad_moe = picked[0][:, :width] + picked[1][:, :width]
    inner = jnp.concatenate([value[:, width : width + 1] for value in picked], axis=1)
    packed = jnp.concatenate([grad_moe, jnp.pad(inner, ((0, 0), (0, 126)))], axis=1)
    packed = tensor_sum(packed.astype(BF16))
    grad_moe, inner = packed[:, :width], packed[:, width : width + 2]
    grad_chosen = inner - gates * jnp.sum(inner, axis=1, keepdims=True)
    grad_logits = jnp.sum(jnp.where(hot, grad_chosen[:, :, None], 0.0), axis=1).astype(BF16)
    grad_router = dot(moe_low.T, grad_logits)
    grad_moe = grad_moe + dot(grad_logits, router_weight.T)
    grad_gain = jnp.sum(grad_moe * hidden * inverse, axis=0)
    grad_hidden = upstream + norm_back(hidden, inverse, gain, grad_moe)
    return grad_hidden, grad_router, grad_gain


def shards(
    tokens,
    cotangent,
    routes,
    buckets,
    gain_attn,
    w_qkv,
    w_attn_out,
    rel_table,
    gain_moe,
    w_router,
    w_expert_in,
    w_expert_out,
):
    core = lax.axis_index("pipe")
    owners = lax.axis_size("expert")
    seq_len = tokens.shape[1]
    experts = w_router.shape[2]
    capacity = 5 * seq_len // (2 * experts)
    first = core == 0

    def both(own):
        other = swap(own)
        return jnp.where(first, own, other), jnp.where(first, other, own)

    qkv_weights = both(w_qkv[0])
    out_weights = both(w_attn_out[0])
    gains = both(jnp.concatenate([gain_attn, gain_moe], axis=0))
    tables = both(rel_table[0])
    router_weights = both(w_router[0])

    def mine_and_theirs(own):
        mine = jnp.where(first, own[0], own[1])
        theirs = jnp.where(first, own[1], own[0])
        other = swap(theirs)
        return jnp.where(first, mine, other), jnp.where(first, other, mine)

    route_ids = mine_and_theirs(routes[0])
    in_weights = mine_and_theirs(w_expert_in[0])
    out_expert = mine_and_theirs(w_expert_out[0])

    inputs = jnp.where(first, tokens[0], tokens[1])
    last_grad = jnp.where(first, cotangent[0], cotangent[1])
    bucket_hot = (
        buckets.reshape(-1)[:, None] == jnp.arange(rel_table.shape[2], dtype=jnp.int32)[None, :]
    ).astype(BF16)
    positions = jnp.arange(seq_len)
    causal = positions[:, None] >= positions[None, :]

    def attention_weights(section):
        table = tables[section]
        rel_bias = jnp.einsum("hb,qb->hq", table, bucket_hot, preferred_element_type=F32)
        rel_bias = rel_bias.reshape(-1, seq_len, seq_len)
        return (gains[section][0], qkv_weights[section], out_weights[section], rel_bias, causal)

    attn_weights = [attention_weights(0), attention_weights(1)]

    def routed(hidden, section):
        return route(
            hidden, gains[section][1], router_weights[section], route_ids[section], capacity, owners
        )

    def combined(back, now):
        picked = [dot(now[4][k], back) * now[2][:, k : k + 1] for k in range(2)]
        return tensor_sum((picked[0] + picked[1]).astype(BF16))

    inputs0 = inputs.astype(F32)
    partial_out, attn0 = attention(inputs0, attn_weights[0])
    hidden0 = inputs0 + tensor_sum(partial_out)
    routed0 = routed(hidden0, 0)
    rows0 = exchange(send_rows(routed0[0], routed0[4]), capacity)
    out0, expert0 = expert_forward(rows0, in_weights[0], out_expert[0])
    mix0 = combined(exchange(out0, capacity), routed0)
    act0 = (hidden0 + mix0).astype(BF16)

    inputs1 = act0.astype(F32)
    partial_out, attn1 = attention(inputs1, attn_weights[1])
    hidden1 = inputs1 + tensor_sum(partial_out)
    routed1 = routed(hidden1, 1)
    sent = send_rows(routed1[0], routed1[4])
    sent_grads = send_grads(last_grad, routed1[4], routed1[2])
    both_rows = exchange(jnp.concatenate([sent, sent_grads], axis=1), capacity)
    width = tokens.shape[2]
    rows1, grads1 = both_rows[:, :width], both_rows[:, width:]
    out1, expert1 = expert_forward(rows1, in_weights[1], out_expert[1])
    back1, grad_in1, grad_out1 = expert_back(grads1, expert1, in_weights[1], out_expert[1])
    returned = exchange(jnp.concatenate([back1, out1], axis=1), capacity)
    back1, out1 = returned[:, : back1.shape[1]], returned[:, back1.shape[1] :]
    upstream1 = last_grad.astype(F32)
    grad_hidden1, grad_router1, grad_moe_gain1 = moe_back(
        upstream1, back1, hidden1, routed1, gains[1][1], router_weights[1]
    )
    mix1 = combined(out1, routed1)
    act1 = (hidden1 + mix1).astype(BF16)
    grad_inputs1, grad_qkv1, grad_attn_out1, grad_table1, grad_gain1 = attention_back(
        grad_hidden1, attn1, attn_weights[1], bucket_hot
    )

    upstream_low = grad_inputs1.astype(BF16)
    grads0 = exchange(send_grads(upstream_low, routed0[4], routed0[2]), capacity)
    back0, grad_in0, grad_out0 = expert_back(grads0, expert0, in_weights[0], out_expert[0])
    back0 = exchange(back0, capacity)
    upstream0 = upstream_low.astype(F32)
    grad_hidden0, grad_router0, grad_moe_gain0 = moe_back(
        upstream0, back0, hidden0, routed0, gains[0][1], router_weights[0]
    )
    grad_inputs0, grad_qkv0, grad_attn_out0, grad_table0, grad_gain0 = attention_back(
        grad_hidden0, attn0, attn_weights[0], bucket_hot
    )

    def packed(grad_qkv, grad_attn_out, grad_router, grad_gain, grad_moe_gain, grad_table):
        table = jnp.pad(grad_table.reshape(-1), (0, width - grad_table.size))
        columns = jnp.stack([grad_gain, grad_moe_gain, table], axis=1)
        used = grad_router.shape[1] + 3
        columns = jnp.pad(columns, ((0, 0), (0, 128 - used)))
        parts = [grad_qkv, grad_attn_out, grad_router, columns]
        return jnp.concatenate(parts, axis=1).astype(BF16)

    shared0 = packed(grad_qkv0, grad_attn_out0, grad_router0, grad_gain0, grad_moe_gain0, grad_table0)
    shared1 = packed(grad_qkv1, grad_attn_out1, grad_router1, grad_gain1, grad_moe_gain1, grad_table1)
    mine = jnp.where(first, shared0, shared1)
    other = swap(jnp.where(first, shared1, shared0))
    pair = (mine.astype(F32) + other.astype(F32)).astype(BF16)
    blocks = pair.reshape(owners, -1, pair.shape[1])
    blocks = lax.all_to_all(blocks, "expert", split_axis=0, concat_axis=0, tiled=True)
    summed = jnp.sum(blocks.astype(F32), axis=0).astype(BF16)
    blocks = jnp.broadcast_to(summed[None], blocks.shape)
    total = lax.all_to_all(blocks, "expert", split_axis=0, concat_axis=0, tiled=True)
    total = total.reshape(pair.shape).astype(F32)
    qkv_end = w_qkv.shape[2]
    out_end = qkv_end + w_attn_out.shape[1]
    router_end = out_end + experts
    grad_qkv = total[:, :qkv_end]
    grad_attn_out = total[:, qkv_end:out_end].T
    grad_router = total[:, out_end:router_end]
    grad_gain = total[:, router_end]
    grad_moe_gain = total[:, router_end + 1]
    grad_table = total[: rel_table[0].size, router_end + 2].reshape(rel_table[0].shape)

    def placed(from0, from1, cast):
        mine = jnp.where(first, from0, from1)
        other = swap(jnp.where(first, from1, from0).astype(cast)).astype(mine.dtype)
        return jnp.stack([jnp.where(first, mine, other), jnp.where(first, other, mine)])

    activations = placed(act0, act1, BF16)
    input_grad = placed(grad_inputs0, grad_inputs1, F32)
    grad_in = placed(grad_in0, grad_in1, BF16)
    grad_out = placed(grad_out0, grad_out1, BF16)
    return (
        activations[None],
        input_grad[None],
        grad_gain[None],
        grad_qkv[None],
        grad_attn_out[None],
        grad_table[None],
        grad_moe_gain[None],
        grad_router[None],
        grad_in[None],
        grad_out[None],
    )


def solution(mesh):
    in_specs = (
        P(None, "expert", None),
        P(None, "expert", None),
        P("pipe", None, "expert", None),
        P(),
        P("pipe", None),
        P("pipe", None, "tensor"),
        P("pipe", "tensor", None),
        P("pipe", "tensor", None),
        P("pipe", None),
        P("pipe", None, None),
        P("pipe", "expert", None, "tensor"),
        P("pipe", "expert", "tensor", None),
    )
    out_specs = (
        P("pipe", None, "expert", None),
        P("pipe", None, "expert", None),
        P("pipe", None),
        P("pipe", None, "tensor"),
        P("pipe", "tensor", None),
        P("pipe", "tensor", None),
        P("pipe", None),
        P("pipe", None, None),
        P("pipe", "expert", None, "tensor"),
        P("pipe", "expert", "tensor", None),
    )
    return jax.shard_map(shards, mesh=mesh, in_specs=in_specs, out_specs=out_specs, check_vma=False)
```

```python
import jax
import jax.numpy as jnp
from jax import lax
from jax.experimental import pallas as pl
from jax.experimental.pallas import tpu as pltpu
from jax.sharding import PartitionSpec as P

EPSILON = 1e-06
F32 = jnp.float32
BF16 = jnp.bfloat16
SEQ = 128
D = 768
HEADS = 3
HEAD_DIM = 64
QKV = 3 * HEADS * HEAD_DIM
HEAD_COLS = HEADS * HEAD_DIM
EXPERTS = 32
OWNERS = 16
BUCKETS = 32
MAIN = 8 * EXPERTS
ROWS = 10 * EXPERTS
WIDE = D + 256
SCALE = HEAD_DIM**-0.5
GELU_C = 0.7978845608028654
GELU_A = 0.044715
VMEM = pl.BlockSpec(memory_space=pltpu.VMEM)
SMEM = pl.BlockSpec(memory_space=pltpu.SMEM)
ANY = pl.BlockSpec(memory_space=pl.ANY)


def shape(*dims, dtype=F32):
    return jax.ShapeDtypeStruct(dims, dtype)


def low(*dims):
    return jax.ShapeDtypeStruct(dims, BF16)


def kernel_call(body, name, inputs, specs, outputs, scratch=(), out_specs=None, micros=4):
    return pl.pallas_call(
        body,
        out_shape=tuple(outputs),
        in_specs=list(specs),
        out_specs=tuple(out_specs or [VMEM] * len(outputs)),
        scratch_shapes=list(scratch),
        compiler_params=pltpu.CompilerParams(vmem_limit_bytes=18 * 2**20),
        cost_estimate=pl.CostEstimate(
            flops=int(micros * 4e8), bytes_accessed=int(micros * 2e6), transcendentals=0
        ),
        name=name,
    )(*inputs)


def dot(a, b):
    return jnp.dot(a, b, preferred_element_type=F32)


def dot_nt(a, b):
    return lax.dot_general(a, b, (((1,), (1,)), ((), ())), preferred_element_type=F32)


def dot_tn(a, b):
    return lax.dot_general(a, b, (((0,), (0,)), ((), ())), preferred_element_type=F32)


def iota(dims, axis):
    return lax.broadcasted_iota(jnp.int32, dims, axis)


def chosen(flag, own, other):
    return jnp.where(flag == 1, own, other)


def fetch(flag, own, other, target, semaphore):
    @pl.when(flag == 1)
    def _():
        pltpu.make_async_copy(own, target, semaphore).start()

    @pl.when(flag != 1)
    def _():
        pltpu.make_async_copy(other, target, semaphore).start()


def fetched(other, target, semaphore):
    pltpu.make_async_copy(other, target, semaphore).wait()


def norm(values):
    return lax.rsqrt(jnp.mean(values * values, axis=-1, keepdims=True) + EPSILON)


def norm_back(values, inverse, gain, upstream):
    weighted = upstream * gain
    inner = jnp.mean(weighted * values, axis=-1, keepdims=True)
    return inverse * weighted - values * (inverse * inverse * inverse) * inner


def total(refs):
    value = refs[0][...].astype(F32)
    for ref in refs[1:]:
        value = value + ref[...].astype(F32)
    return value


def gelu_parts(value):
    square = value * value
    tanh = jnp.tanh(GELU_C * value * (1.0 + GELU_A * square))
    return square, tanh


def pack(rows):
    spread = (iota((MAIN, EXPERTS), 0) // 8 == iota((MAIN, EXPERTS), 1)).astype(BF16)
    place = iota((MAIN, 128), 0) % 8
    parts = [rows[:MAIN]]
    for late in range(2):
        start = MAIN + late * EXPERTS
        copies = dot(spread, rows[start : start + EXPERTS])
        piece = jnp.zeros((MAIN, 128), F32)
        for r in range(D // 128):
            piece = jnp.where(place == r, copies[:, r * 128 : (r + 1) * 128], piece)
        parts.append(piece.astype(BF16))
    return jnp.concatenate(parts, axis=1)


def unpack(block):
    count = D // 128
    dims = (count * EXPERTS, MAIN)
    row = iota(dims, 0)
    gather = (iota(dims, 1) == (row % EXPERTS) * 8 + row // EXPERTS).astype(BF16)
    pieces = dot(gather, block[:, D:]).astype(BF16)
    parts = [block[:, :D]]
    for late in range(2):
        columns = slice(late * 128, (late + 1) * 128)
        blocks = [pieces[r * EXPERTS : (r + 1) * EXPERTS, columns] for r in range(count)]
        parts.append(jnp.concatenate(blocks, axis=1))
    return jnp.concatenate(parts, axis=0)


def column(row):
    return jnp.transpose(jnp.broadcast_to(row, (SEQ, 128)))


def slot_hot(target):
    return target == iota((SEQ, ROWS), 1).astype(F32)


def bias_kernel(core, buckets, own, other, out):
    bucket = buckets[...]
    causal = iota((SEQ, SEQ), 0) >= iota((SEQ, SEQ), 1)
    hot = [bucket == b for b in range(BUCKETS)]
    for section in range(2):
        table = chosen((core[0] == section).astype(jnp.int32), own[2:3, :128], other[2:3, :128])
        for head in range(HEADS):
            value = jnp.zeros((SEQ, SEQ), F32)
            for b in range(BUCKETS):
                at = head * BUCKETS + b
                value = jnp.where(hot[b], table[0:1, at : at + 1], value)
            out[section, head] = jnp.where(causal, value, -1e30)


def attention_body(values, gain, qkv_weight, out_weight, bias, refs):
    partial_out, projected_out, probs_out, attended_out = refs
    normed = (values * norm(values) * gain).astype(BF16)
    projected = dot_nt(normed, qkv_weight).astype(BF16)
    projected_out[...] = projected
    heads = []
    for head in range(HEADS):
        at = head * 3 * HEAD_DIM
        query = projected[:, at : at + HEAD_DIM]
        key = projected[:, at + HEAD_DIM : at + 2 * HEAD_DIM]
        value = projected[:, at + 2 * HEAD_DIM : at + 3 * HEAD_DIM]
        scores = dot_nt(query, key) * SCALE + bias[head]
        exps = jnp.exp(scores - jnp.max(scores, axis=-1, keepdims=True))
        probs = exps / jnp.sum(exps, axis=-1, keepdims=True)
        probs_out[head] = probs
        heads.append(dot(probs.astype(BF16), value))
    attended = jnp.concatenate(heads, axis=1).astype(BF16)
    attended_out[...] = attended
    partial_out[...] = dot(attended, out_weight).astype(BF16)


ATTENTION_OUT = (
    low(SEQ, D),
    low(SEQ, QKV),
    shape(HEADS, SEQ, SEQ),
    low(SEQ, HEAD_COLS),
)
ATTENTION_SCRATCH = (
    pltpu.VMEM((QKV, D), BF16),
    pltpu.VMEM((HEAD_COLS, D), BF16),
    pltpu.SemaphoreType.DMA((2,)),
)


def first_attention_kernel(core, tokens, own, other, bias, qkv, qkv2, out, out2, *refs):
    *results, qkv_weight, out_weight, sems = refs
    flag = (core[0] == 0).astype(jnp.int32)
    fetch(flag, qkv, qkv2, qkv_weight, sems.at[0])
    fetch(flag, out, out2, out_weight, sems.at[1])
    values = tokens[core[0]].astype(F32)
    gain = chosen(flag, own[0:1], other[0:1])
    fetched(qkv2, qkv_weight, sems.at[0])
    fetched(out2, out_weight, sems.at[1])
    attention_body(values, gain, qkv_weight[...], out_weight[...], bias[0], results)


def second_attention_kernel(
    core, hidden, a, b, c, d, own, other, bias, qkv, qkv2, out, out2, act, *refs
):
    *results, qkv_weight, out_weight, sems = refs
    flag = (core[0] == 1).astype(jnp.int32)
    fetch(flag, qkv, qkv2, qkv_weight, sems.at[0])
    fetch(flag, out, out2, out_weight, sems.at[1])
    section_out = (hidden[...] + total((a, b, c, d))).astype(BF16)
    act[...] = section_out
    gain = chosen(flag, own[0:1], other[0:1])
    fetched(qkv2, qkv_weight, sems.at[0])
    fetched(out2, out_weight, sems.at[1])
    attention_body(
        section_out.astype(F32), gain, qkv_weight[...], out_weight[...], bias[1], results
    )


def route_kernel(section, core, values, a, b, c, d, own, other, router, router2, ids, ids2, *refs):
    if section == 1:
        cotangent, hidden_out, low_out, meta_out, sent = refs
    else:
        hidden_out, low_out, meta_out, sent = refs
    me = core[0]
    flag = (me == section).astype(jnp.int32)
    inputs = values[me] if section == 0 else values[...]
    hidden = inputs.astype(F32) + total((a, b, c, d))
    hidden_out[...] = hidden
    gain = chosen(flag, own[1:2], other[1:2])
    moe_low = (hidden * norm(hidden) * gain).astype(BF16)
    low_out[...] = moe_low
    weight = chosen(flag, router[...].astype(F32), router2[...].astype(F32)).astype(BF16)
    logits = dot_nt(moe_low, weight)
    routes = chosen(flag, ids[me], ids2[...]).astype(F32)
    columns = [column(routes[k : k + 1]) for k in range(2)]
    lanes = iota((SEQ, EXPERTS), 1).astype(F32)
    hot = [value[:, :EXPERTS] == lanes for value in columns]
    picked = [jnp.sum(jnp.where(h, logits, 0.0), axis=1, keepdims=True) for h in hot]
    top = jnp.maximum(picked[0], picked[1])
    exps = [jnp.exp(value - top) for value in picked]
    gates = [value / (exps[0] + exps[1]) for value in exps]
    per_row = (hot[0].astype(F32) + hot[1].astype(F32)).astype(BF16)
    earlier = (iota((SEQ, SEQ), 0) > iota((SEQ, SEQ), 1)).astype(BF16)
    before = dot(earlier, per_row)
    targets = []
    for k in range(2):
        slot = jnp.sum(jnp.where(hot[k], before, 0.0), axis=1, keepdims=True)
        expert = columns[k][:, :1]
        half = jnp.floor(expert * 0.5)
        chunk = (expert - 2.0 * half) * OWNERS + half
        targets.append(
            jnp.where(slot < 7.5, chunk * 8 + slot, MAIN + (slot - 8) * EXPERTS + chunk)
        )
    meta = jnp.concatenate(gates + targets + [value[:, :1] for value in columns], axis=1)
    meta_out[:, :6] = meta
    places = [slot_hot(target) for target in targets]
    either = (places[0] | places[1]).astype(BF16)
    sent[:, :WIDE] = pack(dot_tn(either, moe_low).astype(BF16))
    if section == 1:
        scaled = [
            jnp.where(place, gate, 0.0) for place, gate in zip(places, gates)
        ]
        sent[:, WIDE:] = pack(sent_grads(either, scaled, cotangent[me]))


def sent_grads(either, scaled, upstream):
    rows = dot_tn(either, upstream)
    ones = jnp.ones((SEQ, 128), BF16)
    gates = scaled[0] + scaled[1]
    high = gates.astype(BF16)
    rest = (gates - high.astype(F32)).astype(BF16)
    factor = (dot_tn(high, ones) + dot_tn(rest, ones))[:, :1]
    return (rows * factor).astype(BF16)


def expert_weights(flag, core, own_in, other_in, own_out, other_out, weight_in, weight_out, sems):
    fetch(flag, own_in.at[core], other_in, weight_in, sems.at[0])
    fetch(flag, own_out.at[core], other_out, weight_out, sems.at[1])


EXPERT_SCRATCH = (
    pltpu.VMEM((D, D), BF16),
    pltpu.VMEM((D, D), BF16),
    pltpu.SemaphoreType.DMA((2,)),
)


def expert_forward_kernel(
    core, block, own_in, other_in, own_out, other_out, sent, rows_out, pre_out, *scratch
):
    weight_in, weight_out, sems = scratch
    flag = (core[0] == 0).astype(jnp.int32)
    expert_weights(flag, core[0], own_in, other_in, own_out, other_out, *scratch)
    rows = unpack(block[...])
    rows_out[...] = rows
    fetched(other_in, weight_in, sems.at[0])
    pre_act = dot(rows, weight_in[...])
    pre_out[...] = pre_act
    _, tanh = gelu_parts(pre_act)
    act_low = (0.5 * pre_act * (1.0 + tanh)).astype(BF16)
    fetched(other_out, weight_out, sems.at[1])
    sent[...] = pack(dot(act_low, weight_out[...]).astype(BF16))


def expert_back(grads, pre_act, weight_in, weight_out, act_out, grad_pre_out):
    square, tanh = gelu_parts(pre_act)
    act_low = (0.5 * pre_act * (1.0 + tanh)).astype(BF16)
    act_out[...] = act_low
    grad_act = dot_nt(grads, weight_out)
    slope = 0.5 * (1.0 + tanh) + 0.5 * pre_act * (1.0 - tanh * tanh) * GELU_C * (
        1.0 + 3.0 * GELU_A * square
    )
    grad_pre = (grad_act * slope).astype(BF16)
    grad_pre_out[...] = grad_pre
    return act_low, dot_nt(grad_pre, weight_in).astype(BF16)


def expert_both_kernel(
    core, block, own_in, other_in, own_out, other_out, sent, rows_out, grads_out, act_out, pre_out,
    *scratch
):
    weight_in, weight_out, sems = scratch
    flag = (core[0] == 1).astype(jnp.int32)
    expert_weights(flag, core[0], own_in, other_in, own_out, other_out, *scratch)
    rows = unpack(block[:, :WIDE])
    rows_out[...] = rows
    grads = unpack(block[:, WIDE:])
    grads_out[...] = grads
    fetched(other_in, weight_in, sems.at[0])
    pre_act = dot(rows, weight_in[...])
    fetched(other_out, weight_out, sems.at[1])
    act_low, grad_rows = expert_back(
        grads, pre_act, weight_in[...], weight_out[...], act_out, pre_out
    )
    sent[:, WIDE:] = pack(grad_rows)
    sent[:, :WIDE] = pack(dot(act_low, weight_out[...]).astype(BF16))


def expert_back_kernel(
    core, block, pre_act, own_in, other_in, own_out, other_out, sent, grads_out, act_out, pre_out,
    *scratch
):
    weight_in, weight_out, sems = scratch
    flag = (core[0] == 0).astype(jnp.int32)
    expert_weights(flag, core[0], own_in, other_in, own_out, other_out, *scratch)
    grads = unpack(block[...])
    grads_out[...] = grads
    fetched(other_out, weight_out, sems.at[1])
    fetched(other_in, weight_in, sems.at[0])
    _, grad_rows = expert_back(
        grads, pre_act[...], weight_in[...], weight_out[...], act_out, pre_out
    )
    sent[...] = pack(grad_rows)


def expert_grads_kernel(rows, grads, act_low, grad_pre, out):
    out[0] = dot_tn(rows[...], grad_pre[...])
    out[1] = dot_tn(act_low[...], grads[...])


def combine_kernel(meta, block, mix):
    rows = unpack(block[...])
    value = jnp.zeros((SEQ, D), F32)
    for k in range(2):
        place = slot_hot(meta[:, 2 + k : 3 + k]).astype(BF16)
        value = value + meta[:, k : k + 1] * dot(place, rows)
    mix[...] = value.astype(BF16)


def moe_back_body(meta, out_rows, grad_rows, upstream, sent, mix):
    grad = jnp.zeros((SEQ, D), F32)
    value = jnp.zeros((SEQ, D), F32)
    lanes = iota((SEQ, 128), 1)
    tail = jnp.zeros((SEQ, 128), F32)
    for k in range(2):
        place = slot_hot(meta[:, 2 + k : 3 + k]).astype(BF16)
        grad = grad + dot(place, grad_rows)
        picked = dot(place, out_rows)
        value = value + meta[:, k : k + 1] * picked
        inner = jnp.sum(picked * upstream, axis=1, keepdims=True)
        tail = jnp.where(lanes == k, inner, tail)
    sent[:, :D] = grad.astype(BF16)
    sent[:, D:] = tail.astype(BF16)
    if mix is not None:
        mix[...] = value.astype(BF16)


def second_back_kernel(core, meta, block, cotangent, sent, mix):
    out_rows = unpack(block[:, :WIDE])
    grad_rows = unpack(block[:, WIDE:])
    moe_back_body(meta, out_rows, grad_rows, cotangent[core[0]].astype(F32), sent, mix)


def first_back_kernel(meta, out_block, block, upstream, sent):
    moe_back_body(
        meta, unpack(out_block[...]), unpack(block[...]), upstream[...].astype(F32), sent, None
    )


def attention_back_kernel(
    section, core, a, b, c, d, meta, hidden, moe_low, upstream, own, other, router, router2, buckets,
    values, projected, probs, attended, qkv, qkv2, out, out2,
    sent, grad_hidden_out, shared, qkv_weight, out_weight, rel, sems,
):
    me = core[0]
    flag = (me == section).astype(jnp.int32)
    fetch(flag, qkv, qkv2, qkv_weight, sems.at[0])
    fetch(flag, out, out2, out_weight, sems.at[1])
    reduced = total((a, b, c, d))
    grad_moe = reduced[:, :D]
    gain = chosen(flag, own[1:2], other[1:2])
    weight = chosen(flag, router[...].astype(F32), router2[...].astype(F32)).astype(BF16)
    gates = [meta[:, k : k + 1] for k in range(2)]
    grad_gates = [reduced[:, D + k : D + k + 1] for k in range(2)]
    mean = gates[0] * grad_gates[0] + gates[1] * grad_gates[1]
    lanes = iota((SEQ, 128), 1).astype(F32)
    grad_logits = jnp.zeros((SEQ, 128), F32)
    for k in range(2):
        grad = gates[k] * (grad_gates[k] - mean)
        grad_logits = jnp.where(meta[:, 4 + k : 5 + k] == lanes, grad, grad_logits)
    grad_logits = grad_logits.astype(BF16)
    grad_moe = grad_moe + dot(grad_logits[:, :EXPERTS], weight)
    state = hidden[...]
    inverse = norm(state)
    grad_moe_gain = jnp.sum(grad_moe * state * inverse, axis=0, keepdims=True)
    before = upstream[me] if section == 1 else upstream[...]
    grad_hidden = before.astype(F32) + norm_back(state, inverse, gain, grad_moe)
    grad_hidden_out[...] = grad_hidden
    grad_low = grad_hidden.astype(BF16)
    fetched(out2, out_weight, sems.at[1])
    grad_heads = dot_nt(grad_low, out_weight[...]).astype(BF16)
    grads = []
    score_grads = []
    for head in range(HEADS):
        at = head * 3 * HEAD_DIM
        query = projected[:, at : at + HEAD_DIM]
        key = projected[:, at + HEAD_DIM : at + 2 * HEAD_DIM]
        value = projected[:, at + 2 * HEAD_DIM : at + 3 * HEAD_DIM]
        grad_head = grad_heads[:, head * HEAD_DIM : (head + 1) * HEAD_DIM]
        prob = probs[head]
        grad_probs = dot_nt(grad_head, value)
        grad_value = dot_tn(prob.astype(BF16), grad_head)
        inner = jnp.sum(prob * grad_probs, axis=-1, keepdims=True)
        grad_scores = (prob * (grad_probs - inner)).astype(BF16)
        score_grads.append(grad_scores.astype(F32))
        grads.append(SCALE * dot(grad_scores, key))
        grads.append(SCALE * dot_tn(grad_scores, query))
        grads.append(grad_value)
    grad_qkv = jnp.concatenate(grads, axis=1).astype(BF16)
    fetched(qkv2, qkv_weight, sems.at[0])
    sent[...] = dot(grad_qkv, qkv_weight[...]).astype(BF16)
    bucket = buckets[...]
    rel[...] = jnp.zeros_like(rel)
    for b in range(BUCKETS):
        hot = bucket == b
        for head in range(HEADS):
            at = head * BUCKETS + b
            rel[at : at + 1] = jnp.sum(
                jnp.where(hot, score_grads[head], 0.0), axis=0, keepdims=True
            )
    table = jnp.sum(jnp.transpose(rel[...]), axis=0, keepdims=True)
    inputs = (values[me] if section == 0 else values[...]).astype(F32)
    attn_gain = chosen(flag, own[0:1], other[0:1])
    normed = (inputs * norm(inputs) * attn_gain).astype(BF16)
    shared[:QKV, :D] = dot_tn(grad_qkv, normed).astype(BF16)
    shared[QKV:, :D] = dot_tn(attended[...], grad_low).astype(BF16)
    line = iota((128, D), 0)
    wide = jnp.concatenate([table, jnp.zeros((1, D - 128), F32)], axis=1)
    rows = jnp.where(line == EXPERTS + 1, grad_moe_gain, 0.0)
    rows = jnp.where(line == EXPERTS + 2, wide, rows)
    shared[:, D:] = (dot_tn(moe_low[...], grad_logits) + jnp.transpose(rows)).astype(BF16)


def input_back_kernel(section, core, a, b, c, d, values, grad_hidden, own, other, *refs):
    if section == 1:
        meta, grad_out, low_out, sent = refs
    else:
        (grad_out,) = refs
    me = core[0]
    flag = (me == section).astype(jnp.int32)
    grad_normed = total((a, b, c, d))
    inputs = (values[me] if section == 0 else values[...]).astype(F32)
    inverse = norm(inputs)
    gain = chosen(flag, own[0:1], other[0:1])
    grad_inputs = grad_hidden[...] + norm_back(inputs, inverse, gain, grad_normed)
    grad_out[:SEQ] = grad_inputs
    if section == 1:
        upstream = grad_inputs.astype(BF16)
        low_out[...] = upstream
        places = [slot_hot(meta[:, 2 + k : 3 + k]) for k in range(2)]
        either = (places[0] | places[1]).astype(BF16)
        scaled = [jnp.where(places[k], meta[:, k : k + 1], 0.0) for k in range(2)]
        sent[...] = pack(sent_grads(either, scaled, upstream))
    grad_gain = jnp.sum(grad_normed * inputs * inverse, axis=0, keepdims=True)
    grad_out[SEQ:] = jnp.broadcast_to(grad_gain, (8, D))


def pair_kernel(core, *refs):
    out = refs[-1]

    def write(shared, shared2, grad, grad2):
        out[:, :D] = (shared[:, :D].astype(F32) + shared2[:, :D].astype(F32)).astype(BF16)
        row = grad[SEQ : SEQ + 1] + grad2[SEQ : SEQ + 1]
        rows = jnp.where(iota((128, D), 0) == EXPERTS, row, 0.0)
        value = shared[:, D:].astype(F32) + shared2[:, D:].astype(F32) + jnp.transpose(rows)
        out[:, D:] = value.astype(BF16)

    for section in range(2):

        @pl.when(core[0] == section)
        def _(section=section):
            write(*refs[4 * section : 4 * section + 4])


def reduce_kernel(blocks, out):
    value = blocks[0].astype(F32)
    for at in range(1, OWNERS):
        value = value + blocks[at].astype(F32)
    value = value.astype(BF16)
    for at in range(OWNERS):
        out[at] = value


def final_kernel(summed, qkv, attn_out, router, gains, table):
    qkv[...] = summed[:QKV, :D].astype(F32)
    attn_out[...] = summed[QKV:, :D].astype(F32)
    rows = jnp.transpose(summed[:, D:].astype(F32))
    router[...] = rows[:EXPERTS]
    gains[...] = rows[EXPERTS : EXPERTS + 8]
    table[...] = rows[EXPERTS + 2 : EXPERTS + 3, :128]


def place_kernel(core, *refs):
    sources, outs, spaces = refs[:12], refs[12:16], refs[16:20]
    sems_in, sems_out = refs[20:]
    rows = pl.ds(0, SEQ)

    def move(me):
        chosen_refs = []
        for at in range(3):
            own0, got0, own1, got1 = sources[4 * at : 4 * at + 4]
            chosen_refs.append((own0, got0) if me == 0 else (got1, own1))
        expert, act, grad = chosen_refs
        pairs = [
            [ref.at[0] for ref in expert],
            [ref.at[1] for ref in expert],
            list(act),
            [ref.at[rows] for ref in grad],
        ]
        reads, writes = [], []
        for at in range(4):
            for half in range(2):
                room = spaces[at].at[half]
                sem = 2 * at + half
                reads.append(pltpu.make_async_copy(pairs[at][half], room, sems_in.at[sem]))
                writes.append(pltpu.make_async_copy(room, outs[at].at[half], sems_out.at[sem]))
        for copy in reads:
            copy.start()
        for read, write in zip(reads, writes):
            read.wait()
            write.start()
        for copy in writes:
            copy.wait()

    for me in range(2):

        @pl.when(core[0] == me)
        def _(me=me):
            move(me)


def permuted(value, axis, pairs):
    return lax.ppermute(value, axis, pairs)


def swap(value):
    return permuted(value, "pipe", [(0, 1), (1, 0)])


def down(value):
    return permuted(value, "pipe", [(1, 0)])


def up(value):
    return permuted(value, "pipe", [(0, 1)])


def spread(value):
    count = lax.axis_size("tensor")
    return [value] + [
        permuted(value, "tensor", [(i, (i + by) % count) for i in range(count)])
        for by in range(1, count)
    ]


def after(value, *others):
    return lax.optimization_barrier((value, *others))[0]


def exchange(block):
    moved = lax.all_to_all(
        block.reshape(EXPERTS, 8, block.shape[1]),
        ("pipe", "expert"),
        split_axis=0,
        concat_axis=0,
        tiled=True,
    )
    return moved.reshape(block.shape)


def shards(
    tokens,
    cotangent,
    routes,
    buckets,
    gain_attn,
    w_qkv,
    w_attn_out,
    rel_table,
    gain_moe,
    w_router,
    w_expert_in,
    w_expert_out,
):
    index = lax.axis_index("pipe")
    core = jnp.reshape(index, (1,)).astype(jnp.int32)
    qkv = w_qkv[0].T
    attn_out = w_attn_out[0]
    router = w_router[0].T
    ids = jnp.transpose(routes[0], (0, 2, 1))
    table = jnp.pad(rel_table[0].astype(F32).reshape(1, -1), ((0, 0), (0, D - HEADS * BUCKETS)))
    own = jnp.concatenate([gain_attn, gain_moe, table, jnp.zeros((5, D), F32)], axis=0)

    qkv2 = swap(qkv)
    other = swap(own)
    attn_out2 = swap(attn_out)
    router2 = swap(router)
    ids2 = swap(lax.dynamic_index_in_dim(ids, 1 - index, 0, keepdims=False))

    (bias,) = kernel_call(
        bias_kernel,
        "bias",
        (core, buckets, own, other),
        (SMEM, VMEM, VMEM, VMEM),
        (shape(2, HEADS, SEQ, SEQ),),
    )
    attn_args = (qkv, qkv2, attn_out, attn_out2)

    partial0, projected0, probs0, attended0 = kernel_call(
        first_attention_kernel,
        "first_attention",
        (core, tokens, own, other, bias, *attn_args),
        (SMEM, VMEM, VMEM, VMEM, VMEM, ANY, ANY, ANY, ANY),
        ATTENTION_OUT,
        ATTENTION_SCRATCH,
    )
    parts = spread(partial0)
    theirs_in, theirs_out, _ = lax.optimization_barrier((w_expert_in[0], w_expert_out[0], partial0))
    other_in = swap(lax.dynamic_index_in_dim(theirs_in, 1 - index, 0, keepdims=False))
    other_out = swap(lax.dynamic_index_in_dim(theirs_out, 1 - index, 0, keepdims=False))
    expert_args = (w_expert_in[0], other_in, w_expert_out[0], other_out)
    expert_specs = (ANY, ANY, ANY, ANY)
    route_args = (own, other, router, router2, ids, ids2)

    def route(section, values, parts, more, wide):
        return kernel_call(
            lambda *refs: route_kernel(section, *refs),
            "route",
            (core, values, *parts, *route_args, *more),
            (SMEM,) + (VMEM,) * (11 + len(more)),
            (shape(SEQ, D), low(SEQ, D), shape(SEQ, 128), low(MAIN, wide)),
        )

    hidden0, moe_low0, meta0, sent = route(0, tokens, parts, (), WIDE)
    block = exchange(sent)
    sent, rows0, pre0 = kernel_call(
        expert_forward_kernel,
        "expert_forward",
        (core, block, *expert_args),
        (SMEM, VMEM, *expert_specs),
        (low(MAIN, WIDE), low(ROWS, D), shape(ROWS, D)),
        EXPERT_SCRATCH,
    )
    out_block0 = exchange(sent)
    (mix,) = kernel_call(
        combine_kernel, "combine", (meta0, out_block0), (VMEM, VMEM), (low(SEQ, D),)
    )

    act0, partial1, projected1, probs1, attended1 = kernel_call(
        second_attention_kernel,
        "second_attention",
        (core, hidden0, *spread(mix), own, other, bias, *attn_args),
        (SMEM,) + (VMEM,) * 8 + (ANY,) * 4,
        (low(SEQ, D), *ATTENTION_OUT),
        ATTENTION_SCRATCH,
    )
    hidden1, moe_low1, meta1, sent = route(1, act0, spread(partial1), (cotangent,), 2 * WIDE)
    block = exchange(sent)
    sent, rows1, grads1, act_low1, grad_pre1 = kernel_call(
        expert_both_kernel,
        "expert_both",
        (core, block, *expert_args),
        (SMEM, VMEM, *expert_specs),
        (low(MAIN, 2 * WIDE), low(ROWS, D), low(ROWS, D), low(ROWS, D), low(ROWS, D)),
        EXPERT_SCRATCH,
    )
    block = exchange(sent)

    def expert_grads(*args):
        return kernel_call(
            expert_grads_kernel,
            "expert_grads",
            args,
            (VMEM,) * 4,
            (shape(2, D, D),),
        )[0]

    expert_grad1 = expert_grads(rows1, grads1, act_low1, grad_pre1)
    block = after(block, expert_grad1)
    expert_grad1b = up(expert_grad1)
    sent, mix1 = kernel_call(
        second_back_kernel,
        "second_back",
        (core, meta1, block, cotangent),
        (SMEM, VMEM, VMEM, VMEM),
        (low(SEQ, D + 128), low(SEQ, D)),
    )

    def attention_back(section, parts, meta, hidden, moe_low, upstream, values, saved):
        return kernel_call(
            lambda *refs: attention_back_kernel(section, *refs),
            "attention_back",
            (core, *parts, meta, hidden, moe_low, upstream, own, other, router, router2, buckets)
            + (values, *saved, *attn_args),
            (SMEM,) + (VMEM,) * 17 + (ANY,) * 4,
            (low(SEQ, D), shape(SEQ, D), low(D, D + 128)),
            ATTENTION_SCRATCH[:2] + (pltpu.VMEM((128, 128), F32), ATTENTION_SCRATCH[2]),
        )

    partial, grad_hidden1, shared1 = attention_back(
        1, spread(sent), meta1, hidden1, moe_low1, cotangent, act0,
        (projected1, probs1, attended1),
    )
    grad_inputs1, upstream, sent = kernel_call(
        lambda *refs: input_back_kernel(1, *refs),
        "input_back",
        (core, *spread(partial), act0, grad_hidden1, own, other, meta0),
        (SMEM,) + (VMEM,) * 9,
        (shape(SEQ + 8, D), low(SEQ, D), low(MAIN, WIDE)),
    )

    block = exchange(sent)
    mix1, act0_late, shared1, early1 = lax.optimization_barrier((mix1, act0, shared1, sent))[:4]
    shared1b, grad_inputs1b, act0b = up(shared1), up(grad_inputs1), down(act0_late)
    parts = [part.astype(F32) for part in spread(mix1)]
    act1 = (hidden1 + (parts[0] + parts[1] + parts[2] + parts[3])).astype(BF16)
    block = after(block, expert_grad1b, shared1b)
    sent, grads0, act_low0, grad_pre0 = kernel_call(
        expert_back_kernel,
        "expert_back",
        (core, block, pre0, *expert_args),
        (SMEM, VMEM, VMEM, *expert_specs),
        (low(MAIN, WIDE), low(ROWS, D), low(ROWS, D), low(ROWS, D)),
        EXPERT_SCRATCH,
    )
    block = exchange(sent)
    act1b = up(act1)
    expert_grad0 = expert_grads(rows0, grads0, act_low0, grad_pre0)
    block = after(block, expert_grad0, grad_inputs1b, act0b, act1b)
    expert_grad0b = down(expert_grad0)
    (sent,) = kernel_call(
        first_back_kernel,
        "first_back",
        (meta0, out_block0, block, upstream),
        (VMEM,) * 4,
        (low(SEQ, D + 128),),
    )
    partial, grad_hidden0, shared0 = attention_back(
        0, spread(sent), meta0, hidden0, moe_low0, upstream, tokens,
        (projected0, probs0, attended0),
    )
    shared0b = down(shared0)
    (grad_inputs0,) = kernel_call(
        lambda *refs: input_back_kernel(0, *refs),
        "input_back",
        (core, *spread(partial), tokens, grad_hidden0, own, other),
        (SMEM,) + (VMEM,) * 8,
        (shape(SEQ + 8, D),),
    )
    grad_inputs0 = after(grad_inputs0, expert_grad0b, shared0b)
    grad_inputs0b = down(grad_inputs0)

    (pair,) = kernel_call(
        pair_kernel,
        "pair",
        (core, shared0, shared0b, grad_inputs0, grad_inputs0b)
        + (shared1, shared1b, grad_inputs1, grad_inputs1b),
        (SMEM,) + (VMEM,) * 8,
        (low(D, D + 128),),
    )
    blocks = pair.reshape(OWNERS, -1, D + 128)
    blocks = lax.all_to_all(blocks, "expert", split_axis=0, concat_axis=0, tiled=True)
    results = [shape(2, D, D), shape(2, D, D), low(2, SEQ, D), shape(2, SEQ, D)]
    grad_in, grad_out, activations, input_grad = kernel_call(
        place_kernel,
        "place",
        (core, expert_grad0, expert_grad0b, expert_grad1, expert_grad1b)
        + (act0, act0b, act1, act1b)
        + (grad_inputs0, grad_inputs0b, grad_inputs1, grad_inputs1b),
        (SMEM,) + (ANY,) * 12,
        results,
        tuple(pltpu.VMEM(result.shape, result.dtype) for result in results)
        + (pltpu.SemaphoreType.DMA((8,)), pltpu.SemaphoreType.DMA((8,))),
        [ANY] * 4,
    )
    blocks = after(blocks, grad_in, grad_out, activations, input_grad)
    (blocks,) = kernel_call(reduce_kernel, "reduce", (blocks,), (VMEM,), (low(*blocks.shape),))
    blocks = lax.all_to_all(blocks, "expert", split_axis=0, concat_axis=0, tiled=True)
    grad_qkv, grad_attn_out, grad_router, grad_gains, grad_table = kernel_call(
        final_kernel,
        "final",
        (blocks.reshape(pair.shape),),
        (VMEM,),
        (shape(QKV, D), shape(HEAD_COLS, D), shape(EXPERTS, D), shape(8, D), shape(1, 128)),
    )
    return (
        activations[None],
        input_grad[None],
        grad_gains[0:1],
        grad_qkv.T[None],
        grad_attn_out[None],
        grad_table[0, : HEADS * BUCKETS].reshape(1, HEADS, BUCKETS),
        grad_gains[1:2],
        grad_router.T[None],
        grad_in[None],
        grad_out[None],
    )


def solution(mesh):
    in_specs = (
        P(None, "expert", None),
        P(None, "expert", None),
        P("pipe", None, "expert", None),
        P(),
        P("pipe", None),
        P("pipe", None, "tensor"),
        P("pipe", "tensor", None),
        P("pipe", "tensor", None),
        P("pipe", None),
        P("pipe", None, None),
        P("pipe", "expert", None, "tensor"),
        P("pipe", "expert", "tensor", None),
    )
    out_specs = (
        P("pipe", None, "expert", None),
        P("pipe", None, "expert", None),
        P("pipe", None),
        P("pipe", None, "tensor"),
        P("pipe", "tensor", None),
        P("pipe", "tensor", None),
        P("pipe", None),
        P("pipe", None, None),
        P("pipe", "expert", None, "tensor"),
        P("pipe", "expert", "tensor", None),
    )
    return jax.shard_map(shards, mesh=mesh, in_specs=in_specs, out_specs=out_specs, check_vma=False)
```

```python
import jax
import jax.numpy as jnp
from jax import lax
from jax.experimental import pallas as pl
from jax.experimental.pallas import tpu as pltpu
from jax.sharding import PartitionSpec as P

EPSILON = 1e-06
F32 = jnp.float32
BF16 = jnp.bfloat16
SEQ = 128
D = 768
HEADS = 3
HEAD_DIM = 64
QKV = 3 * HEADS * HEAD_DIM
HEAD_COLS = HEADS * HEAD_DIM
EXPERTS = 32
OWNERS = 16
BUCKETS = 32
MAIN = 8 * EXPERTS
ROWS = 10 * EXPERTS
WIDE = D + 256
SCALE = HEAD_DIM**-0.5
GELU_C = 0.7978845608028654
GELU_A = 0.044715
VMEM = pl.BlockSpec(memory_space=pltpu.VMEM)
SMEM = pl.BlockSpec(memory_space=pltpu.SMEM)
ANY = pl.BlockSpec(memory_space=pl.ANY)


def shape(*dims, dtype=F32):
    return jax.ShapeDtypeStruct(dims, dtype)


def low(*dims):
    return jax.ShapeDtypeStruct(dims, BF16)


def kernel_call(body, name, inputs, specs, outputs, scratch=(), out_specs=None, vmem=18):
    return pl.pallas_call(
        body,
        out_shape=tuple(outputs),
        in_specs=list(specs),
        out_specs=tuple(out_specs or [VMEM] * len(outputs)),
        scratch_shapes=list(scratch),
        compiler_params=pltpu.CompilerParams(vmem_limit_bytes=vmem * 2**20),
        cost_estimate=pl.CostEstimate(
            flops=1_600_000_000, bytes_accessed=8_000_000, transcendentals=0
        ),
        name=name,
    )(*inputs)


def dot(a, b):
    return jnp.dot(a, b, preferred_element_type=F32)


def dot_nt(a, b):
    return lax.dot_general(a, b, (((1,), (1,)), ((), ())), preferred_element_type=F32)


def dot_tn(a, b):
    return lax.dot_general(a, b, (((0,), (0,)), ((), ())), preferred_element_type=F32)


def iota(dims, axis):
    return lax.broadcasted_iota(jnp.int32, dims, axis)


def chosen(flag, own, other):
    return jnp.where(flag == 1, own, other)


def fetch(flag, own, other, target, semaphore):
    @pl.when(flag == 1)
    def _():
        pltpu.make_async_copy(own, target, semaphore).start()

    @pl.when(flag != 1)
    def _():
        pltpu.make_async_copy(other, target, semaphore).start()


def fetched(other, target, semaphore):
    pltpu.make_async_copy(other, target, semaphore).wait()


def norm(values):
    return lax.rsqrt(jnp.mean(values * values, axis=-1, keepdims=True) + EPSILON)


def norm_back(values, inverse, gain, upstream):
    weighted = upstream * gain
    inner = jnp.mean(weighted * values, axis=-1, keepdims=True)
    return inverse * weighted - values * (inverse * inverse * inverse) * inner


def total(refs):
    value = refs[0][...].astype(F32)
    for ref in refs[1:]:
        value = value + ref[...].astype(F32)
    return value


def gelu_parts(value):
    square = value * value
    tanh = jnp.tanh(GELU_C * value * (1.0 + GELU_A * square))
    return square, tanh


def pack(rows):
    spread = (iota((MAIN, EXPERTS), 0) // 8 == iota((MAIN, EXPERTS), 1)).astype(BF16)
    place = iota((MAIN, 128), 0) % 8
    parts = [rows[:MAIN]]
    for late in range(2):
        start = MAIN + late * EXPERTS
        copies = dot(spread, rows[start : start + EXPERTS])
        piece = jnp.zeros((MAIN, 128), F32)
        for r in range(D // 128):
            piece = jnp.where(place == r, copies[:, r * 128 : (r + 1) * 128], piece)
        parts.append(piece.astype(BF16))
    return jnp.concatenate(parts, axis=1)


def unpack(block):
    count = D // 128
    dims = (count * EXPERTS, MAIN)
    row = iota(dims, 0)
    gather = (iota(dims, 1) == (row % EXPERTS) * 8 + row // EXPERTS).astype(BF16)
    pieces = dot(gather, block[:, D:]).astype(BF16)
    parts = [block[:, :D]]
    for late in range(2):
        columns = slice(late * 128, (late + 1) * 128)
        blocks = [pieces[r * EXPERTS : (r + 1) * EXPERTS, columns] for r in range(count)]
        parts.append(jnp.concatenate(blocks, axis=1))
    return jnp.concatenate(parts, axis=0)


def column(row):
    return jnp.transpose(jnp.broadcast_to(row, (SEQ, 128)))


def slot_hot(target):
    return target == iota((SEQ, ROWS), 1).astype(F32)


def bias_kernel(core, buckets, own, other, out):
    bucket = buckets[...]
    causal = iota((SEQ, SEQ), 0) >= iota((SEQ, SEQ), 1)
    hot = [bucket == b for b in range(BUCKETS)]
    for section in range(2):
        flag = (core[0] == section).astype(jnp.int32)
        table = chosen(flag, own[...].astype(F32), other[...].astype(F32))
        for head in range(HEADS):
            value = jnp.zeros((SEQ, SEQ), F32)
            for b in range(BUCKETS):
                value = jnp.where(hot[b], table[head : head + 1, b : b + 1], value)
            out[section, head] = jnp.where(causal, value, -1e30)


def attention_body(values, gain, qkv_weight, out_weight, bias, refs):
    partial_out, projected_out, probs_out, attended_out = refs
    normed = (values * norm(values) * gain).astype(BF16)
    projected = dot_nt(normed, qkv_weight).astype(BF16)
    projected_out[...] = projected
    heads = []
    for head in range(HEADS):
        at = head * 3 * HEAD_DIM
        query = projected[:, at : at + HEAD_DIM]
        key = projected[:, at + HEAD_DIM : at + 2 * HEAD_DIM]
        value = projected[:, at + 2 * HEAD_DIM : at + 3 * HEAD_DIM]
        scores = dot_nt(query, key) * SCALE + bias[head]
        exps = jnp.exp(scores - jnp.max(scores, axis=-1, keepdims=True))
        probs = exps / jnp.sum(exps, axis=-1, keepdims=True)
        probs_out[head] = probs
        heads.append(dot(probs.astype(BF16), value))
    attended = jnp.concatenate(heads, axis=1).astype(BF16)
    attended_out[...] = attended
    partial_out[...] = dot(attended, out_weight).astype(BF16)


ATTENTION_OUT = (
    low(SEQ, D),
    low(SEQ, QKV),
    shape(HEADS, SEQ, SEQ),
    low(SEQ, HEAD_COLS),
)
ATTENTION_SCRATCH = (
    pltpu.VMEM((QKV, D), BF16),
    pltpu.VMEM((HEAD_COLS, D), BF16),
    pltpu.SemaphoreType.DMA((2,)),
)


def first_attention_kernel(core, tokens, own, other, bias, qkv, qkv2, out, out2, *refs):
    *results, qkv_weight, out_weight, sems = refs
    flag = (core[0] == 0).astype(jnp.int32)
    fetch(flag, qkv, qkv2, qkv_weight, sems.at[0])
    fetch(flag, out, out2, out_weight, sems.at[1])
    values = tokens[core[0]].astype(F32)
    gain = chosen(flag, own[...], other[...])
    fetched(qkv2, qkv_weight, sems.at[0])
    fetched(out2, out_weight, sems.at[1])
    attention_body(values, gain, qkv_weight[...], out_weight[...], bias[0], results)


def second_attention_kernel(
    core, hidden, a, b, c, d, own, other, bias, qkv, qkv2, out, out2, act, *refs
):
    *results, qkv_weight, out_weight, sems = refs
    flag = (core[0] == 1).astype(jnp.int32)
    fetch(flag, qkv, qkv2, qkv_weight, sems.at[0])
    fetch(flag, out, out2, out_weight, sems.at[1])
    section_out = (hidden[...] + total((a, b, c, d))).astype(BF16)
    act[...] = section_out
    gain = chosen(flag, own[...], other[...])
    fetched(qkv2, qkv_weight, sems.at[0])
    fetched(out2, out_weight, sems.at[1])
    attention_body(
        section_out.astype(F32), gain, qkv_weight[...], out_weight[...], bias[1], results
    )


def route_kernel(section, core, values, a, b, c, d, own, other, router, router2, ids, ids2, *refs):
    if section == 1:
        cotangent, hidden_out, low_out, meta_out, sent = refs
    else:
        hidden_out, low_out, meta_out, sent = refs
    me = core[0]
    flag = (me == section).astype(jnp.int32)
    inputs = values[me] if section == 0 else values[...]
    hidden = inputs.astype(F32) + total((a, b, c, d))
    hidden_out[...] = hidden
    gain = chosen(flag, own[...], other[...])
    moe_low = (hidden * norm(hidden) * gain).astype(BF16)
    low_out[...] = moe_low
    weight = chosen(flag, router[...].astype(F32), router2[...].astype(F32)).astype(BF16)
    logits = dot_nt(moe_low, weight)
    routes = chosen(flag, ids[me], ids2[...]).astype(F32)
    columns = [column(routes[k : k + 1]) for k in range(2)]
    lanes = iota((SEQ, EXPERTS), 1).astype(F32)
    hot = [value[:, :EXPERTS] == lanes for value in columns]
    picked = [jnp.sum(jnp.where(h, logits, 0.0), axis=1, keepdims=True) for h in hot]
    top = jnp.maximum(picked[0], picked[1])
    exps = [jnp.exp(value - top) for value in picked]
    gates = [value / (exps[0] + exps[1]) for value in exps]
    per_row = (hot[0].astype(F32) + hot[1].astype(F32)).astype(BF16)
    earlier = (iota((SEQ, SEQ), 0) > iota((SEQ, SEQ), 1)).astype(BF16)
    before = dot(earlier, per_row)
    targets = []
    for k in range(2):
        slot = jnp.sum(jnp.where(hot[k], before, 0.0), axis=1, keepdims=True)
        expert = columns[k][:, :1]
        half = jnp.floor(expert * 0.5)
        chunk = (expert - 2.0 * half) * OWNERS + half
        targets.append(
            jnp.where(slot < 7.5, chunk * 8 + slot, MAIN + (slot - 8) * EXPERTS + chunk)
        )
    meta = jnp.concatenate(gates + targets + [value[:, :1] for value in columns], axis=1)
    meta_out[:, :6] = meta
    places = [slot_hot(target) for target in targets]
    either = (places[0] | places[1]).astype(BF16)
    sent[:, :WIDE] = pack(dot_tn(either, moe_low).astype(BF16))
    if section == 1:
        scaled = [
            jnp.where(place, gate, 0.0) for place, gate in zip(places, gates)
        ]
        sent[:, WIDE:] = pack(sent_grads(either, scaled, cotangent[me]))


def sent_grads(either, scaled, upstream):
    rows = dot_tn(either, upstream)
    ones = jnp.ones((SEQ, 128), BF16)
    gates = scaled[0] + scaled[1]
    high = gates.astype(BF16)
    rest = (gates - high.astype(F32)).astype(BF16)
    factor = (dot_tn(high, ones) + dot_tn(rest, ones))[:, :1]
    return (rows * factor).astype(BF16)


def expert_weights(flag, core, own_in, other_in, own_out, other_out, weight_in, weight_out, sems):
    fetch(flag, own_in.at[core], other_in.at[core], weight_in, sems.at[0])
    fetch(flag, own_out.at[core], other_out.at[core], weight_out, sems.at[1])


EXPERT_SCRATCH = (
    pltpu.VMEM((D, D), BF16),
    pltpu.VMEM((D, D), BF16),
    pltpu.SemaphoreType.DMA((2,)),
)


def expert_forward_kernel(
    core, block, own_in, other_in, own_out, other_out, sent, rows_out, pre_out, *scratch
):
    weight_in, weight_out, sems = scratch
    flag = (core[0] == 0).astype(jnp.int32)
    expert_weights(flag, core[0], own_in, other_in, own_out, other_out, *scratch)
    rows = unpack(block[...])
    rows_out[...] = rows
    fetched(other_in.at[0], weight_in, sems.at[0])
    pre_act = dot(rows, weight_in[...])
    pre_out[...] = pre_act
    _, tanh = gelu_parts(pre_act)
    act_low = (0.5 * pre_act * (1.0 + tanh)).astype(BF16)
    fetched(other_out.at[0], weight_out, sems.at[1])
    sent[...] = pack(dot(act_low, weight_out[...]).astype(BF16))


def expert_back(grads, pre_act, weight_in, weight_out, act_out, grad_pre_out):
    square, tanh = gelu_parts(pre_act)
    act_low = (0.5 * pre_act * (1.0 + tanh)).astype(BF16)
    act_out[...] = act_low
    grad_act = dot_nt(grads, weight_out)
    slope = 0.5 * (1.0 + tanh) + 0.5 * pre_act * (1.0 - tanh * tanh) * GELU_C * (
        1.0 + 3.0 * GELU_A * square
    )
    grad_pre = (grad_act * slope).astype(BF16)
    grad_pre_out[...] = grad_pre
    return act_low, dot_nt(grad_pre, weight_in).astype(BF16)


def expert_both_kernel(
    core, block, own_in, other_in, own_out, other_out, sent, rows_out, grads_out, act_out, pre_out,
    *scratch
):
    weight_in, weight_out, sems = scratch
    flag = (core[0] == 1).astype(jnp.int32)
    expert_weights(flag, core[0], own_in, other_in, own_out, other_out, *scratch)
    rows = unpack(block[:, :WIDE])
    rows_out[...] = rows
    grads = unpack(block[:, WIDE:])
    grads_out[...] = grads
    fetched(other_in.at[0], weight_in, sems.at[0])
    pre_act = dot(rows, weight_in[...])
    fetched(other_out.at[0], weight_out, sems.at[1])
    act_low, grad_rows = expert_back(
        grads, pre_act, weight_in[...], weight_out[...], act_out, pre_out
    )
    sent[:, WIDE:] = pack(grad_rows)
    sent[:, :WIDE] = pack(dot(act_low, weight_out[...]).astype(BF16))


def expert_back_kernel(
    core, block, pre_act, own_in, other_in, own_out, other_out, sent, grads_out, act_out, pre_out,
    *scratch
):
    weight_in, weight_out, sems = scratch
    flag = (core[0] == 0).astype(jnp.int32)
    expert_weights(flag, core[0], own_in, other_in, own_out, other_out, *scratch)
    grads = unpack(block[...])
    grads_out[...] = grads
    fetched(other_out.at[0], weight_out, sems.at[1])
    fetched(other_in.at[0], weight_in, sems.at[0])
    _, grad_rows = expert_back(
        grads, pre_act[...], weight_in[...], weight_out[...], act_out, pre_out
    )
    sent[...] = pack(grad_rows)


def expert_grads_kernel(core, *refs):
    first, second, mine, theirs, spaces, sems = refs[:4], refs[4:8], *refs[8:]
    flag = (core[0] == 0).astype(jnp.int32)
    for at in range(4):
        fetch(flag, first[at], second[at], spaces.at[at], sems.at[at])
        fetch(flag, second[at], first[at], spaces.at[4 + at], sems.at[4 + at])
    for half, out in enumerate((theirs, mine)):
        start = 4 - 4 * half
        for at in range(start, start + 4):
            fetched(first[0], spaces.at[at], sems.at[at])
        rows, grads, act_low, grad_pre = [spaces[at] for at in range(start, start + 4)]
        out[0] = dot_tn(rows, grad_pre)
        out[1] = dot_tn(act_low, grads)


def combine_kernel(meta, block, mix):
    rows = unpack(block[...])
    value = jnp.zeros((SEQ, D), F32)
    for k in range(2):
        place = slot_hot(meta[:, 2 + k : 3 + k]).astype(BF16)
        value = value + meta[:, k : k + 1] * dot(place, rows)
    mix[...] = value.astype(BF16)


def moe_back_body(meta, out_rows, grad_rows, upstream, sent, mix):
    grad = jnp.zeros((SEQ, D), F32)
    value = jnp.zeros((SEQ, D), F32)
    lanes = iota((SEQ, 128), 1)
    tail = jnp.zeros((SEQ, 128), F32)
    for k in range(2):
        place = slot_hot(meta[:, 2 + k : 3 + k]).astype(BF16)
        grad = grad + dot(place, grad_rows)
        picked = dot(place, out_rows)
        value = value + meta[:, k : k + 1] * picked
        inner = jnp.sum(picked * upstream, axis=1, keepdims=True)
        tail = jnp.where(lanes == k, inner, tail)
    sent[:, :D] = grad.astype(BF16)
    sent[:, D:] = tail.astype(BF16)
    if mix is not None:
        mix[...] = value.astype(BF16)


def second_back_kernel(core, meta, block, cotangent, sent, mix):
    out_rows = unpack(block[:, :WIDE])
    grad_rows = unpack(block[:, WIDE:])
    moe_back_body(meta, out_rows, grad_rows, cotangent[core[0]].astype(F32), sent, mix)


def first_back_kernel(meta, out_block, block, upstream, sent):
    moe_back_body(
        meta, unpack(out_block[...]), unpack(block[...]), upstream[...].astype(F32), sent, None
    )


def attention_back_kernel(
    section, core, a, b, c, d, meta, hidden, moe_low, upstream, own, other, own_attn, other_attn,
    router, router2, buckets,
    values, projected, probs, attended, qkv, qkv2, out, out2, *refs,
):
    if section == 0:
        shared1, sent, grad_hidden_out, mine, theirs, qkv_weight, out_weight, rel, sems, shared = refs
    else:
        sent, grad_hidden_out, shared, qkv_weight, out_weight, rel, sems = refs
    me = core[0]
    flag = (me == section).astype(jnp.int32)
    fetch(flag, qkv, qkv2, qkv_weight, sems.at[0])
    fetch(flag, out, out2, out_weight, sems.at[1])
    reduced = total((a, b, c, d))
    grad_moe = reduced[:, :D]
    gain = chosen(flag, own[...], other[...])
    weight = chosen(flag, router[...].astype(F32), router2[...].astype(F32)).astype(BF16)
    gates = [meta[:, k : k + 1] for k in range(2)]
    grad_gates = [reduced[:, D + k : D + k + 1] for k in range(2)]
    mean = gates[0] * grad_gates[0] + gates[1] * grad_gates[1]
    lanes = iota((SEQ, 128), 1).astype(F32)
    grad_logits = jnp.zeros((SEQ, 128), F32)
    for k in range(2):
        grad = gates[k] * (grad_gates[k] - mean)
        grad_logits = jnp.where(meta[:, 4 + k : 5 + k] == lanes, grad, grad_logits)
    grad_logits = grad_logits.astype(BF16)
    grad_moe = grad_moe + dot(grad_logits[:, :EXPERTS], weight)
    state = hidden[...]
    inverse = norm(state)
    grad_moe_gain = jnp.sum(grad_moe * state * inverse, axis=0, keepdims=True)
    before = upstream[me] if section == 1 else upstream[...]
    grad_hidden = before.astype(F32) + norm_back(state, inverse, gain, grad_moe)
    grad_hidden_out[...] = grad_hidden
    grad_low = grad_hidden.astype(BF16)
    fetched(out2, out_weight, sems.at[1])
    grad_heads = dot_nt(grad_low, out_weight[...]).astype(BF16)
    grads = []
    score_grads = []
    for head in range(HEADS):
        at = head * 3 * HEAD_DIM
        query = projected[:, at : at + HEAD_DIM]
        key = projected[:, at + HEAD_DIM : at + 2 * HEAD_DIM]
        value = projected[:, at + 2 * HEAD_DIM : at + 3 * HEAD_DIM]
        grad_head = grad_heads[:, head * HEAD_DIM : (head + 1) * HEAD_DIM]
        prob = probs[head]
        grad_probs = dot_nt(grad_head, value)
        grad_value = dot_tn(prob.astype(BF16), grad_head)
        inner = jnp.sum(prob * grad_probs, axis=-1, keepdims=True)
        grad_scores = (prob * (grad_probs - inner)).astype(BF16)
        score_grads.append(grad_scores.astype(F32))
        grads.append(SCALE * dot(grad_scores, key))
        grads.append(SCALE * dot_tn(grad_scores, query))
        grads.append(grad_value)
    grad_qkv = jnp.concatenate(grads, axis=1).astype(BF16)
    fetched(qkv2, qkv_weight, sems.at[0])
    sent[...] = dot(grad_qkv, qkv_weight[...]).astype(BF16)
    bucket = buckets[...]
    rel[...] = jnp.zeros_like(rel)
    for b in range(BUCKETS):
        hot = bucket == b
        for head in range(HEADS):
            at = head * BUCKETS + b
            rel[at : at + 1] = jnp.sum(
                jnp.where(hot, score_grads[head], 0.0), axis=0, keepdims=True
            )
    table = jnp.sum(jnp.transpose(rel[...]), axis=0, keepdims=True)
    inputs = (values[me] if section == 0 else values[...]).astype(F32)
    attn_gain = chosen(flag, own_attn[...], other_attn[...])
    normed = (inputs * norm(inputs) * attn_gain).astype(BF16)
    shared[:QKV, :D] = dot_tn(grad_qkv, normed).astype(BF16)
    shared[QKV:, :D] = dot_tn(attended[...], grad_low).astype(BF16)
    line = iota((128, D), 0)
    wide = jnp.concatenate([table, jnp.zeros((1, D - 128), F32)], axis=1)
    rows = jnp.where(line == EXPERTS + 1, grad_moe_gain, 0.0)
    rows = jnp.where(line == EXPERTS + 2, wide, rows)
    shared[:, D:] = (dot_tn(moe_low[...], grad_logits) + jnp.transpose(rows)).astype(BF16)
    if section == 0:

        @pl.when(me == 0)
        def _():
            mine[...] = shared[...]
            theirs[...] = shared1[...]

        @pl.when(me == 1)
        def _():
            mine[...] = shared1[...]
            theirs[...] = shared[...]


def input_back_kernel(section, core, a, b, c, d, values, grad_hidden, own, other, *refs):
    if section == 1:
        meta, grad_out, low_out, sent = refs
    else:
        second, mine, theirs, grad_out = refs
    me = core[0]
    flag = (me == section).astype(jnp.int32)
    grad_normed = total((a, b, c, d))
    inputs = (values[me] if section == 0 else values[...]).astype(F32)
    inverse = norm(inputs)
    gain = chosen(flag, own[...], other[...])
    grad_inputs = grad_hidden[...] + norm_back(inputs, inverse, gain, grad_normed)
    grad_out[:SEQ] = grad_inputs
    if section == 1:
        upstream = grad_inputs.astype(BF16)
        low_out[...] = upstream
        places = [slot_hot(meta[:, 2 + k : 3 + k]) for k in range(2)]
        either = (places[0] | places[1]).astype(BF16)
        scaled = [jnp.where(places[k], meta[:, k : k + 1], 0.0) for k in range(2)]
        sent[...] = pack(sent_grads(either, scaled, upstream))
    grad_gain = jnp.sum(grad_normed * inputs * inverse, axis=0, keepdims=True)
    grad_out[SEQ:] = jnp.broadcast_to(grad_gain, (8, D))
    if section == 0:

        @pl.when(me == 0)
        def _():
            mine[...] = grad_out[...]
            theirs[...] = second[...]

        @pl.when(me == 1)
        def _():
            mine[...] = second[...]
            theirs[...] = grad_out[...]


def output_kernel(core, first, hidden, a, b, c, d, mine, theirs):
    second = (hidden[...] + total((a, b, c, d))).astype(BF16)

    @pl.when(core[0] == 0)
    def _():
        mine[...] = first[...]
        theirs[...] = second

    @pl.when(core[0] == 1)
    def _():
        mine[...] = second
        theirs[...] = first[...]


def pair_kernel(mine, got, out):
    out[...] = (mine[...].astype(F32) + got[...].astype(F32)).astype(BF16)


CHUNK = D // OWNERS
SPARE = 64


def reduce_kernel(blocks, mine, got, out):
    value = blocks[0].astype(F32)
    for at in range(1, OWNERS):
        value = value + blocks[at].astype(F32)
    gain = mine[SEQ : SEQ + 1] + got[SEQ : SEQ + 1]
    columns = jnp.transpose(jnp.broadcast_to(gain, (128, D)))
    lanes = iota((CHUNK, 128), 1)
    side = value[:, D:]
    for at in range(OWNERS):
        side = jnp.where(lanes == SPARE + at, columns[at * CHUNK : (at + 1) * CHUNK], side)
    main_low, side_low = value[:, :D].astype(BF16), side.astype(BF16)
    for at in range(OWNERS):
        out[at, :, :D] = main_low
        out[at, :, D:] = side_low


def final_kernel(blocks, qkv, attn_out, router, gain_attn, gain_moe, table):
    sides = []
    gains = jnp.zeros((CHUNK, 128), F32)
    for at in range(OWNERS):
        main = blocks[at, :, :D].astype(F32)
        rows = slice(at * CHUNK, (at + 1) * CHUNK)
        if (at + 1) * CHUNK <= QKV:
            qkv[rows] = main
        else:
            attn_out[at * CHUNK - QKV : (at + 1) * CHUNK - QKV] = main
        side = blocks[at, :, D:].astype(F32)
        sides.append(side)
        gains = gains + side
    rows = jnp.transpose(jnp.concatenate(sides, axis=0))
    router[...] = rows[:EXPERTS]
    gain_moe[...] = rows[EXPERTS + 1 : EXPERTS + 2]
    line = rows[EXPERTS + 2 : EXPERTS + 3]
    for head in range(HEADS):
        table[0, head : head + 1] = line[:, head * BUCKETS : (head + 1) * BUCKETS]
    padded = jnp.concatenate([gains, jnp.zeros((128 - CHUNK, 128), F32)], axis=0)
    spare = jnp.transpose(padded)
    pieces = [spare[SPARE + at : SPARE + at + 1, :CHUNK] for at in range(OWNERS)]
    gain_attn[...] = jnp.concatenate(pieces, axis=1)


def place_kernel(core, *refs):
    sources, outs, spaces = refs[:6], refs[6:10], refs[10:14]
    sems_in, sems_out = refs[14:]
    rows = pl.ds(0, SEQ)

    def move(me):
        chosen_refs = []
        for at in range(3):
            mine, got = sources[2 * at : 2 * at + 2]
            chosen_refs.append((mine, got) if me == 0 else (got, mine))
        expert, act, grad = chosen_refs
        pairs = [
            [ref.at[0] for ref in expert],
            [ref.at[1] for ref in expert],
            list(act),
            [ref.at[rows] for ref in grad],
        ]
        reads, writes = [], []
        for at in range(4):
            for half in range(2):
                room = spaces[at].at[half]
                sem = 2 * at + half
                reads.append(pltpu.make_async_copy(pairs[at][half], room, sems_in.at[sem]))
                writes.append(pltpu.make_async_copy(room, outs[at].at[half], sems_out.at[sem]))
        for copy in reads:
            copy.start()
        for read, write in zip(reads, writes):
            read.wait()
            write.start()
        for copy in writes:
            copy.wait()

    for me in range(2):

        @pl.when(core[0] == me)
        def _(me=me):
            move(me)


def permuted(value, axis, pairs):
    return lax.ppermute(value, axis, pairs)


def swap(value):
    return permuted(value, "pipe", [(0, 1), (1, 0)])


def down(value):
    return permuted(value, "pipe", [(1, 0)])


def up(value):
    return permuted(value, "pipe", [(0, 1)])


def spread(value):
    count = lax.axis_size("tensor")
    return [value] + [
        permuted(value, "tensor", [(i, (i + by) % count) for i in range(count)])
        for by in range(1, count)
    ]


def after(value, *others):
    return lax.optimization_barrier((value, *others))[0]


def exchange(block):
    moved = lax.all_to_all(
        block.reshape(EXPERTS, 8, block.shape[1]),
        ("pipe", "expert"),
        split_axis=0,
        concat_axis=0,
        tiled=True,
    )
    return moved.reshape(block.shape)


def shards(
    tokens,
    cotangent,
    routes,
    buckets,
    gain_attn,
    w_qkv,
    w_attn_out,
    rel_table,
    gain_moe,
    w_router,
    w_expert_in,
    w_expert_out,
):
    index = lax.axis_index("pipe")
    core = jnp.reshape(index, (1,)).astype(jnp.int32)
    qkv = w_qkv[0].T
    attn_out = w_attn_out[0]
    router = w_router[0].T
    ids = jnp.transpose(routes[0], (0, 2, 1))
    qkv2 = swap(qkv)
    attn_out2 = swap(attn_out)
    tables = (rel_table[0], swap(rel_table[0]))
    attn_gains = (gain_attn, swap(gain_attn))
    moe_gains = (gain_moe, swap(gain_moe))
    router2 = swap(router)
    ids2 = swap(lax.dynamic_index_in_dim(ids, 1 - index, 0, keepdims=False))

    (bias,) = kernel_call(
        bias_kernel,
        "bias",
        (core, buckets, *tables),
        (SMEM, VMEM, VMEM, VMEM),
        (shape(2, HEADS, SEQ, SEQ),),
    )
    attn_args = (qkv, qkv2, attn_out, attn_out2)

    partial0, projected0, probs0, attended0 = kernel_call(
        first_attention_kernel,
        "first_attention",
        (core, after(tokens, ids2, router2, moe_gains[1]), *attn_gains, bias, *attn_args),
        (SMEM, VMEM, VMEM, VMEM, VMEM, ANY, ANY, ANY, ANY),
        ATTENTION_OUT,
        ATTENTION_SCRATCH,
    )
    parts = spread(partial0)
    weights = lax.optimization_barrier(
        (w_expert_in[0], w_expert_out[0], qkv2, attn_out2, tables[1], ids2, router2, moe_gains[1])
    )[:2]
    expert_args = (w_expert_in[0], swap(weights[0]), w_expert_out[0], swap(weights[1]))
    expert_specs = (ANY, ANY, ANY, ANY)
    route_args = (*moe_gains, router, router2, ids, ids2)

    def route(section, values, parts, more, wide):
        return kernel_call(
            lambda *refs: route_kernel(section, *refs),
            "route",
            (core, values, *parts, *route_args, *more),
            (SMEM,) + (VMEM,) * (11 + len(more)),
            (shape(SEQ, D), low(SEQ, D), shape(SEQ, 128), low(MAIN, wide)),
        )

    hidden0, moe_low0, meta0, sent = route(0, tokens, parts, (), WIDE)
    block = exchange(sent)
    sent, rows0, pre0 = kernel_call(
        expert_forward_kernel,
        "expert_forward",
        (core, block, *expert_args),
        (SMEM, VMEM, *expert_specs),
        (low(MAIN, WIDE), low(ROWS, D), shape(ROWS, D)),
        EXPERT_SCRATCH,
    )
    out_block0 = exchange(sent)
    (mix,) = kernel_call(
        combine_kernel, "combine", (meta0, out_block0), (VMEM, VMEM), (low(SEQ, D),)
    )

    act0, partial1, projected1, probs1, attended1 = kernel_call(
        second_attention_kernel,
        "second_attention",
        (core, hidden0, *spread(mix), *attn_gains, bias, *attn_args),
        (SMEM,) + (VMEM,) * 8 + (ANY,) * 4,
        (low(SEQ, D), *ATTENTION_OUT),
        ATTENTION_SCRATCH,
    )
    hidden1, moe_low1, meta1, sent = route(1, act0, spread(partial1), (cotangent,), 2 * WIDE)
    block = exchange(sent)
    sent, rows1, grads1, act_low1, grad_pre1 = kernel_call(
        expert_both_kernel,
        "expert_both",
        (core, block, *expert_args),
        (SMEM, VMEM, *expert_specs),
        (low(MAIN, 2 * WIDE), low(ROWS, D), low(ROWS, D), low(ROWS, D), low(ROWS, D)),
        EXPERT_SCRATCH,
    )
    block = exchange(sent)

    sent, mix1 = kernel_call(
        second_back_kernel,
        "second_back",
        (core, meta1, block, cotangent),
        (SMEM, VMEM, VMEM, VMEM),
        (low(SEQ, D + 128), low(SEQ, D)),
    )

    def attention_back(section, parts, meta, hidden, moe_low, upstream, values, saved, *more):
        shares = (low(D, D + 128),) * (1 + len(more))
        return kernel_call(
            lambda *refs: attention_back_kernel(section, *refs),
            "attention_back",
            (core, *parts, meta, hidden, moe_low, upstream, *moe_gains, *attn_gains, router, router2)
            + (buckets, values, *saved, *attn_args, *more),
            (SMEM,) + (VMEM,) * 19 + (ANY,) * 4 + (VMEM,) * len(more),
            (low(SEQ, D), shape(SEQ, D), *shares),
            ATTENTION_SCRATCH[:2]
            + (pltpu.VMEM((128, 128), F32), ATTENTION_SCRATCH[2])
            + (pltpu.VMEM((D, D + 128), BF16),) * len(more),
        )

    partial, grad_hidden1, shared1 = attention_back(
        1, spread(sent), meta1, hidden1, moe_low1, cotangent, act0,
        (projected1, probs1, attended1),
    )
    grad_inputs1, upstream, sent = kernel_call(
        lambda *refs: input_back_kernel(1, *refs),
        "input_back",
        (core, *spread(partial), act0, grad_hidden1, *attn_gains, meta0),
        (SMEM,) + (VMEM,) * 9,
        (shape(SEQ + 8, D), low(SEQ, D), low(MAIN, WIDE)),
    )

    block = exchange(sent)
    sent, grads0, act_low0, grad_pre0 = kernel_call(
        expert_back_kernel,
        "expert_back",
        (core, block, pre0, *expert_args),
        (SMEM, VMEM, VMEM, *expert_specs),
        (low(MAIN, WIDE), low(ROWS, D), low(ROWS, D), low(ROWS, D)),
        EXPERT_SCRATCH,
    )
    block = exchange(sent)
    (sent,) = kernel_call(
        first_back_kernel,
        "first_back",
        (meta0, out_block0, block, upstream),
        (VMEM,) * 4,
        (low(SEQ, D + 128),),
    )
    parts = spread(sent)
    late = lax.optimization_barrier((rows0, rows1, sent))
    expert_mine, expert_theirs = kernel_call(
        expert_grads_kernel,
        "expert_grads",
        (core, late[0], grads0, act_low0, grad_pre0, late[1], grads1, act_low1, grad_pre1),
        (SMEM,) + (ANY,) * 8,
        (shape(2, D, D), shape(2, D, D)),
        (pltpu.VMEM((8, ROWS, D), BF16), pltpu.SemaphoreType.DMA((8,))),
        vmem=22,
    )
    parts[3] = after(parts[3], expert_theirs)
    partial, grad_hidden0, mine, theirs = attention_back(
        0, parts, meta0, hidden0, moe_low0, upstream, tokens, (projected0, probs0, attended0), shared1
    )
    got = swap(theirs)
    parts = spread(partial)
    expert_theirs = after(expert_theirs, got)
    expert_got = swap(expert_theirs)

    (pair,) = kernel_call(
        pair_kernel, "pair", (mine, got), (VMEM, VMEM), (low(D, D + 128),)
    )
    blocks = pair.reshape(OWNERS, CHUNK, D + 128)
    blocks = lax.all_to_all(blocks, "expert", split_axis=0, concat_axis=0, tiled=True)
    mixes = spread(after(mix1, pair))
    grad_mine, grad_theirs = kernel_call(
        lambda *refs: input_back_kernel(0, *refs),
        "input_back",
        (core, *parts, tokens, grad_hidden0, *attn_gains, grad_inputs1),
        (SMEM,) + (VMEM,) * 9,
        (shape(SEQ + 8, D), shape(SEQ + 8, D)),
        (pltpu.VMEM((SEQ + 8, D), F32),),
    )
    grad_got = swap(grad_theirs)
    (blocks,) = kernel_call(
        reduce_kernel,
        "reduce",
        (blocks, grad_mine, grad_got),
        (VMEM,) * 3,
        (low(*blocks.shape),),
    )
    act_mine, act_theirs = kernel_call(
        output_kernel,
        "output",
        (core, act0, hidden1, *mixes),
        (SMEM,) + (VMEM,) * 6,
        (low(SEQ, D), low(SEQ, D)),
    )
    act_got = swap(act_theirs)
    blocks = lax.all_to_all(blocks, "expert", split_axis=0, concat_axis=0, tiled=True)
    results = [shape(2, D, D), shape(2, D, D), low(2, SEQ, D), shape(2, SEQ, D)]
    grad_in, grad_out, activations, input_grad = kernel_call(
        place_kernel,
        "place",
        (core, expert_mine, expert_got, act_mine, act_got, grad_mine, grad_got),
        (SMEM,) + (ANY,) * 6,
        results,
        tuple(pltpu.VMEM(result.shape, result.dtype) for result in results)
        + (pltpu.SemaphoreType.DMA((8,)), pltpu.SemaphoreType.DMA((8,))),
        [ANY] * 4,
    )
    blocks = after(blocks, grad_in, grad_out, activations, input_grad)
    grad_qkv, grad_attn_out, grad_router, grad_gain, grad_moe_gain, grad_table = kernel_call(
        final_kernel,
        "final",
        (blocks,),
        (VMEM,),
        (shape(QKV, D), shape(HEAD_COLS, D), shape(EXPERTS, D), shape(1, D), shape(1, D))
        + (shape(1, HEADS, BUCKETS),),
    )
    return (
        activations[None],
        input_grad[None],
        grad_gain,
        grad_qkv.T[None],
        grad_attn_out[None],
        grad_table,
        grad_moe_gain,
        grad_router.T[None],
        grad_in[None],
        grad_out[None],
    )


def solution(mesh):
    in_specs = (
        P(None, "expert", None),
        P(None, "expert", None),
        P("pipe", None, "expert", None),
        P(),
        P("pipe", None),
        P("pipe", None, "tensor"),
        P("pipe", "tensor", None),
        P("pipe", "tensor", None),
        P("pipe", None),
        P("pipe", None, None),
        P("pipe", "expert", None, "tensor"),
        P("pipe", "expert", "tensor", None),
    )
    out_specs = (
        P("pipe", None, "expert", None),
        P("pipe", None, "expert", None),
        P("pipe", None),
        P("pipe", None, "tensor"),
        P("pipe", "tensor", None),
        P("pipe", "tensor", None),
        P("pipe", None),
        P("pipe", None, None),
        P("pipe", "expert", None, "tensor"),
        P("pipe", "expert", "tensor", None),
    )
    return jax.shard_map(shards, mesh=mesh, in_specs=in_specs, out_specs=out_specs, check_vma=False)
```

```python
import jax
import jax.numpy as jnp
from jax import lax
from jax.experimental import pallas as pl
from jax.experimental.pallas import tpu as pltpu
from jax.sharding import PartitionSpec as P

EPSILON = 1e-06
F32 = jnp.float32
BF16 = jnp.bfloat16
SEQ = 128
D = 768
HEADS = 3
HEAD_DIM = 64
QKV = 3 * HEADS * HEAD_DIM
HEAD_COLS = HEADS * HEAD_DIM
EXPERTS = 32
OWNERS = 16
BUCKETS = 32
MAIN = 8 * EXPERTS
ROWS = 10 * EXPERTS
WIDE = D + 256
GROUP = 4
PART = D // GROUP
PIECE = 64
LINES = SEQ * PART // 128
SCALE = HEAD_DIM**-0.5
GELU_C = 0.7978845608028654
GELU_A = 0.044715
VMEM = pl.BlockSpec(memory_space=pltpu.VMEM)
SMEM = pl.BlockSpec(memory_space=pltpu.SMEM)
ANY = pl.BlockSpec(memory_space=pl.ANY)


def shape(*dims, dtype=F32):
    return jax.ShapeDtypeStruct(dims, dtype)


def low(*dims):
    return jax.ShapeDtypeStruct(dims, BF16)


def kernel_call(body, name, inputs, specs, outputs, scratch=(), out_specs=None, vmem=12):
    return pl.pallas_call(
        body,
        out_shape=tuple(outputs),
        in_specs=list(specs),
        out_specs=tuple(out_specs or [VMEM] * len(outputs)),
        scratch_shapes=list(scratch),
        compiler_params=pltpu.CompilerParams(vmem_limit_bytes=vmem * 2**20),
        cost_estimate=pl.CostEstimate(
            flops=1_600_000_000, bytes_accessed=8_000_000, transcendentals=0
        ),
        name=name,
    )(*inputs)


def dot(a, b):
    return jnp.dot(a, b, preferred_element_type=F32)


def dot_nt(a, b):
    return lax.dot_general(a, b, (((1,), (1,)), ((), ())), preferred_element_type=F32)


def dot_tn(a, b):
    return lax.dot_general(a, b, (((0,), (0,)), ((), ())), preferred_element_type=F32)


def iota(dims, axis):
    return lax.broadcasted_iota(jnp.int32, dims, axis)


def chosen(flag, own, other):
    return jnp.where(flag == 1, own, other)


def fetch(flag, own, other, target, semaphore):
    @pl.when(flag == 1)
    def _():
        pltpu.make_async_copy(own, target, semaphore).start()

    @pl.when(flag != 1)
    def _():
        pltpu.make_async_copy(other, target, semaphore).start()


def fetched(other, target, semaphore):
    pltpu.make_async_copy(other, target, semaphore).wait()


def norm(values):
    return lax.rsqrt(jnp.mean(values * values, axis=-1, keepdims=True) + EPSILON)


def norm_back(values, inverse, gain, upstream):
    weighted = upstream * gain
    inner = jnp.mean(weighted * values, axis=-1, keepdims=True)
    return inverse * weighted - values * (inverse * inverse * inverse) * inner


def total(refs):
    value = refs[0][...].astype(F32)
    for ref in refs[1:]:
        value = value + ref[...].astype(F32)
    return value


def gelu_parts(value):
    square = value * value
    tanh = jnp.tanh(GELU_C * value * (1.0 + GELU_A * square))
    return square, tanh


def pack(rows):
    spread = (iota((MAIN, EXPERTS), 0) // 8 == iota((MAIN, EXPERTS), 1)).astype(BF16)
    place = iota((MAIN, 128), 0) % 8
    parts = [rows[:MAIN]]
    for late in range(2):
        start = MAIN + late * EXPERTS
        copies = dot(spread, rows[start : start + EXPERTS])
        piece = jnp.zeros((MAIN, 128), F32)
        for r in range(D // 128):
            piece = jnp.where(place == r, copies[:, r * 128 : (r + 1) * 128], piece)
        parts.append(piece.astype(BF16))
    return jnp.concatenate(parts, axis=1)


def unpack(block):
    count = D // 128
    dims = (count * EXPERTS, MAIN)
    row = iota(dims, 0)
    gather = (iota(dims, 1) == (row % EXPERTS) * 8 + row // EXPERTS).astype(BF16)
    pieces = dot(gather, block[:, D:]).astype(BF16)
    parts = [block[:, :D]]
    for late in range(2):
        columns = slice(late * 128, (late + 1) * 128)
        blocks = [pieces[r * EXPERTS : (r + 1) * EXPERTS, columns] for r in range(count)]
        parts.append(jnp.concatenate(blocks, axis=1))
    return jnp.concatenate(parts, axis=0)


def part_of(value, part):
    last = GROUP * 128 + part * PIECE
    return value[:, part * 128 : (part + 1) * 128], value[:, last : last + PIECE]


def pack_parts(rows, out, start):
    spread = (iota((MAIN, EXPERTS), 0) // 8 == iota((MAIN, EXPERTS), 1)).astype(BF16)
    place = iota((MAIN, PIECE), 0) % 8
    copies = []
    for late in range(2):
        first = MAIN + late * EXPERTS
        copies.append(dot(spread, rows[first : first + EXPERTS]))
    for part in range(GROUP):
        piece = jnp.zeros((MAIN, PIECE), F32)
        for late in range(2):
            block, last = part_of(copies[late], part)
            piece = jnp.where(place == 3 * late, block[:, :PIECE], piece)
            piece = jnp.where(place == 3 * late + 1, block[:, PIECE:], piece)
            piece = jnp.where(place == 3 * late + 2, last, piece)
        block = jnp.concatenate([*part_of(rows[:MAIN], part), piece.astype(BF16)], axis=1)
        out[:, part, :, start : start + 256] = block.reshape(EXPERTS, 8, 256)


def unpack_part(block, start):
    value = block[:, 0, :, start : start + 256].astype(F32)
    for sender in range(1, GROUP):
        value = value + block[:, sender, :, start : start + 256].astype(F32)
    value = value.reshape(MAIN, 256).astype(BF16)
    dims = (6 * EXPERTS, MAIN)
    row = iota(dims, 0)
    gather = (iota(dims, 1) == (row % EXPERTS) * 8 + row // EXPERTS).astype(BF16)
    pieces = dot(gather, value[:, PART:]).astype(BF16)
    parts = [value[:, :PART]]
    for late in range(2):
        blocks = [pieces[r * EXPERTS : (r + 1) * EXPERTS] for r in range(3 * late, 3 * late + 3)]
        parts.append(jnp.concatenate(blocks, axis=1))
    return jnp.concatenate(parts, axis=0)


def own_part(index, value):
    block, last = part_of(value, 0)
    for part in range(1, GROUP):
        other_block, other_last = part_of(value, part)
        block = jnp.where(index == part, other_block, block)
        last = jnp.where(index == part, other_last, last)
    return jnp.concatenate([block, last], axis=1)


def fold(part):
    tail = jnp.concatenate([part[: SEQ // 2, 128:], part[SEQ // 2 :, 128:]], axis=1)
    return jnp.concatenate([part[:, :128], tail], axis=0)


def gathered(index, refs):
    parts = [ref[:LINES].astype(F32) for ref in refs]
    blocks, lasts = [], []
    for at in range(GROUP):
        value = parts[0]
        for by in range(1, GROUP):
            value = jnp.where((index + GROUP - by) % GROUP == at, parts[by], value)
        tail = value[SEQ:]
        blocks.append(value[:SEQ])
        lasts.append(jnp.concatenate([tail[:, :PIECE], tail[:, PIECE:]], axis=0))
    return jnp.concatenate(blocks + lasts, axis=1)


def column(row):
    return jnp.transpose(jnp.broadcast_to(row, (SEQ, 128)))


def slot_hot(target):
    return target == iota((SEQ, ROWS), 1).astype(F32)


def bias_kernel(core, buckets, own, other, out):
    bucket = buckets[...]
    causal = iota((SEQ, SEQ), 0) >= iota((SEQ, SEQ), 1)
    hot = [bucket == b for b in range(BUCKETS)]
    for section in range(2):
        flag = (core[0] == section).astype(jnp.int32)
        table = chosen(flag, own[...].astype(F32), other[...].astype(F32))
        for head in range(HEADS):
            value = jnp.zeros((SEQ, SEQ), F32)
            for b in range(BUCKETS):
                value = jnp.where(hot[b], table[head : head + 1, b : b + 1], value)
            out[section, head] = jnp.where(causal, value, -1e30)


def attention_body(values, gain, qkv_weight, out_weight, bias, refs):
    partial_out, projected_out, probs_out, attended_out = refs
    normed = (values * norm(values) * gain).astype(BF16)
    projected = dot_nt(normed, qkv_weight).astype(BF16)
    projected_out[...] = projected
    heads = []
    for head in range(HEADS):
        at = head * 3 * HEAD_DIM
        query = projected[:, at : at + HEAD_DIM]
        key = projected[:, at + HEAD_DIM : at + 2 * HEAD_DIM]
        value = projected[:, at + 2 * HEAD_DIM : at + 3 * HEAD_DIM]
        scores = dot_nt(query, key) * SCALE + bias[head]
        exps = jnp.exp(scores - jnp.max(scores, axis=-1, keepdims=True))
        probs = exps / jnp.sum(exps, axis=-1, keepdims=True)
        probs_out[head] = probs
        heads.append(dot(probs.astype(BF16), value))
    attended = jnp.concatenate(heads, axis=1).astype(BF16)
    attended_out[...] = attended
    partial_out[...] = dot(attended, out_weight).astype(BF16)


ATTENTION_OUT = (
    low(SEQ, D),
    low(SEQ, QKV),
    shape(HEADS, SEQ, SEQ),
    low(SEQ, HEAD_COLS),
)
ATTENTION_SCRATCH = (
    pltpu.VMEM((QKV, D), BF16),
    pltpu.VMEM((HEAD_COLS, D), BF16),
    pltpu.SemaphoreType.DMA((2,)),
)


def first_attention_kernel(core, tokens, own, other, bias, qkv, qkv2, out, out2, *refs):
    partial_out, *kept_outs, qkv_weight, out_weight, sems, projected, probs, attended, more = refs
    flag = (core[0] == 0).astype(jnp.int32)
    fetch(flag, qkv, qkv2, qkv_weight, sems.at[0])
    fetch(flag, out, out2, out_weight, sems.at[1])
    values = tokens[core[0]].astype(F32)
    gain = chosen(flag, own[...], other[...])
    fetched(qkv2, qkv_weight, sems.at[0])
    fetched(out2, out_weight, sems.at[1])
    results = (partial_out, projected, probs, attended)
    attention_body(values, gain, qkv_weight[...], out_weight[...], bias[0], results)
    kept = (projected, probs, attended)
    copies = [
        pltpu.make_async_copy(value, target, more.at[at])
        for at, (value, target) in enumerate(zip(kept, kept_outs))
    ]
    for copy in copies:
        copy.start()
    for copy in copies:
        copy.wait()


def second_attention_kernel(
    core, a, b, c, d, own, other, bias, qkv, qkv2, out, out2, act, *refs
):
    *results, qkv_weight, out_weight, sems = refs
    flag = (core[0] == 1).astype(jnp.int32)
    fetch(flag, qkv, qkv2, qkv_weight, sems.at[0])
    fetch(flag, out, out2, out_weight, sems.at[1])
    section_out = gathered(core[1], (a, b, c, d)).astype(BF16)
    act[...] = section_out
    gain = chosen(flag, own[...], other[...])
    fetched(qkv2, qkv_weight, sems.at[0])
    fetched(out2, out_weight, sems.at[1])
    attention_body(
        section_out.astype(F32), gain, qkv_weight[...], out_weight[...], bias[1], results
    )


def route_kernel(section, core, values, a, b, c, d, own, other, router, router2, ids, ids2, *refs):
    if section == 1:
        cotangent, hidden_out, low_out, meta_out, sent = refs
    else:
        hidden_out, low_out, meta_out, sent = refs
    me = core[0]
    flag = (me == section).astype(jnp.int32)
    inputs = values[me] if section == 0 else values[...]
    hidden = inputs.astype(F32) + total((a, b, c, d))
    hidden_out[...] = hidden
    gain = chosen(flag, own[...], other[...])
    moe_low = (hidden * norm(hidden) * gain).astype(BF16)
    low_out[...] = moe_low
    weight = chosen(flag, router[...].astype(F32), router2[...].astype(F32)).astype(BF16)
    logits = dot_nt(moe_low, weight)
    routes = chosen(flag, ids[me], ids2[...]).astype(F32)
    columns = [column(routes[k : k + 1]) for k in range(2)]
    lanes = iota((SEQ, EXPERTS), 1).astype(F32)
    hot = [value[:, :EXPERTS] == lanes for value in columns]
    picked = [jnp.sum(jnp.where(h, logits, 0.0), axis=1, keepdims=True) for h in hot]
    top = jnp.maximum(picked[0], picked[1])
    exps = [jnp.exp(value - top) for value in picked]
    gates = [value / (exps[0] + exps[1]) for value in exps]
    per_row = (hot[0].astype(F32) + hot[1].astype(F32)).astype(BF16)
    earlier = (iota((SEQ, SEQ), 0) > iota((SEQ, SEQ), 1)).astype(BF16)
    before = dot(earlier, per_row)
    targets = []
    for k in range(2):
        slot = jnp.sum(jnp.where(hot[k], before, 0.0), axis=1, keepdims=True)
        expert = columns[k][:, :1]
        half = jnp.floor(expert * 0.5)
        chunk = (expert - 2.0 * half) * OWNERS + half
        targets.append(
            jnp.where(slot < 7.5, chunk * 8 + slot, MAIN + (slot - 8) * EXPERTS + chunk)
        )
    meta = jnp.concatenate(gates + targets + [value[:, :1] for value in columns], axis=1)
    meta_out[:, :6] = meta
    places = [slot_hot(target) for target in targets]
    either = (places[0] | places[1]).astype(BF16)
    sent[:, :WIDE] = pack(dot_tn(either, moe_low).astype(BF16))
    if section == 1:
        scaled = [
            jnp.where(place, gate, 0.0) for place, gate in zip(places, gates)
        ]
        sent[:, WIDE:] = pack(sent_grads(either, scaled, cotangent[me]))


def sent_grads(either, scaled, upstream):
    rows = dot_tn(either, upstream)
    ones = jnp.ones((SEQ, 128), BF16)
    gates = scaled[0] + scaled[1]
    high = gates.astype(BF16)
    rest = (gates - high.astype(F32)).astype(BF16)
    factor = (dot_tn(high, ones) + dot_tn(rest, ones))[:, :1]
    return (rows * factor).astype(BF16)


def expert_weights(flag, core, own_in, other_in, own_out, other_out, weight_in, weight_out, sems):
    fetch(flag, own_in.at[core], other_in.at[core], weight_in, sems.at[0])
    fetch(flag, own_out.at[core], other_out.at[core], weight_out, sems.at[1])


EXPERT_SCRATCH = (
    pltpu.VMEM((D, D), BF16),
    pltpu.VMEM((D, D), BF16),
    pltpu.SemaphoreType.DMA((2,)),
)


def expert_forward_kernel(
    core, block, own_in, other_in, own_out, other_out, sent, rows_out, pre_out, *scratch
):
    weight_in, weight_out, sems = scratch
    flag = (core[0] == 0).astype(jnp.int32)
    expert_weights(flag, core[0], own_in, other_in, own_out, other_out, *scratch)
    rows = unpack(block[...])
    rows_out[...] = rows
    fetched(other_in.at[0], weight_in, sems.at[0])
    pre_act = dot(rows, weight_in[...])
    pre_out[...] = pre_act
    _, tanh = gelu_parts(pre_act)
    act_low = (0.5 * pre_act * (1.0 + tanh)).astype(BF16)
    fetched(other_out.at[0], weight_out, sems.at[1])
    pack_parts(dot(act_low, weight_out[...]).astype(BF16), sent, 0)


def expert_back(grads, pre_act, weight_in, weight_out, act_out, grad_pre_out):
    square, tanh = gelu_parts(pre_act)
    act_low = (0.5 * pre_act * (1.0 + tanh)).astype(BF16)
    act_out[...] = act_low
    grad_act = dot_nt(grads, weight_out)
    slope = 0.5 * (1.0 + tanh) + 0.5 * pre_act * (1.0 - tanh * tanh) * GELU_C * (
        1.0 + 3.0 * GELU_A * square
    )
    grad_pre = (grad_act * slope).astype(BF16)
    grad_pre_out[...] = grad_pre
    return act_low, dot_nt(grad_pre, weight_in).astype(BF16)


def expert_both_kernel(
    core, block, own_in, other_in, own_out, other_out, sent, rows_out, grads_out, act_out, pre_out,
    *scratch
):
    weight_in, weight_out, sems = scratch
    flag = (core[0] == 1).astype(jnp.int32)
    expert_weights(flag, core[0], own_in, other_in, own_out, other_out, *scratch)
    rows = unpack(block[:, :WIDE])
    rows_out[...] = rows
    grads = unpack(block[:, WIDE:])
    grads_out[...] = grads
    fetched(other_in.at[0], weight_in, sems.at[0])
    pre_act = dot(rows, weight_in[...])
    fetched(other_out.at[0], weight_out, sems.at[1])
    act_low, grad_rows = expert_back(
        grads, pre_act, weight_in[...], weight_out[...], act_out, pre_out
    )
    pack_parts(grad_rows, sent, 256)
    pack_parts(dot(act_low, weight_out[...]).astype(BF16), sent, 0)


def expert_back_kernel(
    core, block, pre_act, own_in, other_in, own_out, other_out, sent, grads_out, act_out, pre_out,
    *scratch
):
    weight_in, weight_out, sems = scratch
    flag = (core[0] == 0).astype(jnp.int32)
    expert_weights(flag, core[0], own_in, other_in, own_out, other_out, *scratch)
    grads = unpack(block[...])
    grads_out[...] = grads
    fetched(other_out.at[0], weight_out, sems.at[1])
    fetched(other_in.at[0], weight_in, sems.at[0])
    _, grad_rows = expert_back(
        grads, pre_act[...], weight_in[...], weight_out[...], act_out, pre_out
    )
    pack_parts(grad_rows, sent, 0)


def expert_grads_kernel(rows, grads, act_low, grad_pre, out):
    out[0] = dot_tn(rows[...], grad_pre[...])
    out[1] = dot_tn(act_low[...], grads[...])


def combine_kernel(core, meta, block, hidden, rows_out, folded):
    rows = unpack_part(block, 0)
    rows_out[...] = rows
    value = own_part(core[1], hidden[...])
    for k in range(2):
        place = slot_hot(meta[:, 2 + k : 3 + k]).astype(BF16)
        value = value + meta[:, k : k + 1] * dot(place, rows)
    folded[...] = fold(value).astype(BF16)


def moe_back_body(meta, out_rows, grad_rows, upstream, sent, value):
    grad = jnp.zeros((SEQ, PART), F32)
    lanes = iota((SEQ, 128), 1)
    tail = jnp.zeros((SEQ, 128), F32)
    for k in range(2):
        place = slot_hot(meta[:, 2 + k : 3 + k]).astype(BF16)
        grad = grad + dot(place, grad_rows)
        picked = dot(place, out_rows)
        if value is not None:
            value = value + meta[:, k : k + 1] * picked
        inner = jnp.sum(picked * upstream, axis=1, keepdims=True)
        tail = jnp.where(lanes == k, inner, tail)
    sent[:LINES] = fold(grad).astype(BF16)
    sent[LINES:] = jnp.transpose(tail)[:16].astype(BF16)
    return value


def second_back_kernel(core, meta, block, cotangent, hidden, sent, folded):
    out_rows = unpack_part(block, 0)
    grad_rows = unpack_part(block, 256)
    upstream = own_part(core[1], cotangent[core[0]].astype(F32))
    value = own_part(core[1], hidden[...])
    folded[...] = fold(moe_back_body(meta, out_rows, grad_rows, upstream, sent, value)).astype(BF16)


def first_back_kernel(core, meta, out_rows, block, upstream, sent):
    part = own_part(core[1], upstream[...].astype(F32))
    moe_back_body(meta, out_rows[...], unpack_part(block, 0), part, sent, None)


def shared_body(
    buckets, scores, inputs, gain, grad_qkv, attended, grad_low, moe_low, grad_logits, moe_gain, rel,
    shared,
):
    bucket = buckets[...]
    rel[...] = jnp.zeros_like(rel)
    for b in range(BUCKETS):
        hot = bucket == b
        for head in range(HEADS):
            at = head * BUCKETS + b
            rel[at : at + 1] = jnp.sum(jnp.where(hot, scores[head], 0.0), axis=0, keepdims=True)
    table = jnp.sum(jnp.transpose(rel[...]), axis=0, keepdims=True)
    normed = (inputs * norm(inputs) * gain).astype(BF16)
    shared[:QKV, :D] = dot_tn(grad_qkv, normed).astype(BF16)
    shared[QKV:, :D] = dot_tn(attended, grad_low).astype(BF16)
    line = iota((128, D), 0)
    wide = jnp.concatenate([table, jnp.zeros((1, D - 128), F32)], axis=1)
    rows = jnp.where(line == EXPERTS + 1, moe_gain, 0.0)
    rows = jnp.where(line == EXPERTS + 2, wide, rows)
    shared[:, D:] = (dot_tn(moe_low, grad_logits) + jnp.transpose(rows)).astype(BF16)


def shared_kernel(
    core, buckets, values, own, other, attended, moe_low, grad_hidden, scores, grad_qkv, logits,
    moe_gain, shared, rel,
):
    gain = chosen((core[0] == 1).astype(jnp.int32), own[...], other[...])
    shared_body(
        buckets, [scores[head].astype(F32) for head in range(HEADS)], values[...].astype(F32), gain,
        grad_qkv[...], attended[...], grad_hidden[...].astype(BF16), moe_low[...], logits[...],
        moe_gain[0:1], rel, shared,
    )


def attention_back_kernel(
    section, core, a, b, c, d, meta, hidden, upstream, own, other, router, router2, projected, probs,
    qkv, qkv2, out, out2, *refs,
):
    if section == 0:
        (moe_low, own_attn, other_attn, buckets, values, attended, shared1) = refs[:7]
        (sent, grad_hidden_out, mine, theirs, qkv_weight, out_weight, sems, rel, shared) = refs[7:]
    else:
        (sent, grad_hidden_out, scores_out, qkv_out, logits_out, gain_out) = refs[:6]
        (qkv_weight, out_weight, sems) = refs[6:]
    me = core[0]
    flag = (me == section).astype(jnp.int32)
    fetch(flag, qkv, qkv2, qkv_weight, sems.at[0])
    fetch(flag, out, out2, out_weight, sems.at[1])
    grad_moe = gathered(core[1], (a, b, c, d))
    tails = total((a.at[pl.ds(LINES, 16)], b.at[pl.ds(LINES, 16)], c.at[pl.ds(LINES, 16)], d.at[pl.ds(LINES, 16)]))
    tails = jnp.transpose(jnp.concatenate([tails, jnp.zeros((112, 128), F32)], axis=0))
    gain = chosen(flag, own[...], other[...])
    weight = chosen(flag, router[...].astype(F32), router2[...].astype(F32)).astype(BF16)
    gates = [meta[:, k : k + 1] for k in range(2)]
    grad_gates = [tails[:, k : k + 1] for k in range(2)]
    mean = gates[0] * grad_gates[0] + gates[1] * grad_gates[1]
    lanes = iota((SEQ, 128), 1).astype(F32)
    grad_logits = jnp.zeros((SEQ, 128), F32)
    for k in range(2):
        grad = gates[k] * (grad_gates[k] - mean)
        grad_logits = jnp.where(meta[:, 4 + k : 5 + k] == lanes, grad, grad_logits)
    grad_logits = grad_logits.astype(BF16)
    grad_moe = grad_moe + dot(grad_logits[:, :EXPERTS], weight)
    state = hidden[...]
    inverse = norm(state)
    grad_moe_gain = jnp.sum(grad_moe * state * inverse, axis=0, keepdims=True)
    before = upstream[me] if section == 1 else upstream[...]
    grad_hidden = before.astype(F32) + norm_back(state, inverse, gain, grad_moe)
    grad_hidden_out[...] = grad_hidden
    grad_low = grad_hidden.astype(BF16)
    fetched(out2, out_weight, sems.at[1])
    grad_heads = dot_nt(grad_low, out_weight[...]).astype(BF16)
    grads = []
    score_grads = []
    for head in range(HEADS):
        at = head * 3 * HEAD_DIM
        query = projected[:, at : at + HEAD_DIM]
        key = projected[:, at + HEAD_DIM : at + 2 * HEAD_DIM]
        value = projected[:, at + 2 * HEAD_DIM : at + 3 * HEAD_DIM]
        grad_head = grad_heads[:, head * HEAD_DIM : (head + 1) * HEAD_DIM]
        prob = probs[head]
        grad_probs = dot_nt(grad_head, value)
        grad_value = dot_tn(prob.astype(BF16), grad_head)
        inner = jnp.sum(prob * grad_probs, axis=-1, keepdims=True)
        grad_scores = (prob * (grad_probs - inner)).astype(BF16)
        score_grads.append(grad_scores.astype(F32))
        grads.append(SCALE * dot(grad_scores, key))
        grads.append(SCALE * dot_tn(grad_scores, query))
        grads.append(grad_value)
    grad_qkv = jnp.concatenate(grads, axis=1).astype(BF16)
    fetched(qkv2, qkv_weight, sems.at[0])
    sent[...] = dot(grad_qkv, qkv_weight[...]).astype(BF16)
    if section == 1:
        for head in range(HEADS):
            scores_out[head] = score_grads[head].astype(BF16)
        qkv_out[...] = grad_qkv
        logits_out[...] = grad_logits
        gain_out[...] = jnp.broadcast_to(grad_moe_gain, (8, D))
    else:
        attn_gain = chosen(flag, own_attn[...], other_attn[...])
        shared_body(
            buckets, score_grads, values[me].astype(F32), attn_gain, grad_qkv, attended[...],
            grad_low, moe_low[...], grad_logits, grad_moe_gain, rel, shared,
        )
    if section == 0:

        @pl.when(me == 0)
        def _():
            mine[...] = shared[...]
            theirs[...] = shared1[...]

        @pl.when(me == 1)
        def _():
            mine[...] = shared1[...]
            theirs[...] = shared[...]


def input_back_kernel(section, core, a, b, c, d, values, grad_hidden, own, other, *refs):
    if section == 1:
        meta, grad_out, low_out, sent = refs
    else:
        second, mine, theirs, grad_out = refs
    me = core[0]
    flag = (me == section).astype(jnp.int32)
    grad_normed = total((a, b, c, d))
    inputs = (values[me] if section == 0 else values[...]).astype(F32)
    inverse = norm(inputs)
    gain = chosen(flag, own[...], other[...])
    grad_inputs = grad_hidden[...] + norm_back(inputs, inverse, gain, grad_normed)
    grad_out[:SEQ] = grad_inputs
    if section == 1:
        upstream = grad_inputs.astype(BF16)
        low_out[...] = upstream
        places = [slot_hot(meta[:, 2 + k : 3 + k]) for k in range(2)]
        either = (places[0] | places[1]).astype(BF16)
        scaled = [jnp.where(places[k], meta[:, k : k + 1], 0.0) for k in range(2)]
        sent[...] = pack(sent_grads(either, scaled, upstream))
    grad_gain = jnp.sum(grad_normed * inputs * inverse, axis=0, keepdims=True)
    grad_out[SEQ:] = jnp.broadcast_to(grad_gain, (8, D))
    if section == 0:

        @pl.when(me == 0)
        def _():
            mine[...] = grad_out[...]
            theirs[...] = second[...]

        @pl.when(me == 1)
        def _():
            mine[...] = second[...]
            theirs[...] = grad_out[...]


def output_kernel(core, first, a, b, c, d, mine, theirs):
    second = gathered(core[1], (a, b, c, d)).astype(BF16)

    @pl.when(core[0] == 0)
    def _():
        mine[...] = first[...]
        theirs[...] = second

    @pl.when(core[0] == 1)
    def _():
        mine[...] = second
        theirs[...] = first[...]


def pair_kernel(mine, got, out):
    out[...] = (mine[...].astype(F32) + got[...].astype(F32)).astype(BF16)


CHUNK = D // OWNERS
SPARE = 64


def reduce_kernel(blocks, mine, got, out):
    value = blocks[0].astype(F32)
    for at in range(1, OWNERS):
        value = value + blocks[at].astype(F32)
    gain = mine[SEQ : SEQ + 1] + got[SEQ : SEQ + 1]
    columns = jnp.transpose(jnp.broadcast_to(gain, (128, D)))
    lanes = iota((CHUNK, 128), 1)
    side = value[:, D:]
    for at in range(OWNERS):
        side = jnp.where(lanes == SPARE + at, columns[at * CHUNK : (at + 1) * CHUNK], side)
    main_low, side_low = value[:, :D].astype(BF16), side.astype(BF16)
    for at in range(OWNERS):
        out[at, :, :D] = main_low
        out[at, :, D:] = side_low


def final_kernel(blocks, qkv, attn_out, router, gain_attn, gain_moe, table):
    sides = []
    gains = jnp.zeros((CHUNK, 128), F32)
    for at in range(OWNERS):
        main = blocks[at, :, :D].astype(F32)
        rows = slice(at * CHUNK, (at + 1) * CHUNK)
        if (at + 1) * CHUNK <= QKV:
            qkv[rows] = main
        else:
            attn_out[at * CHUNK - QKV : (at + 1) * CHUNK - QKV] = main
        side = blocks[at, :, D:].astype(F32)
        sides.append(side)
        gains = gains + side
    rows = jnp.transpose(jnp.concatenate(sides, axis=0))
    router[...] = rows[:EXPERTS]
    gain_moe[...] = rows[EXPERTS + 1 : EXPERTS + 2]
    line = rows[EXPERTS + 2 : EXPERTS + 3]
    for head in range(HEADS):
        table[head] = line[:, head * BUCKETS : (head + 1) * BUCKETS]
    padded = jnp.concatenate([gains, jnp.zeros((128 - CHUNK, 128), F32)], axis=0)
    spare = jnp.transpose(padded)
    pieces = [spare[SPARE + at : SPARE + at + 1, :CHUNK] for at in range(OWNERS)]
    gain_attn[...] = jnp.concatenate(pieces, axis=1)


def place_kernel(core, *refs):
    sources, outs, spaces = refs[:8], refs[8:12], refs[12:16]
    sems_in, sems_out = refs[16:]
    rows = pl.ds(0, SEQ)

    def move(me):
        own0, got0, own1, got1 = sources[:4]
        expert = (own0, got0) if me == 0 else (got1, own1)
        act, grad = [
            tuple(sources[at : at + 2]) if me == 0 else tuple(sources[at : at + 2])[::-1]
            for at in (4, 6)
        ]
        pairs = [
            [ref.at[0] for ref in expert],
            [ref.at[1] for ref in expert],
            list(act),
            [ref.at[rows] for ref in grad],
        ]
        reads, writes = [], []
        for at in range(4):
            for half in range(2):
                room = spaces[at].at[half]
                sem = 2 * at + half
                reads.append(pltpu.make_async_copy(pairs[at][half], room, sems_in.at[sem]))
                writes.append(pltpu.make_async_copy(room, outs[at].at[half], sems_out.at[sem]))
        for copy in reads:
            copy.start()
        for read, write in zip(reads, writes):
            read.wait()
            write.start()
        for copy in writes:
            copy.wait()

    for me in range(2):

        @pl.when(core[0] == me)
        def _(me=me):
            move(me)


def permuted(value, axis, pairs):
    return lax.ppermute(value, axis, pairs)


def swap(value):
    return permuted(value, "pipe", [(0, 1), (1, 0)])


def down(value):
    return permuted(value, "pipe", [(1, 0)])


def up(value):
    return permuted(value, "pipe", [(0, 1)])


def spread(value):
    count = lax.axis_size("tensor")
    return [value] + [
        permuted(value, "tensor", [(i, (i + by) % count) for i in range(count)])
        for by in range(1, count)
    ]


def after(value, *others):
    return lax.optimization_barrier((value, *others))[0]


def exchange(block):
    moved = lax.all_to_all(
        block.reshape(EXPERTS, 8, block.shape[1]),
        ("pipe", "expert"),
        split_axis=0,
        concat_axis=0,
        tiled=True,
    )
    return moved.reshape(block.shape)


def collect(block):
    moved = lax.all_to_all(
        block.reshape(EXPERTS * GROUP, 8, block.shape[3]),
        ("pipe", "expert", "tensor"),
        split_axis=0,
        concat_axis=0,
        tiled=True,
    )
    return moved.reshape(block.shape)


def shards(
    tokens,
    cotangent,
    routes,
    buckets,
    gain_attn,
    w_qkv,
    w_attn_out,
    rel_table,
    gain_moe,
    w_router,
    w_expert_in,
    w_expert_out,
):
    index = lax.axis_index("pipe")
    core = jnp.stack([index, lax.axis_index("tensor")]).astype(jnp.int32)
    qkv = w_qkv[0].T
    attn_out = w_attn_out[0]
    router = w_router[0].T
    ids = jnp.transpose(routes[0], (0, 2, 1))
    qkv2 = swap(qkv)
    attn_out2 = swap(attn_out)
    tables = (rel_table[0], swap(rel_table[0]))
    attn_gains = (gain_attn, swap(gain_attn))
    moe_gains = (gain_moe, swap(gain_moe))
    router2 = swap(router)
    ids2 = swap(lax.dynamic_index_in_dim(ids, 1 - index, 0, keepdims=False))

    attn_args = (qkv, qkv2, attn_out, attn_out2)

    (bias,) = kernel_call(
        bias_kernel,
        "bias",
        (core, buckets, *tables),
        (SMEM, VMEM, VMEM, VMEM),
        (shape(2, HEADS, SEQ, SEQ),),
    )
    partial0, projected0, probs0, attended0 = kernel_call(
        first_attention_kernel,
        "first_attention",
        (core, tokens, *attn_gains, bias, *attn_args),
        (SMEM, VMEM, VMEM, VMEM, VMEM, ANY, ANY, ANY, ANY),
        ATTENTION_OUT,
        ATTENTION_SCRATCH
        + tuple(pltpu.VMEM(kept.shape, kept.dtype) for kept in ATTENTION_OUT[1:])
        + (pltpu.SemaphoreType.DMA((3,)),),
        (VMEM, ANY, ANY, ANY),
    )
    parts = spread(partial0)
    expert_specs = (ANY, ANY, ANY, ANY)
    route_args = (*moe_gains, router, router2, ids, ids2)

    def route(section, values, parts, more, wide):
        return kernel_call(
            lambda *refs: route_kernel(section, *refs),
            "route",
            (core, values, *parts, *route_args, *more),
            (SMEM,) + (VMEM,) * (11 + len(more)),
            (shape(SEQ, D), low(SEQ, D), shape(SEQ, 128), low(MAIN, wide)),
        )

    hidden0, moe_low0, meta0, sent = route(0, tokens, parts, (), WIDE)
    weights = lax.optimization_barrier((w_expert_in[0], w_expert_out[0], sent))[:2]
    expert_args = (w_expert_in[0], swap(weights[0]), w_expert_out[0], swap(weights[1]))
    block = exchange(sent)
    sent, rows0, pre0 = kernel_call(
        expert_forward_kernel,
        "expert_forward",
        (core, block, *expert_args),
        (SMEM, VMEM, *expert_specs),
        (low(EXPERTS, GROUP, 8, 256), low(ROWS, D), shape(ROWS, D)),
        EXPERT_SCRATCH,
    )
    block = collect(sent)
    out_rows0, part0 = kernel_call(
        combine_kernel,
        "combine",
        (core, meta0, block, hidden0),
        (SMEM, VMEM, VMEM, VMEM),
        (low(ROWS, PART), low(LINES, 128)),
    )

    act0, partial1, projected1, probs1, attended1 = kernel_call(
        second_attention_kernel,
        "second_attention",
        (core, *spread(part0), *attn_gains, bias, *attn_args),
        (SMEM,) + (VMEM,) * 7 + (ANY,) * 4,
        (low(SEQ, D), *ATTENTION_OUT),
        ATTENTION_SCRATCH,
    )
    hidden1, moe_low1, meta1, sent = route(1, act0, spread(partial1), (cotangent,), 2 * WIDE)
    block = exchange(sent)
    sent, rows1, grads1, act_low1, grad_pre1 = kernel_call(
        expert_both_kernel,
        "expert_both",
        (core, block, *expert_args),
        (SMEM, VMEM, *expert_specs),
        (low(EXPERTS, GROUP, 8, 512), low(ROWS, D), low(ROWS, D), low(ROWS, D), low(ROWS, D)),
        EXPERT_SCRATCH,
        vmem=16,
    )
    block = collect(sent)

    sent, part1 = kernel_call(
        second_back_kernel,
        "second_back",
        (core, meta1, block, cotangent, hidden1),
        (SMEM, VMEM, VMEM, VMEM, VMEM),
        (low(LINES + 16, 128), low(LINES, 128)),
    )

    def expert_grads(*args):
        return kernel_call(
            expert_grads_kernel, "expert_grads", args, (VMEM,) * 4, (shape(2, D, D),)
        )[0]

    def attention_back(section, parts, meta, hidden, upstream, saved, more, outputs, scratch):
        return kernel_call(
            lambda *refs: attention_back_kernel(section, *refs),
            "attention_back",
            (core, *parts, meta, hidden, upstream, *moe_gains, router, router2, *saved, *attn_args)
            + more,
            (SMEM,) + (VMEM,) * 13 + (ANY,) * 4 + (VMEM,) * len(more),
            (low(SEQ, D), shape(SEQ, D), *outputs),
            ATTENTION_SCRATCH + scratch,
        )

    partial, grad_hidden1, *grads = attention_back(
        1, spread(sent), meta1, hidden1, cotangent, (projected1, probs1), (),
        (low(HEADS, SEQ, SEQ), low(SEQ, QKV), low(SEQ, 128), shape(8, D)), (),
    )
    parts = spread(partial)
    (shared1,) = kernel_call(
        shared_kernel,
        "shared",
        (core, buckets, act0, *attn_gains, attended1, moe_low1, after(grad_hidden1, parts[3]), *grads),
        (SMEM,) + (VMEM,) * 11,
        (low(D, D + 128),),
        (pltpu.VMEM((128, 128), F32),),
    )
    expert_grad1 = expert_grads(after(rows1, parts[3]), grads1, act_low1, grad_pre1)
    parts[1] = after(parts[1], shared1, expert_grad1)
    grad_inputs1, upstream, sent = kernel_call(
        lambda *refs: input_back_kernel(1, *refs),
        "input_back",
        (core, *parts, act0, grad_hidden1, *attn_gains, meta0),
        (SMEM,) + (VMEM,) * 9,
        (shape(SEQ + 8, D), low(SEQ, D), low(MAIN, WIDE)),
    )

    block = exchange(sent)
    sent, grads0, act_low0, grad_pre0 = kernel_call(
        expert_back_kernel,
        "expert_back",
        (core, block, pre0, *expert_args),
        (SMEM, VMEM, VMEM, *expert_specs),
        (low(EXPERTS, GROUP, 8, 256), low(ROWS, D), low(ROWS, D), low(ROWS, D)),
        EXPERT_SCRATCH,
    )
    block = collect(sent)
    (sent,) = kernel_call(
        first_back_kernel,
        "first_back",
        (core, meta0, out_rows0, block, upstream),
        (SMEM,) + (VMEM,) * 4,
        (low(LINES + 16, 128),),
    )
    parts = spread(sent)
    expert_grad0 = expert_grads(after(rows0, sent), grads0, act_low0, grad_pre0)
    parts[3] = after(parts[3], expert_grad0)
    partial, grad_hidden0, mine, theirs = attention_back(
        0, parts, meta0, hidden0, upstream, (projected0, probs0),
        (moe_low0, *attn_gains, buckets, tokens, attended0, shared1),
        (low(D, D + 128), low(D, D + 128)),
        (pltpu.VMEM((128, 128), F32), pltpu.VMEM((D, D + 128), BF16)),
    )
    got = swap(theirs)
    parts = spread(partial)

    (pair,) = kernel_call(
        pair_kernel, "pair", (mine, got), (VMEM, VMEM), (low(D, D + 128),)
    )
    blocks = pair.reshape(OWNERS, CHUNK, D + 128)
    blocks = lax.all_to_all(blocks, "expert", split_axis=0, concat_axis=0, tiled=True)
    act_parts = spread(after(part1, pair))
    grad_mine, grad_theirs = kernel_call(
        lambda *refs: input_back_kernel(0, *refs),
        "input_back",
        (core, *parts, tokens, grad_hidden0, *attn_gains, grad_inputs1),
        (SMEM,) + (VMEM,) * 9,
        (shape(SEQ + 8, D), shape(SEQ + 8, D)),
        (pltpu.VMEM((SEQ + 8, D), F32),),
    )
    grad_got = swap(grad_theirs)
    expert_grad0, expert_grad1, _ = lax.optimization_barrier((expert_grad0, expert_grad1, grad_mine))
    expert_grad0b, expert_grad1b = down(expert_grad0), up(expert_grad1)
    (blocks,) = kernel_call(
        reduce_kernel,
        "reduce",
        (blocks, grad_mine, grad_got),
        (VMEM,) * 3,
        (low(*blocks.shape),),
    )
    act_mine, act_theirs = kernel_call(
        output_kernel,
        "output",
        (core, act0, *act_parts),
        (SMEM,) + (VMEM,) * 5,
        (low(SEQ, D), low(SEQ, D)),
    )
    act_got = swap(act_theirs)
    blocks = lax.all_to_all(blocks, "expert", split_axis=0, concat_axis=0, tiled=True)
    results = [shape(2, D, D), shape(2, D, D), low(2, SEQ, D), shape(2, SEQ, D)]
    grad_in, grad_out, activations, input_grad = kernel_call(
        place_kernel,
        "place",
        (core, expert_grad0, expert_grad0b, expert_grad1, expert_grad1b)
        + (act_mine, act_got, grad_mine, grad_got),
        (SMEM,) + (ANY,) * 8,
        results,
        tuple(pltpu.VMEM(result.shape, result.dtype) for result in results)
        + (pltpu.SemaphoreType.DMA((8,)), pltpu.SemaphoreType.DMA((8,))),
        [ANY] * 4,
    )
    blocks = after(blocks, grad_in, grad_out, activations, input_grad)
    grad_qkv, grad_attn_out, grad_router, grad_gain, grad_moe_gain, grad_table = kernel_call(
        final_kernel,
        "final",
        (blocks,),
        (VMEM,),
        (shape(QKV, D), shape(HEAD_COLS, D), shape(EXPERTS, D), shape(1, D), shape(1, D))
        + (shape(HEADS, 1, BUCKETS),),
    )
    return (
        activations[None],
        input_grad[None],
        grad_gain,
        grad_qkv.T[None],
        grad_attn_out[None],
        jnp.transpose(grad_table, (1, 0, 2)),
        grad_moe_gain,
        grad_router.T[None],
        grad_in[None],
        grad_out[None],
    )


def solution(mesh):
    in_specs = (
        P(None, "expert", None),
        P(None, "expert", None),
        P("pipe", None, "expert", None),
        P(),
        P("pipe", None),
        P("pipe", None, "tensor"),
        P("pipe", "tensor", None),
        P("pipe", "tensor", None),
        P("pipe", None),
        P("pipe", None, None),
        P("pipe", "expert", None, "tensor"),
        P("pipe", "expert", "tensor", None),
    )
    out_specs = (
        P("pipe", None, "expert", None),
        P("pipe", None, "expert", None),
        P("pipe", None),
        P("pipe", None, "tensor"),
        P("pipe", "tensor", None),
        P("pipe", "tensor", None),
        P("pipe", None),
        P("pipe", None, None),
        P("pipe", "expert", None, "tensor"),
        P("pipe", "expert", "tensor", None),
    )
    return jax.shard_map(shards, mesh=mesh, in_specs=in_specs, out_specs=out_specs, check_vma=False)
```

```python
import jax
import jax.numpy as jnp
from jax import lax
from jax.experimental import pallas as pl
from jax.experimental.pallas import tpu as pltpu
from jax.sharding import PartitionSpec as P

EPSILON = 1e-06
F32 = jnp.float32
BF16 = jnp.bfloat16
SEQ = 128
D = 768
HEADS = 3
HEAD_DIM = 64
QKV = 3 * HEADS * HEAD_DIM
HEAD_COLS = HEADS * HEAD_DIM
EXPERTS = 32
OWNERS = 16
BUCKETS = 32
MAIN = 8 * EXPERTS
ROWS = 10 * EXPERTS
WIDE = D + 256
GROUP = 4
PART = D // GROUP
PIECE = 64
LINES = SEQ * PART // 128
SCALE = HEAD_DIM**-0.5
GELU_C = 0.7978845608028654
GELU_A = 0.044715
VMEM = pl.BlockSpec(memory_space=pltpu.VMEM)
SMEM = pl.BlockSpec(memory_space=pltpu.SMEM)
ANY = pl.BlockSpec(memory_space=pl.ANY)


def shape(*dims, dtype=F32):
    return jax.ShapeDtypeStruct(dims, dtype)


def low(*dims):
    return jax.ShapeDtypeStruct(dims, BF16)


def kernel_call(body, name, inputs, specs, outputs, scratch=(), out_specs=None, vmem=12):
    return pl.pallas_call(
        body,
        out_shape=tuple(outputs),
        in_specs=list(specs),
        out_specs=tuple(out_specs or [VMEM] * len(outputs)),
        scratch_shapes=list(scratch),
        compiler_params=pltpu.CompilerParams(vmem_limit_bytes=vmem * 2**20),
        cost_estimate=pl.CostEstimate(
            flops=1_600_000_000, bytes_accessed=8_000_000, transcendentals=0
        ),
        name=name,
    )(*inputs)


def dot(a, b):
    return jnp.dot(a, b, preferred_element_type=F32)


def dot_nt(a, b):
    return lax.dot_general(a, b, (((1,), (1,)), ((), ())), preferred_element_type=F32)


def dot_tn(a, b):
    return lax.dot_general(a, b, (((0,), (0,)), ((), ())), preferred_element_type=F32)


def iota(dims, axis):
    return lax.broadcasted_iota(jnp.int32, dims, axis)


def chosen(flag, own, other):
    return jnp.where(flag == 1, own, other)


def fetch(flag, own, other, target, semaphore):
    @pl.when(flag == 1)
    def _():
        pltpu.make_async_copy(own, target, semaphore).start()

    @pl.when(flag != 1)
    def _():
        pltpu.make_async_copy(other, target, semaphore).start()


def fetched(other, target, semaphore):
    pltpu.make_async_copy(other, target, semaphore).wait()


def norm(values):
    return lax.rsqrt(jnp.mean(values * values, axis=-1, keepdims=True) + EPSILON)


def norm_back(values, inverse, gain, upstream):
    weighted = upstream * gain
    inner = jnp.mean(weighted * values, axis=-1, keepdims=True)
    return inverse * weighted - values * (inverse * inverse * inverse) * inner


def total(refs):
    value = refs[0][...].astype(F32)
    for ref in refs[1:]:
        value = value + ref[...].astype(F32)
    return value


def gelu_parts(value):
    square = value * value
    tanh = jnp.tanh(GELU_C * value * (1.0 + GELU_A * square))
    return square, tanh


def pack(rows):
    spread = (iota((MAIN, EXPERTS), 0) // 8 == iota((MAIN, EXPERTS), 1)).astype(BF16)
    place = iota((MAIN, 128), 0) % 8
    parts = [rows[:MAIN]]
    for late in range(2):
        start = MAIN + late * EXPERTS
        copies = dot(spread, rows[start : start + EXPERTS])
        piece = jnp.zeros((MAIN, 128), F32)
        for r in range(D // 128):
            piece = jnp.where(place == r, copies[:, r * 128 : (r + 1) * 128], piece)
        parts.append(piece.astype(BF16))
    return jnp.concatenate(parts, axis=1)


def unpack(block):
    count = D // 128
    dims = (count * EXPERTS, MAIN)
    row = iota(dims, 0)
    gather = (iota(dims, 1) == (row % EXPERTS) * 8 + row // EXPERTS).astype(BF16)
    pieces = dot(gather, block[:, D:]).astype(BF16)
    parts = [block[:, :D]]
    for late in range(2):
        columns = slice(late * 128, (late + 1) * 128)
        blocks = [pieces[r * EXPERTS : (r + 1) * EXPERTS, columns] for r in range(count)]
        parts.append(jnp.concatenate(blocks, axis=1))
    return jnp.concatenate(parts, axis=0)


def part_of(value, part):
    last = GROUP * 128 + part * PIECE
    return value[:, part * 128 : (part + 1) * 128], value[:, last : last + PIECE]


def pack_parts(rows, out, start):
    spread = (iota((MAIN, EXPERTS), 0) // 8 == iota((MAIN, EXPERTS), 1)).astype(BF16)
    place = iota((MAIN, PIECE), 0) % 8
    copies = []
    for late in range(2):
        first = MAIN + late * EXPERTS
        copies.append(dot(spread, rows[first : first + EXPERTS]))
    for part in range(GROUP):
        piece = jnp.zeros((MAIN, PIECE), F32)
        for late in range(2):
            block, last = part_of(copies[late], part)
            piece = jnp.where(place == 3 * late, block[:, :PIECE], piece)
            piece = jnp.where(place == 3 * late + 1, block[:, PIECE:], piece)
            piece = jnp.where(place == 3 * late + 2, last, piece)
        block = jnp.concatenate([*part_of(rows[:MAIN], part), piece.astype(BF16)], axis=1)
        out[:, part, :, start : start + 256] = block.reshape(EXPERTS, 8, 256)


def unpack_part(block, start):
    value = block[:, 0, :, start : start + 256].astype(F32)
    for sender in range(1, GROUP):
        value = value + block[:, sender, :, start : start + 256].astype(F32)
    value = value.reshape(MAIN, 256).astype(BF16)
    dims = (6 * EXPERTS, MAIN)
    row = iota(dims, 0)
    gather = (iota(dims, 1) == (row % EXPERTS) * 8 + row // EXPERTS).astype(BF16)
    pieces = dot(gather, value[:, PART:]).astype(BF16)
    parts = [value[:, :PART]]
    for late in range(2):
        blocks = [pieces[r * EXPERTS : (r + 1) * EXPERTS] for r in range(3 * late, 3 * late + 3)]
        parts.append(jnp.concatenate(blocks, axis=1))
    return jnp.concatenate(parts, axis=0)


def own_part(index, value):
    block, last = part_of(value, 0)
    for part in range(1, GROUP):
        other_block, other_last = part_of(value, part)
        block = jnp.where(index == part, other_block, block)
        last = jnp.where(index == part, other_last, last)
    return jnp.concatenate([block, last], axis=1)


def fold(part):
    tail = jnp.concatenate([part[: SEQ // 2, 128:], part[SEQ // 2 :, 128:]], axis=1)
    return jnp.concatenate([part[:, :128], tail], axis=0)


def gathered(index, refs):
    parts = [ref[:LINES].astype(F32) for ref in refs]
    blocks, lasts = [], []
    for at in range(GROUP):
        value = parts[0]
        for by in range(1, GROUP):
            value = jnp.where((index + GROUP - by) % GROUP == at, parts[by], value)
        tail = value[SEQ:]
        blocks.append(value[:SEQ])
        lasts.append(jnp.concatenate([tail[:, :PIECE], tail[:, PIECE:]], axis=0))
    return jnp.concatenate(blocks + lasts, axis=1)


def column(row):
    return jnp.transpose(jnp.broadcast_to(row, (SEQ, 128)))


def slot_hot(target):
    return target == iota((SEQ, ROWS), 1).astype(F32)


def bias_kernel(core, buckets, own, other, out):
    bucket = buckets[...]
    causal = iota((SEQ, SEQ), 0) >= iota((SEQ, SEQ), 1)
    hot = [bucket == b for b in range(BUCKETS)]
    for section in range(2):
        flag = (core[0] == section).astype(jnp.int32)
        table = chosen(flag, own[...].astype(F32), other[...].astype(F32))
        for head in range(HEADS):
            value = jnp.zeros((SEQ, SEQ), F32)
            for b in range(BUCKETS):
                value = jnp.where(hot[b], table[head : head + 1, b : b + 1], value)
            out[section, head] = jnp.where(causal, value, -1e30)


def attention_body(values, gain, qkv_weight, out_weight, bias, refs):
    partial_out, projected_out, probs_out, attended_out = refs
    normed = (values * norm(values) * gain).astype(BF16)
    projected = dot_nt(normed, qkv_weight).astype(BF16)
    projected_out[...] = projected
    heads = []
    for head in range(HEADS):
        at = head * 3 * HEAD_DIM
        query = projected[:, at : at + HEAD_DIM]
        key = projected[:, at + HEAD_DIM : at + 2 * HEAD_DIM]
        value = projected[:, at + 2 * HEAD_DIM : at + 3 * HEAD_DIM]
        scores = dot_nt(query, key) * SCALE + bias[head]
        exps = jnp.exp(scores - jnp.max(scores, axis=-1, keepdims=True))
        probs = exps / jnp.sum(exps, axis=-1, keepdims=True)
        probs_out[head] = probs
        heads.append(dot(probs.astype(BF16), value))
    attended = jnp.concatenate(heads, axis=1).astype(BF16)
    attended_out[...] = attended
    partial_out[...] = dot(attended, out_weight).astype(BF16)


ATTENTION_OUT = (
    low(SEQ, D),
    low(SEQ, QKV),
    shape(HEADS, SEQ, SEQ),
    low(SEQ, HEAD_COLS),
)
ATTENTION_SCRATCH = (
    pltpu.VMEM((QKV, D), BF16),
    pltpu.VMEM((HEAD_COLS, D), BF16),
    pltpu.SemaphoreType.DMA((2,)),
)


def first_attention_kernel(core, tokens, own, other, bias, qkv, qkv2, out, out2, *refs):
    *results, qkv_weight, out_weight, sems = refs
    flag = (core[0] == 0).astype(jnp.int32)
    fetch(flag, qkv, qkv2, qkv_weight, sems.at[0])
    fetch(flag, out, out2, out_weight, sems.at[1])
    values = tokens[core[0]].astype(F32)
    gain = chosen(flag, own[...], other[...])
    fetched(qkv2, qkv_weight, sems.at[0])
    fetched(out2, out_weight, sems.at[1])
    attention_body(values, gain, qkv_weight[...], out_weight[...], bias[0], results)


def second_attention_kernel(
    core, a, b, c, d, own, other, bias, qkv, qkv2, out, out2, act, *refs
):
    *results, qkv_weight, out_weight, sems = refs
    flag = (core[0] == 1).astype(jnp.int32)
    fetch(flag, qkv, qkv2, qkv_weight, sems.at[0])
    fetch(flag, out, out2, out_weight, sems.at[1])
    section_out = gathered(core[1], (a, b, c, d)).astype(BF16)
    act[...] = section_out
    gain = chosen(flag, own[...], other[...])
    fetched(qkv2, qkv_weight, sems.at[0])
    fetched(out2, out_weight, sems.at[1])
    attention_body(
        section_out.astype(F32), gain, qkv_weight[...], out_weight[...], bias[1], results
    )


def route_kernel(section, core, values, a, b, c, d, own, other, router, router2, ids, ids2, *refs):
    if section == 1:
        cotangent, hidden_out, low_out, meta_out, sent = refs
    else:
        hidden_out, low_out, meta_out, sent = refs
    me = core[0]
    flag = (me == section).astype(jnp.int32)
    inputs = values[me] if section == 0 else values[...]
    hidden = inputs.astype(F32) + total((a, b, c, d))
    hidden_out[...] = hidden
    gain = chosen(flag, own[...], other[...])
    moe_low = (hidden * norm(hidden) * gain).astype(BF16)
    low_out[...] = moe_low
    weight = chosen(flag, router[...].astype(F32), router2[...].astype(F32)).astype(BF16)
    logits = dot_nt(moe_low, weight)
    routes = chosen(flag, ids[me], ids2[...]).astype(F32)
    columns = [column(routes[k : k + 1]) for k in range(2)]
    lanes = iota((SEQ, EXPERTS), 1).astype(F32)
    hot = [value[:, :EXPERTS] == lanes for value in columns]
    picked = [jnp.sum(jnp.where(h, logits, 0.0), axis=1, keepdims=True) for h in hot]
    top = jnp.maximum(picked[0], picked[1])
    exps = [jnp.exp(value - top) for value in picked]
    gates = [value / (exps[0] + exps[1]) for value in exps]
    per_row = (hot[0].astype(F32) + hot[1].astype(F32)).astype(BF16)
    earlier = (iota((SEQ, SEQ), 0) > iota((SEQ, SEQ), 1)).astype(BF16)
    before = dot(earlier, per_row)
    targets = []
    for k in range(2):
        slot = jnp.sum(jnp.where(hot[k], before, 0.0), axis=1, keepdims=True)
        expert = columns[k][:, :1]
        half = jnp.floor(expert * 0.5)
        chunk = (expert - 2.0 * half) * OWNERS + half
        targets.append(
            jnp.where(slot < 7.5, chunk * 8 + slot, MAIN + (slot - 8) * EXPERTS + chunk)
        )
    meta = jnp.concatenate(gates + targets + [value[:, :1] for value in columns], axis=1)
    meta_out[:, :6] = meta
    places = [slot_hot(target) for target in targets]
    either = (places[0] | places[1]).astype(BF16)
    sent[:, :WIDE] = pack(dot_tn(either, moe_low).astype(BF16))
    if section == 1:
        scaled = [
            jnp.where(place, gate, 0.0) for place, gate in zip(places, gates)
        ]
        sent[:, WIDE:] = pack(sent_grads(either, scaled, cotangent[me]))


def sent_grads(either, scaled, upstream):
    rows = dot_tn(either, upstream)
    ones = jnp.ones((SEQ, 128), BF16)
    gates = scaled[0] + scaled[1]
    high = gates.astype(BF16)
    rest = (gates - high.astype(F32)).astype(BF16)
    factor = (dot_tn(high, ones) + dot_tn(rest, ones))[:, :1]
    return (rows * factor).astype(BF16)


def expert_weights(flag, core, own_in, other_in, own_out, other_out, weight_in, weight_out, sems):
    fetch(flag, own_in.at[core], other_in.at[core], weight_in, sems.at[0])
    fetch(flag, own_out.at[core], other_out.at[core], weight_out, sems.at[1])


EXPERT_SCRATCH = (
    pltpu.VMEM((D, D), BF16),
    pltpu.VMEM((D, D), BF16),
    pltpu.SemaphoreType.DMA((2,)),
)


def expert_forward_kernel(
    core, block, own_in, other_in, own_out, other_out, sent, rows_out, pre_out, *scratch
):
    weight_in, weight_out, sems = scratch
    flag = (core[0] == 0).astype(jnp.int32)
    expert_weights(flag, core[0], own_in, other_in, own_out, other_out, *scratch)
    rows = unpack(block[...])
    rows_out[...] = rows
    fetched(other_in.at[0], weight_in, sems.at[0])
    pre_act = dot(rows, weight_in[...])
    pre_out[...] = pre_act
    _, tanh = gelu_parts(pre_act)
    act_low = (0.5 * pre_act * (1.0 + tanh)).astype(BF16)
    fetched(other_out.at[0], weight_out, sems.at[1])
    pack_parts(dot(act_low, weight_out[...]).astype(BF16), sent, 0)


def expert_back(grads, pre_act, weight_in, weight_out, act_out, grad_pre_out):
    square, tanh = gelu_parts(pre_act)
    act_low = (0.5 * pre_act * (1.0 + tanh)).astype(BF16)
    act_out[...] = act_low
    grad_act = dot_nt(grads, weight_out)
    slope = 0.5 * (1.0 + tanh) + 0.5 * pre_act * (1.0 - tanh * tanh) * GELU_C * (
        1.0 + 3.0 * GELU_A * square
    )
    grad_pre = (grad_act * slope).astype(BF16)
    grad_pre_out[...] = grad_pre
    return act_low, dot_nt(grad_pre, weight_in).astype(BF16)


def expert_both_kernel(
    core, block, own_in, other_in, own_out, other_out, sent, rows_out, grads_out, act_out, pre_out,
    *scratch
):
    weight_in, weight_out, sems = scratch
    flag = (core[0] == 1).astype(jnp.int32)
    expert_weights(flag, core[0], own_in, other_in, own_out, other_out, *scratch)
    rows = unpack(block[:, :WIDE])
    rows_out[...] = rows
    grads = unpack(block[:, WIDE:])
    grads_out[...] = grads
    fetched(other_in.at[0], weight_in, sems.at[0])
    pre_act = dot(rows, weight_in[...])
    fetched(other_out.at[0], weight_out, sems.at[1])
    act_low, grad_rows = expert_back(
        grads, pre_act, weight_in[...], weight_out[...], act_out, pre_out
    )
    pack_parts(grad_rows, sent, 256)
    pack_parts(dot(act_low, weight_out[...]).astype(BF16), sent, 0)


def expert_back_kernel(
    core, block, pre_act, own_in, other_in, own_out, other_out, sent, grads_out, act_out, pre_out,
    *scratch
):
    weight_in, weight_out, sems = scratch
    flag = (core[0] == 0).astype(jnp.int32)
    expert_weights(flag, core[0], own_in, other_in, own_out, other_out, *scratch)
    grads = unpack(block[...])
    grads_out[...] = grads
    fetched(other_out.at[0], weight_out, sems.at[1])
    fetched(other_in.at[0], weight_in, sems.at[0])
    _, grad_rows = expert_back(
        grads, pre_act[...], weight_in[...], weight_out[...], act_out, pre_out
    )
    pack_parts(grad_rows, sent, 0)


def expert_grads_kernel(rows, grads, act_low, grad_pre, out):
    out[0] = dot_tn(rows[...], grad_pre[...])
    out[1] = dot_tn(act_low[...], grads[...])


def combine_kernel(core, meta, block, hidden, rows_out, folded):
    rows = unpack_part(block, 0)
    rows_out[...] = rows
    value = own_part(core[1], hidden[...])
    for k in range(2):
        place = slot_hot(meta[:, 2 + k : 3 + k]).astype(BF16)
        value = value + meta[:, k : k + 1] * dot(place, rows)
    folded[...] = fold(value).astype(BF16)


def moe_back_body(meta, out_rows, grad_rows, upstream, sent, value):
    grad = jnp.zeros((SEQ, PART), F32)
    lanes = iota((SEQ, 128), 1)
    tail = jnp.zeros((SEQ, 128), F32)
    for k in range(2):
        place = slot_hot(meta[:, 2 + k : 3 + k]).astype(BF16)
        grad = grad + dot(place, grad_rows)
        picked = dot(place, out_rows)
        if value is not None:
            value = value + meta[:, k : k + 1] * picked
        inner = jnp.sum(picked * upstream, axis=1, keepdims=True)
        tail = jnp.where(lanes == k, inner, tail)
    sent[:LINES] = fold(grad).astype(BF16)
    sent[LINES:] = jnp.transpose(tail)[:16].astype(BF16)
    return value


def second_back_kernel(core, meta, block, cotangent, hidden, sent, folded):
    out_rows = unpack_part(block, 0)
    grad_rows = unpack_part(block, 256)
    upstream = own_part(core[1], cotangent[core[0]].astype(F32))
    value = own_part(core[1], hidden[...])
    folded[...] = fold(moe_back_body(meta, out_rows, grad_rows, upstream, sent, value)).astype(BF16)


def first_back_kernel(core, meta, out_rows, block, upstream, sent):
    part = own_part(core[1], upstream[...].astype(F32))
    moe_back_body(meta, out_rows[...], unpack_part(block, 0), part, sent, None)


def shared_body(
    buckets, scores, inputs, gain, grad_qkv, attended, grad_low, moe_low, grad_logits, moe_gain, rel,
    shared,
):
    bucket = buckets[...]
    rel[...] = jnp.zeros_like(rel)
    for b in range(BUCKETS):
        hot = bucket == b
        for head in range(HEADS):
            at = head * BUCKETS + b
            rel[at : at + 1] = jnp.sum(jnp.where(hot, scores[head], 0.0), axis=0, keepdims=True)
    table = jnp.sum(jnp.transpose(rel[...]), axis=0, keepdims=True)
    normed = (inputs * norm(inputs) * gain).astype(BF16)
    shared[:QKV, :D] = dot_tn(grad_qkv, normed).astype(BF16)
    shared[QKV:, :D] = dot_tn(attended, grad_low).astype(BF16)
    line = iota((128, D), 0)
    wide = jnp.concatenate([table, jnp.zeros((1, D - 128), F32)], axis=1)
    rows = jnp.where(line == EXPERTS + 1, moe_gain, 0.0)
    rows = jnp.where(line == EXPERTS + 2, wide, rows)
    shared[:, D:] = (dot_tn(moe_low, grad_logits) + jnp.transpose(rows)).astype(BF16)


def shared_kernel(
    core, buckets, values, own, other, attended, moe_low, grad_hidden, scores, grad_qkv, logits,
    moe_gain, shared, rel,
):
    gain = chosen((core[0] == 1).astype(jnp.int32), own[...], other[...])
    shared_body(
        buckets, [scores[head].astype(F32) for head in range(HEADS)], values[...].astype(F32), gain,
        grad_qkv[...], attended[...], grad_hidden[...].astype(BF16), moe_low[...], logits[...],
        moe_gain[0:1], rel, shared,
    )


def attention_back_kernel(
    section, core, a, b, c, d, meta, hidden, upstream, own, other, router, router2, projected, probs,
    qkv, qkv2, out, out2, *refs,
):
    if section == 0:
        (moe_low, own_attn, other_attn, buckets, values, attended, shared1) = refs[:7]
        (sent, grad_hidden_out, mine, theirs, qkv_weight, out_weight, sems, rel, shared) = refs[7:]
    else:
        (sent, grad_hidden_out, scores_out, qkv_out, logits_out, gain_out) = refs[:6]
        (qkv_weight, out_weight, sems) = refs[6:]
    me = core[0]
    flag = (me == section).astype(jnp.int32)
    fetch(flag, qkv, qkv2, qkv_weight, sems.at[0])
    fetch(flag, out, out2, out_weight, sems.at[1])
    grad_moe = gathered(core[1], (a, b, c, d))
    tails = total((a.at[pl.ds(LINES, 16)], b.at[pl.ds(LINES, 16)], c.at[pl.ds(LINES, 16)], d.at[pl.ds(LINES, 16)]))
    tails = jnp.transpose(jnp.concatenate([tails, jnp.zeros((112, 128), F32)], axis=0))
    gain = chosen(flag, own[...], other[...])
    weight = chosen(flag, router[...].astype(F32), router2[...].astype(F32)).astype(BF16)
    gates = [meta[:, k : k + 1] for k in range(2)]
    grad_gates = [tails[:, k : k + 1] for k in range(2)]
    mean = gates[0] * grad_gates[0] + gates[1] * grad_gates[1]
    lanes = iota((SEQ, 128), 1).astype(F32)
    grad_logits = jnp.zeros((SEQ, 128), F32)
    for k in range(2):
        grad = gates[k] * (grad_gates[k] - mean)
        grad_logits = jnp.where(meta[:, 4 + k : 5 + k] == lanes, grad, grad_logits)
    grad_logits = grad_logits.astype(BF16)
    grad_moe = grad_moe + dot(grad_logits[:, :EXPERTS], weight)
    state = hidden[...]
    inverse = norm(state)
    grad_moe_gain = jnp.sum(grad_moe * state * inverse, axis=0, keepdims=True)
    before = upstream[me] if section == 1 else upstream[...]
    grad_hidden = before.astype(F32) + norm_back(state, inverse, gain, grad_moe)
    grad_hidden_out[...] = grad_hidden
    grad_low = grad_hidden.astype(BF16)
    fetched(out2, out_weight, sems.at[1])
    grad_heads = dot_nt(grad_low, out_weight[...]).astype(BF16)
    grads = []
    score_grads = []
    for head in range(HEADS):
        at = head * 3 * HEAD_DIM
        query = projected[:, at : at + HEAD_DIM]
        key = projected[:, at + HEAD_DIM : at + 2 * HEAD_DIM]
        value = projected[:, at + 2 * HEAD_DIM : at + 3 * HEAD_DIM]
        grad_head = grad_heads[:, head * HEAD_DIM : (head + 1) * HEAD_DIM]
        prob = probs[head]
        grad_probs = dot_nt(grad_head, value)
        grad_value = dot_tn(prob.astype(BF16), grad_head)
        inner = jnp.sum(prob * grad_probs, axis=-1, keepdims=True)
        grad_scores = (prob * (grad_probs - inner)).astype(BF16)
        score_grads.append(grad_scores.astype(F32))
        grads.append(SCALE * dot(grad_scores, key))
        grads.append(SCALE * dot_tn(grad_scores, query))
        grads.append(grad_value)
    grad_qkv = jnp.concatenate(grads, axis=1).astype(BF16)
    fetched(qkv2, qkv_weight, sems.at[0])
    sent[...] = dot(grad_qkv, qkv_weight[...]).astype(BF16)
    if section == 1:
        for head in range(HEADS):
            scores_out[head] = score_grads[head].astype(BF16)
        qkv_out[...] = grad_qkv
        logits_out[...] = grad_logits
        gain_out[...] = jnp.broadcast_to(grad_moe_gain, (8, D))
    else:
        attn_gain = chosen(flag, own_attn[...], other_attn[...])
        shared_body(
            buckets, score_grads, values[me].astype(F32), attn_gain, grad_qkv, attended[...],
            grad_low, moe_low[...], grad_logits, grad_moe_gain, rel, shared,
        )
    if section == 0:

        @pl.when(me == 0)
        def _():
            mine[...] = shared[...]
            theirs[...] = shared1[...]

        @pl.when(me == 1)
        def _():
            mine[...] = shared1[...]
            theirs[...] = shared[...]


def input_back_kernel(section, core, a, b, c, d, values, grad_hidden, own, other, *refs):
    if section == 1:
        meta, grad_out, low_out, sent = refs
    else:
        second, mine, theirs, grad_out = refs
    me = core[0]
    flag = (me == section).astype(jnp.int32)
    grad_normed = total((a, b, c, d))
    inputs = (values[me] if section == 0 else values[...]).astype(F32)
    inverse = norm(inputs)
    gain = chosen(flag, own[...], other[...])
    grad_inputs = grad_hidden[...] + norm_back(inputs, inverse, gain, grad_normed)
    grad_out[:SEQ] = grad_inputs
    if section == 1:
        upstream = grad_inputs.astype(BF16)
        low_out[...] = upstream
        places = [slot_hot(meta[:, 2 + k : 3 + k]) for k in range(2)]
        either = (places[0] | places[1]).astype(BF16)
        scaled = [jnp.where(places[k], meta[:, k : k + 1], 0.0) for k in range(2)]
        sent[...] = pack(sent_grads(either, scaled, upstream))
    grad_gain = jnp.sum(grad_normed * inputs * inverse, axis=0, keepdims=True)
    grad_out[SEQ:] = jnp.broadcast_to(grad_gain, (8, D))
    if section == 0:

        @pl.when(me == 0)
        def _():
            mine[...] = grad_out[...]
            theirs[...] = second[...]

        @pl.when(me == 1)
        def _():
            mine[...] = second[...]
            theirs[...] = grad_out[...]


def output_kernel(core, first, a, b, c, d, mine, theirs):
    second = gathered(core[1], (a, b, c, d)).astype(BF16)

    @pl.when(core[0] == 0)
    def _():
        mine[...] = first[...]
        theirs[...] = second

    @pl.when(core[0] == 1)
    def _():
        mine[...] = second
        theirs[...] = first[...]


def pair_kernel(mine, got, out):
    out[...] = (mine[...].astype(F32) + got[...].astype(F32)).astype(BF16)


CHUNK = D // OWNERS
SPARE = 64


def reduce_kernel(blocks, mine, got, out):
    value = blocks[0].astype(F32)
    for at in range(1, OWNERS):
        value = value + blocks[at].astype(F32)
    gain = mine[SEQ : SEQ + 1] + got[SEQ : SEQ + 1]
    columns = jnp.transpose(jnp.broadcast_to(gain, (128, D)))
    lanes = iota((CHUNK, 128), 1)
    side = value[:, D:]
    for at in range(OWNERS):
        side = jnp.where(lanes == SPARE + at, columns[at * CHUNK : (at + 1) * CHUNK], side)
    main_low, side_low = value[:, :D].astype(BF16), side.astype(BF16)
    for at in range(OWNERS):
        out[at, :, :D] = main_low
        out[at, :, D:] = side_low


def final_kernel(blocks, qkv, attn_out, router, gain_attn, gain_moe, table):
    sides = []
    gains = jnp.zeros((CHUNK, 128), F32)
    for at in range(OWNERS):
        main = blocks[at, :, :D].astype(F32)
        rows = slice(at * CHUNK, (at + 1) * CHUNK)
        if (at + 1) * CHUNK <= QKV:
            qkv[rows] = main
        else:
            attn_out[at * CHUNK - QKV : (at + 1) * CHUNK - QKV] = main
        side = blocks[at, :, D:].astype(F32)
        sides.append(side)
        gains = gains + side
    rows = jnp.transpose(jnp.concatenate(sides, axis=0))
    router[...] = rows[:EXPERTS]
    gain_moe[...] = rows[EXPERTS + 1 : EXPERTS + 2]
    line = rows[EXPERTS + 2 : EXPERTS + 3]
    for head in range(HEADS):
        table[head] = line[:, head * BUCKETS : (head + 1) * BUCKETS]
    padded = jnp.concatenate([gains, jnp.zeros((128 - CHUNK, 128), F32)], axis=0)
    spare = jnp.transpose(padded)
    pieces = [spare[SPARE + at : SPARE + at + 1, :CHUNK] for at in range(OWNERS)]
    gain_attn[...] = jnp.concatenate(pieces, axis=1)


def place_kernel(core, *refs):
    sources, outs, spaces = refs[:7], refs[7:11], refs[11:15]
    sems_in, sems_out = refs[15:]
    rows = pl.ds(0, SEQ)

    def move(me):
        own0, own1, expert_got = sources[:3]
        expert = (own0, expert_got) if me == 0 else (expert_got, own1)
        act, grad = [
            tuple(sources[at : at + 2]) if me == 0 else tuple(sources[at : at + 2])[::-1]
            for at in (3, 5)
        ]
        pairs = [
            [ref.at[0] for ref in expert],
            [ref.at[1] for ref in expert],
            list(act),
            [ref.at[rows] for ref in grad],
        ]
        reads, writes = [], []
        for at in range(4):
            for half in range(2):
                room = spaces[at].at[half]
                sem = 2 * at + half
                reads.append(pltpu.make_async_copy(pairs[at][half], room, sems_in.at[sem]))
                writes.append(pltpu.make_async_copy(room, outs[at].at[half], sems_out.at[sem]))
        for copy in reads:
            copy.start()
        for read, write in zip(reads, writes):
            read.wait()
            write.start()
        for copy in writes:
            copy.wait()

    for me in range(2):

        @pl.when(core[0] == me)
        def _(me=me):
            move(me)


def permuted(value, axis, pairs):
    return lax.ppermute(value, axis, pairs)


def swap(value):
    return permuted(value, "pipe", [(0, 1), (1, 0)])


def down(value):
    return permuted(value, "pipe", [(1, 0)])


def up(value):
    return permuted(value, "pipe", [(0, 1)])


def spread(value):
    count = lax.axis_size("tensor")
    return [value] + [
        permuted(value, "tensor", [(i, (i + by) % count) for i in range(count)])
        for by in range(1, count)
    ]


def after(value, *others):
    return lax.optimization_barrier((value, *others))[0]


def exchange(block):
    moved = lax.all_to_all(
        block.reshape(EXPERTS, 8, block.shape[1]),
        ("pipe", "expert"),
        split_axis=0,
        concat_axis=0,
        tiled=True,
    )
    return moved.reshape(block.shape)


def collect(block):
    moved = lax.all_to_all(
        block.reshape(EXPERTS * GROUP, 8, block.shape[3]),
        ("pipe", "expert", "tensor"),
        split_axis=0,
        concat_axis=0,
        tiled=True,
    )
    return moved.reshape(block.shape)


def shards(
    tokens,
    cotangent,
    routes,
    buckets,
    gain_attn,
    w_qkv,
    w_attn_out,
    rel_table,
    gain_moe,
    w_router,
    w_expert_in,
    w_expert_out,
):
    index = lax.axis_index("pipe")
    core = jnp.stack([index, lax.axis_index("tensor")]).astype(jnp.int32)
    qkv = w_qkv[0].T
    attn_out = w_attn_out[0]
    router = w_router[0].T
    ids = jnp.transpose(routes[0], (0, 2, 1))
    qkv2 = swap(qkv)
    attn_out2 = swap(attn_out)
    tables = (rel_table[0], swap(rel_table[0]))
    attn_gains = (gain_attn, swap(gain_attn))
    moe_gains = (gain_moe, swap(gain_moe))
    router2 = swap(router)
    ids2 = swap(lax.dynamic_index_in_dim(ids, 1 - index, 0, keepdims=False))

    attn_args = (qkv, qkv2, attn_out, attn_out2)

    (bias,) = kernel_call(
        bias_kernel,
        "bias",
        (core, buckets, *tables),
        (SMEM, VMEM, VMEM, VMEM),
        (shape(2, HEADS, SEQ, SEQ),),
    )
    partial0, projected0, probs0, attended0 = kernel_call(
        first_attention_kernel,
        "first_attention",
        (core, tokens, *attn_gains, bias, *attn_args),
        (SMEM, VMEM, VMEM, VMEM, VMEM, ANY, ANY, ANY, ANY),
        ATTENTION_OUT,
        ATTENTION_SCRATCH,
    )
    parts = spread(partial0)
    expert_specs = (ANY, ANY, ANY, ANY)
    route_args = (*moe_gains, router, router2, ids, ids2)

    def route(section, values, parts, more, wide):
        return kernel_call(
            lambda *refs: route_kernel(section, *refs),
            "route",
            (core, values, *parts, *route_args, *more),
            (SMEM,) + (VMEM,) * (11 + len(more)),
            (shape(SEQ, D), low(SEQ, D), shape(SEQ, 128), low(MAIN, wide)),
        )

    hidden0, moe_low0, meta0, sent = route(0, tokens, parts, (), WIDE)
    weights = lax.optimization_barrier((w_expert_in[0], w_expert_out[0], sent))[:2]
    expert_args = (w_expert_in[0], swap(weights[0]), w_expert_out[0], swap(weights[1]))
    block = exchange(sent)
    sent, rows0, pre0 = kernel_call(
        expert_forward_kernel,
        "expert_forward",
        (core, block, *expert_args),
        (SMEM, VMEM, *expert_specs),
        (low(EXPERTS, GROUP, 8, 256), low(ROWS, D), shape(ROWS, D)),
        EXPERT_SCRATCH,
    )
    block = collect(sent)
    out_rows0, part0 = kernel_call(
        combine_kernel,
        "combine",
        (core, meta0, block, hidden0),
        (SMEM, VMEM, VMEM, VMEM),
        (low(ROWS, PART), low(LINES, 128)),
    )

    act0, partial1, projected1, probs1, attended1 = kernel_call(
        second_attention_kernel,
        "second_attention",
        (core, *spread(part0), *attn_gains, bias, *attn_args),
        (SMEM,) + (VMEM,) * 7 + (ANY,) * 4,
        (low(SEQ, D), *ATTENTION_OUT),
        ATTENTION_SCRATCH,
    )
    hidden1, moe_low1, meta1, sent = route(1, act0, spread(partial1), (cotangent,), 2 * WIDE)
    block = exchange(sent)
    sent, rows1, grads1, act_low1, grad_pre1 = kernel_call(
        expert_both_kernel,
        "expert_both",
        (core, block, *expert_args),
        (SMEM, VMEM, *expert_specs),
        (low(EXPERTS, GROUP, 8, 512), low(ROWS, D), low(ROWS, D), low(ROWS, D), low(ROWS, D)),
        EXPERT_SCRATCH,
        vmem=16,
    )
    block = collect(sent)

    sent, part1 = kernel_call(
        second_back_kernel,
        "second_back",
        (core, meta1, block, cotangent, hidden1),
        (SMEM, VMEM, VMEM, VMEM, VMEM),
        (low(LINES + 16, 128), low(LINES, 128)),
    )

    def expert_grads(*args):
        return kernel_call(
            expert_grads_kernel, "expert_grads", args, (VMEM,) * 4, (shape(2, D, D),)
        )[0]

    def attention_back(section, parts, meta, hidden, upstream, saved, more, outputs, scratch):
        return kernel_call(
            lambda *refs: attention_back_kernel(section, *refs),
            "attention_back",
            (core, *parts, meta, hidden, upstream, *moe_gains, router, router2, *saved, *attn_args)
            + more,
            (SMEM,) + (VMEM,) * 13 + (ANY,) * 4 + (VMEM,) * len(more),
            (low(SEQ, D), shape(SEQ, D), *outputs),
            ATTENTION_SCRATCH + scratch,
        )

    partial, grad_hidden1, *grads = attention_back(
        1, spread(sent), meta1, hidden1, cotangent, (projected1, probs1), (),
        (low(HEADS, SEQ, SEQ), low(SEQ, QKV), low(SEQ, 128), shape(8, D)), (),
    )
    parts = spread(partial)
    (shared1,) = kernel_call(
        shared_kernel,
        "shared",
        (core, buckets, act0, *attn_gains, attended1, moe_low1, after(grad_hidden1, parts[3]), *grads),
        (SMEM,) + (VMEM,) * 11,
        (low(D, D + 128),),
        (pltpu.VMEM((128, 128), F32),),
    )
    expert_grad1 = expert_grads(after(rows1, parts[3]), grads1, act_low1, grad_pre1)
    parts[1] = after(parts[1], shared1, expert_grad1)
    grad_inputs1, upstream, sent = kernel_call(
        lambda *refs: input_back_kernel(1, *refs),
        "input_back",
        (core, *parts, act0, grad_hidden1, *attn_gains, meta0),
        (SMEM,) + (VMEM,) * 9,
        (shape(SEQ + 8, D), low(SEQ, D), low(MAIN, WIDE)),
    )

    block = exchange(sent)
    sent, grads0, act_low0, grad_pre0 = kernel_call(
        expert_back_kernel,
        "expert_back",
        (core, block, pre0, *expert_args),
        (SMEM, VMEM, VMEM, *expert_specs),
        (low(EXPERTS, GROUP, 8, 256), low(ROWS, D), low(ROWS, D), low(ROWS, D)),
        EXPERT_SCRATCH,
    )
    block = collect(sent)
    (sent,) = kernel_call(
        first_back_kernel,
        "first_back",
        (core, meta0, out_rows0, block, upstream),
        (SMEM,) + (VMEM,) * 4,
        (low(LINES + 16, 128),),
    )
    parts = spread(sent)
    expert_grad0 = expert_grads(after(rows0, sent), grads0, act_low0, grad_pre0)
    parts[3] = after(parts[3], expert_grad0)
    partial, grad_hidden0, mine, theirs = attention_back(
        0, parts, meta0, hidden0, upstream, (projected0, probs0),
        (moe_low0, *attn_gains, buckets, tokens, attended0, shared1),
        (low(D, D + 128), low(D, D + 128)),
        (pltpu.VMEM((128, 128), F32), pltpu.VMEM((D, D + 128), BF16)),
    )
    got = swap(theirs)

    (pair,) = kernel_call(
        pair_kernel, "pair", (mine, got), (VMEM, VMEM), (low(D, D + 128),)
    )
    parts = spread(after(partial, pair))
    blocks = pair.reshape(OWNERS, CHUNK, D + 128)
    blocks = lax.all_to_all(blocks, "expert", split_axis=0, concat_axis=0, tiled=True)
    act_parts = spread(after(part1, pair))
    grad_mine, grad_theirs = kernel_call(
        lambda *refs: input_back_kernel(0, *refs),
        "input_back",
        (core, *parts, tokens, grad_hidden0, *attn_gains, grad_inputs1),
        (SMEM,) + (VMEM,) * 9,
        (shape(SEQ + 8, D), shape(SEQ + 8, D)),
        (pltpu.VMEM((SEQ + 8, D), F32),),
    )
    grad_got = swap(grad_theirs)
    late = lax.optimization_barrier((expert_grad0, expert_grad1, parts[3]))
    expert_got = swap(jnp.where(index == 0, late[1], late[0]))
    (blocks,) = kernel_call(
        reduce_kernel,
        "reduce",
        (blocks, grad_mine, grad_got),
        (VMEM,) * 3,
        (low(*blocks.shape),),
    )
    act_mine, act_theirs = kernel_call(
        output_kernel,
        "output",
        (core, act0, *act_parts),
        (SMEM,) + (VMEM,) * 5,
        (low(SEQ, D), low(SEQ, D)),
    )
    act_got = swap(act_theirs)
    blocks = lax.all_to_all(blocks, "expert", split_axis=0, concat_axis=0, tiled=True)
    results = [shape(2, D, D), shape(2, D, D), low(2, SEQ, D), shape(2, SEQ, D)]
    grad_in, grad_out, activations, input_grad = kernel_call(
        place_kernel,
        "place",
        (core, expert_grad0, expert_grad1, expert_got)
        + (act_mine, act_got, grad_mine, grad_got),
        (SMEM,) + (ANY,) * 7,
        results,
        tuple(pltpu.VMEM(result.shape, result.dtype) for result in results)
        + (pltpu.SemaphoreType.DMA((8,)), pltpu.SemaphoreType.DMA((8,))),
        [ANY] * 4,
    )
    blocks = after(blocks, grad_in, grad_out, activations, input_grad)
    grad_qkv, grad_attn_out, grad_router, grad_gain, grad_moe_gain, grad_table = kernel_call(
        final_kernel,
        "final",
        (blocks,),
        (VMEM,),
        (shape(QKV, D), shape(HEAD_COLS, D), shape(EXPERTS, D), shape(1, D), shape(1, D))
        + (shape(HEADS, 1, BUCKETS),),
    )
    return (
        activations[None],
        input_grad[None],
        grad_gain,
        grad_qkv.T[None],
        grad_attn_out[None],
        jnp.transpose(grad_table, (1, 0, 2)),
        grad_moe_gain,
        grad_router.T[None],
        grad_in[None],
        grad_out[None],
    )


def solution(mesh):
    in_specs = (
        P(None, "expert", None),
        P(None, "expert", None),
        P("pipe", None, "expert", None),
        P(),
        P("pipe", None),
        P("pipe", None, "tensor"),
        P("pipe", "tensor", None),
        P("pipe", "tensor", None),
        P("pipe", None),
        P("pipe", None, None),
        P("pipe", "expert", None, "tensor"),
        P("pipe", "expert", "tensor", None),
    )
    out_specs = (
        P("pipe", None, "expert", None),
        P("pipe", None, "expert", None),
        P("pipe", None),
        P("pipe", None, "tensor"),
        P("pipe", "tensor", None),
        P("pipe", "tensor", None),
        P("pipe", None),
        P("pipe", None, None),
        P("pipe", "expert", None, "tensor"),
        P("pipe", "expert", "tensor", None),
    )
    return jax.shard_map(shards, mesh=mesh, in_specs=in_specs, out_specs=out_specs, check_vma=False)
```

```python
import jax
import jax.numpy as jnp
from jax import lax
from jax.experimental import pallas as pl
from jax.experimental.pallas import tpu as pltpu
from jax.sharding import PartitionSpec as P

EPSILON = 1e-06
F32 = jnp.float32
BF16 = jnp.bfloat16
SEQ = 128
D = 768
HEADS = 3
HEAD_DIM = 64
QKV = 3 * HEADS * HEAD_DIM
HEAD_COLS = HEADS * HEAD_DIM
EXPERTS = 32
OWNERS = 16
BUCKETS = 32
MAIN = 8 * EXPERTS
ROWS = 10 * EXPERTS
WIDE = D + 256
GROUP = 4
PART = D // GROUP
PIECE = 64
LINES = SEQ * PART // 128
SCALE = HEAD_DIM**-0.5
GELU_C = 0.7978845608028654
GELU_A = 0.044715
VMEM = pl.BlockSpec(memory_space=pltpu.VMEM)
SMEM = pl.BlockSpec(memory_space=pltpu.SMEM)
ANY = pl.BlockSpec(memory_space=pl.ANY)


def shape(*dims, dtype=F32):
    return jax.ShapeDtypeStruct(dims, dtype)


def low(*dims):
    return jax.ShapeDtypeStruct(dims, BF16)


def kernel_call(body, name, inputs, specs, outputs, scratch=(), out_specs=None, vmem=12):
    return pl.pallas_call(
        body,
        out_shape=tuple(outputs),
        in_specs=list(specs),
        out_specs=tuple(out_specs or [VMEM] * len(outputs)),
        scratch_shapes=list(scratch),
        compiler_params=pltpu.CompilerParams(vmem_limit_bytes=vmem * 2**20),
        cost_estimate=pl.CostEstimate(
            flops=1_600_000_000, bytes_accessed=8_000_000, transcendentals=0
        ),
        name=name,
    )(*inputs)


def dot(a, b):
    return jnp.dot(a, b, preferred_element_type=F32)


def dot_nt(a, b):
    return lax.dot_general(a, b, (((1,), (1,)), ((), ())), preferred_element_type=F32)


def dot_tn(a, b):
    return lax.dot_general(a, b, (((0,), (0,)), ((), ())), preferred_element_type=F32)


def iota(dims, axis):
    return lax.broadcasted_iota(jnp.int32, dims, axis)


def chosen(flag, own, other):
    return jnp.where(flag == 1, own, other)


def fetch(flag, own, other, target, semaphore):
    @pl.when(flag == 1)
    def _():
        pltpu.make_async_copy(own, target, semaphore).start()

    @pl.when(flag != 1)
    def _():
        pltpu.make_async_copy(other, target, semaphore).start()


def fetched(other, target, semaphore):
    pltpu.make_async_copy(other, target, semaphore).wait()


def norm(values):
    return lax.rsqrt(jnp.mean(values * values, axis=-1, keepdims=True) + EPSILON)


def norm_back(values, inverse, gain, upstream):
    weighted = upstream * gain
    inner = jnp.mean(weighted * values, axis=-1, keepdims=True)
    return inverse * weighted - values * (inverse * inverse * inverse) * inner


def total(refs):
    value = refs[0][...].astype(F32)
    for ref in refs[1:]:
        value = value + ref[...].astype(F32)
    return value


def gelu_parts(value):
    square = value * value
    tanh = jnp.tanh(GELU_C * value * (1.0 + GELU_A * square))
    return square, tanh


def pack(rows):
    spread = (iota((MAIN, EXPERTS), 0) // 8 == iota((MAIN, EXPERTS), 1)).astype(BF16)
    place = iota((MAIN, 128), 0) % 8
    parts = [rows[:MAIN]]
    for late in range(2):
        start = MAIN + late * EXPERTS
        copies = dot(spread, rows[start : start + EXPERTS])
        piece = jnp.zeros((MAIN, 128), F32)
        for r in range(D // 128):
            piece = jnp.where(place == r, copies[:, r * 128 : (r + 1) * 128], piece)
        parts.append(piece.astype(BF16))
    return jnp.concatenate(parts, axis=1)


def unpack(block):
    count = D // 128
    dims = (count * EXPERTS, MAIN)
    row = iota(dims, 0)
    gather = (iota(dims, 1) == (row % EXPERTS) * 8 + row // EXPERTS).astype(BF16)
    pieces = dot(gather, block[:, D:]).astype(BF16)
    parts = [block[:, :D]]
    for late in range(2):
        columns = slice(late * 128, (late + 1) * 128)
        blocks = [pieces[r * EXPERTS : (r + 1) * EXPERTS, columns] for r in range(count)]
        parts.append(jnp.concatenate(blocks, axis=1))
    return jnp.concatenate(parts, axis=0)


def part_of(value, part):
    last = GROUP * 128 + part * PIECE
    return value[:, part * 128 : (part + 1) * 128], value[:, last : last + PIECE]


def pack_parts(rows, out, start):
    spread = (iota((MAIN, EXPERTS), 0) // 8 == iota((MAIN, EXPERTS), 1)).astype(BF16)
    place = iota((MAIN, PIECE), 0) % 8
    copies = []
    for late in range(2):
        first = MAIN + late * EXPERTS
        copies.append(dot(spread, rows[first : first + EXPERTS]))
    for part in range(GROUP):
        piece = jnp.zeros((MAIN, PIECE), F32)
        for late in range(2):
            block, last = part_of(copies[late], part)
            piece = jnp.where(place == 3 * late, block[:, :PIECE], piece)
            piece = jnp.where(place == 3 * late + 1, block[:, PIECE:], piece)
            piece = jnp.where(place == 3 * late + 2, last, piece)
        block = jnp.concatenate([*part_of(rows[:MAIN], part), piece.astype(BF16)], axis=1)
        out[:, part, :, start : start + 256] = block.reshape(EXPERTS, 8, 256)


def unpack_part(block, start):
    value = block[:, 0, :, start : start + 256].astype(F32)
    for sender in range(1, GROUP):
        value = value + block[:, sender, :, start : start + 256].astype(F32)
    value = value.reshape(MAIN, 256).astype(BF16)
    dims = (6 * EXPERTS, MAIN)
    row = iota(dims, 0)
    gather = (iota(dims, 1) == (row % EXPERTS) * 8 + row // EXPERTS).astype(BF16)
    pieces = dot(gather, value[:, PART:]).astype(BF16)
    parts = [value[:, :PART]]
    for late in range(2):
        blocks = [pieces[r * EXPERTS : (r + 1) * EXPERTS] for r in range(3 * late, 3 * late + 3)]
        parts.append(jnp.concatenate(blocks, axis=1))
    return jnp.concatenate(parts, axis=0)


def own_part(index, value):
    block, last = part_of(value, 0)
    for part in range(1, GROUP):
        other_block, other_last = part_of(value, part)
        block = jnp.where(index == part, other_block, block)
        last = jnp.where(index == part, other_last, last)
    return jnp.concatenate([block, last], axis=1)


def fold(part):
    tail = jnp.concatenate([part[: SEQ // 2, 128:], part[SEQ // 2 :, 128:]], axis=1)
    return jnp.concatenate([part[:, :128], tail], axis=0)


def gathered(index, refs):
    parts = [ref[:LINES].astype(F32) for ref in refs]
    blocks, lasts = [], []
    for at in range(GROUP):
        value = parts[0]
        for by in range(1, GROUP):
            value = jnp.where((index + GROUP - by) % GROUP == at, parts[by], value)
        tail = value[SEQ:]
        blocks.append(value[:SEQ])
        lasts.append(jnp.concatenate([tail[:, :PIECE], tail[:, PIECE:]], axis=0))
    return jnp.concatenate(blocks + lasts, axis=1)


def column(row):
    return jnp.transpose(jnp.broadcast_to(row, (SEQ, 128)))


def slot_hot(target):
    return target == iota((SEQ, ROWS), 1).astype(F32)


def bias_kernel(core, buckets, own, other, out):
    bucket = buckets[...]
    causal = iota((SEQ, SEQ), 0) >= iota((SEQ, SEQ), 1)
    hot = [bucket == b for b in range(BUCKETS)]
    for section in range(2):
        flag = (core[0] == section).astype(jnp.int32)
        table = chosen(flag, own[...].astype(F32), other[...].astype(F32))
        for head in range(HEADS):
            value = jnp.zeros((SEQ, SEQ), F32)
            for b in range(BUCKETS):
                value = jnp.where(hot[b], table[head : head + 1, b : b + 1], value)
            out[section, head] = jnp.where(causal, value, -1e30)


def attention_body(values, gain, qkv_weight, out_weight, bias, refs):
    partial_out, projected_out, probs_out, attended_out = refs
    normed = (values * norm(values) * gain).astype(BF16)
    projected = dot_nt(normed, qkv_weight).astype(BF16)
    projected_out[...] = projected
    heads = []
    for head in range(HEADS):
        at = head * 3 * HEAD_DIM
        query = projected[:, at : at + HEAD_DIM]
        key = projected[:, at + HEAD_DIM : at + 2 * HEAD_DIM]
        value = projected[:, at + 2 * HEAD_DIM : at + 3 * HEAD_DIM]
        scores = dot_nt(query, key) * SCALE + bias[head]
        exps = jnp.exp(scores - jnp.max(scores, axis=-1, keepdims=True))
        probs = exps / jnp.sum(exps, axis=-1, keepdims=True)
        probs_out[head] = probs
        heads.append(dot(probs.astype(BF16), value))
    attended = jnp.concatenate(heads, axis=1).astype(BF16)
    attended_out[...] = attended
    partial_out[...] = dot(attended, out_weight).astype(BF16)


ATTENTION_OUT = (
    low(SEQ, D),
    low(SEQ, QKV),
    shape(HEADS, SEQ, SEQ),
    low(SEQ, HEAD_COLS),
)
ATTENTION_SCRATCH = (
    pltpu.VMEM((QKV, D), BF16),
    pltpu.VMEM((HEAD_COLS, D), BF16),
    pltpu.SemaphoreType.DMA((2,)),
)


def first_attention_kernel(core, tokens, own, other, bias, qkv, qkv2, out, out2, *refs):
    *results, qkv_weight, out_weight, sems = refs
    flag = (core[0] == 0).astype(jnp.int32)
    fetch(flag, qkv, qkv2, qkv_weight, sems.at[0])
    fetch(flag, out, out2, out_weight, sems.at[1])
    values = tokens[core[0]].astype(F32)
    gain = chosen(flag, own[...], other[...])
    fetched(qkv2, qkv_weight, sems.at[0])
    fetched(out2, out_weight, sems.at[1])
    attention_body(values, gain, qkv_weight[...], out_weight[...], bias[0], results)


def second_attention_kernel(
    core, a, b, c, d, own, other, bias, qkv, qkv2, out, out2, act, *refs
):
    *results, qkv_weight, out_weight, sems = refs
    flag = (core[0] == 1).astype(jnp.int32)
    fetch(flag, qkv, qkv2, qkv_weight, sems.at[0])
    fetch(flag, out, out2, out_weight, sems.at[1])
    section_out = gathered(core[1], (a, b, c, d)).astype(BF16)
    act[...] = section_out
    gain = chosen(flag, own[...], other[...])
    fetched(qkv2, qkv_weight, sems.at[0])
    fetched(out2, out_weight, sems.at[1])
    attention_body(
        section_out.astype(F32), gain, qkv_weight[...], out_weight[...], bias[1], results
    )


def route_kernel(section, core, values, a, b, c, d, own, other, router, router2, ids, ids2, *refs):
    if section == 1:
        cotangent, hidden_out, low_out, meta_out, sent = refs
    else:
        hidden_out, low_out, meta_out, sent = refs
    me = core[0]
    flag = (me == section).astype(jnp.int32)
    inputs = values[me] if section == 0 else values[...]
    hidden = inputs.astype(F32) + total((a, b, c, d))
    hidden_out[...] = hidden
    gain = chosen(flag, own[...], other[...])
    moe_low = (hidden * norm(hidden) * gain).astype(BF16)
    low_out[...] = moe_low
    weight = chosen(flag, router[...].astype(F32), router2[...].astype(F32)).astype(BF16)
    logits = dot_nt(moe_low, weight)
    routes = chosen(flag, ids[me], ids2[...]).astype(F32)
    columns = [column(routes[k : k + 1]) for k in range(2)]
    lanes = iota((SEQ, EXPERTS), 1).astype(F32)
    hot = [value[:, :EXPERTS] == lanes for value in columns]
    picked = [jnp.sum(jnp.where(h, logits, 0.0), axis=1, keepdims=True) for h in hot]
    top = jnp.maximum(picked[0], picked[1])
    exps = [jnp.exp(value - top) for value in picked]
    gates = [value / (exps[0] + exps[1]) for value in exps]
    per_row = (hot[0].astype(F32) + hot[1].astype(F32)).astype(BF16)
    earlier = (iota((SEQ, SEQ), 0) > iota((SEQ, SEQ), 1)).astype(BF16)
    before = dot(earlier, per_row)
    targets = []
    for k in range(2):
        slot = jnp.sum(jnp.where(hot[k], before, 0.0), axis=1, keepdims=True)
        expert = columns[k][:, :1]
        half = jnp.floor(expert * 0.5)
        chunk = (expert - 2.0 * half) * OWNERS + half
        targets.append(
            jnp.where(slot < 7.5, chunk * 8 + slot, MAIN + (slot - 8) * EXPERTS + chunk)
        )
    meta = jnp.concatenate(gates + targets + [value[:, :1] for value in columns], axis=1)
    meta_out[:, :6] = meta
    places = [slot_hot(target) for target in targets]
    either = (places[0] | places[1]).astype(BF16)
    sent[:, :WIDE] = pack(dot_tn(either, moe_low).astype(BF16))
    if section == 1:
        scaled = [
            jnp.where(place, gate, 0.0) for place, gate in zip(places, gates)
        ]
        sent[:, WIDE:] = pack(sent_grads(either, scaled, cotangent[me]))


def sent_grads(either, scaled, upstream):
    rows = dot_tn(either, upstream)
    ones = jnp.ones((SEQ, 128), BF16)
    gates = scaled[0] + scaled[1]
    high = gates.astype(BF16)
    rest = (gates - high.astype(F32)).astype(BF16)
    factor = (dot_tn(high, ones) + dot_tn(rest, ones))[:, :1]
    return (rows * factor).astype(BF16)


def expert_weights(flag, core, own_in, other_in, own_out, other_out, weight_in, weight_out, sems):
    fetch(flag, own_in.at[core], other_in.at[core], weight_in, sems.at[0])
    fetch(flag, own_out.at[core], other_out.at[core], weight_out, sems.at[1])


EXPERT_SCRATCH = (
    pltpu.VMEM((D, D), BF16),
    pltpu.VMEM((D, D), BF16),
    pltpu.SemaphoreType.DMA((2,)),
)


def expert_forward_kernel(
    core, block, own_in, other_in, own_out, other_out, sent, rows_out, pre_out, *scratch
):
    weight_in, weight_out, sems = scratch
    flag = (core[0] == 0).astype(jnp.int32)
    expert_weights(flag, core[0], own_in, other_in, own_out, other_out, *scratch)
    rows = unpack(block[...])
    rows_out[...] = rows
    fetched(other_in.at[0], weight_in, sems.at[0])
    pre_act = dot(rows, weight_in[...])
    pre_out[...] = pre_act
    _, tanh = gelu_parts(pre_act)
    act_low = (0.5 * pre_act * (1.0 + tanh)).astype(BF16)
    fetched(other_out.at[0], weight_out, sems.at[1])
    pack_parts(dot(act_low, weight_out[...]).astype(BF16), sent, 0)


def expert_back(grads, pre_act, weight_in, weight_out, act_out, grad_pre_out):
    square, tanh = gelu_parts(pre_act)
    act_low = (0.5 * pre_act * (1.0 + tanh)).astype(BF16)
    act_out[...] = act_low
    grad_act = dot_nt(grads, weight_out)
    slope = 0.5 * (1.0 + tanh) + 0.5 * pre_act * (1.0 - tanh * tanh) * GELU_C * (
        1.0 + 3.0 * GELU_A * square
    )
    grad_pre = (grad_act * slope).astype(BF16)
    grad_pre_out[...] = grad_pre
    return act_low, dot_nt(grad_pre, weight_in).astype(BF16)


def expert_both_kernel(
    core, block, own_in, other_in, own_out, other_out, sent, rows_out, grads_out, act_out, pre_out,
    *scratch
):
    weight_in, weight_out, sems = scratch
    flag = (core[0] == 1).astype(jnp.int32)
    expert_weights(flag, core[0], own_in, other_in, own_out, other_out, *scratch)
    rows = unpack(block[:, :WIDE])
    rows_out[...] = rows
    grads = unpack(block[:, WIDE:])
    grads_out[...] = grads
    fetched(other_in.at[0], weight_in, sems.at[0])
    pre_act = dot(rows, weight_in[...])
    fetched(other_out.at[0], weight_out, sems.at[1])
    act_low, grad_rows = expert_back(
        grads, pre_act, weight_in[...], weight_out[...], act_out, pre_out
    )
    pack_parts(grad_rows, sent, 256)
    pack_parts(dot(act_low, weight_out[...]).astype(BF16), sent, 0)


def expert_back_kernel(
    core, block, pre_act, own_in, other_in, own_out, other_out, sent, grads_out, act_out, pre_out,
    *scratch
):
    weight_in, weight_out, sems = scratch
    flag = (core[0] == 0).astype(jnp.int32)
    expert_weights(flag, core[0], own_in, other_in, own_out, other_out, *scratch)
    grads = unpack(block[...])
    grads_out[...] = grads
    fetched(other_out.at[0], weight_out, sems.at[1])
    fetched(other_in.at[0], weight_in, sems.at[0])
    _, grad_rows = expert_back(
        grads, pre_act[...], weight_in[...], weight_out[...], act_out, pre_out
    )
    pack_parts(grad_rows, sent, 0)


def expert_grads_kernel(rows, grads, act_low, grad_pre, out):
    out[0] = dot_tn(rows[...], grad_pre[...])
    out[1] = dot_tn(act_low[...], grads[...])


def combine_kernel(core, meta, block, hidden, rows_out, folded):
    rows = unpack_part(block, 0)
    rows_out[...] = rows
    value = own_part(core[1], hidden[...])
    for k in range(2):
        place = slot_hot(meta[:, 2 + k : 3 + k]).astype(BF16)
        value = value + meta[:, k : k + 1] * dot(place, rows)
    folded[...] = fold(value).astype(BF16)


def moe_back_body(meta, out_rows, grad_rows, upstream, sent, value):
    grad = jnp.zeros((SEQ, PART), F32)
    lanes = iota((SEQ, 128), 1)
    tail = jnp.zeros((SEQ, 128), F32)
    for k in range(2):
        place = slot_hot(meta[:, 2 + k : 3 + k]).astype(BF16)
        grad = grad + dot(place, grad_rows)
        picked = dot(place, out_rows)
        if value is not None:
            value = value + meta[:, k : k + 1] * picked
        inner = jnp.sum(picked * upstream, axis=1, keepdims=True)
        tail = jnp.where(lanes == k, inner, tail)
    sent[:LINES] = fold(grad).astype(BF16)
    sent[LINES:] = jnp.transpose(tail)[:16].astype(BF16)
    return value


def second_back_kernel(core, meta, block, cotangent, hidden, sent, folded):
    out_rows = unpack_part(block, 0)
    grad_rows = unpack_part(block, 256)
    upstream = own_part(core[1], cotangent[core[0]].astype(F32))
    value = own_part(core[1], hidden[...])
    folded[...] = fold(moe_back_body(meta, out_rows, grad_rows, upstream, sent, value)).astype(BF16)


def first_back_kernel(core, meta, out_rows, block, upstream, sent):
    part = own_part(core[1], upstream[...].astype(F32))
    moe_back_body(meta, out_rows[...], unpack_part(block, 0), part, sent, None)


def shared_body(
    buckets, scores, inputs, gain, grad_qkv, attended, grad_low, moe_low, grad_logits, moe_gain, rel,
    shared,
):
    bucket = buckets[...]
    rel[...] = jnp.zeros_like(rel)
    for b in range(BUCKETS):
        hot = bucket == b
        for head in range(HEADS):
            at = head * BUCKETS + b
            rel[at : at + 1] = jnp.sum(jnp.where(hot, scores[head], 0.0), axis=0, keepdims=True)
    table = jnp.sum(jnp.transpose(rel[...]), axis=0, keepdims=True)
    normed = (inputs * norm(inputs) * gain).astype(BF16)
    shared[:QKV, :D] = dot_tn(grad_qkv, normed).astype(BF16)
    shared[QKV:, :D] = dot_tn(attended, grad_low).astype(BF16)
    line = iota((128, D), 0)
    wide = jnp.concatenate([table, jnp.zeros((1, D - 128), F32)], axis=1)
    rows = jnp.where(line == EXPERTS + 1, moe_gain, 0.0)
    rows = jnp.where(line == EXPERTS + 2, wide, rows)
    shared[:, D:] = (dot_tn(moe_low, grad_logits) + jnp.transpose(rows)).astype(BF16)


def shared_kernel(
    core, buckets, values, own, other, attended, moe_low, grad_hidden, scores, grad_qkv, logits,
    moe_gain, shared, rel,
):
    gain = chosen((core[0] == 1).astype(jnp.int32), own[...], other[...])
    shared_body(
        buckets, [scores[head].astype(F32) for head in range(HEADS)], values[...].astype(F32), gain,
        grad_qkv[...], attended[...], grad_hidden[...].astype(BF16), moe_low[...], logits[...],
        moe_gain[0:1], rel, shared,
    )


def attention_back_kernel(
    section, core, a, b, c, d, meta, hidden, upstream, own, other, router, router2, projected, probs,
    qkv, qkv2, out, out2, *refs,
):
    if section == 0:
        (moe_low, own_attn, other_attn, buckets, values, attended, shared1) = refs[:7]
        (sent, grad_hidden_out, mine, theirs, qkv_weight, out_weight, sems, rel, shared) = refs[7:]
    else:
        (sent, grad_hidden_out, scores_out, qkv_out, logits_out, gain_out) = refs[:6]
        (qkv_weight, out_weight, sems) = refs[6:]
    me = core[0]
    flag = (me == section).astype(jnp.int32)
    fetch(flag, qkv, qkv2, qkv_weight, sems.at[0])
    fetch(flag, out, out2, out_weight, sems.at[1])
    grad_moe = gathered(core[1], (a, b, c, d))
    tails = total((a.at[pl.ds(LINES, 16)], b.at[pl.ds(LINES, 16)], c.at[pl.ds(LINES, 16)], d.at[pl.ds(LINES, 16)]))
    tails = jnp.transpose(jnp.concatenate([tails, jnp.zeros((112, 128), F32)], axis=0))
    gain = chosen(flag, own[...], other[...])
    weight = chosen(flag, router[...].astype(F32), router2[...].astype(F32)).astype(BF16)
    gates = [meta[:, k : k + 1] for k in range(2)]
    grad_gates = [tails[:, k : k + 1] for k in range(2)]
    mean = gates[0] * grad_gates[0] + gates[1] * grad_gates[1]
    lanes = iota((SEQ, 128), 1).astype(F32)
    grad_logits = jnp.zeros((SEQ, 128), F32)
    for k in range(2):
        grad = gates[k] * (grad_gates[k] - mean)
        grad_logits = jnp.where(meta[:, 4 + k : 5 + k] == lanes, grad, grad_logits)
    grad_logits = grad_logits.astype(BF16)
    grad_moe = grad_moe + dot(grad_logits[:, :EXPERTS], weight)
    state = hidden[...]
    inverse = norm(state)
    grad_moe_gain = jnp.sum(grad_moe * state * inverse, axis=0, keepdims=True)
    before = upstream[me] if section == 1 else upstream[...]
    grad_hidden = before.astype(F32) + norm_back(state, inverse, gain, grad_moe)
    grad_hidden_out[...] = grad_hidden
    grad_low = grad_hidden.astype(BF16)
    fetched(out2, out_weight, sems.at[1])
    grad_heads = dot_nt(grad_low, out_weight[...]).astype(BF16)
    grads = []
    score_grads = []
    for head in range(HEADS):
        at = head * 3 * HEAD_DIM
        query = projected[:, at : at + HEAD_DIM]
        key = projected[:, at + HEAD_DIM : at + 2 * HEAD_DIM]
        value = projected[:, at + 2 * HEAD_DIM : at + 3 * HEAD_DIM]
        grad_head = grad_heads[:, head * HEAD_DIM : (head + 1) * HEAD_DIM]
        prob = probs[head]
        grad_probs = dot_nt(grad_head, value)
        grad_value = dot_tn(prob.astype(BF16), grad_head)
        inner = jnp.sum(prob * grad_probs, axis=-1, keepdims=True)
        grad_scores = (prob * (grad_probs - inner)).astype(BF16)
        score_grads.append(grad_scores.astype(F32))
        grads.append(SCALE * dot(grad_scores, key))
        grads.append(SCALE * dot_tn(grad_scores, query))
        grads.append(grad_value)
    grad_qkv = jnp.concatenate(grads, axis=1).astype(BF16)
    fetched(qkv2, qkv_weight, sems.at[0])
    sent[...] = dot(grad_qkv, qkv_weight[...]).astype(BF16)
    if section == 1:
        for head in range(HEADS):
            scores_out[head] = score_grads[head].astype(BF16)
        qkv_out[...] = grad_qkv
        logits_out[...] = grad_logits
        gain_out[...] = jnp.broadcast_to(grad_moe_gain, (8, D))
    else:
        attn_gain = chosen(flag, own_attn[...], other_attn[...])
        shared_body(
            buckets, score_grads, values[me].astype(F32), attn_gain, grad_qkv, attended[...],
            grad_low, moe_low[...], grad_logits, grad_moe_gain, rel, shared,
        )
    if section == 0:

        @pl.when(me == 0)
        def _():
            mine[...] = shared[...]
            theirs[...] = shared1[...]

        @pl.when(me == 1)
        def _():
            mine[...] = shared1[...]
            theirs[...] = shared[...]


def input_back_kernel(section, core, a, b, c, d, values, grad_hidden, own, other, *refs):
    if section == 1:
        meta, grad_out, low_out, sent = refs
    else:
        second, mine, theirs, grad_out = refs
    me = core[0]
    flag = (me == section).astype(jnp.int32)
    grad_normed = total((a, b, c, d))
    inputs = (values[me] if section == 0 else values[...]).astype(F32)
    inverse = norm(inputs)
    gain = chosen(flag, own[...], other[...])
    grad_inputs = grad_hidden[...] + norm_back(inputs, inverse, gain, grad_normed)
    grad_out[:SEQ] = grad_inputs
    if section == 1:
        upstream = grad_inputs.astype(BF16)
        low_out[...] = upstream
        places = [slot_hot(meta[:, 2 + k : 3 + k]) for k in range(2)]
        either = (places[0] | places[1]).astype(BF16)
        scaled = [jnp.where(places[k], meta[:, k : k + 1], 0.0) for k in range(2)]
        sent[...] = pack(sent_grads(either, scaled, upstream))
    grad_gain = jnp.sum(grad_normed * inputs * inverse, axis=0, keepdims=True)
    grad_out[SEQ:] = jnp.broadcast_to(grad_gain, (8, D))
    if section == 0:

        @pl.when(me == 0)
        def _():
            mine[...] = grad_out[...]
            theirs[...] = second[...]

        @pl.when(me == 1)
        def _():
            mine[...] = second[...]
            theirs[...] = grad_out[...]


def output_kernel(core, first, a, b, c, d, mine, theirs):
    second = gathered(core[1], (a, b, c, d)).astype(BF16)

    @pl.when(core[0] == 0)
    def _():
        mine[...] = first[...]
        theirs[...] = second

    @pl.when(core[0] == 1)
    def _():
        mine[...] = second
        theirs[...] = first[...]


def pair_kernel(mine, got, out):
    out[...] = (mine[...].astype(F32) + got[...].astype(F32)).astype(BF16)


CHUNK = D // OWNERS
SPARE = 64


def reduce_kernel(blocks, mine, got, out):
    value = blocks[0].astype(F32)
    for at in range(1, OWNERS):
        value = value + blocks[at].astype(F32)
    gain = mine[SEQ : SEQ + 1] + got[SEQ : SEQ + 1]
    columns = jnp.transpose(jnp.broadcast_to(gain, (128, D)))
    lanes = iota((CHUNK, 128), 1)
    side = value[:, D:]
    for at in range(OWNERS):
        side = jnp.where(lanes == SPARE + at, columns[at * CHUNK : (at + 1) * CHUNK], side)
    main_low, side_low = value[:, :D].astype(BF16), side.astype(BF16)
    for at in range(OWNERS):
        out[at, :, :D] = main_low
        out[at, :, D:] = side_low


def final_kernel(blocks, qkv, attn_out, router, gain_attn, gain_moe, table):
    sides = []
    gains = jnp.zeros((CHUNK, 128), F32)
    for at in range(OWNERS):
        main = blocks[at, :, :D].astype(F32)
        rows = slice(at * CHUNK, (at + 1) * CHUNK)
        if (at + 1) * CHUNK <= QKV:
            qkv[rows] = main
        else:
            attn_out[at * CHUNK - QKV : (at + 1) * CHUNK - QKV] = main
        side = blocks[at, :, D:].astype(F32)
        sides.append(side)
        gains = gains + side
    rows = jnp.transpose(jnp.concatenate(sides, axis=0))
    router[...] = rows[:EXPERTS]
    gain_moe[...] = rows[EXPERTS + 1 : EXPERTS + 2]
    line = rows[EXPERTS + 2 : EXPERTS + 3]
    for head in range(HEADS):
        table[head] = line[:, head * BUCKETS : (head + 1) * BUCKETS]
    padded = jnp.concatenate([gains, jnp.zeros((128 - CHUNK, 128), F32)], axis=0)
    spare = jnp.transpose(padded)
    pieces = [spare[SPARE + at : SPARE + at + 1, :CHUNK] for at in range(OWNERS)]
    gain_attn[...] = jnp.concatenate(pieces, axis=1)


def place_kernel(core, *refs):
    sources, outs, spaces = refs[:8], refs[8:12], refs[12:16]
    sems_in, sems_out = refs[16:]
    rows = pl.ds(0, SEQ)

    def move(me):
        own0, got0, own1, got1 = sources[:4]
        expert = (own0, got0) if me == 0 else (got1, own1)
        act, grad = [
            tuple(sources[at : at + 2]) if me == 0 else tuple(sources[at : at + 2])[::-1]
            for at in (4, 6)
        ]
        pairs = [
            [ref.at[0] for ref in expert],
            [ref.at[1] for ref in expert],
            list(act),
            [ref.at[rows] for ref in grad],
        ]
        reads, writes = [], []
        for at in range(4):
            for half in range(2):
                room = spaces[at].at[half]
                sem = 2 * at + half
                reads.append(pltpu.make_async_copy(pairs[at][half], room, sems_in.at[sem]))
                writes.append(pltpu.make_async_copy(room, outs[at].at[half], sems_out.at[sem]))
        for copy in reads:
            copy.start()
        for read, write in zip(reads, writes):
            read.wait()
            write.start()
        for copy in writes:
            copy.wait()

    for me in range(2):

        @pl.when(core[0] == me)
        def _(me=me):
            move(me)


def permuted(value, axis, pairs):
    return lax.ppermute(value, axis, pairs)


def swap(value):
    return permuted(value, "pipe", [(0, 1), (1, 0)])


def down(value):
    return permuted(value, "pipe", [(1, 0)])


def up(value):
    return permuted(value, "pipe", [(0, 1)])


def spread(value):
    count = lax.axis_size("tensor")
    return [value] + [
        permuted(value, "tensor", [(i, (i + by) % count) for i in range(count)])
        for by in range(1, count)
    ]


def after(value, *others):
    return lax.optimization_barrier((value, *others))[0]


def exchange(block):
    moved = lax.all_to_all(
        block.reshape(EXPERTS, 8, block.shape[1]),
        ("pipe", "expert"),
        split_axis=0,
        concat_axis=0,
        tiled=True,
    )
    return moved.reshape(block.shape)


def collect(block):
    moved = lax.all_to_all(
        block.reshape(EXPERTS * GROUP, 8, block.shape[3]),
        ("pipe", "expert", "tensor"),
        split_axis=0,
        concat_axis=0,
        tiled=True,
    )
    return moved.reshape(block.shape)


def shards(
    tokens,
    cotangent,
    routes,
    buckets,
    gain_attn,
    w_qkv,
    w_attn_out,
    rel_table,
    gain_moe,
    w_router,
    w_expert_in,
    w_expert_out,
):
    index = lax.axis_index("pipe")
    core = jnp.stack([index, lax.axis_index("tensor")]).astype(jnp.int32)
    qkv = w_qkv[0].T
    attn_out = w_attn_out[0]
    router = w_router[0].T
    ids = jnp.transpose(routes[0], (0, 2, 1))
    qkv2 = swap(qkv)
    attn_out2 = swap(attn_out)
    tables = (rel_table[0], swap(rel_table[0]))
    attn_gains = (gain_attn, swap(gain_attn))
    moe_gains = (gain_moe, swap(gain_moe))
    router2 = swap(router)
    ids2 = swap(lax.dynamic_index_in_dim(ids, 1 - index, 0, keepdims=False))

    attn_args = (qkv, qkv2, attn_out, attn_out2)

    (bias,) = kernel_call(
        bias_kernel,
        "bias",
        (core, buckets, *tables),
        (SMEM, VMEM, VMEM, VMEM),
        (shape(2, HEADS, SEQ, SEQ),),
    )
    partial0, projected0, probs0, attended0 = kernel_call(
        first_attention_kernel,
        "first_attention",
        (core, tokens, *attn_gains, bias, *attn_args),
        (SMEM, VMEM, VMEM, VMEM, VMEM, ANY, ANY, ANY, ANY),
        ATTENTION_OUT,
        ATTENTION_SCRATCH,
    )
    parts = spread(partial0)
    expert_specs = (ANY, ANY, ANY, ANY)
    route_args = (*moe_gains, router, router2, ids, ids2)

    def route(section, values, parts, more, wide):
        return kernel_call(
            lambda *refs: route_kernel(section, *refs),
            "route",
            (core, values, *parts, *route_args, *more),
            (SMEM,) + (VMEM,) * (11 + len(more)),
            (shape(SEQ, D), low(SEQ, D), shape(SEQ, 128), low(MAIN, wide)),
        )

    hidden0, moe_low0, meta0, sent = route(0, tokens, parts, (), WIDE)
    weights = lax.optimization_barrier((w_expert_in[0], w_expert_out[0], sent))[:2]
    expert_args = (w_expert_in[0], swap(weights[0]), w_expert_out[0], swap(weights[1]))
    block = exchange(sent)
    sent, rows0, pre0 = kernel_call(
        expert_forward_kernel,
        "expert_forward",
        (core, block, *expert_args),
        (SMEM, VMEM, *expert_specs),
        (low(EXPERTS, GROUP, 8, 256), low(ROWS, D), shape(ROWS, D)),
        EXPERT_SCRATCH,
    )
    block = collect(sent)
    out_rows0, part0 = kernel_call(
        combine_kernel,
        "combine",
        (core, meta0, block, hidden0),
        (SMEM, VMEM, VMEM, VMEM),
        (low(ROWS, PART), low(LINES, 128)),
    )

    act0, partial1, projected1, probs1, attended1 = kernel_call(
        second_attention_kernel,
        "second_attention",
        (core, *spread(part0), *attn_gains, bias, *attn_args),
        (SMEM,) + (VMEM,) * 7 + (ANY,) * 4,
        (low(SEQ, D), *ATTENTION_OUT),
        ATTENTION_SCRATCH,
    )
    hidden1, moe_low1, meta1, sent = route(1, act0, spread(partial1), (cotangent,), 2 * WIDE)
    block = exchange(sent)
    sent, rows1, grads1, act_low1, grad_pre1 = kernel_call(
        expert_both_kernel,
        "expert_both",
        (core, block, *expert_args),
        (SMEM, VMEM, *expert_specs),
        (low(EXPERTS, GROUP, 8, 512), low(ROWS, D), low(ROWS, D), low(ROWS, D), low(ROWS, D)),
        EXPERT_SCRATCH,
        vmem=16,
    )
    block = collect(sent)

    sent, part1 = kernel_call(
        second_back_kernel,
        "second_back",
        (core, meta1, block, cotangent, hidden1),
        (SMEM, VMEM, VMEM, VMEM, VMEM),
        (low(LINES + 16, 128), low(LINES, 128)),
    )

    def expert_grads(*args):
        return kernel_call(
            expert_grads_kernel, "expert_grads", args, (VMEM,) * 4, (shape(2, D, D),)
        )[0]

    def attention_back(section, parts, meta, hidden, upstream, saved, more, outputs, scratch):
        return kernel_call(
            lambda *refs: attention_back_kernel(section, *refs),
            "attention_back",
            (core, *parts, meta, hidden, upstream, *moe_gains, router, router2, *saved, *attn_args)
            + more,
            (SMEM,) + (VMEM,) * 13 + (ANY,) * 4 + (VMEM,) * len(more),
            (low(SEQ, D), shape(SEQ, D), *outputs),
            ATTENTION_SCRATCH + scratch,
        )

    partial, grad_hidden1, *grads = attention_back(
        1, spread(sent), meta1, hidden1, cotangent, (projected1, probs1), (),
        (low(HEADS, SEQ, SEQ), low(SEQ, QKV), low(SEQ, 128), shape(8, D)), (),
    )
    parts = spread(partial)
    (shared1,) = kernel_call(
        shared_kernel,
        "shared",
        (core, buckets, act0, *attn_gains, attended1, moe_low1, after(grad_hidden1, parts[3]), *grads),
        (SMEM,) + (VMEM,) * 11,
        (low(D, D + 128),),
        (pltpu.VMEM((128, 128), F32),),
    )
    expert_grad1 = expert_grads(after(rows1, parts[3]), grads1, act_low1, grad_pre1)
    parts[1] = after(parts[1], shared1, expert_grad1)
    grad_inputs1, upstream, sent = kernel_call(
        lambda *refs: input_back_kernel(1, *refs),
        "input_back",
        (core, *parts, act0, grad_hidden1, *attn_gains, meta0),
        (SMEM,) + (VMEM,) * 9,
        (shape(SEQ + 8, D), low(SEQ, D), low(MAIN, WIDE)),
    )

    expert_grad1 = after(expert_grad1, sent)
    expert_grad1b = up(expert_grad1)
    block = after(exchange(sent), expert_grad1b)
    sent, grads0, act_low0, grad_pre0 = kernel_call(
        expert_back_kernel,
        "expert_back",
        (core, block, pre0, *expert_args),
        (SMEM, VMEM, VMEM, *expert_specs),
        (low(EXPERTS, GROUP, 8, 256), low(ROWS, D), low(ROWS, D), low(ROWS, D)),
        EXPERT_SCRATCH,
    )
    block = collect(sent)
    (sent,) = kernel_call(
        first_back_kernel,
        "first_back",
        (core, meta0, out_rows0, block, upstream),
        (SMEM,) + (VMEM,) * 4,
        (low(LINES + 16, 128),),
    )
    parts = spread(sent)
    expert_grad0 = expert_grads(after(rows0, sent), grads0, act_low0, grad_pre0)
    parts[3] = after(parts[3], expert_grad0)
    partial, grad_hidden0, mine, theirs = attention_back(
        0, parts, meta0, hidden0, upstream, (projected0, probs0),
        (moe_low0, *attn_gains, buckets, tokens, attended0, shared1),
        (low(D, D + 128), low(D, D + 128)),
        (pltpu.VMEM((128, 128), F32), pltpu.VMEM((D, D + 128), BF16)),
    )
    got = swap(theirs)
    parts = spread(partial)
    expert_grad0 = after(expert_grad0, got)
    expert_grad0b = down(expert_grad0)

    (pair,) = kernel_call(
        pair_kernel, "pair", (mine, got), (VMEM, VMEM), (low(D, D + 128),)
    )
    blocks = pair.reshape(OWNERS, CHUNK, D + 128)
    blocks = lax.all_to_all(blocks, "expert", split_axis=0, concat_axis=0, tiled=True)
    act_parts = spread(after(part1, pair))
    grad_mine, grad_theirs = kernel_call(
        lambda *refs: input_back_kernel(0, *refs),
        "input_back",
        (core, *parts, tokens, grad_hidden0, *attn_gains, grad_inputs1),
        (SMEM,) + (VMEM,) * 9,
        (shape(SEQ + 8, D), shape(SEQ + 8, D)),
        (pltpu.VMEM((SEQ + 8, D), F32),),
    )
    grad_got = swap(grad_theirs)
    (blocks,) = kernel_call(
        reduce_kernel,
        "reduce",
        (blocks, grad_mine, grad_got),
        (VMEM,) * 3,
        (low(*blocks.shape),),
    )
    act_mine, act_theirs = kernel_call(
        output_kernel,
        "output",
        (core, act0, *act_parts),
        (SMEM,) + (VMEM,) * 5,
        (low(SEQ, D), low(SEQ, D)),
    )
    act_got = swap(act_theirs)
    blocks = lax.all_to_all(blocks, "expert", split_axis=0, concat_axis=0, tiled=True)
    results = [shape(2, D, D), shape(2, D, D), low(2, SEQ, D), shape(2, SEQ, D)]
    grad_in, grad_out, activations, input_grad = kernel_call(
        place_kernel,
        "place",
        (core, expert_grad0, expert_grad0b, expert_grad1, expert_grad1b)
        + (act_mine, act_got, grad_mine, grad_got),
        (SMEM,) + (ANY,) * 8,
        results,
        tuple(pltpu.VMEM(result.shape, result.dtype) for result in results)
        + (pltpu.SemaphoreType.DMA((8,)), pltpu.SemaphoreType.DMA((8,))),
        [ANY] * 4,
    )
    blocks = after(blocks, grad_in, grad_out, activations, input_grad)
    grad_qkv, grad_attn_out, grad_router, grad_gain, grad_moe_gain, grad_table = kernel_call(
        final_kernel,
        "final",
        (blocks,),
        (VMEM,),
        (shape(QKV, D), shape(HEAD_COLS, D), shape(EXPERTS, D), shape(1, D), shape(1, D))
        + (shape(HEADS, 1, BUCKETS),),
    )
    return (
        activations[None],
        input_grad[None],
        grad_gain,
        grad_qkv.T[None],
        grad_attn_out[None],
        jnp.transpose(grad_table, (1, 0, 2)),
        grad_moe_gain,
        grad_router.T[None],
        grad_in[None],
        grad_out[None],
    )


def solution(mesh):
    in_specs = (
        P(None, "expert", None),
        P(None, "expert", None),
        P("pipe", None, "expert", None),
        P(),
        P("pipe", None),
        P("pipe", None, "tensor"),
        P("pipe", "tensor", None),
        P("pipe", "tensor", None),
        P("pipe", None),
        P("pipe", None, None),
        P("pipe", "expert", None, "tensor"),
        P("pipe", "expert", "tensor", None),
    )
    out_specs = (
        P("pipe", None, "expert", None),
        P("pipe", None, "expert", None),
        P("pipe", None),
        P("pipe", None, "tensor"),
        P("pipe", "tensor", None),
        P("pipe", "tensor", None),
        P("pipe", None),
        P("pipe", None, None),
        P("pipe", "expert", None, "tensor"),
        P("pipe", "expert", "tensor", None),
    )
    return jax.shard_map(shards, mesh=mesh, in_specs=in_specs, out_specs=out_specs, check_vma=False)
```

```python
import jax
import jax.numpy as jnp
from jax import lax
from jax.experimental import pallas as pl
from jax.experimental.pallas import tpu as pltpu
from jax.sharding import PartitionSpec as P

EPSILON = 1e-06
F32 = jnp.float32
BF16 = jnp.bfloat16
SEQ = 128
D = 768
HEADS = 3
HEAD_DIM = 64
QKV = 3 * HEADS * HEAD_DIM
HEAD_COLS = HEADS * HEAD_DIM
EXPERTS = 32
OWNERS = 16
BUCKETS = 32
MAIN = 8 * EXPERTS
ROWS = 10 * EXPERTS
WIDE = D + 256
GROUP = 4
PART = D // GROUP
PIECE = 64
LINES = SEQ * PART // 128
SCALE = HEAD_DIM**-0.5
GELU_C = 0.7978845608028654
GELU_A = 0.044715
VMEM = pl.BlockSpec(memory_space=pltpu.VMEM)
SMEM = pl.BlockSpec(memory_space=pltpu.SMEM)
ANY = pl.BlockSpec(memory_space=pl.ANY)
HBM = pl.BlockSpec(memory_space=pltpu.HBM)


def shape(*dims, dtype=F32):
    return jax.ShapeDtypeStruct(dims, dtype)


def low(*dims):
    return jax.ShapeDtypeStruct(dims, BF16)


def kernel_call(body, name, inputs, specs, outputs, scratch=(), out_specs=None, vmem=12):
    return pl.pallas_call(
        body,
        out_shape=tuple(outputs),
        in_specs=list(specs),
        out_specs=tuple(out_specs or [VMEM] * len(outputs)),
        scratch_shapes=list(scratch),
        compiler_params=pltpu.CompilerParams(vmem_limit_bytes=vmem * 2**20),
        cost_estimate=pl.CostEstimate(
            flops=1_600_000_000, bytes_accessed=8_000_000, transcendentals=0
        ),
        name=name,
    )(*inputs)


def dot(a, b):
    return jnp.dot(a, b, preferred_element_type=F32)


def dot_nt(a, b):
    return lax.dot_general(a, b, (((1,), (1,)), ((), ())), preferred_element_type=F32)


def dot_tn(a, b):
    return lax.dot_general(a, b, (((0,), (0,)), ((), ())), preferred_element_type=F32)


def iota(dims, axis):
    return lax.broadcasted_iota(jnp.int32, dims, axis)


def chosen(flag, own, other):
    return jnp.where(flag == 1, own, other)


def fetch(flag, own, other, target, semaphore):
    @pl.when(flag == 1)
    def _():
        pltpu.make_async_copy(own, target, semaphore).start()

    @pl.when(flag != 1)
    def _():
        pltpu.make_async_copy(other, target, semaphore).start()


def fetched(other, target, semaphore):
    pltpu.make_async_copy(other, target, semaphore).wait()


def norm(values):
    return lax.rsqrt(jnp.mean(values * values, axis=-1, keepdims=True) + EPSILON)


def norm_back(values, inverse, gain, upstream):
    weighted = upstream * gain
    inner = jnp.mean(weighted * values, axis=-1, keepdims=True)
    return inverse * weighted - values * (inverse * inverse * inverse) * inner


def total(refs):
    value = refs[0][...].astype(F32)
    for ref in refs[1:]:
        value = value + ref[...].astype(F32)
    return value


def gelu_parts(value):
    square = value * value
    tanh = jnp.tanh(GELU_C * value * (1.0 + GELU_A * square))
    return square, tanh


def pack(rows):
    spread = (iota((MAIN, EXPERTS), 0) // 8 == iota((MAIN, EXPERTS), 1)).astype(BF16)
    place = iota((MAIN, 128), 0) % 8
    parts = [rows[:MAIN]]
    for late in range(2):
        start = MAIN + late * EXPERTS
        copies = dot(spread, rows[start : start + EXPERTS])
        piece = jnp.zeros((MAIN, 128), F32)
        for r in range(D // 128):
            piece = jnp.where(place == r, copies[:, r * 128 : (r + 1) * 128], piece)
        parts.append(piece.astype(BF16))
    return jnp.concatenate(parts, axis=1)


def unpack(block):
    count = D // 128
    dims = (count * EXPERTS, MAIN)
    row = iota(dims, 0)
    gather = (iota(dims, 1) == (row % EXPERTS) * 8 + row // EXPERTS).astype(BF16)
    pieces = dot(gather, block[:, D:]).astype(BF16)
    parts = [block[:, :D]]
    for late in range(2):
        columns = slice(late * 128, (late + 1) * 128)
        blocks = [pieces[r * EXPERTS : (r + 1) * EXPERTS, columns] for r in range(count)]
        parts.append(jnp.concatenate(blocks, axis=1))
    return jnp.concatenate(parts, axis=0)


def part_of(value, part):
    last = GROUP * 128 + part * PIECE
    return value[:, part * 128 : (part + 1) * 128], value[:, last : last + PIECE]


def pack_parts(rows, out, start):
    spread = (iota((MAIN, EXPERTS), 0) // 8 == iota((MAIN, EXPERTS), 1)).astype(BF16)
    place = iota((MAIN, PIECE), 0) % 8
    copies = []
    for late in range(2):
        first = MAIN + late * EXPERTS
        copies.append(dot(spread, rows[first : first + EXPERTS]))
    for part in range(GROUP):
        piece = jnp.zeros((MAIN, PIECE), F32)
        for late in range(2):
            block, last = part_of(copies[late], part)
            piece = jnp.where(place == 3 * late, block[:, :PIECE], piece)
            piece = jnp.where(place == 3 * late + 1, block[:, PIECE:], piece)
            piece = jnp.where(place == 3 * late + 2, last, piece)
        block = jnp.concatenate([*part_of(rows[:MAIN], part), piece.astype(BF16)], axis=1)
        out[:, part, :, start : start + 256] = block.reshape(EXPERTS, 8, 256)


def unpack_part(block, start):
    value = block[:, 0, :, start : start + 256].astype(F32)
    for sender in range(1, GROUP):
        value = value + block[:, sender, :, start : start + 256].astype(F32)
    value = value.reshape(MAIN, 256).astype(BF16)
    dims = (6 * EXPERTS, MAIN)
    row = iota(dims, 0)
    gather = (iota(dims, 1) == (row % EXPERTS) * 8 + row // EXPERTS).astype(BF16)
    pieces = dot(gather, value[:, PART:]).astype(BF16)
    parts = [value[:, :PART]]
    for late in range(2):
        blocks = [pieces[r * EXPERTS : (r + 1) * EXPERTS] for r in range(3 * late, 3 * late + 3)]
        parts.append(jnp.concatenate(blocks, axis=1))
    return jnp.concatenate(parts, axis=0)


def own_part(index, value):
    block, last = part_of(value, 0)
    for part in range(1, GROUP):
        other_block, other_last = part_of(value, part)
        block = jnp.where(index == part, other_block, block)
        last = jnp.where(index == part, other_last, last)
    return jnp.concatenate([block, last], axis=1)


def fold(part):
    tail = jnp.concatenate([part[: SEQ // 2, 128:], part[SEQ // 2 :, 128:]], axis=1)
    return jnp.concatenate([part[:, :128], tail], axis=0)


def gathered(index, refs):
    parts = [ref[:LINES].astype(F32) for ref in refs]
    blocks, lasts = [], []
    for at in range(GROUP):
        value = parts[0]
        for by in range(1, GROUP):
            value = jnp.where((index + GROUP - by) % GROUP == at, parts[by], value)
        tail = value[SEQ:]
        blocks.append(value[:SEQ])
        lasts.append(jnp.concatenate([tail[:, :PIECE], tail[:, PIECE:]], axis=0))
    return jnp.concatenate(blocks + lasts, axis=1)


def column(row):
    return jnp.transpose(jnp.broadcast_to(row, (SEQ, 128)))


def slot_hot(target):
    return target == iota((SEQ, ROWS), 1).astype(F32)


def bias_kernel(core, buckets, own, other, out):
    bucket = buckets[...]
    causal = iota((SEQ, SEQ), 0) >= iota((SEQ, SEQ), 1)
    hot = [bucket == b for b in range(BUCKETS)]
    for section in range(2):
        flag = (core[0] == section).astype(jnp.int32)
        table = chosen(flag, own[...].astype(F32), other[...].astype(F32))
        for head in range(HEADS):
            value = jnp.zeros((SEQ, SEQ), F32)
            for b in range(BUCKETS):
                value = jnp.where(hot[b], table[head : head + 1, b : b + 1], value)
            out[section, head] = jnp.where(causal, value, -1e30)


def attention_body(values, gain, qkv_weight, out_weight, bias, refs):
    partial_out, projected_out, probs_out, attended_out = refs
    normed = (values * norm(values) * gain).astype(BF16)
    projected = dot_nt(normed, qkv_weight).astype(BF16)
    projected_out[...] = projected
    heads = []
    for head in range(HEADS):
        at = head * 3 * HEAD_DIM
        query = projected[:, at : at + HEAD_DIM]
        key = projected[:, at + HEAD_DIM : at + 2 * HEAD_DIM]
        value = projected[:, at + 2 * HEAD_DIM : at + 3 * HEAD_DIM]
        scores = dot_nt(query, key) * SCALE + bias[head]
        exps = jnp.exp(scores - jnp.max(scores, axis=-1, keepdims=True))
        probs = exps / jnp.sum(exps, axis=-1, keepdims=True)
        probs_out[head] = probs
        heads.append(dot(probs.astype(BF16), value))
    attended = jnp.concatenate(heads, axis=1).astype(BF16)
    attended_out[...] = attended
    partial_out[...] = dot(attended, out_weight).astype(BF16)


ATTENTION_OUT = (
    low(SEQ, D),
    low(SEQ, QKV),
    shape(HEADS, SEQ, SEQ),
    low(SEQ, HEAD_COLS),
)
ATTENTION_SCRATCH = (
    pltpu.VMEM((QKV, D), BF16),
    pltpu.VMEM((HEAD_COLS, D), BF16),
    pltpu.SemaphoreType.DMA((2,)),
)


def first_attention_kernel(core, tokens, own, other, bias, qkv, qkv2, out, out2, *refs):
    partial_out, *kept_outs, qkv_weight, out_weight, sems, projected, probs, attended, more = refs
    flag = (core[0] == 0).astype(jnp.int32)
    fetch(flag, qkv, qkv2, qkv_weight, sems.at[0])
    fetch(flag, out, out2, out_weight, sems.at[1])
    values = tokens[core[0]].astype(F32)
    gain = chosen(flag, own[...], other[...])
    fetched(qkv2, qkv_weight, sems.at[0])
    fetched(out2, out_weight, sems.at[1])
    results = (partial_out, projected, probs, attended)
    attention_body(values, gain, qkv_weight[...], out_weight[...], bias[0], results)
    kept = (projected, probs, attended)
    copies = [
        pltpu.make_async_copy(value, target, more.at[at])
        for at, (value, target) in enumerate(zip(kept, kept_outs))
    ]
    for copy in copies:
        copy.start()
    for copy in copies:
        copy.wait()


def second_attention_kernel(
    core, a, b, c, d, own, other, bias, qkv, qkv2, out, out2, act, *refs
):
    *results, qkv_weight, out_weight, sems = refs
    flag = (core[0] == 1).astype(jnp.int32)
    fetch(flag, qkv, qkv2, qkv_weight, sems.at[0])
    fetch(flag, out, out2, out_weight, sems.at[1])
    section_out = gathered(core[1], (a, b, c, d)).astype(BF16)
    act[...] = section_out
    gain = chosen(flag, own[...], other[...])
    fetched(qkv2, qkv_weight, sems.at[0])
    fetched(out2, out_weight, sems.at[1])
    attention_body(
        section_out.astype(F32), gain, qkv_weight[...], out_weight[...], bias[1], results
    )


def route_kernel(section, core, values, a, b, c, d, own, other, router, router2, ids, ids2, *refs):
    if section == 1:
        cotangent, hidden_out, low_out, meta_out, sent = refs
    else:
        hidden_out, low_out, meta_out, sent = refs
    me = core[0]
    flag = (me == section).astype(jnp.int32)
    inputs = values[me] if section == 0 else values[...]
    hidden = inputs.astype(F32) + total((a, b, c, d))
    hidden_out[...] = hidden
    gain = chosen(flag, own[...], other[...])
    moe_low = (hidden * norm(hidden) * gain).astype(BF16)
    low_out[...] = moe_low
    weight = chosen(flag, router[...].astype(F32), router2[...].astype(F32)).astype(BF16)
    logits = dot_nt(moe_low, weight)
    routes = chosen(flag, ids[me], ids2[...]).astype(F32)
    columns = [column(routes[k : k + 1]) for k in range(2)]
    lanes = iota((SEQ, EXPERTS), 1).astype(F32)
    hot = [value[:, :EXPERTS] == lanes for value in columns]
    picked = [jnp.sum(jnp.where(h, logits, 0.0), axis=1, keepdims=True) for h in hot]
    top = jnp.maximum(picked[0], picked[1])
    exps = [jnp.exp(value - top) for value in picked]
    gates = [value / (exps[0] + exps[1]) for value in exps]
    per_row = (hot[0].astype(F32) + hot[1].astype(F32)).astype(BF16)
    earlier = (iota((SEQ, SEQ), 0) > iota((SEQ, SEQ), 1)).astype(BF16)
    before = dot(earlier, per_row)
    targets = []
    for k in range(2):
        slot = jnp.sum(jnp.where(hot[k], before, 0.0), axis=1, keepdims=True)
        expert = columns[k][:, :1]
        half = jnp.floor(expert * 0.5)
        chunk = (expert - 2.0 * half) * OWNERS + half
        targets.append(
            jnp.where(slot < 7.5, chunk * 8 + slot, MAIN + (slot - 8) * EXPERTS + chunk)
        )
    meta = jnp.concatenate(gates + targets + [value[:, :1] for value in columns], axis=1)
    meta_out[:, :6] = meta
    places = [slot_hot(target) for target in targets]
    either = (places[0] | places[1]).astype(BF16)
    sent[:, :WIDE] = pack(dot_tn(either, moe_low).astype(BF16))
    if section == 1:
        scaled = [
            jnp.where(place, gate, 0.0) for place, gate in zip(places, gates)
        ]
        sent[:, WIDE:] = pack(sent_grads(either, scaled, cotangent[me]))


def sent_grads(either, scaled, upstream):
    rows = dot_tn(either, upstream)
    ones = jnp.ones((SEQ, 128), BF16)
    gates = scaled[0] + scaled[1]
    high = gates.astype(BF16)
    rest = (gates - high.astype(F32)).astype(BF16)
    factor = (dot_tn(high, ones) + dot_tn(rest, ones))[:, :1]
    return (rows * factor).astype(BF16)


def expert_weights(flag, core, own_in, other_in, own_out, other_out, weight_in, weight_out, sems):
    fetch(flag, own_in.at[core], other_in.at[core], weight_in, sems.at[0])
    fetch(flag, own_out.at[core], other_out.at[core], weight_out, sems.at[1])


EXPERT_SCRATCH = (
    pltpu.VMEM((D, D), BF16),
    pltpu.VMEM((D, D), BF16),
    pltpu.SemaphoreType.DMA((2,)),
)


def expert_forward_kernel(
    core, block, own_in, other_in, own_out, other_out, sent, rows_out, pre_out, *scratch
):
    weight_in, weight_out, sems = scratch
    flag = (core[0] == 0).astype(jnp.int32)
    expert_weights(flag, core[0], own_in, other_in, own_out, other_out, *scratch)
    rows = unpack(block[...])
    rows_out[...] = rows
    fetched(other_in.at[0], weight_in, sems.at[0])
    pre_act = dot(rows, weight_in[...])
    pre_out[...] = pre_act
    _, tanh = gelu_parts(pre_act)
    act_low = (0.5 * pre_act * (1.0 + tanh)).astype(BF16)
    fetched(other_out.at[0], weight_out, sems.at[1])
    pack_parts(dot(act_low, weight_out[...]).astype(BF16), sent, 0)


def expert_back(grads, pre_act, weight_in, weight_out, act_out, grad_pre_out):
    square, tanh = gelu_parts(pre_act)
    act_low = (0.5 * pre_act * (1.0 + tanh)).astype(BF16)
    act_out[...] = act_low
    grad_act = dot_nt(grads, weight_out)
    slope = 0.5 * (1.0 + tanh) + 0.5 * pre_act * (1.0 - tanh * tanh) * GELU_C * (
        1.0 + 3.0 * GELU_A * square
    )
    grad_pre = (grad_act * slope).astype(BF16)
    grad_pre_out[...] = grad_pre
    return act_low, dot_nt(grad_pre, weight_in).astype(BF16)


def expert_both_kernel(
    core, block, own_in, other_in, own_out, other_out, sent, rows_out, grads_out, act_out, pre_out,
    *scratch
):
    weight_in, weight_out, sems = scratch
    flag = (core[0] == 1).astype(jnp.int32)
    expert_weights(flag, core[0], own_in, other_in, own_out, other_out, *scratch)
    rows = unpack(block[:, :WIDE])
    rows_out[...] = rows
    grads = unpack(block[:, WIDE:])
    grads_out[...] = grads
    fetched(other_in.at[0], weight_in, sems.at[0])
    pre_act = dot(rows, weight_in[...])
    fetched(other_out.at[0], weight_out, sems.at[1])
    act_low, grad_rows = expert_back(
        grads, pre_act, weight_in[...], weight_out[...], act_out, pre_out
    )
    pack_parts(grad_rows, sent, 256)
    pack_parts(dot(act_low, weight_out[...]).astype(BF16), sent, 0)


def expert_back_kernel(
    core, block, pre_act, own_in, other_in, own_out, other_out, sent, grads_out, act_out, pre_out,
    *scratch
):
    weight_in, weight_out, sems = scratch
    flag = (core[0] == 0).astype(jnp.int32)
    expert_weights(flag, core[0], own_in, other_in, own_out, other_out, *scratch)
    grads = unpack(block[...])
    grads_out[...] = grads
    fetched(other_out.at[0], weight_out, sems.at[1])
    fetched(other_in.at[0], weight_in, sems.at[0])
    _, grad_rows = expert_back(
        grads, pre_act[...], weight_in[...], weight_out[...], act_out, pre_out
    )
    pack_parts(grad_rows, sent, 0)


def expert_grads_kernel(rows, grads, act_low, grad_pre, out, space, sems):
    copies = [pltpu.make_async_copy(space.at[at], out.at[at], sems.at[at]) for at in range(2)]
    for at, (left, right) in enumerate(((rows, grad_pre), (act_low, grads))):
        space[at] = dot_tn(left[...], right[...])
        copies[at].start()
    for copy in copies:
        copy.wait()


def combine_kernel(core, meta, block, hidden, rows_out, folded):
    rows = unpack_part(block, 0)
    rows_out[...] = rows
    value = own_part(core[1], hidden[...])
    for k in range(2):
        place = slot_hot(meta[:, 2 + k : 3 + k]).astype(BF16)
        value = value + meta[:, k : k + 1] * dot(place, rows)
    folded[...] = fold(value).astype(BF16)


def moe_back_body(meta, out_rows, grad_rows, upstream, sent, value):
    grad = jnp.zeros((SEQ, PART), F32)
    lanes = iota((SEQ, 128), 1)
    tail = jnp.zeros((SEQ, 128), F32)
    for k in range(2):
        place = slot_hot(meta[:, 2 + k : 3 + k]).astype(BF16)
        grad = grad + dot(place, grad_rows)
        picked = dot(place, out_rows)
        if value is not None:
            value = value + meta[:, k : k + 1] * picked
        inner = jnp.sum(picked * upstream, axis=1, keepdims=True)
        tail = jnp.where(lanes == k, inner, tail)
    sent[:LINES] = fold(grad).astype(BF16)
    sent[LINES:] = jnp.transpose(tail)[:16].astype(BF16)
    return value


def second_back_kernel(core, meta, block, cotangent, hidden, sent, folded):
    out_rows = unpack_part(block, 0)
    grad_rows = unpack_part(block, 256)
    upstream = own_part(core[1], cotangent[core[0]].astype(F32))
    value = own_part(core[1], hidden[...])
    folded[...] = fold(moe_back_body(meta, out_rows, grad_rows, upstream, sent, value)).astype(BF16)


def first_back_kernel(core, meta, out_rows, block, upstream, sent):
    part = own_part(core[1], upstream[...].astype(F32))
    moe_back_body(meta, out_rows[...], unpack_part(block, 0), part, sent, None)


def shared_body(
    buckets, scores, inputs, gain, grad_qkv, attended, grad_low, moe_low, grad_logits, moe_gain, rel,
    shared,
):
    bucket = buckets[...]
    rel[...] = jnp.zeros_like(rel)
    for b in range(BUCKETS):
        hot = bucket == b
        for head in range(HEADS):
            at = head * BUCKETS + b
            rel[at : at + 1] = jnp.sum(jnp.where(hot, scores[head], 0.0), axis=0, keepdims=True)
    table = jnp.sum(jnp.transpose(rel[...]), axis=0, keepdims=True)
    normed = (inputs * norm(inputs) * gain).astype(BF16)
    shared[:QKV, :D] = dot_tn(grad_qkv, normed).astype(BF16)
    shared[QKV:, :D] = dot_tn(attended, grad_low).astype(BF16)
    line = iota((128, D), 0)
    wide = jnp.concatenate([table, jnp.zeros((1, D - 128), F32)], axis=1)
    rows = jnp.where(line == EXPERTS + 1, moe_gain, 0.0)
    rows = jnp.where(line == EXPERTS + 2, wide, rows)
    shared[:, D:] = (dot_tn(moe_low, grad_logits) + jnp.transpose(rows)).astype(BF16)


def shared_kernel(
    core, buckets, values, own, other, attended, moe_low, grad_hidden, scores, grad_qkv, logits,
    moe_gain, shared, rel,
):
    gain = chosen((core[0] == 1).astype(jnp.int32), own[...], other[...])
    shared_body(
        buckets, [scores[head].astype(F32) for head in range(HEADS)], values[...].astype(F32), gain,
        grad_qkv[...], attended[...], grad_hidden[...].astype(BF16), moe_low[...], logits[...],
        moe_gain[0:1], rel, shared,
    )


def attention_back_kernel(
    section, core, a, b, c, d, meta, hidden, upstream, own, other, router, router2, projected, probs,
    qkv, qkv2, out, out2, *refs,
):
    if section == 0:
        (moe_low, own_attn, other_attn, buckets, values, attended, shared1) = refs[:7]
        (sent, grad_hidden_out, mine, theirs, qkv_weight, out_weight, sems, rel, shared) = refs[7:]
    else:
        (sent, grad_hidden_out, scores_out, qkv_out, logits_out, gain_out) = refs[:6]
        (qkv_weight, out_weight, sems) = refs[6:]
    me = core[0]
    flag = (me == section).astype(jnp.int32)
    fetch(flag, qkv, qkv2, qkv_weight, sems.at[0])
    fetch(flag, out, out2, out_weight, sems.at[1])
    grad_moe = gathered(core[1], (a, b, c, d))
    tails = total((a.at[pl.ds(LINES, 16)], b.at[pl.ds(LINES, 16)], c.at[pl.ds(LINES, 16)], d.at[pl.ds(LINES, 16)]))
    tails = jnp.transpose(jnp.concatenate([tails, jnp.zeros((112, 128), F32)], axis=0))
    gain = chosen(flag, own[...], other[...])
    weight = chosen(flag, router[...].astype(F32), router2[...].astype(F32)).astype(BF16)
    gates = [meta[:, k : k + 1] for k in range(2)]
    grad_gates = [tails[:, k : k + 1] for k in range(2)]
    mean = gates[0] * grad_gates[0] + gates[1] * grad_gates[1]
    lanes = iota((SEQ, 128), 1).astype(F32)
    grad_logits = jnp.zeros((SEQ, 128), F32)
    for k in range(2):
        grad = gates[k] * (grad_gates[k] - mean)
        grad_logits = jnp.where(meta[:, 4 + k : 5 + k] == lanes, grad, grad_logits)
    grad_logits = grad_logits.astype(BF16)
    grad_moe = grad_moe + dot(grad_logits[:, :EXPERTS], weight)
    state = hidden[...]
    inverse = norm(state)
    grad_moe_gain = jnp.sum(grad_moe * state * inverse, axis=0, keepdims=True)
    before = upstream[me] if section == 1 else upstream[...]
    grad_hidden = before.astype(F32) + norm_back(state, inverse, gain, grad_moe)
    grad_hidden_out[...] = grad_hidden
    grad_low = grad_hidden.astype(BF16)
    fetched(out2, out_weight, sems.at[1])
    grad_heads = dot_nt(grad_low, out_weight[...]).astype(BF16)
    grads = []
    score_grads = []
    for head in range(HEADS):
        at = head * 3 * HEAD_DIM
        query = projected[:, at : at + HEAD_DIM]
        key = projected[:, at + HEAD_DIM : at + 2 * HEAD_DIM]
        value = projected[:, at + 2 * HEAD_DIM : at + 3 * HEAD_DIM]
        grad_head = grad_heads[:, head * HEAD_DIM : (head + 1) * HEAD_DIM]
        prob = probs[head]
        grad_probs = dot_nt(grad_head, value)
        grad_value = dot_tn(prob.astype(BF16), grad_head)
        inner = jnp.sum(prob * grad_probs, axis=-1, keepdims=True)
        grad_scores = (prob * (grad_probs - inner)).astype(BF16)
        score_grads.append(grad_scores.astype(F32))
        grads.append(SCALE * dot(grad_scores, key))
        grads.append(SCALE * dot_tn(grad_scores, query))
        grads.append(grad_value)
    grad_qkv = jnp.concatenate(grads, axis=1).astype(BF16)
    fetched(qkv2, qkv_weight, sems.at[0])
    sent[...] = dot(grad_qkv, qkv_weight[...]).astype(BF16)
    if section == 1:
        for head in range(HEADS):
            scores_out[head] = score_grads[head].astype(BF16)
        qkv_out[...] = grad_qkv
        logits_out[...] = grad_logits
        gain_out[...] = jnp.broadcast_to(grad_moe_gain, (8, D))
    else:
        attn_gain = chosen(flag, own_attn[...], other_attn[...])
        shared_body(
            buckets, score_grads, values[me].astype(F32), attn_gain, grad_qkv, attended[...],
            grad_low, moe_low[...], grad_logits, grad_moe_gain, rel, shared,
        )
    if section == 0:

        @pl.when(me == 0)
        def _():
            mine[...] = shared[...]
            theirs[...] = shared1[...]

        @pl.when(me == 1)
        def _():
            mine[...] = shared1[...]
            theirs[...] = shared[...]


def input_back_kernel(section, core, a, b, c, d, values, grad_hidden, own, other, *refs):
    if section == 1:
        meta, grad_out, low_out, sent = refs
    else:
        second, mine, theirs, grad_out = refs
    me = core[0]
    flag = (me == section).astype(jnp.int32)
    grad_normed = total((a, b, c, d))
    inputs = (values[me] if section == 0 else values[...]).astype(F32)
    inverse = norm(inputs)
    gain = chosen(flag, own[...], other[...])
    grad_inputs = grad_hidden[...] + norm_back(inputs, inverse, gain, grad_normed)
    grad_out[:SEQ] = grad_inputs
    if section == 1:
        upstream = grad_inputs.astype(BF16)
        low_out[...] = upstream
        places = [slot_hot(meta[:, 2 + k : 3 + k]) for k in range(2)]
        either = (places[0] | places[1]).astype(BF16)
        scaled = [jnp.where(places[k], meta[:, k : k + 1], 0.0) for k in range(2)]
        sent[...] = pack(sent_grads(either, scaled, upstream))
    grad_gain = jnp.sum(grad_normed * inputs * inverse, axis=0, keepdims=True)
    grad_out[SEQ:] = jnp.broadcast_to(grad_gain, (8, D))
    if section == 0:

        @pl.when(me == 0)
        def _():
            mine[...] = grad_out[...]
            theirs[...] = second[...]

        @pl.when(me == 1)
        def _():
            mine[...] = second[...]
            theirs[...] = grad_out[...]


def output_kernel(core, first, a, b, c, d, mine, theirs):
    second = gathered(core[1], (a, b, c, d)).astype(BF16)

    @pl.when(core[0] == 0)
    def _():
        mine[...] = first[...]
        theirs[...] = second

    @pl.when(core[0] == 1)
    def _():
        mine[...] = second
        theirs[...] = first[...]


def pair_kernel(mine, got, out):
    out[...] = (mine[...].astype(F32) + got[...].astype(F32)).astype(BF16)


CHUNK = D // OWNERS
SPARE = 64


def reduce_kernel(blocks, mine, got, out):
    value = blocks[0].astype(F32)
    for at in range(1, OWNERS):
        value = value + blocks[at].astype(F32)
    gain = mine[SEQ : SEQ + 1] + got[SEQ : SEQ + 1]
    columns = jnp.transpose(jnp.broadcast_to(gain, (128, D)))
    lanes = iota((CHUNK, 128), 1)
    side = value[:, D:]
    for at in range(OWNERS):
        side = jnp.where(lanes == SPARE + at, columns[at * CHUNK : (at + 1) * CHUNK], side)
    main_low, side_low = value[:, :D].astype(BF16), side.astype(BF16)
    for at in range(OWNERS):
        out[at, :, :D] = main_low
        out[at, :, D:] = side_low


def final_kernel(blocks, qkv, attn_out, router, gain_attn, gain_moe, table):
    sides = []
    gains = jnp.zeros((CHUNK, 128), F32)
    for at in range(OWNERS):
        main = blocks[at, :, :D].astype(F32)
        rows = slice(at * CHUNK, (at + 1) * CHUNK)
        if (at + 1) * CHUNK <= QKV:
            qkv[rows] = main
        else:
            attn_out[at * CHUNK - QKV : (at + 1) * CHUNK - QKV] = main
        side = blocks[at, :, D:].astype(F32)
        sides.append(side)
        gains = gains + side
    rows = jnp.transpose(jnp.concatenate(sides, axis=0))
    router[...] = rows[:EXPERTS]
    gain_moe[...] = rows[EXPERTS + 1 : EXPERTS + 2]
    line = rows[EXPERTS + 2 : EXPERTS + 3]
    for head in range(HEADS):
        table[head] = line[:, head * BUCKETS : (head + 1) * BUCKETS]
    padded = jnp.concatenate([gains, jnp.zeros((128 - CHUNK, 128), F32)], axis=0)
    spare = jnp.transpose(padded)
    pieces = [spare[SPARE + at : SPARE + at + 1, :CHUNK] for at in range(OWNERS)]
    gain_attn[...] = jnp.concatenate(pieces, axis=1)


def place_kernel(core, *refs):
    sources, outs, spaces = refs[:8], refs[8:12], refs[12:16]
    sems_in, sems_out = refs[16:]
    rows = pl.ds(0, SEQ)

    def move(me):
        own0, got0, own1, got1 = sources[:4]
        expert = (own0, got0) if me == 0 else (got1, own1)
        act, grad = [
            tuple(sources[at : at + 2]) if me == 0 else tuple(sources[at : at + 2])[::-1]
            for at in (4, 6)
        ]
        pairs = [
            [ref.at[0] for ref in expert],
            [ref.at[1] for ref in expert],
            list(act),
            [ref.at[rows] for ref in grad],
        ]
        reads, writes = [], []
        for at in range(4):
            for half in range(2):
                room = spaces[at].at[half]
                sem = 2 * at + half
                reads.append(pltpu.make_async_copy(pairs[at][half], room, sems_in.at[sem]))
                writes.append(pltpu.make_async_copy(room, outs[at].at[half], sems_out.at[sem]))
        for copy in reads:
            copy.start()
        for read, write in zip(reads, writes):
            read.wait()
            write.start()
        for copy in writes:
            copy.wait()

    for me in range(2):

        @pl.when(core[0] == me)
        def _(me=me):
            move(me)


def permuted(value, axis, pairs):
    return lax.ppermute(value, axis, pairs)


def swap(value):
    return permuted(value, "pipe", [(0, 1), (1, 0)])


def down(value):
    return permuted(value, "pipe", [(1, 0)])


def up(value):
    return permuted(value, "pipe", [(0, 1)])


def spread(value):
    count = lax.axis_size("tensor")
    return [value] + [
        permuted(value, "tensor", [(i, (i + by) % count) for i in range(count)])
        for by in range(1, count)
    ]


def after(value, *others):
    return lax.optimization_barrier((value, *others))[0]


def exchange(block):
    moved = lax.all_to_all(
        block.reshape(EXPERTS, 8, block.shape[1]),
        ("pipe", "expert"),
        split_axis=0,
        concat_axis=0,
        tiled=True,
    )
    return moved.reshape(block.shape)


def collect(block):
    moved = lax.all_to_all(
        block.reshape(EXPERTS * GROUP, 8, block.shape[3]),
        ("pipe", "expert", "tensor"),
        split_axis=0,
        concat_axis=0,
        tiled=True,
    )
    return moved.reshape(block.shape)


def shards(
    tokens,
    cotangent,
    routes,
    buckets,
    gain_attn,
    w_qkv,
    w_attn_out,
    rel_table,
    gain_moe,
    w_router,
    w_expert_in,
    w_expert_out,
):
    index = lax.axis_index("pipe")
    core = jnp.stack([index, lax.axis_index("tensor")]).astype(jnp.int32)
    qkv = w_qkv[0].T
    attn_out = w_attn_out[0]
    router = w_router[0].T
    ids = jnp.transpose(routes[0], (0, 2, 1))
    qkv2 = swap(qkv)
    attn_out2 = swap(attn_out)
    tables = (rel_table[0], swap(rel_table[0]))
    attn_gains = (gain_attn, swap(gain_attn))
    moe_gains = (gain_moe, swap(gain_moe))
    router2 = swap(router)
    ids2 = swap(lax.dynamic_index_in_dim(ids, 1 - index, 0, keepdims=False))

    attn_args = (qkv, qkv2, attn_out, attn_out2)

    (bias,) = kernel_call(
        bias_kernel,
        "bias",
        (core, buckets, *tables),
        (SMEM, VMEM, VMEM, VMEM),
        (shape(2, HEADS, SEQ, SEQ),),
    )
    partial0, projected0, probs0, attended0 = kernel_call(
        first_attention_kernel,
        "first_attention",
        (core, tokens, *attn_gains, bias, *attn_args),
        (SMEM, VMEM, VMEM, VMEM, VMEM, ANY, ANY, ANY, ANY),
        ATTENTION_OUT,
        ATTENTION_SCRATCH
        + tuple(pltpu.VMEM(kept.shape, kept.dtype) for kept in ATTENTION_OUT[1:])
        + (pltpu.SemaphoreType.DMA((3,)),),
        (VMEM, HBM, HBM, HBM),
    )
    parts = spread(partial0)
    expert_specs = (ANY, ANY, ANY, ANY)
    route_args = (*moe_gains, router, router2, ids, ids2)

    def route(section, values, parts, more, wide):
        return kernel_call(
            lambda *refs: route_kernel(section, *refs),
            "route",
            (core, values, *parts, *route_args, *more),
            (SMEM,) + (VMEM,) * (11 + len(more)),
            (shape(SEQ, D), low(SEQ, D), shape(SEQ, 128), low(MAIN, wide)),
        )

    hidden0, moe_low0, meta0, sent = route(0, tokens, parts, (), WIDE)
    weights = lax.optimization_barrier((w_expert_in[0], w_expert_out[0], sent))[:2]
    expert_args = (w_expert_in[0], swap(weights[0]), w_expert_out[0], swap(weights[1]))
    block = exchange(sent)
    sent, rows0, pre0 = kernel_call(
        expert_forward_kernel,
        "expert_forward",
        (core, block, *expert_args),
        (SMEM, VMEM, *expert_specs),
        (low(EXPERTS, GROUP, 8, 256), low(ROWS, D), shape(ROWS, D)),
        EXPERT_SCRATCH,
    )
    block = collect(sent)
    out_rows0, part0 = kernel_call(
        combine_kernel,
        "combine",
        (core, meta0, block, hidden0),
        (SMEM, VMEM, VMEM, VMEM),
        (low(ROWS, PART), low(LINES, 128)),
    )

    act0, partial1, projected1, probs1, attended1 = kernel_call(
        second_attention_kernel,
        "second_attention",
        (core, *spread(part0), *attn_gains, bias, *attn_args),
        (SMEM,) + (VMEM,) * 7 + (ANY,) * 4,
        (low(SEQ, D), *ATTENTION_OUT),
        ATTENTION_SCRATCH,
    )
    hidden1, moe_low1, meta1, sent = route(1, act0, spread(partial1), (cotangent,), 2 * WIDE)
    block = exchange(sent)
    sent, rows1, grads1, act_low1, grad_pre1 = kernel_call(
        expert_both_kernel,
        "expert_both",
        (core, block, *expert_args),
        (SMEM, VMEM, *expert_specs),
        (low(EXPERTS, GROUP, 8, 512), low(ROWS, D), low(ROWS, D), low(ROWS, D), low(ROWS, D)),
        EXPERT_SCRATCH,
        vmem=16,
    )
    block = collect(sent)

    sent, part1 = kernel_call(
        second_back_kernel,
        "second_back",
        (core, meta1, block, cotangent, hidden1),
        (SMEM, VMEM, VMEM, VMEM, VMEM),
        (low(LINES + 16, 128), low(LINES, 128)),
    )

    def expert_grads(*args):
        return kernel_call(
            expert_grads_kernel,
            "expert_grads",
            args,
            (VMEM,) * 4,
            (shape(2, D, D),),
            (pltpu.VMEM((2, D, D), F32), pltpu.SemaphoreType.DMA((2,))),
            (HBM,),
        )[0]

    def attention_back(section, parts, meta, hidden, upstream, saved, more, outputs, scratch):
        return kernel_call(
            lambda *refs: attention_back_kernel(section, *refs),
            "attention_back",
            (core, *parts, meta, hidden, upstream, *moe_gains, router, router2, *saved, *attn_args)
            + more,
            (SMEM,) + (VMEM,) * 13 + (ANY,) * 4 + (VMEM,) * len(more),
            (low(SEQ, D), shape(SEQ, D), *outputs),
            ATTENTION_SCRATCH + scratch,
        )

    partial, grad_hidden1, *grads = attention_back(
        1, spread(sent), meta1, hidden1, cotangent, (projected1, probs1), (),
        (low(HEADS, SEQ, SEQ), low(SEQ, QKV), low(SEQ, 128), shape(8, D)), (),
    )
    parts = spread(partial)
    (shared1,) = kernel_call(
        shared_kernel,
        "shared",
        (core, buckets, act0, *attn_gains, attended1, moe_low1, after(grad_hidden1, parts[3]), *grads),
        (SMEM,) + (VMEM,) * 11,
        (low(D, D + 128),),
        (pltpu.VMEM((128, 128), F32),),
    )
    expert_grad1 = expert_grads(after(rows1, parts[3]), grads1, act_low1, grad_pre1)
    parts[1] = after(parts[1], shared1, expert_grad1)
    grad_inputs1, upstream, sent = kernel_call(
        lambda *refs: input_back_kernel(1, *refs),
        "input_back",
        (core, *parts, act0, grad_hidden1, *attn_gains, meta0),
        (SMEM,) + (VMEM,) * 9,
        (shape(SEQ + 8, D), low(SEQ, D), low(MAIN, WIDE)),
    )

    expert_grad1 = after(expert_grad1, sent)
    expert_grad1b = up(expert_grad1)
    block = after(exchange(sent), expert_grad1b)
    sent, grads0, act_low0, grad_pre0 = kernel_call(
        expert_back_kernel,
        "expert_back",
        (core, block, pre0, *expert_args),
        (SMEM, VMEM, VMEM, *expert_specs),
        (low(EXPERTS, GROUP, 8, 256), low(ROWS, D), low(ROWS, D), low(ROWS, D)),
        EXPERT_SCRATCH,
    )
    block = collect(sent)
    (sent,) = kernel_call(
        first_back_kernel,
        "first_back",
        (core, meta0, out_rows0, block, upstream),
        (SMEM,) + (VMEM,) * 4,
        (low(LINES + 16, 128),),
    )
    parts = spread(sent)
    expert_grad0 = expert_grads(after(rows0, sent), grads0, act_low0, grad_pre0)
    parts[3] = after(parts[3], expert_grad0)
    partial, grad_hidden0, mine, theirs = attention_back(
        0, parts, meta0, hidden0, upstream, (projected0, probs0),
        (moe_low0, *attn_gains, buckets, tokens, attended0, shared1),
        (low(D, D + 128), low(D, D + 128)),
        (pltpu.VMEM((128, 128), F32), pltpu.VMEM((D, D + 128), BF16)),
    )
    got = swap(theirs)
    parts = spread(partial)
    expert_grad0 = after(expert_grad0, got)
    expert_grad0b = down(expert_grad0)

    (pair,) = kernel_call(
        pair_kernel, "pair", (mine, got), (VMEM, VMEM), (low(D, D + 128),)
    )
    blocks = pair.reshape(OWNERS, CHUNK, D + 128)
    blocks = lax.all_to_all(blocks, "expert", split_axis=0, concat_axis=0, tiled=True)
    act_parts = spread(after(part1, pair))
    grad_mine, grad_theirs = kernel_call(
        lambda *refs: input_back_kernel(0, *refs),
        "input_back",
        (core, *parts, tokens, grad_hidden0, *attn_gains, grad_inputs1),
        (SMEM,) + (VMEM,) * 9,
        (shape(SEQ + 8, D), shape(SEQ + 8, D)),
        (pltpu.VMEM((SEQ + 8, D), F32),),
    )
    grad_got = swap(grad_theirs)
    (blocks,) = kernel_call(
        reduce_kernel,
        "reduce",
        (blocks, grad_mine, grad_got),
        (VMEM,) * 3,
        (low(*blocks.shape),),
    )
    act_mine, act_theirs = kernel_call(
        output_kernel,
        "output",
        (core, act0, *act_parts),
        (SMEM,) + (VMEM,) * 5,
        (low(SEQ, D), low(SEQ, D)),
    )
    act_got = swap(act_theirs)
    blocks = lax.all_to_all(blocks, "expert", split_axis=0, concat_axis=0, tiled=True)
    results = [shape(2, D, D), shape(2, D, D), low(2, SEQ, D), shape(2, SEQ, D)]
    grad_in, grad_out, activations, input_grad = kernel_call(
        place_kernel,
        "place",
        (core, expert_grad0, expert_grad0b, expert_grad1, expert_grad1b)
        + (act_mine, act_got, grad_mine, grad_got),
        (SMEM,) + (HBM,) * 4 + (ANY,) * 4,
        results,
        tuple(pltpu.VMEM(result.shape, result.dtype) for result in results)
        + (pltpu.SemaphoreType.DMA((8,)), pltpu.SemaphoreType.DMA((8,))),
        [ANY] * 4,
    )
    blocks = after(blocks, grad_in, grad_out, activations, input_grad)
    grad_qkv, grad_attn_out, grad_router, grad_gain, grad_moe_gain, grad_table = kernel_call(
        final_kernel,
        "final",
        (blocks,),
        (VMEM,),
        (shape(QKV, D), shape(HEAD_COLS, D), shape(EXPERTS, D), shape(1, D), shape(1, D))
        + (shape(HEADS, 1, BUCKETS),),
    )
    return (
        activations[None],
        input_grad[None],
        grad_gain,
        grad_qkv.T[None],
        grad_attn_out[None],
        jnp.transpose(grad_table, (1, 0, 2)),
        grad_moe_gain,
        grad_router.T[None],
        grad_in[None],
        grad_out[None],
    )


def solution(mesh):
    in_specs = (
        P(None, "expert", None),
        P(None, "expert", None),
        P("pipe", None, "expert", None),
        P(),
        P("pipe", None),
        P("pipe", None, "tensor"),
        P("pipe", "tensor", None),
        P("pipe", "tensor", None),
        P("pipe", None),
        P("pipe", None, None),
        P("pipe", "expert", None, "tensor"),
        P("pipe", "expert", "tensor", None),
    )
    out_specs = (
        P("pipe", None, "expert", None),
        P("pipe", None, "expert", None),
        P("pipe", None),
        P("pipe", None, "tensor"),
        P("pipe", "tensor", None),
        P("pipe", "tensor", None),
        P("pipe", None),
        P("pipe", None, None),
        P("pipe", "expert", None, "tensor"),
        P("pipe", "expert", "tensor", None),
    )
    return jax.shard_map(shards, mesh=mesh, in_specs=in_specs, out_specs=out_specs, check_vma=False)
```

```python
import jax
import jax.numpy as jnp
from jax import lax
from jax.experimental import pallas as pl
from jax.experimental.pallas import tpu as pltpu
from jax.sharding import PartitionSpec as P

EPSILON = 1e-06
F32 = jnp.float32
BF16 = jnp.bfloat16
SEQ = 128
D = 768
HEADS = 3
HEAD_DIM = 64
QKV = 3 * HEADS * HEAD_DIM
HEAD_COLS = HEADS * HEAD_DIM
EXPERTS = 32
OWNERS = 16
BUCKETS = 32
MAIN = 8 * EXPERTS
ROWS = 10 * EXPERTS
WIDE = D + 256
GROUP = 4
PART = D // GROUP
PIECE = 64
LINES = SEQ * PART // 128
SCALE = HEAD_DIM**-0.5
GELU_C = 0.7978845608028654
GELU_A = 0.044715
VMEM = pl.BlockSpec(memory_space=pltpu.VMEM)
SMEM = pl.BlockSpec(memory_space=pltpu.SMEM)
ANY = pl.BlockSpec(memory_space=pl.ANY)


def shape(*dims, dtype=F32):
    return jax.ShapeDtypeStruct(dims, dtype)


def low(*dims):
    return jax.ShapeDtypeStruct(dims, BF16)


def kernel_call(body, name, inputs, specs, outputs, scratch=(), out_specs=None, vmem=12):
    return pl.pallas_call(
        body,
        out_shape=tuple(outputs),
        in_specs=list(specs),
        out_specs=tuple(out_specs or [VMEM] * len(outputs)),
        scratch_shapes=list(scratch),
        compiler_params=pltpu.CompilerParams(vmem_limit_bytes=vmem * 2**20),
        cost_estimate=pl.CostEstimate(
            flops=1_600_000_000, bytes_accessed=8_000_000, transcendentals=0
        ),
        name=name,
    )(*inputs)


def dot(a, b):
    return jnp.dot(a, b, preferred_element_type=F32)


def dot_nt(a, b):
    return lax.dot_general(a, b, (((1,), (1,)), ((), ())), preferred_element_type=F32)


def dot_tn(a, b):
    return lax.dot_general(a, b, (((0,), (0,)), ((), ())), preferred_element_type=F32)


def iota(dims, axis):
    return lax.broadcasted_iota(jnp.int32, dims, axis)


def chosen(flag, own, other):
    return jnp.where(flag == 1, own, other)


def fetch(flag, own, other, target, semaphore):
    @pl.when(flag == 1)
    def _():
        pltpu.make_async_copy(own, target, semaphore).start()

    @pl.when(flag != 1)
    def _():
        pltpu.make_async_copy(other, target, semaphore).start()


def fetched(other, target, semaphore):
    pltpu.make_async_copy(other, target, semaphore).wait()


def norm(values):
    return lax.rsqrt(jnp.mean(values * values, axis=-1, keepdims=True) + EPSILON)


def norm_back(values, inverse, gain, upstream):
    weighted = upstream * gain
    inner = jnp.mean(weighted * values, axis=-1, keepdims=True)
    return inverse * weighted - values * (inverse * inverse * inverse) * inner


def total(refs):
    value = refs[0][...].astype(F32)
    for ref in refs[1:]:
        value = value + ref[...].astype(F32)
    return value


def gelu_parts(value):
    square = value * value
    tanh = jnp.tanh(GELU_C * value * (1.0 + GELU_A * square))
    return square, tanh


def pack(rows):
    spread = (iota((MAIN, EXPERTS), 0) // 8 == iota((MAIN, EXPERTS), 1)).astype(BF16)
    place = iota((MAIN, 128), 0) % 8
    parts = [rows[:MAIN]]
    for late in range(2):
        start = MAIN + late * EXPERTS
        copies = dot(spread, rows[start : start + EXPERTS])
        piece = jnp.zeros((MAIN, 128), F32)
        for r in range(D // 128):
            piece = jnp.where(place == r, copies[:, r * 128 : (r + 1) * 128], piece)
        parts.append(piece.astype(BF16))
    return jnp.concatenate(parts, axis=1)


def unpack(block):
    count = D // 128
    dims = (count * EXPERTS, MAIN)
    row = iota(dims, 0)
    gather = (iota(dims, 1) == (row % EXPERTS) * 8 + row // EXPERTS).astype(BF16)
    pieces = dot(gather, block[:, D:]).astype(BF16)
    parts = [block[:, :D]]
    for late in range(2):
        columns = slice(late * 128, (late + 1) * 128)
        blocks = [pieces[r * EXPERTS : (r + 1) * EXPERTS, columns] for r in range(count)]
        parts.append(jnp.concatenate(blocks, axis=1))
    return jnp.concatenate(parts, axis=0)


def part_of(value, part):
    last = GROUP * 128 + part * PIECE
    return value[:, part * 128 : (part + 1) * 128], value[:, last : last + PIECE]


def pack_parts(rows, out, start):
    spread = (iota((MAIN, EXPERTS), 0) // 8 == iota((MAIN, EXPERTS), 1)).astype(BF16)
    place = iota((MAIN, PIECE), 0) % 8
    copies = []
    for late in range(2):
        first = MAIN + late * EXPERTS
        copies.append(dot(spread, rows[first : first + EXPERTS]))
    for part in range(GROUP):
        piece = jnp.zeros((MAIN, PIECE), F32)
        for late in range(2):
            block, last = part_of(copies[late], part)
            piece = jnp.where(place == 3 * late, block[:, :PIECE], piece)
            piece = jnp.where(place == 3 * late + 1, block[:, PIECE:], piece)
            piece = jnp.where(place == 3 * late + 2, last, piece)
        block = jnp.concatenate([*part_of(rows[:MAIN], part), piece.astype(BF16)], axis=1)
        out[:, part, :, start : start + 256] = block.reshape(EXPERTS, 8, 256)


def unpack_part(block, start):
    value = block[:, 0, :, start : start + 256].astype(F32)
    for sender in range(1, GROUP):
        value = value + block[:, sender, :, start : start + 256].astype(F32)
    value = value.reshape(MAIN, 256).astype(BF16)
    dims = (6 * EXPERTS, MAIN)
    row = iota(dims, 0)
    gather = (iota(dims, 1) == (row % EXPERTS) * 8 + row // EXPERTS).astype(BF16)
    pieces = dot(gather, value[:, PART:]).astype(BF16)
    parts = [value[:, :PART]]
    for late in range(2):
        blocks = [pieces[r * EXPERTS : (r + 1) * EXPERTS] for r in range(3 * late, 3 * late + 3)]
        parts.append(jnp.concatenate(blocks, axis=1))
    return jnp.concatenate(parts, axis=0)


def own_part(index, value):
    block, last = part_of(value, 0)
    for part in range(1, GROUP):
        other_block, other_last = part_of(value, part)
        block = jnp.where(index == part, other_block, block)
        last = jnp.where(index == part, other_last, last)
    return jnp.concatenate([block, last], axis=1)


def fold(part):
    tail = jnp.concatenate([part[: SEQ // 2, 128:], part[SEQ // 2 :, 128:]], axis=1)
    return jnp.concatenate([part[:, :128], tail], axis=0)


def gathered(index, refs):
    parts = [ref[:LINES].astype(F32) for ref in refs]
    blocks, lasts = [], []
    for at in range(GROUP):
        value = parts[0]
        for by in range(1, GROUP):
            value = jnp.where((index + GROUP - by) % GROUP == at, parts[by], value)
        tail = value[SEQ:]
        blocks.append(value[:SEQ])
        lasts.append(jnp.concatenate([tail[:, :PIECE], tail[:, PIECE:]], axis=0))
    return jnp.concatenate(blocks + lasts, axis=1)


def column(row):
    return jnp.transpose(jnp.broadcast_to(row, (SEQ, 128)))


def slot_hot(target):
    return target == iota((SEQ, ROWS), 1).astype(F32)


def bias_kernel(core, buckets, own, other, out):
    bucket = buckets[...]
    causal = iota((SEQ, SEQ), 0) >= iota((SEQ, SEQ), 1)
    hot = [bucket == b for b in range(BUCKETS)]
    for section in range(2):
        flag = (core[0] == section).astype(jnp.int32)
        table = chosen(flag, own[...].astype(F32), other[...].astype(F32))
        for head in range(HEADS):
            value = jnp.zeros((SEQ, SEQ), F32)
            for b in range(BUCKETS):
                value = jnp.where(hot[b], table[head : head + 1, b : b + 1], value)
            out[section, head] = jnp.where(causal, value, -1e30)


def attention_body(values, gain, qkv_weight, out_weight, bias, refs):
    partial_out, projected_out, probs_out, attended_out = refs
    normed = (values * norm(values) * gain).astype(BF16)
    projected = dot_nt(normed, qkv_weight).astype(BF16)
    projected_out[...] = projected
    heads = []
    for head in range(HEADS):
        at = head * 3 * HEAD_DIM
        query = projected[:, at : at + HEAD_DIM]
        key = projected[:, at + HEAD_DIM : at + 2 * HEAD_DIM]
        value = projected[:, at + 2 * HEAD_DIM : at + 3 * HEAD_DIM]
        scores = dot_nt(query, key) * SCALE + bias[head]
        exps = jnp.exp(scores - jnp.max(scores, axis=-1, keepdims=True))
        probs = exps / jnp.sum(exps, axis=-1, keepdims=True)
        probs_out[head] = probs
        heads.append(dot(probs.astype(BF16), value))
    attended = jnp.concatenate(heads, axis=1).astype(BF16)
    attended_out[...] = attended
    partial_out[...] = dot(attended, out_weight).astype(BF16)


ATTENTION_OUT = (
    low(SEQ, D),
    low(SEQ, QKV),
    shape(HEADS, SEQ, SEQ),
    low(SEQ, HEAD_COLS),
)
ATTENTION_SCRATCH = (
    pltpu.VMEM((QKV, D), BF16),
    pltpu.VMEM((HEAD_COLS, D), BF16),
    pltpu.SemaphoreType.DMA((2,)),
)


def first_attention_kernel(core, tokens, own, other, bias, qkv, qkv2, out, out2, *refs):
    *results, qkv_weight, out_weight, sems = refs
    flag = (core[0] == 0).astype(jnp.int32)
    fetch(flag, qkv, qkv2, qkv_weight, sems.at[0])
    fetch(flag, out, out2, out_weight, sems.at[1])
    values = tokens[core[0]].astype(F32)
    gain = chosen(flag, own[...], other[...])
    fetched(qkv2, qkv_weight, sems.at[0])
    fetched(out2, out_weight, sems.at[1])
    attention_body(values, gain, qkv_weight[...], out_weight[...], bias[0], results)


def second_attention_kernel(
    core, a, b, c, d, own, other, bias, qkv, qkv2, out, out2, act, *refs
):
    *results, qkv_weight, out_weight, sems = refs
    flag = (core[0] == 1).astype(jnp.int32)
    fetch(flag, qkv, qkv2, qkv_weight, sems.at[0])
    fetch(flag, out, out2, out_weight, sems.at[1])
    section_out = gathered(core[1], (a, b, c, d)).astype(BF16)
    act[...] = section_out
    gain = chosen(flag, own[...], other[...])
    fetched(qkv2, qkv_weight, sems.at[0])
    fetched(out2, out_weight, sems.at[1])
    attention_body(
        section_out.astype(F32), gain, qkv_weight[...], out_weight[...], bias[1], results
    )


def route_kernel(section, core, values, a, b, c, d, own, other, router, router2, ids, ids2, *refs):
    if section == 1:
        cotangent, hidden_out, low_out, meta_out, sent = refs
    else:
        hidden_out, low_out, meta_out, sent = refs
    me = core[0]
    flag = (me == section).astype(jnp.int32)
    inputs = values[me] if section == 0 else values[...]
    hidden = inputs.astype(F32) + total((a, b, c, d))
    hidden_out[...] = hidden
    gain = chosen(flag, own[...], other[...])
    moe_low = (hidden * norm(hidden) * gain).astype(BF16)
    low_out[...] = moe_low
    weight = chosen(flag, router[...].astype(F32), router2[...].astype(F32)).astype(BF16)
    logits = dot_nt(moe_low, weight)
    routes = chosen(flag, ids[me], ids2[...]).astype(F32)
    columns = [column(routes[k : k + 1]) for k in range(2)]
    lanes = iota((SEQ, EXPERTS), 1).astype(F32)
    hot = [value[:, :EXPERTS] == lanes for value in columns]
    picked = [jnp.sum(jnp.where(h, logits, 0.0), axis=1, keepdims=True) for h in hot]
    top = jnp.maximum(picked[0], picked[1])
    exps = [jnp.exp(value - top) for value in picked]
    gates = [value / (exps[0] + exps[1]) for value in exps]
    per_row = (hot[0].astype(F32) + hot[1].astype(F32)).astype(BF16)
    earlier = (iota((SEQ, SEQ), 0) > iota((SEQ, SEQ), 1)).astype(BF16)
    before = dot(earlier, per_row)
    targets = []
    for k in range(2):
        slot = jnp.sum(jnp.where(hot[k], before, 0.0), axis=1, keepdims=True)
        expert = columns[k][:, :1]
        half = jnp.floor(expert * 0.5)
        chunk = (expert - 2.0 * half) * OWNERS + half
        targets.append(
            jnp.where(slot < 7.5, chunk * 8 + slot, MAIN + (slot - 8) * EXPERTS + chunk)
        )
    meta = jnp.concatenate(gates + targets + [value[:, :1] for value in columns], axis=1)
    meta_out[:, :6] = meta
    places = [slot_hot(target) for target in targets]
    either = (places[0] | places[1]).astype(BF16)
    sent[:, :WIDE] = pack(dot_tn(either, moe_low).astype(BF16))
    if section == 1:
        scaled = [
            jnp.where(place, gate, 0.0) for place, gate in zip(places, gates)
        ]
        sent[:, WIDE:] = pack(sent_grads(either, scaled, cotangent[me]))


def sent_grads(either, scaled, upstream):
    rows = dot_tn(either, upstream)
    ones = jnp.ones((SEQ, 128), BF16)
    gates = scaled[0] + scaled[1]
    high = gates.astype(BF16)
    rest = (gates - high.astype(F32)).astype(BF16)
    factor = (dot_tn(high, ones) + dot_tn(rest, ones))[:, :1]
    return (rows * factor).astype(BF16)


def expert_weights(flag, core, own_in, other_in, own_out, other_out, weight_in, weight_out, sems):
    fetch(flag, own_in.at[core], other_in.at[core], weight_in, sems.at[0])
    fetch(flag, own_out.at[core], other_out.at[core], weight_out, sems.at[1])


EXPERT_SCRATCH = (
    pltpu.VMEM((D, D), BF16),
    pltpu.VMEM((D, D), BF16),
    pltpu.SemaphoreType.DMA((2,)),
)


def expert_forward_kernel(
    core, block, own_in, other_in, own_out, other_out, sent, rows_out, pre_out, *scratch
):
    weight_in, weight_out, sems = scratch
    flag = (core[0] == 0).astype(jnp.int32)
    expert_weights(flag, core[0], own_in, other_in, own_out, other_out, *scratch)
    rows = unpack(block[...])
    rows_out[...] = rows
    fetched(other_in.at[0], weight_in, sems.at[0])
    pre_act = dot(rows, weight_in[...])
    pre_out[...] = pre_act
    _, tanh = gelu_parts(pre_act)
    act_low = (0.5 * pre_act * (1.0 + tanh)).astype(BF16)
    fetched(other_out.at[0], weight_out, sems.at[1])
    pack_parts(dot(act_low, weight_out[...]).astype(BF16), sent, 0)


def expert_back(grads, pre_act, weight_in, weight_out, act_out, grad_pre_out):
    square, tanh = gelu_parts(pre_act)
    act_low = (0.5 * pre_act * (1.0 + tanh)).astype(BF16)
    act_out[...] = act_low
    grad_act = dot_nt(grads, weight_out)
    slope = 0.5 * (1.0 + tanh) + 0.5 * pre_act * (1.0 - tanh * tanh) * GELU_C * (
        1.0 + 3.0 * GELU_A * square
    )
    grad_pre = (grad_act * slope).astype(BF16)
    grad_pre_out[...] = grad_pre
    return act_low, dot_nt(grad_pre, weight_in).astype(BF16)


def expert_both_kernel(
    core, block, own_in, other_in, own_out, other_out, sent, rows_out, grads_out, act_out, pre_out,
    *scratch
):
    weight_in, weight_out, sems = scratch
    flag = (core[0] == 1).astype(jnp.int32)
    expert_weights(flag, core[0], own_in, other_in, own_out, other_out, *scratch)
    rows = unpack(block[:, :WIDE])
    rows_out[...] = rows
    grads = unpack(block[:, WIDE:])
    grads_out[...] = grads
    fetched(other_in.at[0], weight_in, sems.at[0])
    pre_act = dot(rows, weight_in[...])
    fetched(other_out.at[0], weight_out, sems.at[1])
    act_low, grad_rows = expert_back(
        grads, pre_act, weight_in[...], weight_out[...], act_out, pre_out
    )
    pack_parts(grad_rows, sent, 256)
    pack_parts(dot(act_low, weight_out[...]).astype(BF16), sent, 0)


def expert_back_kernel(
    core, block, pre_act, own_in, other_in, own_out, other_out, sent, grads_out, act_out, pre_out,
    *scratch
):
    weight_in, weight_out, sems = scratch
    flag = (core[0] == 0).astype(jnp.int32)
    expert_weights(flag, core[0], own_in, other_in, own_out, other_out, *scratch)
    grads = unpack(block[...])
    grads_out[...] = grads
    fetched(other_out.at[0], weight_out, sems.at[1])
    fetched(other_in.at[0], weight_in, sems.at[0])
    _, grad_rows = expert_back(
        grads, pre_act[...], weight_in[...], weight_out[...], act_out, pre_out
    )
    pack_parts(grad_rows, sent, 0)


def expert_grads_kernel(rows, grads, act_low, grad_pre, out):
    out[0] = dot_tn(rows[...], grad_pre[...])
    out[1] = dot_tn(act_low[...], grads[...])


def combine_kernel(core, meta, block, hidden, rows_out, folded):
    rows = unpack_part(block, 0)
    rows_out[...] = rows
    value = own_part(core[1], hidden[...])
    for k in range(2):
        place = slot_hot(meta[:, 2 + k : 3 + k]).astype(BF16)
        value = value + meta[:, k : k + 1] * dot(place, rows)
    folded[...] = fold(value).astype(BF16)


def moe_back_body(meta, out_rows, grad_rows, upstream, sent, value):
    grad = jnp.zeros((SEQ, PART), F32)
    lanes = iota((SEQ, 128), 1)
    tail = jnp.zeros((SEQ, 128), F32)
    for k in range(2):
        place = slot_hot(meta[:, 2 + k : 3 + k]).astype(BF16)
        grad = grad + dot(place, grad_rows)
        picked = dot(place, out_rows)
        if value is not None:
            value = value + meta[:, k : k + 1] * picked
        inner = jnp.sum(picked * upstream, axis=1, keepdims=True)
        tail = jnp.where(lanes == k, inner, tail)
    sent[:LINES] = fold(grad).astype(BF16)
    sent[LINES:] = jnp.transpose(tail)[:16].astype(BF16)
    return value


def second_back_kernel(core, meta, block, cotangent, hidden, sent, folded):
    out_rows = unpack_part(block, 0)
    grad_rows = unpack_part(block, 256)
    upstream = own_part(core[1], cotangent[core[0]].astype(F32))
    value = own_part(core[1], hidden[...])
    folded[...] = fold(moe_back_body(meta, out_rows, grad_rows, upstream, sent, value)).astype(BF16)


def first_back_kernel(core, meta, out_rows, block, upstream, sent):
    part = own_part(core[1], upstream[...].astype(F32))
    moe_back_body(meta, out_rows[...], unpack_part(block, 0), part, sent, None)


def shared_body(
    buckets, scores, inputs, gain, grad_qkv, attended, grad_low, moe_low, grad_logits, moe_gain, rel,
    shared,
):
    bucket = buckets[...]
    rel[...] = jnp.zeros_like(rel)
    for b in range(BUCKETS):
        hot = bucket == b
        for head in range(HEADS):
            at = head * BUCKETS + b
            rel[at : at + 1] = jnp.sum(jnp.where(hot, scores[head], 0.0), axis=0, keepdims=True)
    table = jnp.sum(jnp.transpose(rel[...]), axis=0, keepdims=True)
    normed = (inputs * norm(inputs) * gain).astype(BF16)
    shared[:QKV, :D] = dot_tn(grad_qkv, normed).astype(BF16)
    shared[QKV:, :D] = dot_tn(attended, grad_low).astype(BF16)
    line = iota((128, D), 0)
    wide = jnp.concatenate([table, jnp.zeros((1, D - 128), F32)], axis=1)
    rows = jnp.where(line == EXPERTS + 1, moe_gain, 0.0)
    rows = jnp.where(line == EXPERTS + 2, wide, rows)
    shared[:, D:] = (dot_tn(moe_low, grad_logits) + jnp.transpose(rows)).astype(BF16)


def shared_kernel(
    core, buckets, values, own, other, attended, moe_low, grad_hidden, scores, grad_qkv, logits,
    moe_gain, shared, rel,
):
    gain = chosen((core[0] == 1).astype(jnp.int32), own[...], other[...])
    shared_body(
        buckets, [scores[head].astype(F32) for head in range(HEADS)], values[...].astype(F32), gain,
        grad_qkv[...], attended[...], grad_hidden[...].astype(BF16), moe_low[...], logits[...],
        moe_gain[0:1], rel, shared,
    )


def attention_back_kernel(
    section, core, a, b, c, d, meta, hidden, upstream, own, other, router, router2, projected, probs,
    qkv, qkv2, out, out2, *refs,
):
    if section == 0:
        (moe_low, own_attn, other_attn, buckets, values, attended, shared1) = refs[:7]
        (sent, grad_hidden_out, mine, theirs, qkv_weight, out_weight, sems, rel, shared) = refs[7:]
    else:
        (sent, grad_hidden_out, scores_out, qkv_out, logits_out, gain_out) = refs[:6]
        (qkv_weight, out_weight, sems) = refs[6:]
    me = core[0]
    flag = (me == section).astype(jnp.int32)
    fetch(flag, qkv, qkv2, qkv_weight, sems.at[0])
    fetch(flag, out, out2, out_weight, sems.at[1])
    grad_moe = gathered(core[1], (a, b, c, d))
    tails = total((a.at[pl.ds(LINES, 16)], b.at[pl.ds(LINES, 16)], c.at[pl.ds(LINES, 16)], d.at[pl.ds(LINES, 16)]))
    tails = jnp.transpose(jnp.concatenate([tails, jnp.zeros((112, 128), F32)], axis=0))
    gain = chosen(flag, own[...], other[...])
    weight = chosen(flag, router[...].astype(F32), router2[...].astype(F32)).astype(BF16)
    gates = [meta[:, k : k + 1] for k in range(2)]
    grad_gates = [tails[:, k : k + 1] for k in range(2)]
    mean = gates[0] * grad_gates[0] + gates[1] * grad_gates[1]
    lanes = iota((SEQ, 128), 1).astype(F32)
    grad_logits = jnp.zeros((SEQ, 128), F32)
    for k in range(2):
        grad = gates[k] * (grad_gates[k] - mean)
        grad_logits = jnp.where(meta[:, 4 + k : 5 + k] == lanes, grad, grad_logits)
    grad_logits = grad_logits.astype(BF16)
    grad_moe = grad_moe + dot(grad_logits[:, :EXPERTS], weight)
    state = hidden[...]
    inverse = norm(state)
    grad_moe_gain = jnp.sum(grad_moe * state * inverse, axis=0, keepdims=True)
    before = upstream[me] if section == 1 else upstream[...]
    grad_hidden = before.astype(F32) + norm_back(state, inverse, gain, grad_moe)
    grad_hidden_out[...] = grad_hidden
    grad_low = grad_hidden.astype(BF16)
    fetched(out2, out_weight, sems.at[1])
    grad_heads = dot_nt(grad_low, out_weight[...]).astype(BF16)
    grads = []
    score_grads = []
    for head in range(HEADS):
        at = head * 3 * HEAD_DIM
        query = projected[:, at : at + HEAD_DIM]
        key = projected[:, at + HEAD_DIM : at + 2 * HEAD_DIM]
        value = projected[:, at + 2 * HEAD_DIM : at + 3 * HEAD_DIM]
        grad_head = grad_heads[:, head * HEAD_DIM : (head + 1) * HEAD_DIM]
        prob = probs[head]
        grad_probs = dot_nt(grad_head, value)
        grad_value = dot_tn(prob.astype(BF16), grad_head)
        inner = jnp.sum(prob * grad_probs, axis=-1, keepdims=True)
        grad_scores = (prob * (grad_probs - inner)).astype(BF16)
        score_grads.append(grad_scores.astype(F32))
        grads.append(SCALE * dot(grad_scores, key))
        grads.append(SCALE * dot_tn(grad_scores, query))
        grads.append(grad_value)
    grad_qkv = jnp.concatenate(grads, axis=1).astype(BF16)
    fetched(qkv2, qkv_weight, sems.at[0])
    sent[...] = dot(grad_qkv, qkv_weight[...]).astype(BF16)
    if section == 1:
        for head in range(HEADS):
            scores_out[head] = score_grads[head].astype(BF16)
        qkv_out[...] = grad_qkv
        logits_out[...] = grad_logits
        gain_out[...] = jnp.broadcast_to(grad_moe_gain, (8, D))
    else:
        attn_gain = chosen(flag, own_attn[...], other_attn[...])
        shared_body(
            buckets, score_grads, values[me].astype(F32), attn_gain, grad_qkv, attended[...],
            grad_low, moe_low[...], grad_logits, grad_moe_gain, rel, shared,
        )
    if section == 0:

        @pl.when(me == 0)
        def _():
            mine[...] = shared[...]
            theirs[...] = shared1[...]

        @pl.when(me == 1)
        def _():
            mine[...] = shared1[...]
            theirs[...] = shared[...]


def input_back_kernel(section, core, a, b, c, d, values, grad_hidden, own, other, *refs):
    if section == 1:
        meta, grad_out, low_out, sent = refs
    else:
        second, mine, theirs, grad_out = refs
    me = core[0]
    flag = (me == section).astype(jnp.int32)
    grad_normed = total((a, b, c, d))
    inputs = (values[me] if section == 0 else values[...]).astype(F32)
    inverse = norm(inputs)
    gain = chosen(flag, own[...], other[...])
    grad_inputs = grad_hidden[...] + norm_back(inputs, inverse, gain, grad_normed)
    grad_out[:SEQ] = grad_inputs
    if section == 1:
        upstream = grad_inputs.astype(BF16)
        low_out[...] = upstream
        places = [slot_hot(meta[:, 2 + k : 3 + k]) for k in range(2)]
        either = (places[0] | places[1]).astype(BF16)
        scaled = [jnp.where(places[k], meta[:, k : k + 1], 0.0) for k in range(2)]
        sent[...] = pack(sent_grads(either, scaled, upstream))
    grad_gain = jnp.sum(grad_normed * inputs * inverse, axis=0, keepdims=True)
    grad_out[SEQ:] = jnp.broadcast_to(grad_gain, (8, D))
    if section == 0:

        @pl.when(me == 0)
        def _():
            mine[...] = grad_out[...]
            theirs[...] = second[...]

        @pl.when(me == 1)
        def _():
            mine[...] = second[...]
            theirs[...] = grad_out[...]


def output_kernel(core, first, a, b, c, d, mine, theirs):
    second = gathered(core[1], (a, b, c, d)).astype(BF16)

    @pl.when(core[0] == 0)
    def _():
        mine[...] = first[...]
        theirs[...] = second

    @pl.when(core[0] == 1)
    def _():
        mine[...] = second
        theirs[...] = first[...]


def pair_kernel(mine, got, out):
    out[...] = (mine[...].astype(F32) + got[...].astype(F32)).astype(BF16)


CHUNK = D // OWNERS
SPARE = 64


def reduce_kernel(blocks, mine, got, out):
    value = blocks[0].astype(F32)
    for at in range(1, OWNERS):
        value = value + blocks[at].astype(F32)
    gain = mine[SEQ : SEQ + 1] + got[SEQ : SEQ + 1]
    columns = jnp.transpose(jnp.broadcast_to(gain, (128, D)))
    lanes = iota((CHUNK, 128), 1)
    side = value[:, D:]
    for at in range(OWNERS):
        side = jnp.where(lanes == SPARE + at, columns[at * CHUNK : (at + 1) * CHUNK], side)
    main_low, side_low = value[:, :D].astype(BF16), side.astype(BF16)
    for at in range(OWNERS):
        out[at, :, :D] = main_low
        out[at, :, D:] = side_low


def final_kernel(blocks, qkv, attn_out, router, gain_attn, gain_moe, table):
    sides = []
    gains = jnp.zeros((CHUNK, 128), F32)
    for at in range(OWNERS):
        main = blocks[at, :, :D].astype(F32)
        rows = slice(at * CHUNK, (at + 1) * CHUNK)
        if (at + 1) * CHUNK <= QKV:
            qkv[rows] = main
        else:
            attn_out[at * CHUNK - QKV : (at + 1) * CHUNK - QKV] = main
        side = blocks[at, :, D:].astype(F32)
        sides.append(side)
        gains = gains + side
    rows = jnp.transpose(jnp.concatenate(sides, axis=0))
    router[...] = rows[:EXPERTS]
    gain_moe[...] = rows[EXPERTS + 1 : EXPERTS + 2]
    line = rows[EXPERTS + 2 : EXPERTS + 3]
    for head in range(HEADS):
        table[head] = line[:, head * BUCKETS : (head + 1) * BUCKETS]
    padded = jnp.concatenate([gains, jnp.zeros((128 - CHUNK, 128), F32)], axis=0)
    spare = jnp.transpose(padded)
    pieces = [spare[SPARE + at : SPARE + at + 1, :CHUNK] for at in range(OWNERS)]
    gain_attn[...] = jnp.concatenate(pieces, axis=1)


def place_copies(core, outs, spaces, sems_in, sems_out, sources_of):
    def move(me):
        reads, writes = [], []
        for at, pair in enumerate(sources_of(me)):
            for half, source in enumerate(pair):
                room, sem = spaces[at].at[half], 2 * at + half
                reads.append(pltpu.make_async_copy(source, room, sems_in.at[sem]))
                writes.append(pltpu.make_async_copy(room, outs[at].at[half], sems_out.at[sem]))
        for copy in reads:
            copy.start()
        for read, write in zip(reads, writes):
            read.wait()
            write.start()
        for copy in writes:
            copy.wait()

    for me in range(2):

        @pl.when(core[0] == me)
        def _(me=me):
            move(me)


def place_expert_kernel(core, own0, got0, own1, got1, grad_in, grad_out, *refs):
    def sources_of(me):
        pair = (own0, got0) if me == 0 else (got1, own1)
        return [[ref.at[at] for ref in pair] for at in range(2)]

    place_copies(core, (grad_in, grad_out), refs[:2], *refs[2:], sources_of)


def place_kernel(core, act, act_got, grad, grad_got, activations, input_grad, *refs):
    rows = pl.ds(0, SEQ)

    def sources_of(me):
        pairs = [(act, act_got), (grad.at[rows], grad_got.at[rows])]
        return [pair if me == 0 else pair[::-1] for pair in pairs]

    place_copies(core, (activations, input_grad), refs[:2], *refs[2:], sources_of)


def permuted(value, axis, pairs):
    return lax.ppermute(value, axis, pairs)


def swap(value):
    return permuted(value, "pipe", [(0, 1), (1, 0)])


def down(value):
    return permuted(value, "pipe", [(1, 0)])


def up(value):
    return permuted(value, "pipe", [(0, 1)])


def spread(value):
    count = lax.axis_size("tensor")
    return [value] + [
        permuted(value, "tensor", [(i, (i + by) % count) for i in range(count)])
        for by in range(1, count)
    ]


def after(value, *others):
    return lax.optimization_barrier((value, *others))[0]


def exchange(block):
    moved = lax.all_to_all(
        block.reshape(EXPERTS, 8, block.shape[1]),
        ("pipe", "expert"),
        split_axis=0,
        concat_axis=0,
        tiled=True,
    )
    return moved.reshape(block.shape)


def collect(block):
    moved = lax.all_to_all(
        block.reshape(EXPERTS * GROUP, 8, block.shape[3]),
        ("pipe", "expert", "tensor"),
        split_axis=0,
        concat_axis=0,
        tiled=True,
    )
    return moved.reshape(block.shape)


def shards(
    tokens,
    cotangent,
    routes,
    buckets,
    gain_attn,
    w_qkv,
    w_attn_out,
    rel_table,
    gain_moe,
    w_router,
    w_expert_in,
    w_expert_out,
):
    index = lax.axis_index("pipe")
    core = jnp.stack([index, lax.axis_index("tensor")]).astype(jnp.int32)
    qkv = w_qkv[0].T
    attn_out = w_attn_out[0]
    router = w_router[0].T
    ids = jnp.transpose(routes[0], (0, 2, 1))
    qkv2 = swap(qkv)
    attn_out2 = swap(attn_out)
    tables = (rel_table[0], swap(rel_table[0]))
    attn_gains = (gain_attn, swap(gain_attn))
    moe_gains = (gain_moe, swap(gain_moe))
    router2 = swap(router)
    ids2 = swap(lax.dynamic_index_in_dim(ids, 1 - index, 0, keepdims=False))

    attn_args = (qkv, qkv2, attn_out, attn_out2)

    (bias,) = kernel_call(
        bias_kernel,
        "bias",
        (core, buckets, *tables),
        (SMEM, VMEM, VMEM, VMEM),
        (shape(2, HEADS, SEQ, SEQ),),
    )
    partial0, projected0, probs0, attended0 = kernel_call(
        first_attention_kernel,
        "first_attention",
        (core, tokens, *attn_gains, bias, *attn_args),
        (SMEM, VMEM, VMEM, VMEM, VMEM, ANY, ANY, ANY, ANY),
        ATTENTION_OUT,
        ATTENTION_SCRATCH,
    )
    parts = spread(partial0)
    expert_specs = (ANY, ANY, ANY, ANY)
    route_args = (*moe_gains, router, router2, ids, ids2)

    def route(section, values, parts, more, wide):
        return kernel_call(
            lambda *refs: route_kernel(section, *refs),
            "route",
            (core, values, *parts, *route_args, *more),
            (SMEM,) + (VMEM,) * (11 + len(more)),
            (shape(SEQ, D), low(SEQ, D), shape(SEQ, 128), low(MAIN, wide)),
        )

    hidden0, moe_low0, meta0, sent = route(0, tokens, parts, (), WIDE)
    weights = lax.optimization_barrier((w_expert_in[0], w_expert_out[0], sent))[:2]
    expert_args = (w_expert_in[0], swap(weights[0]), w_expert_out[0], swap(weights[1]))
    block = exchange(sent)
    sent, rows0, pre0 = kernel_call(
        expert_forward_kernel,
        "expert_forward",
        (core, block, *expert_args),
        (SMEM, VMEM, *expert_specs),
        (low(EXPERTS, GROUP, 8, 256), low(ROWS, D), shape(ROWS, D)),
        EXPERT_SCRATCH,
    )
    block = collect(sent)
    out_rows0, part0 = kernel_call(
        combine_kernel,
        "combine",
        (core, meta0, block, hidden0),
        (SMEM, VMEM, VMEM, VMEM),
        (low(ROWS, PART), low(LINES, 128)),
    )

    act0, partial1, projected1, probs1, attended1 = kernel_call(
        second_attention_kernel,
        "second_attention",
        (core, *spread(part0), *attn_gains, bias, *attn_args),
        (SMEM,) + (VMEM,) * 7 + (ANY,) * 4,
        (low(SEQ, D), *ATTENTION_OUT),
        ATTENTION_SCRATCH,
    )
    hidden1, moe_low1, meta1, sent = route(1, act0, spread(partial1), (cotangent,), 2 * WIDE)
    block = exchange(sent)
    sent, rows1, grads1, act_low1, grad_pre1 = kernel_call(
        expert_both_kernel,
        "expert_both",
        (core, block, *expert_args),
        (SMEM, VMEM, *expert_specs),
        (low(EXPERTS, GROUP, 8, 512), low(ROWS, D), low(ROWS, D), low(ROWS, D), low(ROWS, D)),
        EXPERT_SCRATCH,
        vmem=16,
    )
    block = collect(sent)

    sent, part1 = kernel_call(
        second_back_kernel,
        "second_back",
        (core, meta1, block, cotangent, hidden1),
        (SMEM, VMEM, VMEM, VMEM, VMEM),
        (low(LINES + 16, 128), low(LINES, 128)),
    )

    def expert_grads(*args):
        return kernel_call(
            expert_grads_kernel, "expert_grads", args, (VMEM,) * 4, (shape(2, D, D),)
        )[0]

    def attention_back(section, parts, meta, hidden, upstream, saved, more, outputs, scratch):
        return kernel_call(
            lambda *refs: attention_back_kernel(section, *refs),
            "attention_back",
            (core, *parts, meta, hidden, upstream, *moe_gains, router, router2, *saved, *attn_args)
            + more,
            (SMEM,) + (VMEM,) * 13 + (ANY,) * 4 + (VMEM,) * len(more),
            (low(SEQ, D), shape(SEQ, D), *outputs),
            ATTENTION_SCRATCH + scratch,
        )

    partial, grad_hidden1, *grads = attention_back(
        1, spread(sent), meta1, hidden1, cotangent, (projected1, probs1), (),
        (low(HEADS, SEQ, SEQ), low(SEQ, QKV), low(SEQ, 128), shape(8, D)), (),
    )
    parts = spread(partial)
    (shared1,) = kernel_call(
        shared_kernel,
        "shared",
        (core, buckets, act0, *attn_gains, attended1, moe_low1, after(grad_hidden1, parts[3]), *grads),
        (SMEM,) + (VMEM,) * 11,
        (low(D, D + 128),),
        (pltpu.VMEM((128, 128), F32),),
    )
    expert_grad1 = expert_grads(after(rows1, parts[3]), grads1, act_low1, grad_pre1)
    parts[1] = after(parts[1], shared1, expert_grad1)
    grad_inputs1, upstream, sent = kernel_call(
        lambda *refs: input_back_kernel(1, *refs),
        "input_back",
        (core, *parts, act0, grad_hidden1, *attn_gains, meta0),
        (SMEM,) + (VMEM,) * 9,
        (shape(SEQ + 8, D), low(SEQ, D), low(MAIN, WIDE)),
    )

    expert_grad1 = after(expert_grad1, sent)
    expert_grad1b = up(expert_grad1)
    block = after(exchange(sent), expert_grad1b)
    sent, grads0, act_low0, grad_pre0 = kernel_call(
        expert_back_kernel,
        "expert_back",
        (core, block, pre0, *expert_args),
        (SMEM, VMEM, VMEM, *expert_specs),
        (low(EXPERTS, GROUP, 8, 256), low(ROWS, D), low(ROWS, D), low(ROWS, D)),
        EXPERT_SCRATCH,
    )
    block = collect(sent)
    (sent,) = kernel_call(
        first_back_kernel,
        "first_back",
        (core, meta0, out_rows0, block, upstream),
        (SMEM,) + (VMEM,) * 4,
        (low(LINES + 16, 128),),
    )
    parts = spread(sent)
    expert_grad0 = expert_grads(after(rows0, sent), grads0, act_low0, grad_pre0)
    parts[3] = after(parts[3], expert_grad0)
    partial, grad_hidden0, mine, theirs = attention_back(
        0, parts, meta0, hidden0, upstream, (projected0, probs0),
        (moe_low0, *attn_gains, buckets, tokens, attended0, shared1),
        (low(D, D + 128), low(D, D + 128)),
        (pltpu.VMEM((128, 128), F32), pltpu.VMEM((D, D + 128), BF16)),
    )
    got = swap(theirs)
    parts = spread(partial)
    expert_grad0 = after(expert_grad0, got)
    expert_grad0b = down(expert_grad0)

    (pair,) = kernel_call(
        pair_kernel, "pair", (mine, got), (VMEM, VMEM), (low(D, D + 128),)
    )
    blocks = pair.reshape(OWNERS, CHUNK, D + 128)
    blocks = lax.all_to_all(blocks, "expert", split_axis=0, concat_axis=0, tiled=True)
    act_parts = spread(after(part1, pair))
    grad_mine, grad_theirs = kernel_call(
        lambda *refs: input_back_kernel(0, *refs),
        "input_back",
        (core, *parts, tokens, grad_hidden0, *attn_gains, grad_inputs1),
        (SMEM,) + (VMEM,) * 9,
        (shape(SEQ + 8, D), shape(SEQ + 8, D)),
        (pltpu.VMEM((SEQ + 8, D), F32),),
    )
    grad_got = swap(grad_theirs)
    def place(body, sources, results):
        return kernel_call(
            body,
            "place",
            (core, *sources),
            (SMEM,) + (ANY,) * 4,
            results,
            tuple(pltpu.VMEM(result.shape, result.dtype) for result in results)
            + (pltpu.SemaphoreType.DMA((4,)), pltpu.SemaphoreType.DMA((4,))),
            (ANY, ANY),
        )

    grad_in, grad_out = place(
        place_expert_kernel,
        (expert_grad0, expert_grad0b, expert_grad1, expert_grad1b),
        (shape(2, D, D), shape(2, D, D)),
    )
    (blocks,) = kernel_call(
        reduce_kernel,
        "reduce",
        (after(blocks, grad_in, grad_out), grad_mine, grad_got),
        (VMEM,) * 3,
        (low(*blocks.shape),),
    )
    act_mine, act_theirs = kernel_call(
        output_kernel,
        "output",
        (core, act0, *act_parts),
        (SMEM,) + (VMEM,) * 5,
        (low(SEQ, D), low(SEQ, D)),
    )
    act_got = swap(act_theirs)
    blocks = lax.all_to_all(blocks, "expert", split_axis=0, concat_axis=0, tiled=True)
    activations, input_grad = place(
        place_kernel,
        (act_mine, act_got, grad_mine, grad_got),
        (low(2, SEQ, D), shape(2, SEQ, D)),
    )
    blocks = after(blocks, activations, input_grad)
    grad_qkv, grad_attn_out, grad_router, grad_gain, grad_moe_gain, grad_table = kernel_call(
        final_kernel,
        "final",
        (blocks,),
        (VMEM,),
        (shape(QKV, D), shape(HEAD_COLS, D), shape(EXPERTS, D), shape(1, D), shape(1, D))
        + (shape(HEADS, 1, BUCKETS),),
    )
    return (
        activations[None],
        input_grad[None],
        grad_gain,
        grad_qkv.T[None],
        grad_attn_out[None],
        jnp.transpose(grad_table, (1, 0, 2)),
        grad_moe_gain,
        grad_router.T[None],
        grad_in[None],
        grad_out[None],
    )


def solution(mesh):
    in_specs = (
        P(None, "expert", None),
        P(None, "expert", None),
        P("pipe", None, "expert", None),
        P(),
        P("pipe", None),
        P("pipe", None, "tensor"),
        P("pipe", "tensor", None),
        P("pipe", "tensor", None),
        P("pipe", None),
        P("pipe", None, None),
        P("pipe", "expert", None, "tensor"),
        P("pipe", "expert", "tensor", None),
    )
    out_specs = (
        P("pipe", None, "expert", None),
        P("pipe", None, "expert", None),
        P("pipe", None),
        P("pipe", None, "tensor"),
        P("pipe", "tensor", None),
        P("pipe", "tensor", None),
        P("pipe", None),
        P("pipe", None, None),
        P("pipe", "expert", None, "tensor"),
        P("pipe", "expert", "tensor", None),
    )
    return jax.shard_map(shards, mesh=mesh, in_specs=in_specs, out_specs=out_specs, check_vma=False)
```

```python
import jax
import jax.numpy as jnp
from jax import lax
from jax.experimental import pallas as pl
from jax.experimental.pallas import tpu as pltpu
from jax.sharding import PartitionSpec as P

EPSILON = 1e-06
F32 = jnp.float32
BF16 = jnp.bfloat16
SEQ = 128
D = 768
HEADS = 3
HEAD_DIM = 64
QKV = 3 * HEADS * HEAD_DIM
HEAD_COLS = HEADS * HEAD_DIM
EXPERTS = 32
OWNERS = 16
BUCKETS = 32
MAIN = 8 * EXPERTS
ROWS = 10 * EXPERTS
WIDE = D + 256
GROUP = 4
PART = D // GROUP
PIECE = 64
LINES = SEQ * PART // 128
SCALE = HEAD_DIM**-0.5
GELU_C = 0.7978845608028654
GELU_A = 0.044715
VMEM = pl.BlockSpec(memory_space=pltpu.VMEM)
SMEM = pl.BlockSpec(memory_space=pltpu.SMEM)
ANY = pl.BlockSpec(memory_space=pl.ANY)


def shape(*dims, dtype=F32):
    return jax.ShapeDtypeStruct(dims, dtype)


def low(*dims):
    return jax.ShapeDtypeStruct(dims, BF16)


def kernel_call(body, name, inputs, specs, outputs, scratch=(), out_specs=None, vmem=12):
    return pl.pallas_call(
        body,
        out_shape=tuple(outputs),
        in_specs=list(specs),
        out_specs=tuple(out_specs or [VMEM] * len(outputs)),
        scratch_shapes=list(scratch),
        compiler_params=pltpu.CompilerParams(vmem_limit_bytes=vmem * 2**20),
        cost_estimate=pl.CostEstimate(
            flops=1_600_000_000, bytes_accessed=8_000_000, transcendentals=0
        ),
        name=name,
    )(*inputs)


def dot(a, b):
    return jnp.dot(a, b, preferred_element_type=F32)


def dot_nt(a, b):
    return lax.dot_general(a, b, (((1,), (1,)), ((), ())), preferred_element_type=F32)


def dot_tn(a, b):
    return lax.dot_general(a, b, (((0,), (0,)), ((), ())), preferred_element_type=F32)


def iota(dims, axis):
    return lax.broadcasted_iota(jnp.int32, dims, axis)


def chosen(flag, own, other):
    return jnp.where(flag == 1, own, other)


def fetch(flag, own, other, target, semaphore):
    @pl.when(flag == 1)
    def _():
        pltpu.make_async_copy(own, target, semaphore).start()

    @pl.when(flag != 1)
    def _():
        pltpu.make_async_copy(other, target, semaphore).start()


def fetched(other, target, semaphore):
    pltpu.make_async_copy(other, target, semaphore).wait()


def norm(values):
    return lax.rsqrt(jnp.mean(values * values, axis=-1, keepdims=True) + EPSILON)


def norm_back(values, inverse, gain, upstream):
    weighted = upstream * gain
    inner = jnp.mean(weighted * values, axis=-1, keepdims=True)
    return inverse * weighted - values * (inverse * inverse * inverse) * inner


def total(refs):
    value = refs[0][...].astype(F32)
    for ref in refs[1:]:
        value = value + ref[...].astype(F32)
    return value


def gelu_parts(value):
    square = value * value
    tanh = jnp.tanh(GELU_C * value * (1.0 + GELU_A * square))
    return square, tanh


def pack(rows):
    spread = (iota((MAIN, EXPERTS), 0) // 8 == iota((MAIN, EXPERTS), 1)).astype(BF16)
    place = iota((MAIN, 128), 0) % 8
    parts = [rows[:MAIN]]
    for late in range(2):
        start = MAIN + late * EXPERTS
        copies = dot(spread, rows[start : start + EXPERTS])
        piece = jnp.zeros((MAIN, 128), F32)
        for r in range(D // 128):
            piece = jnp.where(place == r, copies[:, r * 128 : (r + 1) * 128], piece)
        parts.append(piece.astype(BF16))
    return jnp.concatenate(parts, axis=1)


def unpack(block):
    count = D // 128
    dims = (count * EXPERTS, MAIN)
    row = iota(dims, 0)
    gather = (iota(dims, 1) == (row % EXPERTS) * 8 + row // EXPERTS).astype(BF16)
    pieces = dot(gather, block[:, D:]).astype(BF16)
    parts = [block[:, :D]]
    for late in range(2):
        columns = slice(late * 128, (late + 1) * 128)
        blocks = [pieces[r * EXPERTS : (r + 1) * EXPERTS, columns] for r in range(count)]
        parts.append(jnp.concatenate(blocks, axis=1))
    return jnp.concatenate(parts, axis=0)


def part_of(value, part):
    last = GROUP * 128 + part * PIECE
    return value[:, part * 128 : (part + 1) * 128], value[:, last : last + PIECE]


def pack_parts(rows, out, start):
    spread = (iota((MAIN, EXPERTS), 0) // 8 == iota((MAIN, EXPERTS), 1)).astype(BF16)
    place = iota((MAIN, PIECE), 0) % 8
    copies = []
    for late in range(2):
        first = MAIN + late * EXPERTS
        copies.append(dot(spread, rows[first : first + EXPERTS]))
    for part in range(GROUP):
        piece = jnp.zeros((MAIN, PIECE), F32)
        for late in range(2):
            block, last = part_of(copies[late], part)
            piece = jnp.where(place == 3 * late, block[:, :PIECE], piece)
            piece = jnp.where(place == 3 * late + 1, block[:, PIECE:], piece)
            piece = jnp.where(place == 3 * late + 2, last, piece)
        block = jnp.concatenate([*part_of(rows[:MAIN], part), piece.astype(BF16)], axis=1)
        out[:, part, :, start : start + 256] = block.reshape(EXPERTS, 8, 256)


def unpack_part(block, start):
    value = block[:, 0, :, start : start + 256].astype(F32)
    for sender in range(1, GROUP):
        value = value + block[:, sender, :, start : start + 256].astype(F32)
    value = value.reshape(MAIN, 256).astype(BF16)
    dims = (6 * EXPERTS, MAIN)
    row = iota(dims, 0)
    gather = (iota(dims, 1) == (row % EXPERTS) * 8 + row // EXPERTS).astype(BF16)
    pieces = dot(gather, value[:, PART:]).astype(BF16)
    parts = [value[:, :PART]]
    for late in range(2):
        blocks = [pieces[r * EXPERTS : (r + 1) * EXPERTS] for r in range(3 * late, 3 * late + 3)]
        parts.append(jnp.concatenate(blocks, axis=1))
    return jnp.concatenate(parts, axis=0)


def own_part(index, value):
    block, last = part_of(value, 0)
    for part in range(1, GROUP):
        other_block, other_last = part_of(value, part)
        block = jnp.where(index == part, other_block, block)
        last = jnp.where(index == part, other_last, last)
    return jnp.concatenate([block, last], axis=1)


def fold(part):
    tail = jnp.concatenate([part[: SEQ // 2, 128:], part[SEQ // 2 :, 128:]], axis=1)
    return jnp.concatenate([part[:, :128], tail], axis=0)


def gathered(index, refs):
    parts = [ref[:LINES].astype(F32) for ref in refs]
    blocks, lasts = [], []
    for at in range(GROUP):
        value = parts[0]
        for by in range(1, GROUP):
            value = jnp.where((index + GROUP - by) % GROUP == at, parts[by], value)
        tail = value[SEQ:]
        blocks.append(value[:SEQ])
        lasts.append(jnp.concatenate([tail[:, :PIECE], tail[:, PIECE:]], axis=0))
    return jnp.concatenate(blocks + lasts, axis=1)


def column(row):
    return jnp.transpose(jnp.broadcast_to(row, (SEQ, 128)))


def slot_hot(target):
    return target == iota((SEQ, ROWS), 1).astype(F32)


def bias_kernel(core, buckets, own, other, out):
    bucket = buckets[...]
    causal = iota((SEQ, SEQ), 0) >= iota((SEQ, SEQ), 1)
    hot = [bucket == b for b in range(BUCKETS)]
    for section in range(2):
        flag = (core[0] == section).astype(jnp.int32)
        table = chosen(flag, own[...].astype(F32), other[...].astype(F32))
        for head in range(HEADS):
            value = jnp.zeros((SEQ, SEQ), F32)
            for b in range(BUCKETS):
                value = jnp.where(hot[b], table[head : head + 1, b : b + 1], value)
            out[section, head] = jnp.where(causal, value, -1e30)


def attention_body(values, gain, qkv_weight, out_weight, bias, refs):
    partial_out, projected_out, probs_out, attended_out = refs
    normed = (values * norm(values) * gain).astype(BF16)
    projected = dot_nt(normed, qkv_weight).astype(BF16)
    projected_out[...] = projected
    heads = []
    for head in range(HEADS):
        at = head * 3 * HEAD_DIM
        query = projected[:, at : at + HEAD_DIM]
        key = projected[:, at + HEAD_DIM : at + 2 * HEAD_DIM]
        value = projected[:, at + 2 * HEAD_DIM : at + 3 * HEAD_DIM]
        scores = dot_nt(query, key) * SCALE + bias[head]
        exps = jnp.exp(scores - jnp.max(scores, axis=-1, keepdims=True))
        probs = exps / jnp.sum(exps, axis=-1, keepdims=True)
        probs_out[head] = probs
        heads.append(dot(probs.astype(BF16), value))
    attended = jnp.concatenate(heads, axis=1).astype(BF16)
    attended_out[...] = attended
    partial_out[...] = dot(attended, out_weight).astype(BF16)


ATTENTION_OUT = (
    low(SEQ, D),
    low(SEQ, QKV),
    shape(HEADS, SEQ, SEQ),
    low(SEQ, HEAD_COLS),
)
ATTENTION_SCRATCH = (
    pltpu.VMEM((QKV, D), BF16),
    pltpu.VMEM((HEAD_COLS, D), BF16),
    pltpu.SemaphoreType.DMA((2,)),
)


def first_attention_kernel(core, tokens, own, other, bias, qkv, qkv2, out, out2, *refs):
    *results, qkv_weight, out_weight, sems = refs
    flag = (core[0] == 0).astype(jnp.int32)
    fetch(flag, qkv, qkv2, qkv_weight, sems.at[0])
    fetch(flag, out, out2, out_weight, sems.at[1])
    values = tokens[core[0]].astype(F32)
    gain = chosen(flag, own[...], other[...])
    fetched(qkv2, qkv_weight, sems.at[0])
    fetched(out2, out_weight, sems.at[1])
    attention_body(values, gain, qkv_weight[...], out_weight[...], bias[0], results)


def second_attention_kernel(
    core, a, b, c, d, own, other, bias, qkv, qkv2, out, out2, act, *refs
):
    *results, qkv_weight, out_weight, sems = refs
    flag = (core[0] == 1).astype(jnp.int32)
    fetch(flag, qkv, qkv2, qkv_weight, sems.at[0])
    fetch(flag, out, out2, out_weight, sems.at[1])
    section_out = gathered(core[1], (a, b, c, d)).astype(BF16)
    act[...] = section_out
    gain = chosen(flag, own[...], other[...])
    fetched(qkv2, qkv_weight, sems.at[0])
    fetched(out2, out_weight, sems.at[1])
    attention_body(
        section_out.astype(F32), gain, qkv_weight[...], out_weight[...], bias[1], results
    )


def route_kernel(section, core, values, a, b, c, d, own, other, router, router2, ids, ids2, *refs):
    if section == 1:
        cotangent, hidden_out, low_out, meta_out, sent = refs
    else:
        hidden_out, low_out, meta_out, sent = refs
    me = core[0]
    flag = (me == section).astype(jnp.int32)
    inputs = values[me] if section == 0 else values[...]
    hidden = inputs.astype(F32) + total((a, b, c, d))
    hidden_out[...] = hidden
    gain = chosen(flag, own[...], other[...])
    moe_low = (hidden * norm(hidden) * gain).astype(BF16)
    low_out[...] = moe_low
    weight = chosen(flag, router[...].astype(F32), router2[...].astype(F32)).astype(BF16)
    logits = dot_nt(moe_low, weight)
    routes = chosen(flag, ids[me], ids2[...]).astype(F32)
    columns = [column(routes[k : k + 1]) for k in range(2)]
    lanes = iota((SEQ, EXPERTS), 1).astype(F32)
    hot = [value[:, :EXPERTS] == lanes for value in columns]
    picked = [jnp.sum(jnp.where(h, logits, 0.0), axis=1, keepdims=True) for h in hot]
    top = jnp.maximum(picked[0], picked[1])
    exps = [jnp.exp(value - top) for value in picked]
    gates = [value / (exps[0] + exps[1]) for value in exps]
    per_row = (hot[0].astype(F32) + hot[1].astype(F32)).astype(BF16)
    earlier = (iota((SEQ, SEQ), 0) > iota((SEQ, SEQ), 1)).astype(BF16)
    before = dot(earlier, per_row)
    targets = []
    for k in range(2):
        slot = jnp.sum(jnp.where(hot[k], before, 0.0), axis=1, keepdims=True)
        expert = columns[k][:, :1]
        half = jnp.floor(expert * 0.5)
        chunk = (expert - 2.0 * half) * OWNERS + half
        targets.append(
            jnp.where(slot < 7.5, chunk * 8 + slot, MAIN + (slot - 8) * EXPERTS + chunk)
        )
    meta = jnp.concatenate(gates + targets + [value[:, :1] for value in columns], axis=1)
    meta_out[:, :6] = meta
    places = [slot_hot(target) for target in targets]
    either = (places[0] | places[1]).astype(BF16)
    sent[:, :WIDE] = pack(dot_tn(either, moe_low).astype(BF16))
    if section == 1:
        scaled = [
            jnp.where(place, gate, 0.0) for place, gate in zip(places, gates)
        ]
        sent[:, WIDE:] = pack(sent_grads(either, scaled, cotangent[me]))


def sent_grads(either, scaled, upstream):
    rows = dot_tn(either, upstream)
    ones = jnp.ones((SEQ, 128), BF16)
    gates = scaled[0] + scaled[1]
    high = gates.astype(BF16)
    rest = (gates - high.astype(F32)).astype(BF16)
    factor = (dot_tn(high, ones) + dot_tn(rest, ones))[:, :1]
    return (rows * factor).astype(BF16)


def expert_weights(flag, core, own_in, other_in, own_out, other_out, weight_in, weight_out, sems):
    fetch(flag, own_in.at[core], other_in.at[core], weight_in, sems.at[0])
    fetch(flag, own_out.at[core], other_out.at[core], weight_out, sems.at[1])


EXPERT_SCRATCH = (
    pltpu.VMEM((D, D), BF16),
    pltpu.VMEM((D, D), BF16),
    pltpu.SemaphoreType.DMA((2,)),
)


def expert_forward_kernel(
    core, block, own_in, other_in, own_out, other_out, sent, rows_out, pre_out, *scratch
):
    weight_in, weight_out, sems = scratch
    flag = (core[0] == 0).astype(jnp.int32)
    expert_weights(flag, core[0], own_in, other_in, own_out, other_out, *scratch)
    rows = unpack(block[...])
    rows_out[...] = rows
    fetched(other_in.at[0], weight_in, sems.at[0])
    pre_act = dot(rows, weight_in[...])
    pre_out[...] = pre_act
    _, tanh = gelu_parts(pre_act)
    act_low = (0.5 * pre_act * (1.0 + tanh)).astype(BF16)
    fetched(other_out.at[0], weight_out, sems.at[1])
    pack_parts(dot(act_low, weight_out[...]).astype(BF16), sent, 0)


def expert_back(grads, pre_act, weight_in, weight_out, act_out, grad_pre_out):
    square, tanh = gelu_parts(pre_act)
    act_low = (0.5 * pre_act * (1.0 + tanh)).astype(BF16)
    act_out[...] = act_low
    grad_act = dot_nt(grads, weight_out)
    slope = 0.5 * (1.0 + tanh) + 0.5 * pre_act * (1.0 - tanh * tanh) * GELU_C * (
        1.0 + 3.0 * GELU_A * square
    )
    grad_pre = (grad_act * slope).astype(BF16)
    grad_pre_out[...] = grad_pre
    return act_low, dot_nt(grad_pre, weight_in).astype(BF16)


def expert_both_kernel(
    core, block, own_in, other_in, own_out, other_out, sent, rows_out, grads_out, act_out, pre_out,
    *scratch
):
    weight_in, weight_out, sems = scratch
    flag = (core[0] == 1).astype(jnp.int32)
    expert_weights(flag, core[0], own_in, other_in, own_out, other_out, *scratch)
    rows = unpack(block[:, :WIDE])
    rows_out[...] = rows
    grads = unpack(block[:, WIDE:])
    grads_out[...] = grads
    fetched(other_in.at[0], weight_in, sems.at[0])
    pre_act = dot(rows, weight_in[...])
    fetched(other_out.at[0], weight_out, sems.at[1])
    act_low, grad_rows = expert_back(
        grads, pre_act, weight_in[...], weight_out[...], act_out, pre_out
    )
    pack_parts(grad_rows, sent, 256)
    pack_parts(dot(act_low, weight_out[...]).astype(BF16), sent, 0)


def expert_back_kernel(
    core, block, pre_act, own_in, other_in, own_out, other_out, sent, grads_out, act_out, pre_out,
    *scratch
):
    weight_in, weight_out, sems = scratch
    flag = (core[0] == 0).astype(jnp.int32)
    expert_weights(flag, core[0], own_in, other_in, own_out, other_out, *scratch)
    grads = unpack(block[...])
    grads_out[...] = grads
    fetched(other_out.at[0], weight_out, sems.at[1])
    fetched(other_in.at[0], weight_in, sems.at[0])
    _, grad_rows = expert_back(
        grads, pre_act[...], weight_in[...], weight_out[...], act_out, pre_out
    )
    pack_parts(grad_rows, sent, 0)


def expert_grads_kernel(rows, grads, act_low, grad_pre, out):
    out[0] = dot_tn(rows[...], grad_pre[...])
    out[1] = dot_tn(act_low[...], grads[...])


def combine_kernel(core, meta, block, hidden, rows_out, folded):
    rows = unpack_part(block, 0)
    rows_out[...] = rows
    value = own_part(core[1], hidden[...])
    for k in range(2):
        place = slot_hot(meta[:, 2 + k : 3 + k]).astype(BF16)
        value = value + meta[:, k : k + 1] * dot(place, rows)
    folded[...] = fold(value).astype(BF16)


def moe_back_body(meta, out_rows, grad_rows, upstream, sent, value):
    grad = jnp.zeros((SEQ, PART), F32)
    lanes = iota((SEQ, 128), 1)
    tail = jnp.zeros((SEQ, 128), F32)
    for k in range(2):
        place = slot_hot(meta[:, 2 + k : 3 + k]).astype(BF16)
        grad = grad + dot(place, grad_rows)
        picked = dot(place, out_rows)
        if value is not None:
            value = value + meta[:, k : k + 1] * picked
        inner = jnp.sum(picked * upstream, axis=1, keepdims=True)
        tail = jnp.where(lanes == k, inner, tail)
    sent[:LINES] = fold(grad).astype(BF16)
    sent[LINES:] = jnp.transpose(tail)[:16].astype(BF16)
    return value


def second_back_kernel(core, meta, block, cotangent, hidden, sent, folded):
    out_rows = unpack_part(block, 0)
    grad_rows = unpack_part(block, 256)
    upstream = own_part(core[1], cotangent[core[0]].astype(F32))
    value = own_part(core[1], hidden[...])
    folded[...] = fold(moe_back_body(meta, out_rows, grad_rows, upstream, sent, value)).astype(BF16)


def first_back_kernel(core, meta, out_rows, block, upstream, sent):
    part = own_part(core[1], upstream[...].astype(F32))
    moe_back_body(meta, out_rows[...], unpack_part(block, 0), part, sent, None)


def shared_body(
    buckets, scores, inputs, gain, grad_qkv, attended, grad_low, moe_low, grad_logits, moe_gain, rel,
    shared,
):
    bucket = buckets[...]
    rel[...] = jnp.zeros_like(rel)
    for b in range(BUCKETS):
        hot = bucket == b
        for head in range(HEADS):
            at = head * BUCKETS + b
            rel[at : at + 1] = jnp.sum(jnp.where(hot, scores[head], 0.0), axis=0, keepdims=True)
    table = jnp.sum(jnp.transpose(rel[...]), axis=0, keepdims=True)
    normed = (inputs * norm(inputs) * gain).astype(BF16)
    shared[:QKV, :D] = dot_tn(grad_qkv, normed).astype(BF16)
    shared[QKV:, :D] = dot_tn(attended, grad_low).astype(BF16)
    line = iota((128, D), 0)
    wide = jnp.concatenate([table, jnp.zeros((1, D - 128), F32)], axis=1)
    rows = jnp.where(line == EXPERTS + 1, moe_gain, 0.0)
    rows = jnp.where(line == EXPERTS + 2, wide, rows)
    shared[:, D:] = (dot_tn(moe_low, grad_logits) + jnp.transpose(rows)).astype(BF16)


def shared_kernel(
    core, buckets, values, own, other, attended, moe_low, grad_hidden, scores, grad_qkv, logits,
    moe_gain, shared, rel,
):
    gain = chosen((core[0] == 1).astype(jnp.int32), own[...], other[...])
    shared_body(
        buckets, [scores[head].astype(F32) for head in range(HEADS)], values[...].astype(F32), gain,
        grad_qkv[...], attended[...], grad_hidden[...].astype(BF16), moe_low[...], logits[...],
        moe_gain[0:1], rel, shared,
    )


def attention_back_kernel(
    section, core, a, b, c, d, meta, hidden, upstream, own, other, router, router2, projected, probs,
    qkv, qkv2, out, out2, *refs,
):
    if section == 0:
        (moe_low, own_attn, other_attn, buckets, values, attended, shared1) = refs[:7]
        (sent, grad_hidden_out, mine, theirs, qkv_weight, out_weight, sems, rel, shared) = refs[7:]
    else:
        (sent, grad_hidden_out, scores_out, qkv_out, logits_out, gain_out) = refs[:6]
        (qkv_weight, out_weight, sems) = refs[6:]
    me = core[0]
    flag = (me == section).astype(jnp.int32)
    fetch(flag, qkv, qkv2, qkv_weight, sems.at[0])
    fetch(flag, out, out2, out_weight, sems.at[1])
    grad_moe = gathered(core[1], (a, b, c, d))
    tails = total((a.at[pl.ds(LINES, 16)], b.at[pl.ds(LINES, 16)], c.at[pl.ds(LINES, 16)], d.at[pl.ds(LINES, 16)]))
    tails = jnp.transpose(jnp.concatenate([tails, jnp.zeros((112, 128), F32)], axis=0))
    gain = chosen(flag, own[...], other[...])
    weight = chosen(flag, router[...].astype(F32), router2[...].astype(F32)).astype(BF16)
    gates = [meta[:, k : k + 1] for k in range(2)]
    grad_gates = [tails[:, k : k + 1] for k in range(2)]
    mean = gates[0] * grad_gates[0] + gates[1] * grad_gates[1]
    lanes = iota((SEQ, 128), 1).astype(F32)
    grad_logits = jnp.zeros((SEQ, 128), F32)
    for k in range(2):
        grad = gates[k] * (grad_gates[k] - mean)
        grad_logits = jnp.where(meta[:, 4 + k : 5 + k] == lanes, grad, grad_logits)
    grad_logits = grad_logits.astype(BF16)
    grad_moe = grad_moe + dot(grad_logits[:, :EXPERTS], weight)
    state = hidden[...]
    inverse = norm(state)
    grad_moe_gain = jnp.sum(grad_moe * state * inverse, axis=0, keepdims=True)
    before = upstream[me] if section == 1 else upstream[...]
    grad_hidden = before.astype(F32) + norm_back(state, inverse, gain, grad_moe)
    grad_hidden_out[...] = grad_hidden
    grad_low = grad_hidden.astype(BF16)
    fetched(out2, out_weight, sems.at[1])
    grad_heads = dot_nt(grad_low, out_weight[...]).astype(BF16)
    grads = []
    score_grads = []
    for head in range(HEADS):
        at = head * 3 * HEAD_DIM
        query = projected[:, at : at + HEAD_DIM]
        key = projected[:, at + HEAD_DIM : at + 2 * HEAD_DIM]
        value = projected[:, at + 2 * HEAD_DIM : at + 3 * HEAD_DIM]
        grad_head = grad_heads[:, head * HEAD_DIM : (head + 1) * HEAD_DIM]
        prob = probs[head]
        grad_probs = dot_nt(grad_head, value)
        grad_value = dot_tn(prob.astype(BF16), grad_head)
        inner = jnp.sum(prob * grad_probs, axis=-1, keepdims=True)
        grad_scores = (prob * (grad_probs - inner)).astype(BF16)
        score_grads.append(grad_scores.astype(F32))
        grads.append(SCALE * dot(grad_scores, key))
        grads.append(SCALE * dot_tn(grad_scores, query))
        grads.append(grad_value)
    grad_qkv = jnp.concatenate(grads, axis=1).astype(BF16)
    fetched(qkv2, qkv_weight, sems.at[0])
    sent[...] = dot(grad_qkv, qkv_weight[...]).astype(BF16)
    if section == 1:
        for head in range(HEADS):
            scores_out[head] = score_grads[head].astype(BF16)
        qkv_out[...] = grad_qkv
        logits_out[...] = grad_logits
        gain_out[...] = jnp.broadcast_to(grad_moe_gain, (8, D))
    else:
        attn_gain = chosen(flag, own_attn[...], other_attn[...])
        shared_body(
            buckets, score_grads, values[me].astype(F32), attn_gain, grad_qkv, attended[...],
            grad_low, moe_low[...], grad_logits, grad_moe_gain, rel, shared,
        )
    if section == 0:

        @pl.when(me == 0)
        def _():
            mine[...] = shared[...]
            theirs[...] = shared1[...]

        @pl.when(me == 1)
        def _():
            mine[...] = shared1[...]
            theirs[...] = shared[...]


def input_back_kernel(section, core, a, b, c, d, values, grad_hidden, own, other, *refs):
    if section == 1:
        meta, grad_out, low_out, sent = refs
    else:
        second, mine, theirs, grad_out = refs
    me = core[0]
    flag = (me == section).astype(jnp.int32)
    grad_normed = total((a, b, c, d))
    inputs = (values[me] if section == 0 else values[...]).astype(F32)
    inverse = norm(inputs)
    gain = chosen(flag, own[...], other[...])
    grad_inputs = grad_hidden[...] + norm_back(inputs, inverse, gain, grad_normed)
    grad_out[:SEQ] = grad_inputs
    if section == 1:
        upstream = grad_inputs.astype(BF16)
        low_out[...] = upstream
        places = [slot_hot(meta[:, 2 + k : 3 + k]) for k in range(2)]
        either = (places[0] | places[1]).astype(BF16)
        scaled = [jnp.where(places[k], meta[:, k : k + 1], 0.0) for k in range(2)]
        sent[...] = pack(sent_grads(either, scaled, upstream))
    grad_gain = jnp.sum(grad_normed * inputs * inverse, axis=0, keepdims=True)
    grad_out[SEQ:] = jnp.broadcast_to(grad_gain, (8, D))
    if section == 0:

        @pl.when(me == 0)
        def _():
            mine[...] = grad_out[...]
            theirs[...] = second[...]

        @pl.when(me == 1)
        def _():
            mine[...] = second[...]
            theirs[...] = grad_out[...]


def output_kernel(core, first, a, b, c, d, mine, theirs):
    second = gathered(core[1], (a, b, c, d)).astype(BF16)

    @pl.when(core[0] == 0)
    def _():
        mine[...] = first[...]
        theirs[...] = second

    @pl.when(core[0] == 1)
    def _():
        mine[...] = second
        theirs[...] = first[...]


def pair_kernel(mine, got, out):
    out[...] = (mine[...].astype(F32) + got[...].astype(F32)).astype(BF16)


CHUNK = D // OWNERS
SPARE = 64


def reduce_kernel(blocks, mine, got, out):
    value = blocks[0].astype(F32)
    for at in range(1, OWNERS):
        value = value + blocks[at].astype(F32)
    gain = mine[SEQ : SEQ + 1] + got[SEQ : SEQ + 1]
    columns = jnp.transpose(jnp.broadcast_to(gain, (128, D)))
    lanes = iota((CHUNK, 128), 1)
    side = value[:, D:]
    for at in range(OWNERS):
        side = jnp.where(lanes == SPARE + at, columns[at * CHUNK : (at + 1) * CHUNK], side)
    main_low, side_low = value[:, :D].astype(BF16), side.astype(BF16)
    for at in range(OWNERS):
        out[at, :, :D] = main_low
        out[at, :, D:] = side_low


def final_kernel(blocks, qkv, attn_out, router, gain_attn, gain_moe, table):
    sides = []
    gains = jnp.zeros((CHUNK, 128), F32)
    for at in range(OWNERS):
        main = blocks[at, :, :D].astype(F32)
        rows = slice(at * CHUNK, (at + 1) * CHUNK)
        if (at + 1) * CHUNK <= QKV:
            qkv[rows] = main
        else:
            attn_out[at * CHUNK - QKV : (at + 1) * CHUNK - QKV] = main
        side = blocks[at, :, D:].astype(F32)
        sides.append(side)
        gains = gains + side
    rows = jnp.transpose(jnp.concatenate(sides, axis=0))
    router[...] = rows[:EXPERTS]
    gain_moe[...] = rows[EXPERTS + 1 : EXPERTS + 2]
    line = rows[EXPERTS + 2 : EXPERTS + 3]
    for head in range(HEADS):
        table[head] = line[:, head * BUCKETS : (head + 1) * BUCKETS]
    padded = jnp.concatenate([gains, jnp.zeros((128 - CHUNK, 128), F32)], axis=0)
    spare = jnp.transpose(padded)
    pieces = [spare[SPARE + at : SPARE + at + 1, :CHUNK] for at in range(OWNERS)]
    gain_attn[...] = jnp.concatenate(pieces, axis=1)


def place_copies(core, outs, spaces, sems_in, sems_out, sources_of):
    def move(me):
        reads, writes = [], []
        for at, pair in enumerate(sources_of(me)):
            for half, source in enumerate(pair):
                room, sem = spaces[at].at[half], 2 * at + half
                reads.append(pltpu.make_async_copy(source, room, sems_in.at[sem]))
                writes.append(pltpu.make_async_copy(room, outs[at].at[half], sems_out.at[sem]))
        for copy in reads:
            copy.start()
        for read, write in zip(reads, writes):
            read.wait()
            write.start()
        for copy in writes:
            copy.wait()

    for me in range(2):

        @pl.when(core[0] == me)
        def _(me=me):
            move(me)


def place_expert_kernel(core, own0, got0, own1, got1, grad_in, grad_out, *refs):
    def sources_of(me):
        pair = (own0, got0) if me == 0 else (got1, own1)
        return [[ref.at[at] for ref in pair] for at in range(2)]

    place_copies(core, (grad_in, grad_out), refs[:2], *refs[2:], sources_of)


def place_kernel(core, act, act_got, grad, grad_got, activations, input_grad, *refs):
    rows = pl.ds(0, SEQ)

    def sources_of(me):
        pairs = [(act, act_got), (grad.at[rows], grad_got.at[rows])]
        return [pair if me == 0 else pair[::-1] for pair in pairs]

    place_copies(core, (activations, input_grad), refs[:2], *refs[2:], sources_of)


def permuted(value, axis, pairs):
    return lax.ppermute(value, axis, pairs)


def swap(value):
    return permuted(value, "pipe", [(0, 1), (1, 0)])


def down(value):
    return permuted(value, "pipe", [(1, 0)])


def up(value):
    return permuted(value, "pipe", [(0, 1)])


def spread(value):
    count = lax.axis_size("tensor")
    return [value] + [
        permuted(value, "tensor", [(i, (i + by) % count) for i in range(count)])
        for by in range(1, count)
    ]


def after(value, *others):
    return lax.optimization_barrier((value, *others))[0]


def exchange(block):
    moved = lax.all_to_all(
        block.reshape(EXPERTS, 8, block.shape[1]),
        ("pipe", "expert"),
        split_axis=0,
        concat_axis=0,
        tiled=True,
    )
    return moved.reshape(block.shape)


def collect(block):
    moved = lax.all_to_all(
        block.reshape(EXPERTS * GROUP, 8, block.shape[3]),
        ("pipe", "expert", "tensor"),
        split_axis=0,
        concat_axis=0,
        tiled=True,
    )
    return moved.reshape(block.shape)


def shards(
    tokens,
    cotangent,
    routes,
    buckets,
    gain_attn,
    w_qkv,
    w_attn_out,
    rel_table,
    gain_moe,
    w_router,
    w_expert_in,
    w_expert_out,
):
    index = lax.axis_index("pipe")
    core = jnp.stack([index, lax.axis_index("tensor")]).astype(jnp.int32)
    qkv = w_qkv[0].T
    attn_out = w_attn_out[0]
    router = w_router[0].T
    ids = jnp.transpose(routes[0], (0, 2, 1))
    qkv2 = swap(qkv)
    attn_out2 = swap(attn_out)
    tables = (rel_table[0], swap(rel_table[0]))
    attn_gains = (gain_attn, swap(gain_attn))
    moe_gains = (gain_moe, swap(gain_moe))
    router2 = swap(router)
    ids2 = swap(lax.dynamic_index_in_dim(ids, 1 - index, 0, keepdims=False))

    attn_args = (qkv, qkv2, attn_out, attn_out2)

    (bias,) = kernel_call(
        bias_kernel,
        "bias",
        (core, buckets, *tables),
        (SMEM, VMEM, VMEM, VMEM),
        (shape(2, HEADS, SEQ, SEQ),),
    )
    partial0, projected0, probs0, attended0 = kernel_call(
        first_attention_kernel,
        "first_attention",
        (core, tokens, *attn_gains, bias, *attn_args),
        (SMEM, VMEM, VMEM, VMEM, VMEM, ANY, ANY, ANY, ANY),
        ATTENTION_OUT,
        ATTENTION_SCRATCH,
    )
    parts = spread(partial0)
    expert_specs = (ANY, ANY, ANY, ANY)
    route_args = (*moe_gains, router, router2, ids, ids2)

    def route(section, values, parts, more, wide):
        return kernel_call(
            lambda *refs: route_kernel(section, *refs),
            "route",
            (core, values, *parts, *route_args, *more),
            (SMEM,) + (VMEM,) * (11 + len(more)),
            (shape(SEQ, D), low(SEQ, D), shape(SEQ, 128), low(MAIN, wide)),
        )

    hidden0, moe_low0, meta0, sent = route(0, tokens, parts, (), WIDE)
    weights = lax.optimization_barrier((w_expert_in[0], w_expert_out[0], sent))[:2]
    expert_args = (w_expert_in[0], swap(weights[0]), w_expert_out[0], swap(weights[1]))
    block = exchange(sent)
    sent, rows0, pre0 = kernel_call(
        expert_forward_kernel,
        "expert_forward",
        (core, block, *expert_args),
        (SMEM, VMEM, *expert_specs),
        (low(EXPERTS, GROUP, 8, 256), low(ROWS, D), shape(ROWS, D)),
        EXPERT_SCRATCH,
    )
    block = collect(sent)
    out_rows0, part0 = kernel_call(
        combine_kernel,
        "combine",
        (core, meta0, block, hidden0),
        (SMEM, VMEM, VMEM, VMEM),
        (low(ROWS, PART), low(LINES, 128)),
    )

    act0, partial1, projected1, probs1, attended1 = kernel_call(
        second_attention_kernel,
        "second_attention",
        (core, *spread(part0), *attn_gains, bias, *attn_args),
        (SMEM,) + (VMEM,) * 7 + (ANY,) * 4,
        (low(SEQ, D), *ATTENTION_OUT),
        ATTENTION_SCRATCH,
    )
    hidden1, moe_low1, meta1, sent = route(1, act0, spread(partial1), (cotangent,), 2 * WIDE)
    block = exchange(sent)
    sent, rows1, grads1, act_low1, grad_pre1 = kernel_call(
        expert_both_kernel,
        "expert_both",
        (core, block, *expert_args),
        (SMEM, VMEM, *expert_specs),
        (low(EXPERTS, GROUP, 8, 512), low(ROWS, D), low(ROWS, D), low(ROWS, D), low(ROWS, D)),
        EXPERT_SCRATCH,
        vmem=16,
    )
    block = collect(sent)

    sent, part1 = kernel_call(
        second_back_kernel,
        "second_back",
        (core, meta1, block, cotangent, hidden1),
        (SMEM, VMEM, VMEM, VMEM, VMEM),
        (low(LINES + 16, 128), low(LINES, 128)),
    )

    def expert_grads(*args):
        return kernel_call(
            expert_grads_kernel, "expert_grads", args, (VMEM,) * 4, (shape(2, D, D),)
        )[0]

    def attention_back(section, parts, meta, hidden, upstream, saved, more, outputs, scratch):
        return kernel_call(
            lambda *refs: attention_back_kernel(section, *refs),
            "attention_back",
            (core, *parts, meta, hidden, upstream, *moe_gains, router, router2, *saved, *attn_args)
            + more,
            (SMEM,) + (VMEM,) * 13 + (ANY,) * 4 + (VMEM,) * len(more),
            (low(SEQ, D), shape(SEQ, D), *outputs),
            ATTENTION_SCRATCH + scratch,
        )

    partial, grad_hidden1, *grads = attention_back(
        1, spread(sent), meta1, hidden1, cotangent, (projected1, probs1), (),
        (low(HEADS, SEQ, SEQ), low(SEQ, QKV), low(SEQ, 128), shape(8, D)), (),
    )
    parts = spread(partial)
    (shared1,) = kernel_call(
        shared_kernel,
        "shared",
        (core, buckets, act0, *attn_gains, attended1, moe_low1, after(grad_hidden1, parts[3]), *grads),
        (SMEM,) + (VMEM,) * 11,
        (low(D, D + 128),),
        (pltpu.VMEM((128, 128), F32),),
    )
    expert_grad1 = expert_grads(after(rows1, parts[3]), grads1, act_low1, grad_pre1)
    parts[1] = after(parts[1], shared1, expert_grad1)
    grad_inputs1, upstream, sent = kernel_call(
        lambda *refs: input_back_kernel(1, *refs),
        "input_back",
        (core, *parts, act0, grad_hidden1, *attn_gains, meta0),
        (SMEM,) + (VMEM,) * 9,
        (shape(SEQ + 8, D), low(SEQ, D), low(MAIN, WIDE)),
    )

    block = exchange(sent)
    sent, grads0, act_low0, grad_pre0 = kernel_call(
        expert_back_kernel,
        "expert_back",
        (core, block, pre0, *expert_args),
        (SMEM, VMEM, VMEM, *expert_specs),
        (low(EXPERTS, GROUP, 8, 256), low(ROWS, D), low(ROWS, D), low(ROWS, D)),
        EXPERT_SCRATCH,
    )
    block = collect(sent)
    (sent,) = kernel_call(
        first_back_kernel,
        "first_back",
        (core, meta0, out_rows0, block, upstream),
        (SMEM,) + (VMEM,) * 4,
        (low(LINES + 16, 128),),
    )
    parts = spread(sent)
    expert_grad0 = expert_grads(after(rows0, sent), grads0, act_low0, grad_pre0)
    expert_grad1 = after(expert_grad1, sent)
    expert_grad1b = up(expert_grad1)
    parts[3] = after(parts[3], expert_grad0)
    partial, grad_hidden0, mine, theirs = attention_back(
        0, parts, meta0, hidden0, upstream, (projected0, probs0),
        (moe_low0, *attn_gains, buckets, tokens, attended0, shared1),
        (low(D, D + 128), low(D, D + 128)),
        (pltpu.VMEM((128, 128), F32), pltpu.VMEM((D, D + 128), BF16)),
    )
    got = swap(theirs)
    parts = spread(partial)
    expert_grad0 = after(expert_grad0, got, expert_grad1b)
    expert_grad0b = down(expert_grad0)

    (pair,) = kernel_call(
        pair_kernel, "pair", (mine, got), (VMEM, VMEM), (low(D, D + 128),)
    )
    blocks = pair.reshape(OWNERS, CHUNK, D + 128)
    blocks = lax.all_to_all(blocks, "expert", split_axis=0, concat_axis=0, tiled=True)
    act_parts = spread(after(part1, pair))
    grad_mine, grad_theirs = kernel_call(
        lambda *refs: input_back_kernel(0, *refs),
        "input_back",
        (core, *parts, tokens, grad_hidden0, *attn_gains, grad_inputs1),
        (SMEM,) + (VMEM,) * 9,
        (shape(SEQ + 8, D), shape(SEQ + 8, D)),
        (pltpu.VMEM((SEQ + 8, D), F32),),
    )
    grad_got = swap(grad_theirs)
    def place(body, sources, results):
        return kernel_call(
            body,
            "place",
            (core, *sources),
            (SMEM,) + (ANY,) * 4,
            results,
            tuple(pltpu.VMEM(result.shape, result.dtype) for result in results)
            + (pltpu.SemaphoreType.DMA((4,)), pltpu.SemaphoreType.DMA((4,))),
            (ANY, ANY),
        )

    grad_in, grad_out = place(
        place_expert_kernel,
        (expert_grad0, expert_grad0b, expert_grad1, expert_grad1b),
        (shape(2, D, D), shape(2, D, D)),
    )
    (blocks,) = kernel_call(
        reduce_kernel,
        "reduce",
        (blocks, grad_mine, grad_got),
        (VMEM,) * 3,
        (low(*blocks.shape),),
    )
    act_mine, act_theirs = kernel_call(
        output_kernel,
        "output",
        (core, act0, *act_parts),
        (SMEM,) + (VMEM,) * 5,
        (low(SEQ, D), low(SEQ, D)),
    )
    act_got = swap(act_theirs)
    blocks = lax.all_to_all(blocks, "expert", split_axis=0, concat_axis=0, tiled=True)
    activations, input_grad = place(
        place_kernel,
        (act_mine, act_got, grad_mine, grad_got),
        (low(2, SEQ, D), shape(2, SEQ, D)),
    )
    blocks = after(blocks, grad_in, grad_out, activations, input_grad)
    grad_qkv, grad_attn_out, grad_router, grad_gain, grad_moe_gain, grad_table = kernel_call(
        final_kernel,
        "final",
        (blocks,),
        (VMEM,),
        (shape(QKV, D), shape(HEAD_COLS, D), shape(EXPERTS, D), shape(1, D), shape(1, D))
        + (shape(HEADS, 1, BUCKETS),),
    )
    return (
        activations[None],
        input_grad[None],
        grad_gain,
        grad_qkv.T[None],
        grad_attn_out[None],
        jnp.transpose(grad_table, (1, 0, 2)),
        grad_moe_gain,
        grad_router.T[None],
        grad_in[None],
        grad_out[None],
    )


def solution(mesh):
    in_specs = (
        P(None, "expert", None),
        P(None, "expert", None),
        P("pipe", None, "expert", None),
        P(),
        P("pipe", None),
        P("pipe", None, "tensor"),
        P("pipe", "tensor", None),
        P("pipe", "tensor", None),
        P("pipe", None),
        P("pipe", None, None),
        P("pipe", "expert", None, "tensor"),
        P("pipe", "expert", "tensor", None),
    )
    out_specs = (
        P("pipe", None, "expert", None),
        P("pipe", None, "expert", None),
        P("pipe", None),
        P("pipe", None, "tensor"),
        P("pipe", "tensor", None),
        P("pipe", "tensor", None),
        P("pipe", None),
        P("pipe", None, None),
        P("pipe", "expert", None, "tensor"),
        P("pipe", "expert", "tensor", None),
    )
    return jax.shard_map(shards, mesh=mesh, in_specs=in_specs, out_specs=out_specs, check_vma=False)
```

```python
import jax
import jax.numpy as jnp
from jax import lax
from jax.experimental import pallas as pl
from jax.experimental.pallas import tpu as pltpu
from jax.sharding import PartitionSpec as P

EPSILON = 1e-06
F32 = jnp.float32
BF16 = jnp.bfloat16
SEQ = 128
D = 768
HEADS = 3
HEAD_DIM = 64
QKV = 3 * HEADS * HEAD_DIM
HEAD_COLS = HEADS * HEAD_DIM
EXPERTS = 32
OWNERS = 16
BUCKETS = 32
MAIN = 8 * EXPERTS
ROWS = 10 * EXPERTS
WIDE = D + 256
GROUP = 4
PART = D // GROUP
PIECE = 64
LINES = SEQ * PART // 128
SCALE = HEAD_DIM**-0.5
GELU_C = 0.7978845608028654
GELU_A = 0.044715
VMEM = pl.BlockSpec(memory_space=pltpu.VMEM)
SMEM = pl.BlockSpec(memory_space=pltpu.SMEM)
ANY = pl.BlockSpec(memory_space=pl.ANY)


def shape(*dims, dtype=F32):
    return jax.ShapeDtypeStruct(dims, dtype)


def low(*dims):
    return jax.ShapeDtypeStruct(dims, BF16)


def kernel_call(body, name, inputs, specs, outputs, scratch=(), out_specs=None, vmem=12):
    return pl.pallas_call(
        body,
        out_shape=tuple(outputs),
        in_specs=list(specs),
        out_specs=tuple(out_specs or [VMEM] * len(outputs)),
        scratch_shapes=list(scratch),
        compiler_params=pltpu.CompilerParams(vmem_limit_bytes=vmem * 2**20),
        cost_estimate=pl.CostEstimate(
            flops=1_600_000_000, bytes_accessed=8_000_000, transcendentals=0
        ),
        name=name,
    )(*inputs)


def dot(a, b):
    return jnp.dot(a, b, preferred_element_type=F32)


def dot_nt(a, b):
    return lax.dot_general(a, b, (((1,), (1,)), ((), ())), preferred_element_type=F32)


def dot_tn(a, b):
    return lax.dot_general(a, b, (((0,), (0,)), ((), ())), preferred_element_type=F32)


def iota(dims, axis):
    return lax.broadcasted_iota(jnp.int32, dims, axis)


def chosen(flag, own, other):
    return jnp.where(flag == 1, own, other)


def fetch(flag, own, other, target, semaphore):
    @pl.when(flag == 1)
    def _():
        pltpu.make_async_copy(own, target, semaphore).start()

    @pl.when(flag != 1)
    def _():
        pltpu.make_async_copy(other, target, semaphore).start()


def fetched(other, target, semaphore):
    pltpu.make_async_copy(other, target, semaphore).wait()


def norm(values):
    return lax.rsqrt(jnp.mean(values * values, axis=-1, keepdims=True) + EPSILON)


def norm_back(values, inverse, gain, upstream):
    weighted = upstream * gain
    inner = jnp.mean(weighted * values, axis=-1, keepdims=True)
    return inverse * weighted - values * (inverse * inverse * inverse) * inner


def total(refs):
    value = refs[0][...].astype(F32)
    for ref in refs[1:]:
        value = value + ref[...].astype(F32)
    return value


def gelu_parts(value):
    square = value * value
    tanh = jnp.tanh(GELU_C * value * (1.0 + GELU_A * square))
    return square, tanh


def pack(rows):
    spread = (iota((MAIN, EXPERTS), 0) // 8 == iota((MAIN, EXPERTS), 1)).astype(BF16)
    place = iota((MAIN, 128), 0) % 8
    parts = [rows[:MAIN]]
    for late in range(2):
        start = MAIN + late * EXPERTS
        copies = dot(spread, rows[start : start + EXPERTS])
        piece = jnp.zeros((MAIN, 128), F32)
        for r in range(D // 128):
            piece = jnp.where(place == r, copies[:, r * 128 : (r + 1) * 128], piece)
        parts.append(piece.astype(BF16))
    return jnp.concatenate(parts, axis=1)


def unpack(block):
    count = D // 128
    dims = (count * EXPERTS, MAIN)
    row = iota(dims, 0)
    gather = (iota(dims, 1) == (row % EXPERTS) * 8 + row // EXPERTS).astype(BF16)
    pieces = dot(gather, block[:, D:]).astype(BF16)
    parts = [block[:, :D]]
    for late in range(2):
        columns = slice(late * 128, (late + 1) * 128)
        blocks = [pieces[r * EXPERTS : (r + 1) * EXPERTS, columns] for r in range(count)]
        parts.append(jnp.concatenate(blocks, axis=1))
    return jnp.concatenate(parts, axis=0)


def part_of(value, part):
    last = GROUP * 128 + part * PIECE
    return value[:, part * 128 : (part + 1) * 128], value[:, last : last + PIECE]


def pack_parts(rows, out, start):
    spread = (iota((MAIN, EXPERTS), 0) // 8 == iota((MAIN, EXPERTS), 1)).astype(BF16)
    place = iota((MAIN, PIECE), 0) % 8
    copies = []
    for late in range(2):
        first = MAIN + late * EXPERTS
        copies.append(dot(spread, rows[first : first + EXPERTS]))
    for part in range(GROUP):
        piece = jnp.zeros((MAIN, PIECE), F32)
        for late in range(2):
            block, last = part_of(copies[late], part)
            piece = jnp.where(place == 3 * late, block[:, :PIECE], piece)
            piece = jnp.where(place == 3 * late + 1, block[:, PIECE:], piece)
            piece = jnp.where(place == 3 * late + 2, last, piece)
        block = jnp.concatenate([*part_of(rows[:MAIN], part), piece.astype(BF16)], axis=1)
        out[:, part, :, start : start + 256] = block.reshape(EXPERTS, 8, 256)


def unpack_part(block, start):
    value = block[:, 0, :, start : start + 256].astype(F32)
    for sender in range(1, GROUP):
        value = value + block[:, sender, :, start : start + 256].astype(F32)
    value = value.reshape(MAIN, 256).astype(BF16)
    dims = (6 * EXPERTS, MAIN)
    row = iota(dims, 0)
    gather = (iota(dims, 1) == (row % EXPERTS) * 8 + row // EXPERTS).astype(BF16)
    pieces = dot(gather, value[:, PART:]).astype(BF16)
    parts = [value[:, :PART]]
    for late in range(2):
        blocks = [pieces[r * EXPERTS : (r + 1) * EXPERTS] for r in range(3 * late, 3 * late + 3)]
        parts.append(jnp.concatenate(blocks, axis=1))
    return jnp.concatenate(parts, axis=0)


def own_part(index, value):
    block, last = part_of(value, 0)
    for part in range(1, GROUP):
        other_block, other_last = part_of(value, part)
        block = jnp.where(index == part, other_block, block)
        last = jnp.where(index == part, other_last, last)
    return jnp.concatenate([block, last], axis=1)


def fold(part):
    tail = jnp.concatenate([part[: SEQ // 2, 128:], part[SEQ // 2 :, 128:]], axis=1)
    return jnp.concatenate([part[:, :128], tail], axis=0)


def gathered(index, refs):
    parts = [ref[:LINES].astype(F32) for ref in refs]
    blocks, lasts = [], []
    for at in range(GROUP):
        value = parts[0]
        for by in range(1, GROUP):
            value = jnp.where((index + GROUP - by) % GROUP == at, parts[by], value)
        tail = value[SEQ:]
        blocks.append(value[:SEQ])
        lasts.append(jnp.concatenate([tail[:, :PIECE], tail[:, PIECE:]], axis=0))
    return jnp.concatenate(blocks + lasts, axis=1)


def column(row):
    return jnp.transpose(jnp.broadcast_to(row, (SEQ, 128)))


def slot_hot(target):
    return target == iota((SEQ, ROWS), 1).astype(F32)


def bias_kernel(core, buckets, own, other, out):
    bucket = buckets[...]
    causal = iota((SEQ, SEQ), 0) >= iota((SEQ, SEQ), 1)
    hot = [bucket == b for b in range(BUCKETS)]
    for section in range(2):
        flag = (core[0] == section).astype(jnp.int32)
        table = chosen(flag, own[...].astype(F32), other[...].astype(F32))
        for head in range(HEADS):
            value = jnp.zeros((SEQ, SEQ), F32)
            for b in range(BUCKETS):
                value = jnp.where(hot[b], table[head : head + 1, b : b + 1], value)
            out[section, head] = jnp.where(causal, value, -1e30)


def attention_body(values, gain, qkv_weight, out_weight, bias, refs):
    partial_out, projected_out, probs_out, attended_out = refs
    normed = (values * norm(values) * gain).astype(BF16)
    projected = dot_nt(normed, qkv_weight).astype(BF16)
    projected_out[...] = projected
    heads = []
    for head in range(HEADS):
        at = head * 3 * HEAD_DIM
        query = projected[:, at : at + HEAD_DIM]
        key = projected[:, at + HEAD_DIM : at + 2 * HEAD_DIM]
        value = projected[:, at + 2 * HEAD_DIM : at + 3 * HEAD_DIM]
        scores = dot_nt(query, key) * SCALE + bias[head]
        exps = jnp.exp(scores - jnp.max(scores, axis=-1, keepdims=True))
        probs = exps / jnp.sum(exps, axis=-1, keepdims=True)
        probs_out[head] = probs
        heads.append(dot(probs.astype(BF16), value))
    attended = jnp.concatenate(heads, axis=1).astype(BF16)
    attended_out[...] = attended
    partial_out[...] = dot(attended, out_weight).astype(BF16)


ATTENTION_OUT = (
    low(SEQ, D),
    low(SEQ, QKV),
    shape(HEADS, SEQ, SEQ),
    low(SEQ, HEAD_COLS),
)
ATTENTION_SCRATCH = (
    pltpu.VMEM((QKV, D), BF16),
    pltpu.VMEM((HEAD_COLS, D), BF16),
    pltpu.SemaphoreType.DMA((2,)),
)


def first_attention_kernel(core, tokens, own, other, bias, qkv, qkv2, out, out2, *refs):
    *results, qkv_weight, out_weight, sems = refs
    flag = (core[0] == 0).astype(jnp.int32)
    fetch(flag, qkv, qkv2, qkv_weight, sems.at[0])
    fetch(flag, out, out2, out_weight, sems.at[1])
    values = tokens[core[0]].astype(F32)
    gain = chosen(flag, own[...], other[...])
    fetched(qkv2, qkv_weight, sems.at[0])
    fetched(out2, out_weight, sems.at[1])
    attention_body(values, gain, qkv_weight[...], out_weight[...], bias[0], results)


def second_attention_kernel(
    core, a, b, c, d, own, other, bias, qkv, qkv2, out, out2, act, *refs
):
    *results, qkv_weight, out_weight, sems = refs
    flag = (core[0] == 1).astype(jnp.int32)
    fetch(flag, qkv, qkv2, qkv_weight, sems.at[0])
    fetch(flag, out, out2, out_weight, sems.at[1])
    section_out = gathered(core[1], (a, b, c, d)).astype(BF16)
    act[...] = section_out
    gain = chosen(flag, own[...], other[...])
    fetched(qkv2, qkv_weight, sems.at[0])
    fetched(out2, out_weight, sems.at[1])
    attention_body(
        section_out.astype(F32), gain, qkv_weight[...], out_weight[...], bias[1], results
    )


def route_kernel(section, core, values, a, b, c, d, own, other, router, router2, ids, ids2, *refs):
    if section == 1:
        cotangent, hidden_out, low_out, meta_out, sent = refs
    else:
        hidden_out, low_out, meta_out, sent = refs
    me = core[0]
    flag = (me == section).astype(jnp.int32)
    inputs = values[me] if section == 0 else values[...]
    hidden = inputs.astype(F32) + total((a, b, c, d))
    hidden_out[...] = hidden
    gain = chosen(flag, own[...], other[...])
    moe_low = (hidden * norm(hidden) * gain).astype(BF16)
    low_out[...] = moe_low
    weight = chosen(flag, router[...].astype(F32), router2[...].astype(F32)).astype(BF16)
    logits = dot_nt(moe_low, weight)
    routes = chosen(flag, ids[me], ids2[...]).astype(F32)
    columns = [column(routes[k : k + 1]) for k in range(2)]
    lanes = iota((SEQ, EXPERTS), 1).astype(F32)
    hot = [value[:, :EXPERTS] == lanes for value in columns]
    picked = [jnp.sum(jnp.where(h, logits, 0.0), axis=1, keepdims=True) for h in hot]
    top = jnp.maximum(picked[0], picked[1])
    exps = [jnp.exp(value - top) for value in picked]
    gates = [value / (exps[0] + exps[1]) for value in exps]
    per_row = (hot[0].astype(F32) + hot[1].astype(F32)).astype(BF16)
    earlier = (iota((SEQ, SEQ), 0) > iota((SEQ, SEQ), 1)).astype(BF16)
    before = dot(earlier, per_row)
    targets = []
    for k in range(2):
        slot = jnp.sum(jnp.where(hot[k], before, 0.0), axis=1, keepdims=True)
        expert = columns[k][:, :1]
        half = jnp.floor(expert * 0.5)
        chunk = (expert - 2.0 * half) * OWNERS + half
        targets.append(
            jnp.where(slot < 7.5, chunk * 8 + slot, MAIN + (slot - 8) * EXPERTS + chunk)
        )
    meta = jnp.concatenate(gates + targets + [value[:, :1] for value in columns], axis=1)
    meta_out[:, :6] = meta
    places = [slot_hot(target) for target in targets]
    either = (places[0] | places[1]).astype(BF16)
    sent[:, :WIDE] = pack(dot_tn(either, moe_low).astype(BF16))
    if section == 1:
        scaled = [
            jnp.where(place, gate, 0.0) for place, gate in zip(places, gates)
        ]
        sent[:, WIDE:] = pack(sent_grads(either, scaled, cotangent[me]))


def sent_grads(either, scaled, upstream):
    rows = dot_tn(either, upstream)
    ones = jnp.ones((SEQ, 128), BF16)
    gates = scaled[0] + scaled[1]
    high = gates.astype(BF16)
    rest = (gates - high.astype(F32)).astype(BF16)
    factor = (dot_tn(high, ones) + dot_tn(rest, ones))[:, :1]
    return (rows * factor).astype(BF16)


def expert_weights(flag, core, own_in, other_in, own_out, other_out, weight_in, weight_out, sems):
    fetch(flag, own_in.at[core], other_in.at[core], weight_in, sems.at[0])
    fetch(flag, own_out.at[core], other_out.at[core], weight_out, sems.at[1])


EXPERT_SCRATCH = (
    pltpu.VMEM((D, D), BF16),
    pltpu.VMEM((D, D), BF16),
    pltpu.SemaphoreType.DMA((2,)),
)


def expert_forward_kernel(
    core, block, own_in, other_in, own_out, other_out, sent, rows_out, pre_out, *scratch
):
    weight_in, weight_out, sems = scratch
    flag = (core[0] == 0).astype(jnp.int32)
    expert_weights(flag, core[0], own_in, other_in, own_out, other_out, *scratch)
    rows = unpack(block[...])
    rows_out[...] = rows
    fetched(other_in.at[0], weight_in, sems.at[0])
    pre_act = dot(rows, weight_in[...])
    pre_out[...] = pre_act
    _, tanh = gelu_parts(pre_act)
    act_low = (0.5 * pre_act * (1.0 + tanh)).astype(BF16)
    fetched(other_out.at[0], weight_out, sems.at[1])
    pack_parts(dot(act_low, weight_out[...]).astype(BF16), sent, 0)


def expert_back(grads, pre_act, weight_in, weight_out, act_out, grad_pre_out):
    square, tanh = gelu_parts(pre_act)
    act_low = (0.5 * pre_act * (1.0 + tanh)).astype(BF16)
    act_out[...] = act_low
    grad_act = dot_nt(grads, weight_out)
    slope = 0.5 * (1.0 + tanh) + 0.5 * pre_act * (1.0 - tanh * tanh) * GELU_C * (
        1.0 + 3.0 * GELU_A * square
    )
    grad_pre = (grad_act * slope).astype(BF16)
    grad_pre_out[...] = grad_pre
    return act_low, dot_nt(grad_pre, weight_in).astype(BF16)


def expert_both_kernel(
    core, block, own_in, other_in, own_out, other_out, sent, rows_out, grads_out, act_out, pre_out,
    *scratch
):
    weight_in, weight_out, sems = scratch
    flag = (core[0] == 1).astype(jnp.int32)
    expert_weights(flag, core[0], own_in, other_in, own_out, other_out, *scratch)
    rows = unpack(block[:, :WIDE])
    rows_out[...] = rows
    grads = unpack(block[:, WIDE:])
    grads_out[...] = grads
    fetched(other_in.at[0], weight_in, sems.at[0])
    pre_act = dot(rows, weight_in[...])
    fetched(other_out.at[0], weight_out, sems.at[1])
    act_low, grad_rows = expert_back(
        grads, pre_act, weight_in[...], weight_out[...], act_out, pre_out
    )
    pack_parts(grad_rows, sent, 256)
    pack_parts(dot(act_low, weight_out[...]).astype(BF16), sent, 0)


def expert_back_kernel(
    core, block, pre_act, own_in, other_in, own_out, other_out, sent, grads_out, act_out, pre_out,
    *scratch
):
    weight_in, weight_out, sems = scratch
    flag = (core[0] == 0).astype(jnp.int32)
    expert_weights(flag, core[0], own_in, other_in, own_out, other_out, *scratch)
    grads = unpack(block[...])
    grads_out[...] = grads
    fetched(other_out.at[0], weight_out, sems.at[1])
    fetched(other_in.at[0], weight_in, sems.at[0])
    _, grad_rows = expert_back(
        grads, pre_act[...], weight_in[...], weight_out[...], act_out, pre_out
    )
    pack_parts(grad_rows, sent, 0)


def expert_grads_kernel(rows, grads, act_low, grad_pre, out):
    out[0] = dot_tn(rows[...], grad_pre[...])
    out[1] = dot_tn(act_low[...], grads[...])


def combine_kernel(core, meta, block, hidden, rows_out, folded):
    rows = unpack_part(block, 0)
    rows_out[...] = rows
    value = own_part(core[1], hidden[...])
    for k in range(2):
        place = slot_hot(meta[:, 2 + k : 3 + k]).astype(BF16)
        value = value + meta[:, k : k + 1] * dot(place, rows)
    folded[...] = fold(value).astype(BF16)


def moe_back_body(meta, out_rows, grad_rows, upstream, sent, value):
    grad = jnp.zeros((SEQ, PART), F32)
    lanes = iota((SEQ, 128), 1)
    tail = jnp.zeros((SEQ, 128), F32)
    for k in range(2):
        place = slot_hot(meta[:, 2 + k : 3 + k]).astype(BF16)
        grad = grad + dot(place, grad_rows)
        picked = dot(place, out_rows)
        if value is not None:
            value = value + meta[:, k : k + 1] * picked
        inner = jnp.sum(picked * upstream, axis=1, keepdims=True)
        tail = jnp.where(lanes == k, inner, tail)
    sent[:LINES] = fold(grad).astype(BF16)
    sent[LINES:] = jnp.transpose(tail)[:16].astype(BF16)
    return value


def second_back_kernel(core, meta, block, cotangent, hidden, sent, folded):
    out_rows = unpack_part(block, 0)
    grad_rows = unpack_part(block, 256)
    upstream = own_part(core[1], cotangent[core[0]].astype(F32))
    value = own_part(core[1], hidden[...])
    folded[...] = fold(moe_back_body(meta, out_rows, grad_rows, upstream, sent, value)).astype(BF16)


def first_back_kernel(core, meta, out_rows, block, upstream, sent):
    part = own_part(core[1], upstream[...].astype(F32))
    moe_back_body(meta, out_rows[...], unpack_part(block, 0), part, sent, None)


def shared_body(
    buckets, scores, inputs, gain, grad_qkv, attended, grad_low, moe_low, grad_logits, moe_gain, rel,
    shared,
):
    bucket = buckets[...]
    rel[...] = jnp.zeros_like(rel)
    for b in range(BUCKETS):
        hot = bucket == b
        for head in range(HEADS):
            at = head * BUCKETS + b
            rel[at : at + 1] = jnp.sum(jnp.where(hot, scores[head], 0.0), axis=0, keepdims=True)
    table = jnp.sum(jnp.transpose(rel[...]), axis=0, keepdims=True)
    normed = (inputs * norm(inputs) * gain).astype(BF16)
    shared[:QKV, :D] = dot_tn(grad_qkv, normed).astype(BF16)
    shared[QKV:, :D] = dot_tn(attended, grad_low).astype(BF16)
    line = iota((128, D), 0)
    wide = jnp.concatenate([table, jnp.zeros((1, D - 128), F32)], axis=1)
    rows = jnp.where(line == EXPERTS + 1, moe_gain, 0.0)
    rows = jnp.where(line == EXPERTS + 2, wide, rows)
    shared[:, D:] = (dot_tn(moe_low, grad_logits) + jnp.transpose(rows)).astype(BF16)


def shared_kernel(
    core, buckets, values, own, other, attended, moe_low, grad_hidden, scores, grad_qkv, logits,
    moe_gain, shared, rel,
):
    gain = chosen((core[0] == 1).astype(jnp.int32), own[...], other[...])
    shared_body(
        buckets, [scores[head].astype(F32) for head in range(HEADS)], values[...].astype(F32), gain,
        grad_qkv[...], attended[...], grad_hidden[...].astype(BF16), moe_low[...], logits[...],
        moe_gain[0:1], rel, shared,
    )


def attention_back_kernel(
    section, core, a, b, c, d, meta, hidden, upstream, own, other, router, router2, projected, probs,
    qkv, qkv2, out, out2, *refs,
):
    if section == 0:
        (moe_low, own_attn, other_attn, buckets, values, attended, shared1) = refs[:7]
        (sent, grad_hidden_out, mine, theirs, qkv_weight, out_weight, sems, rel, shared) = refs[7:]
    else:
        (sent, grad_hidden_out, scores_out, qkv_out, logits_out, gain_out) = refs[:6]
        (qkv_weight, out_weight, sems) = refs[6:]
    me = core[0]
    flag = (me == section).astype(jnp.int32)
    fetch(flag, qkv, qkv2, qkv_weight, sems.at[0])
    fetch(flag, out, out2, out_weight, sems.at[1])
    grad_moe = gathered(core[1], (a, b, c, d))
    tails = total((a.at[pl.ds(LINES, 16)], b.at[pl.ds(LINES, 16)], c.at[pl.ds(LINES, 16)], d.at[pl.ds(LINES, 16)]))
    tails = jnp.transpose(jnp.concatenate([tails, jnp.zeros((112, 128), F32)], axis=0))
    gain = chosen(flag, own[...], other[...])
    weight = chosen(flag, router[...].astype(F32), router2[...].astype(F32)).astype(BF16)
    gates = [meta[:, k : k + 1] for k in range(2)]
    grad_gates = [tails[:, k : k + 1] for k in range(2)]
    mean = gates[0] * grad_gates[0] + gates[1] * grad_gates[1]
    lanes = iota((SEQ, 128), 1).astype(F32)
    grad_logits = jnp.zeros((SEQ, 128), F32)
    for k in range(2):
        grad = gates[k] * (grad_gates[k] - mean)
        grad_logits = jnp.where(meta[:, 4 + k : 5 + k] == lanes, grad, grad_logits)
    grad_logits = grad_logits.astype(BF16)
    grad_moe = grad_moe + dot(grad_logits[:, :EXPERTS], weight)
    state = hidden[...]
    inverse = norm(state)
    grad_moe_gain = jnp.sum(grad_moe * state * inverse, axis=0, keepdims=True)
    before = upstream[me] if section == 1 else upstream[...]
    grad_hidden = before.astype(F32) + norm_back(state, inverse, gain, grad_moe)
    grad_hidden_out[...] = grad_hidden
    grad_low = grad_hidden.astype(BF16)
    fetched(out2, out_weight, sems.at[1])
    grad_heads = dot_nt(grad_low, out_weight[...]).astype(BF16)
    grads = []
    score_grads = []
    for head in range(HEADS):
        at = head * 3 * HEAD_DIM
        query = projected[:, at : at + HEAD_DIM]
        key = projected[:, at + HEAD_DIM : at + 2 * HEAD_DIM]
        value = projected[:, at + 2 * HEAD_DIM : at + 3 * HEAD_DIM]
        grad_head = grad_heads[:, head * HEAD_DIM : (head + 1) * HEAD_DIM]
        prob = probs[head]
        grad_probs = dot_nt(grad_head, value)
        grad_value = dot_tn(prob.astype(BF16), grad_head)
        inner = jnp.sum(prob * grad_probs, axis=-1, keepdims=True)
        grad_scores = (prob * (grad_probs - inner)).astype(BF16)
        score_grads.append(grad_scores.astype(F32))
        grads.append(SCALE * dot(grad_scores, key))
        grads.append(SCALE * dot_tn(grad_scores, query))
        grads.append(grad_value)
    grad_qkv = jnp.concatenate(grads, axis=1).astype(BF16)
    fetched(qkv2, qkv_weight, sems.at[0])
    sent[...] = dot(grad_qkv, qkv_weight[...]).astype(BF16)
    if section == 1:
        for head in range(HEADS):
            scores_out[head] = score_grads[head].astype(BF16)
        qkv_out[...] = grad_qkv
        logits_out[...] = grad_logits
        gain_out[...] = jnp.broadcast_to(grad_moe_gain, (8, D))
    else:
        attn_gain = chosen(flag, own_attn[...], other_attn[...])
        shared_body(
            buckets, score_grads, values[me].astype(F32), attn_gain, grad_qkv, attended[...],
            grad_low, moe_low[...], grad_logits, grad_moe_gain, rel, shared,
        )
    if section == 0:

        @pl.when(me == 0)
        def _():
            mine[...] = shared[...]
            theirs[...] = shared1[...]

        @pl.when(me == 1)
        def _():
            mine[...] = shared1[...]
            theirs[...] = shared[...]


def input_back_kernel(section, core, a, b, c, d, values, grad_hidden, own, other, *refs):
    if section == 1:
        meta, grad_out, low_out, sent = refs
    else:
        second, mine, theirs, grad_out = refs
    me = core[0]
    flag = (me == section).astype(jnp.int32)
    grad_normed = total((a, b, c, d))
    inputs = (values[me] if section == 0 else values[...]).astype(F32)
    inverse = norm(inputs)
    gain = chosen(flag, own[...], other[...])
    grad_inputs = grad_hidden[...] + norm_back(inputs, inverse, gain, grad_normed)
    grad_out[:SEQ] = grad_inputs
    if section == 1:
        upstream = grad_inputs.astype(BF16)
        low_out[...] = upstream
        places = [slot_hot(meta[:, 2 + k : 3 + k]) for k in range(2)]
        either = (places[0] | places[1]).astype(BF16)
        scaled = [jnp.where(places[k], meta[:, k : k + 1], 0.0) for k in range(2)]
        sent[...] = pack(sent_grads(either, scaled, upstream))
    grad_gain = jnp.sum(grad_normed * inputs * inverse, axis=0, keepdims=True)
    grad_out[SEQ:] = jnp.broadcast_to(grad_gain, (8, D))
    if section == 0:

        @pl.when(me == 0)
        def _():
            mine[...] = grad_out[...]
            theirs[...] = second[...]

        @pl.when(me == 1)
        def _():
            mine[...] = second[...]
            theirs[...] = grad_out[...]


def output_kernel(core, first, a, b, c, d, mine, theirs):
    second = gathered(core[1], (a, b, c, d)).astype(BF16)

    @pl.when(core[0] == 0)
    def _():
        mine[...] = first[...]
        theirs[...] = second

    @pl.when(core[0] == 1)
    def _():
        mine[...] = second
        theirs[...] = first[...]


def pair_kernel(mine, got, out):
    out[...] = (mine[...].astype(F32) + got[...].astype(F32)).astype(BF16)


CHUNK = D // OWNERS
SPARE = 64


def reduce_kernel(blocks, mine, got, out):
    value = blocks[0].astype(F32)
    for at in range(1, OWNERS):
        value = value + blocks[at].astype(F32)
    gain = mine[SEQ : SEQ + 1] + got[SEQ : SEQ + 1]
    columns = jnp.transpose(jnp.broadcast_to(gain, (128, D)))
    lanes = iota((CHUNK, 128), 1)
    side = value[:, D:]
    for at in range(OWNERS):
        side = jnp.where(lanes == SPARE + at, columns[at * CHUNK : (at + 1) * CHUNK], side)
    main_low, side_low = value[:, :D].astype(BF16), side.astype(BF16)
    for at in range(OWNERS):
        out[at, :, :D] = main_low
        out[at, :, D:] = side_low


def final_kernel(blocks, qkv, attn_out, router, gain_attn, gain_moe, table):
    sides = []
    gains = jnp.zeros((CHUNK, 128), F32)
    for at in range(OWNERS):
        main = blocks[at, :, :D].astype(F32)
        rows = slice(at * CHUNK, (at + 1) * CHUNK)
        if (at + 1) * CHUNK <= QKV:
            qkv[rows] = main
        else:
            attn_out[at * CHUNK - QKV : (at + 1) * CHUNK - QKV] = main
        side = blocks[at, :, D:].astype(F32)
        sides.append(side)
        gains = gains + side
    rows = jnp.transpose(jnp.concatenate(sides, axis=0))
    router[...] = rows[:EXPERTS]
    gain_moe[...] = rows[EXPERTS + 1 : EXPERTS + 2]
    line = rows[EXPERTS + 2 : EXPERTS + 3]
    for head in range(HEADS):
        table[head] = line[:, head * BUCKETS : (head + 1) * BUCKETS]
    padded = jnp.concatenate([gains, jnp.zeros((128 - CHUNK, 128), F32)], axis=0)
    spare = jnp.transpose(padded)
    pieces = [spare[SPARE + at : SPARE + at + 1, :CHUNK] for at in range(OWNERS)]
    gain_attn[...] = jnp.concatenate(pieces, axis=1)


def place_copies(core, outs, spaces, sems_in, sems_out, sources_of):
    def move(me):
        reads, writes = [], []
        for at, pair in enumerate(sources_of(me)):
            for half, source in enumerate(pair):
                room, sem = spaces[at].at[half], 2 * at + half
                reads.append(pltpu.make_async_copy(source, room, sems_in.at[sem]))
                writes.append(pltpu.make_async_copy(room, outs[at].at[half], sems_out.at[sem]))
        for copy in reads:
            copy.start()
        for read, write in zip(reads, writes):
            read.wait()
            write.start()
        for copy in writes:
            copy.wait()

    for me in range(2):

        @pl.when(core[0] == me)
        def _(me=me):
            move(me)


def place_expert_kernel(core, own0, got0, own1, got1, grad_in, grad_out, *refs):
    def sources_of(me):
        pair = (own0, got0) if me == 0 else (got1, own1)
        return [[ref.at[at] for ref in pair] for at in range(2)]

    place_copies(core, (grad_in, grad_out), refs[:2], *refs[2:], sources_of)


def place_kernel(core, act, act_got, grad, grad_got, activations, input_grad, *refs):
    rows = pl.ds(0, SEQ)

    def sources_of(me):
        pairs = [(act, act_got), (grad.at[rows], grad_got.at[rows])]
        return [pair if me == 0 else pair[::-1] for pair in pairs]

    place_copies(core, (activations, input_grad), refs[:2], *refs[2:], sources_of)


def permuted(value, axis, pairs):
    return lax.ppermute(value, axis, pairs)


def swap(value):
    return permuted(value, "pipe", [(0, 1), (1, 0)])


def down(value):
    return permuted(value, "pipe", [(1, 0)])


def up(value):
    return permuted(value, "pipe", [(0, 1)])


def spread(value):
    count = lax.axis_size("tensor")
    return [value] + [
        permuted(value, "tensor", [(i, (i + by) % count) for i in range(count)])
        for by in range(1, count)
    ]


def after(value, *others):
    return lax.optimization_barrier((value, *others))[0]


def exchange(block):
    moved = lax.all_to_all(
        block.reshape(EXPERTS, 8, block.shape[1]),
        ("pipe", "expert"),
        split_axis=0,
        concat_axis=0,
        tiled=True,
    )
    return moved.reshape(block.shape)


def collect(block):
    moved = lax.all_to_all(
        block.reshape(EXPERTS * GROUP, 8, block.shape[3]),
        ("pipe", "expert", "tensor"),
        split_axis=0,
        concat_axis=0,
        tiled=True,
    )
    return moved.reshape(block.shape)


def shards(
    tokens,
    cotangent,
    routes,
    buckets,
    gain_attn,
    w_qkv,
    w_attn_out,
    rel_table,
    gain_moe,
    w_router,
    w_expert_in,
    w_expert_out,
):
    index = lax.axis_index("pipe")
    core = jnp.stack([index, lax.axis_index("tensor")]).astype(jnp.int32)
    qkv = w_qkv[0].T
    attn_out = w_attn_out[0]
    router = w_router[0].T
    ids = jnp.transpose(routes[0], (0, 2, 1))
    qkv2 = swap(qkv)
    attn_out2 = swap(attn_out)
    tables = (rel_table[0], swap(rel_table[0]))
    attn_gains = (gain_attn, swap(gain_attn))
    moe_gains = (gain_moe, swap(gain_moe))
    router2 = swap(router)
    ids2 = swap(lax.dynamic_index_in_dim(ids, 1 - index, 0, keepdims=False))

    attn_args = (qkv, qkv2, attn_out, attn_out2)

    (bias,) = kernel_call(
        bias_kernel,
        "bias",
        (core, buckets, *tables),
        (SMEM, VMEM, VMEM, VMEM),
        (shape(2, HEADS, SEQ, SEQ),),
    )
    partial0, projected0, probs0, attended0 = kernel_call(
        first_attention_kernel,
        "first_attention",
        (core, tokens, *attn_gains, bias, *attn_args),
        (SMEM, VMEM, VMEM, VMEM, VMEM, ANY, ANY, ANY, ANY),
        ATTENTION_OUT,
        ATTENTION_SCRATCH,
    )
    parts = spread(partial0)
    expert_specs = (ANY, ANY, ANY, ANY)
    route_args = (*moe_gains, router, router2, ids, ids2)

    def route(section, values, parts, more, wide):
        return kernel_call(
            lambda *refs: route_kernel(section, *refs),
            "route",
            (core, values, *parts, *route_args, *more),
            (SMEM,) + (VMEM,) * (11 + len(more)),
            (shape(SEQ, D), low(SEQ, D), shape(SEQ, 128), low(MAIN, wide)),
        )

    hidden0, moe_low0, meta0, sent = route(0, tokens, parts, (), WIDE)
    weights = lax.optimization_barrier((w_expert_in[0], w_expert_out[0], sent))[:2]
    expert_args = (w_expert_in[0], swap(weights[0]), w_expert_out[0], swap(weights[1]))
    block = exchange(sent)
    sent, rows0, pre0 = kernel_call(
        expert_forward_kernel,
        "expert_forward",
        (core, block, *expert_args),
        (SMEM, VMEM, *expert_specs),
        (low(EXPERTS, GROUP, 8, 256), low(ROWS, D), shape(ROWS, D)),
        EXPERT_SCRATCH,
    )
    block = collect(sent)
    out_rows0, part0 = kernel_call(
        combine_kernel,
        "combine",
        (core, meta0, block, hidden0),
        (SMEM, VMEM, VMEM, VMEM),
        (low(ROWS, PART), low(LINES, 128)),
    )

    act0, partial1, projected1, probs1, attended1 = kernel_call(
        second_attention_kernel,
        "second_attention",
        (core, *spread(part0), *attn_gains, bias, *attn_args),
        (SMEM,) + (VMEM,) * 7 + (ANY,) * 4,
        (low(SEQ, D), *ATTENTION_OUT),
        ATTENTION_SCRATCH,
    )
    hidden1, moe_low1, meta1, sent = route(1, act0, spread(partial1), (cotangent,), 2 * WIDE)
    block = exchange(sent)
    sent, rows1, grads1, act_low1, grad_pre1 = kernel_call(
        expert_both_kernel,
        "expert_both",
        (core, block, *expert_args),
        (SMEM, VMEM, *expert_specs),
        (low(EXPERTS, GROUP, 8, 512), low(ROWS, D), low(ROWS, D), low(ROWS, D), low(ROWS, D)),
        EXPERT_SCRATCH,
        vmem=16,
    )
    block = collect(sent)

    sent, part1 = kernel_call(
        second_back_kernel,
        "second_back",
        (core, meta1, block, cotangent, hidden1),
        (SMEM, VMEM, VMEM, VMEM, VMEM),
        (low(LINES + 16, 128), low(LINES, 128)),
    )

    def expert_grads(*args):
        return kernel_call(
            expert_grads_kernel, "expert_grads", args, (VMEM,) * 4, (shape(2, D, D),)
        )[0]

    def attention_back(section, parts, meta, hidden, upstream, saved, more, outputs, scratch):
        return kernel_call(
            lambda *refs: attention_back_kernel(section, *refs),
            "attention_back",
            (core, *parts, meta, hidden, upstream, *moe_gains, router, router2, *saved, *attn_args)
            + more,
            (SMEM,) + (VMEM,) * 13 + (ANY,) * 4 + (VMEM,) * len(more),
            (low(SEQ, D), shape(SEQ, D), *outputs),
            ATTENTION_SCRATCH + scratch,
        )

    partial, grad_hidden1, *grads = attention_back(
        1, spread(sent), meta1, hidden1, cotangent, (projected1, probs1), (),
        (low(HEADS, SEQ, SEQ), low(SEQ, QKV), low(SEQ, 128), shape(8, D)), (),
    )
    parts = spread(partial)
    (shared1,) = kernel_call(
        shared_kernel,
        "shared",
        (core, buckets, act0, *attn_gains, attended1, moe_low1, after(grad_hidden1, parts[3]), *grads),
        (SMEM,) + (VMEM,) * 11,
        (low(D, D + 128),),
        (pltpu.VMEM((128, 128), F32),),
    )
    expert_grad1 = expert_grads(after(rows1, parts[3]), grads1, act_low1, grad_pre1)
    parts[1] = after(parts[1], shared1, expert_grad1)
    grad_inputs1, upstream, sent = kernel_call(
        lambda *refs: input_back_kernel(1, *refs),
        "input_back",
        (core, *parts, act0, grad_hidden1, *attn_gains, meta0),
        (SMEM,) + (VMEM,) * 9,
        (shape(SEQ + 8, D), low(SEQ, D), low(MAIN, WIDE)),
    )

    block = exchange(sent)
    sent, grads0, act_low0, grad_pre0 = kernel_call(
        expert_back_kernel,
        "expert_back",
        (core, block, pre0, *expert_args),
        (SMEM, VMEM, VMEM, *expert_specs),
        (low(EXPERTS, GROUP, 8, 256), low(ROWS, D), low(ROWS, D), low(ROWS, D)),
        EXPERT_SCRATCH,
    )
    block = collect(sent)
    (sent,) = kernel_call(
        first_back_kernel,
        "first_back",
        (core, meta0, out_rows0, block, upstream),
        (SMEM,) + (VMEM,) * 4,
        (low(LINES + 16, 128),),
    )
    parts = spread(sent)
    expert_grad0 = expert_grads(after(rows0, sent), grads0, act_low0, grad_pre0)
    expert_grad1 = after(expert_grad1, sent)
    expert_grad1b = up(expert_grad1)
    parts[3] = after(parts[3], expert_grad0)
    partial, grad_hidden0, mine, theirs = attention_back(
        0, parts, meta0, hidden0, upstream, (projected0, probs0),
        (moe_low0, *attn_gains, buckets, tokens, attended0, shared1),
        (low(D, D + 128), low(D, D + 128)),
        (pltpu.VMEM((128, 128), F32), pltpu.VMEM((D, D + 128), BF16)),
    )
    got = swap(theirs)
    parts = spread(partial)
    expert_grad0 = after(expert_grad0, got, expert_grad1b)
    expert_grad0b = down(expert_grad0)

    (pair,) = kernel_call(
        pair_kernel, "pair", (mine, got), (VMEM, VMEM), (low(D, D + 128),)
    )
    blocks = pair.reshape(OWNERS, CHUNK, D + 128)
    blocks = lax.all_to_all(blocks, "expert", split_axis=0, concat_axis=0, tiled=True)
    act_parts = spread(after(part1, pair))
    grad_mine, grad_theirs = kernel_call(
        lambda *refs: input_back_kernel(0, *refs),
        "input_back",
        (core, *parts, tokens, grad_hidden0, *attn_gains, grad_inputs1),
        (SMEM,) + (VMEM,) * 9,
        (shape(SEQ + 8, D), shape(SEQ + 8, D)),
        (pltpu.VMEM((SEQ + 8, D), F32),),
    )
    grad_got = swap(grad_theirs)
    def place(body, sources, results):
        return kernel_call(
            body,
            "place",
            (core, *sources),
            (SMEM,) + (ANY,) * 4,
            results,
            tuple(pltpu.VMEM(result.shape, result.dtype) for result in results)
            + (pltpu.SemaphoreType.DMA((4,)), pltpu.SemaphoreType.DMA((4,))),
            (ANY, ANY),
        )

    (blocks,) = kernel_call(
        reduce_kernel,
        "reduce",
        (blocks, grad_mine, grad_got),
        (VMEM,) * 3,
        (low(*blocks.shape),),
    )
    grad_in, grad_out = place(
        place_expert_kernel,
        (expert_grad0, expert_grad0b, expert_grad1, expert_grad1b),
        (shape(2, D, D), shape(2, D, D)),
    )
    act_mine, act_theirs = kernel_call(
        output_kernel,
        "output",
        (core, after(act0, grad_in), *act_parts),
        (SMEM,) + (VMEM,) * 5,
        (low(SEQ, D), low(SEQ, D)),
    )
    act_got = swap(act_theirs)
    blocks = lax.all_to_all(blocks, "expert", split_axis=0, concat_axis=0, tiled=True)
    activations, input_grad = place(
        place_kernel,
        (act_mine, act_got, grad_mine, grad_got),
        (low(2, SEQ, D), shape(2, SEQ, D)),
    )
    blocks = after(blocks, grad_in, grad_out, activations, input_grad)
    grad_qkv, grad_attn_out, grad_router, grad_gain, grad_moe_gain, grad_table = kernel_call(
        final_kernel,
        "final",
        (blocks,),
        (VMEM,),
        (shape(QKV, D), shape(HEAD_COLS, D), shape(EXPERTS, D), shape(1, D), shape(1, D))
        + (shape(HEADS, 1, BUCKETS),),
    )
    return (
        activations[None],
        input_grad[None],
        grad_gain,
        grad_qkv.T[None],
        grad_attn_out[None],
        jnp.transpose(grad_table, (1, 0, 2)),
        grad_moe_gain,
        grad_router.T[None],
        grad_in[None],
        grad_out[None],
    )


def solution(mesh):
    in_specs = (
        P(None, "expert", None),
        P(None, "expert", None),
        P("pipe", None, "expert", None),
        P(),
        P("pipe", None),
        P("pipe", None, "tensor"),
        P("pipe", "tensor", None),
        P("pipe", "tensor", None),
        P("pipe", None),
        P("pipe", None, None),
        P("pipe", "expert", None, "tensor"),
        P("pipe", "expert", "tensor", None),
    )
    out_specs = (
        P("pipe", None, "expert", None),
        P("pipe", None, "expert", None),
        P("pipe", None),
        P("pipe", None, "tensor"),
        P("pipe", "tensor", None),
        P("pipe", "tensor", None),
        P("pipe", None),
        P("pipe", None, None),
        P("pipe", "expert", None, "tensor"),
        P("pipe", "expert", "tensor", None),
    )
    return jax.shard_map(shards, mesh=mesh, in_specs=in_specs, out_specs=out_specs, check_vma=False)
```
